128 devices in a mesh: seq: 64 (over z, y, x), mp: 2 (over core).
Axes of the slice: x: 4, y: 4, z: 4, core: 2. Of those that a mesh axis runs over, the one named last changes fastest.
Arguments:
- tokens: bfloat16 [16384, 2048], P('seq'), may hold values from -6 to 6
- cotangent: bfloat16 [16384, 2048], P('seq'), may hold values from -6 to 6
- starts: int32 [16384], P('seq'), may hold values from 0 to 1, as said below
- valid: int32 [16384], P('seq'), may hold values 0 or 1
- w_rec: bfloat16 [2048, 2, 2560], P('seq', None, 'mp'), may hold values from -0.125 to 0.125
- w_out: bfloat16 [2560, 2048], P('mp', 'seq'), may hold values from -0.25 to 0.25
- w_mlp: bfloat16 [2048, 2, 6144], P('seq', None, 'mp'), may hold values from -0.125 to 0.125
- w_down: bfloat16 [6144, 2048], P('mp', 'seq'), may hold values from -0.15625 to 0.15625
- lru_gates: bfloat16 [2, 10, 256, 256], P(None, 'mp'), may hold values from -0.375 to 0.375
- lru_bias: float32 [2, 2560], P(None, 'mp'), may hold values from -4 to 4
- lam: float32 [2560], P('mp'), may hold values from 4 to 16
- conv_w: float32 [4, 2560], P(None, 'mp'), may hold values from -3 to 3
- conv_b: float32 [2560], P('mp'), may hold values from -2 to 2
- gain_rec: float32 [2048], replicated, may hold values from 0.1 to 1.9
- gain_mlp: float32 [2048], replicated, may hold values from 0.1 to 1.9
- h_init: float32 [2560], P('mp'), may hold values from -5 to 5
- conv_state: float32 [3, 2560], P(None, 'mp'), may hold values from -5 to 5
Outputs:
- result: bfloat16 [16384, 2048], P('seq')
- rms_rec: float32 [16384], P('seq')
- rms_mlp: float32 [16384], P('seq')
- grad_tokens: float32 [16384, 2048], P('seq')
- grad_w_rec: float32 [2048, 2, 2560], P('seq', None, 'mp')
- grad_w_out: float32 [2560, 2048], P('mp', 'seq')
- grad_w_mlp: float32 [2048, 2, 6144], P('seq', None, 'mp')
- grad_w_down: float32 [6144, 2048], P('mp', 'seq')
- grad_lru_gates: float32 [2, 10, 256, 256], P(None, 'mp')
- grad_lru_bias: float32 [2, 2560], P(None, 'mp')
- grad_lam: float32 [2560], P('mp')
- grad_conv_w: float32 [4, 2560], P(None, 'mp')
- conv_bias_gradient: float32 [2560], P('mp')
- grad_gain_rec: float32 [2048], replicated
- grad_gain_mlp: float32 [2048], replicated
- grad_h_init: float32 [2560], P('mp')
- grad_conv_state: float32 [3, 2560], P(None, 'mp')
The draws below stay inside these ranges and needn't reach their ends.
Inputs may be any that keep to these rules, and one draw needn't show every extreme that they name: `starts`: 1 at exactly two tokens: one among the first 256 tokens but not the very first, one among the last 256; 0 elsewhere.
All inputs are finite; a program needn't handle non-finite values. No bound on the sum of `valid` on one device may be relied on, other than what follows from the above.
Results may differ from the reference program's by a relative error of at most 0.018.
Values may be sent and summed in bfloat16 or wider, within the bound.
A program may use at most 448 MiB of HBM per device.

```python
import math
from functools import partial
import jax
import jax.numpy as jnp
from jax import lax

D = 2048
NBLK = 10
BLOCK = 256
FF = 6144
CONV = 4
TOK_DEV = 256
R = 2560
TOKENS = 16384


def draw_starts(key, part):
    key = jax.random.fold_in(key, 5)
    first_key, last_key = jax.random.split(key)
    first_start = jax.random.randint(first_key, (), 1, TOK_DEV)
    last_start = jax.random.randint(last_key, (), TOKENS - TOK_DEV, TOKENS)
    positions = jnp.arange(TOKENS)
    return ((positions == first_start) | (positions == last_start)).astype(jnp.int32)


def draw_lam(key, part):
    key = jax.random.fold_in(key, 9)
    pick_key, fast_key, slow_key = jax.random.split(key, 3)
    fast_share = 0.5
    chosen = jax.random.bernoulli(pick_key, fast_share, (R,))
    fast_rates = jnp.exp(jax.random.uniform(fast_key, (R,), jnp.float32, math.log(0.004), math.log(0.012)))
    slow_rates = jnp.exp(jax.random.uniform(slow_key, (R,), jnp.float32, math.log(0.03 / TOKENS), math.log(0.25 / TOKENS)))
    rates = jnp.where(chosen, fast_rates, slow_rates)
    return -jnp.log(jnp.expm1(rates))


def plant(drawn, key, low, largest):
    longest = drawn.shape.index(max(drawn.shape))
    spots = []
    for shift in (0, 1):
        where = [jax.random.randint(jax.random.fold_in(key, axis), (), 0, length) for axis, length in enumerate(drawn.shape)]
        where[longest] = (where[longest] + shift) % drawn.shape[longest]
        spots.append(tuple(where))
    return drawn.at[spots[0]].set(low).at[spots[1]].set(largest)


def level_of(stream_key, extent, shards, least, high):
    gain, own = 1.0, jax.random.fold_in(stream_key, 6)
    for position, shards_of in shards:
        steps = jnp.exp(jax.random.uniform(jax.random.fold_in(own, position), (shards_of,), jnp.float32, least / len(shards), high / len(shards)))
        gain = gain * jnp.repeat(steps, extent[position] // shards_of).reshape([-1 if axis == position else 1 for axis in range(len(extent))])
    return gain


def bell_draw(rng, shape, scale, reach, pieces=(), dtype=jnp.bfloat16):
    level = level_of(rng, shape, pieces, -0.22, 0.18) if pieces else 1.0
    values = jax.random.normal(rng, shape, jnp.float32) * scale * level
    return jnp.minimum(jnp.maximum(values, -reach), reach).astype(dtype)


def setup_inputs(seed: int = 0) -> dict:
    streams_of = jax.random.split(jax.random.key(seed), 18)
    return {
        "tokens": bell_draw(streams_of[0], (TOKENS, D), 1.0, 6.0, ((0, 64),)),
        "cotangent": bell_draw(streams_of[1], (TOKENS, D), 1.0, 6.0, ((0, 64),)),
        "starts": draw_starts(jax.random.fold_in(streams_of[17], 71), 0),
        "valid": plant((jax.random.randint(streams_of[3], (TOKENS,), 0, 8) < 7).astype(jnp.int32), jax.random.fold_in(streams_of[3], 1), 0, 1),
        "w_rec": bell_draw(streams_of[4], (D, 2, R), D ** -0.5, 0.125, ((0, 64), (2, 2))),
        "w_out": bell_draw(streams_of[5], (R, D), (R // 4) ** -0.5, 0.25, ((0, 2), (1, 64))),
        "w_mlp": bell_draw(streams_of[6], (D, 2, FF), D ** -0.5, 0.125, ((0, 64), (2, 2))),
        "w_down": bell_draw(streams_of[7], (FF, D), (FF // 4) ** -0.5, 0.15625, ((0, 2), (1, 64))),
        "lru_gates": bell_draw(streams_of[8], (2, NBLK, BLOCK, BLOCK), BLOCK ** -0.5, 0.375, ((1, 2),)),
        "lru_bias": bell_draw(streams_of[9], (2, R), 1.0, 4.0, ((1, 2),), jnp.float32),
        "lam": draw_lam(jax.random.fold_in(streams_of[17], 71), 0),
        "conv_w": bell_draw(streams_of[11], (CONV, R), CONV ** -0.5, 3.0, ((1, 2),), jnp.float32),
        "conv_b": bell_draw(streams_of[12], (R,), 0.3, 2.0, ((0, 2),), jnp.float32),
        "gain_rec": jnp.clip(1.0 + 0.18 * jax.random.normal(streams_of[13], (D,), jnp.float32), 0.1, 1.9),
        "gain_mlp": jnp.clip(1.0 + 0.18 * jax.random.normal(streams_of[14], (D,), jnp.float32), 0.1, 1.9),
        "h_init": bell_draw(streams_of[15], (R,), 1.0, 5.0, ((0, 2),), jnp.float32),
        "conv_state": bell_draw(streams_of[16], (CONV - 1, R), 1.0, 5.0, ((1, 2),), jnp.float32),
    }


EPSILON = 1e-06
HIGH = lax.Precision.HIGHEST

@jax.custom_vjp
def low(v):
    return lax.optimization_barrier(v.astype(jnp.bfloat16)).astype(jnp.float32)

@jax.custom_vjp
def low_back(v):
    return v

def low_keep(v):
    return (low(v), None)

def low_pass(kept, grad):
    return (grad,)

def back_keep(v):
    return (v, None)

def back_low(kept, grad):
    return (low(grad),)
low.defvjp(low_keep, low_pass)
low_back.defvjp(back_keep, back_low)

def rms_norm(values, scales):
    mean_sq = lax.optimization_barrier(jnp.mean(values * values, axis=-1, keepdims=True))
    return (values * lax.rsqrt(mean_sq + EPSILON) * scales, jnp.sqrt(mean_sq[:, 0] + EPSILON))

def recur_step(state, inputs):
    new_state = inputs[0] * state + inputs[1]
    return (new_state, new_state)

def forward(keep_mask, tokens, w_rec, w_out, w_mlp, w_down, lru_gates, lru_bias, lam, conv_w, conv_b, gain_rec, gain_mlp, h_init, conv_state):
    token_count = tokens.shape[0]
    normed_rec, rms_rec = rms_norm(tokens, gain_rec)
    normed_rec = low(normed_rec)
    projected = low_back(jnp.einsum('td,dkr->tkr', normed_rec, w_rec, precision=HIGH))
    gate_lin = projected[:, 0]
    rec_lin = projected[:, 1]
    conv_in = jnp.concatenate([conv_state, rec_lin], axis=0)
    mixed = conv_b + sum((conv_w[offset] * conv_in[offset:offset + token_count] for offset in range(CONV)))
    mixed = low(mixed)
    blocks = mixed.reshape(token_count, NBLK, BLOCK)
    gate_logits = jnp.einsum('tnk,gnkj->gtnj', blocks, lru_gates, precision=HIGH).reshape(2, token_count, R)
    gate_logits = low_back(gate_logits + lru_bias[:, None, :])
    reset_gate = jax.nn.sigmoid(gate_logits[0])
    input_gate = jax.nn.sigmoid(gate_logits[1])
    log_decay = -8.0 * jax.nn.softplus(-lam) * reset_gate
    decay_multipliers = jnp.exp(log_decay) * keep_mask[:, None]
    driven = jnp.sqrt(-jnp.expm1(2.0 * log_decay)) * input_gate * mixed
    final_state, states = lax.scan(recur_step, h_init, (decay_multipliers, driven))
    branch_in = low(jax.nn.gelu(gate_lin) * states)
    hidden = tokens + low_back(jnp.dot(branch_in, w_out, precision=HIGH))
    normed_mlp, rms_mlp = rms_norm(hidden, gain_mlp)
    normed_mlp = low(normed_mlp)
    gate_up = low_back(jnp.einsum('td,dkf->tkf', normed_mlp, w_mlp, precision=HIGH))
    mlp_in = low(jax.nn.gelu(gate_up[:, 0]) * gate_up[:, 1])
    result = hidden + low_back(jnp.dot(mlp_in, w_down, precision=HIGH))
    return (result, (rms_rec, rms_mlp))

def reference(tokens, cotangent, starts, valid, w_rec, w_out, w_mlp, w_down, lru_gates, lru_bias, lam, conv_w, conv_b, gain_rec, gain_mlp, h_init, conv_state):
    keep_mask = (1 - starts).astype(jnp.float32)
    primals = tuple((array.astype(jnp.float32) for array in (tokens, w_rec, w_out, w_mlp, w_down, lru_gates, lru_bias, lam, conv_w, conv_b, gain_rec, gain_mlp, h_init, conv_state)))
    result, pull_back, stats = jax.vjp(partial(forward, keep_mask), *primals, has_aux=True)
    grads = pull_back(cotangent.astype(jnp.float32) * valid.astype(jnp.float32)[:, None])
    return (result.astype(jnp.bfloat16), stats[0], stats[1], grads[0], grads[1], grads[2], grads[3], grads[4], grads[5], grads[6], grads[7], grads[8], grads[9], grads[10], grads[11], grads[12], grads[13])
```

```python
import functools
import jax
import jax.numpy as jnp
from jax import lax
from jax.experimental import pallas as pl
from jax.experimental.pallas import tpu as pltpu
from jax.sharding import Mesh, PartitionSpec as P

CONV = 4
EDGE = CONV - 1
EPSILON = 1e-06
MESH = pl.DeviceIdType.MESH
ANY = pl.BlockSpec(memory_space=pl.ANY)
VM = pl.BlockSpec(memory_space=pltpu.VMEM)
MIB = 1024 * 1024
AXES = ("z", "y", "x")
SEQ = ("z", "y", "x")
ORDERS = (("x", "y", "z"), ("y", "z", "x"), ("z", "x", "y"))
F32, BF16 = jnp.float32, jnp.bfloat16
DMA = pltpu.SemaphoreType.DMA


def greet(peers):
    sem = pltpu.get_barrier_semaphore()
    for peer in peers:
        pl.semaphore_signal(sem, inc=1, device_id=peer, device_id_type=MESH)
    pl.semaphore_wait(sem, len(peers))


def push(src, dst, send, recv, peer):
    return pltpu.make_async_remote_copy(
        src_ref=src, dst_ref=dst, send_sem=send, recv_sem=recv, device_id=peer, device_id_type=MESH
    )


def ring(axis):
    me = lax.axis_index(axis)
    return me, lax.rem(me + 1, 4), lax.rem(me + 2, 4), lax.rem(me + 3, 4)


def all_neighbours():
    peers = []
    for axis in AXES:
        _, up, _, down = ring(axis)
        peers += [{axis: up}, {axis: down}]
    return peers


def params(cid, mib):
    return pltpu.CompilerParams(
        collective_id=cid, has_side_effects=True, vmem_limit_bytes=mib * MIB
    )


def part_of(done, axis, index, rows, cols):
    spot = []
    for name in AXES:
        if name in done:
            spot.append(pl.ds(0, 4))
        elif name == axis:
            spot.append(index)
        else:
            spot.append(lax.axis_index(name))
    return tuple(spot) + (rows, cols)


def torus_gather_kernel(count, chunks, *refs):
    ins, outs = refs[:count], refs[count : 2 * count]
    send_sem, recv_sem, own_sem = refs[2 * count :]
    rows = ins[0].shape[0]
    half = rows // 2
    every, top, low = pl.ds(0, rows), pl.ds(0, half), pl.ds(half, half)
    greet(all_neighbours())
    entries = []
    for chunk in range(chunks):
        for a in range(count):
            width = ins[a].shape[1] // chunks
            entries.append((a, pl.ds(chunk * width, width), ORDERS[a % 3]))
    mine = []
    for a in range(count):
        spot = part_of((), "x", lax.axis_index("x"), every, pl.ds(0, ins[a].shape[1]))
        copy = pltpu.make_async_copy(ins[a], outs[a].at[spot], own_sem.at[a])
        copy.start()
        mine.append(copy)
    ended = []
    for phase in range(3):
        first = []
        for e, (a, cols, order) in enumerate(entries):
            axis, done = order[phase], order[:phase]
            me, up, _, down = ring(axis)
            spot = outs[a].at[part_of(done, axis, me, every, cols)]
            source = ins[a].at[every, cols] if phase == 0 else spot
            if phase > 0:
                for copy in ended[e]:
                    copy.wait()
            pair = []
            for way, peer in enumerate((up, down)):
                copy = push(
                    source,
                    spot,
                    send_sem.at[e, phase, 0, way],
                    recv_sem.at[e, phase, 0, way],
                    {axis: peer},
                )
                copy.start()
                pair.append(copy)
            first.append(pair)
        second = []
        for e, (a, cols, order) in enumerate(entries):
            axis, done = order[phase], order[:phase]
            me, up, _, down = ring(axis)
            pair = []
            for way, (peer, origin, piece) in enumerate(((up, down, top), (down, up, low))):
                first[e][way].wait_recv()
                spot = outs[a].at[part_of(done, axis, origin, piece, cols)]
                copy = push(
                    spot,
                    spot,
                    send_sem.at[e, phase, 1, way],
                    recv_sem.at[e, phase, 1, way],
                    {axis: peer},
                )
                copy.start()
                pair.append(copy)
            second.append(pair)
        for e in range(len(entries)):
            for way in range(2):
                first[e][way].wait_send()
        ended = second
        if phase == 0:
            for copy in mine:
                copy.wait()
    for pair in ended:
        for copy in pair:
            copy.wait()


def torus_gather(parts, cid, chunks=1):
    count = len(parts)
    outs = pl.pallas_call(
        functools.partial(torus_gather_kernel, count, chunks),
        out_shape=[jax.ShapeDtypeStruct((4, 4, 4) + p.shape, p.dtype) for p in parts],
        in_specs=[ANY] * count,
        out_specs=[ANY] * count,
        scratch_shapes=[
            DMA((count * chunks, 3, 2, 2)),
            DMA((count * chunks, 3, 2, 2)),
            DMA((count,)),
        ],
        compiler_params=params(cid, 16),
    )(*parts)
    return [o.reshape(64 * o.shape[3], o.shape[4]) for o in outs]


def pick(names, axis, index, others):
    spot, rest = [], iter(others)
    for name in names:
        spot.append(index if name == axis else next(rest))
    return tuple(spot)


def torus_scatter_kernel(count, *refs):
    ins, outs = refs[:count], refs[count : 2 * count]
    bufs = refs[2 * count : 2 * count + 8 * count]
    send_sem, recv_sem = refs[10 * count :]
    greet(all_neighbours())
    rows = ins[0].shape[3]
    half = rows // 2
    top, low = pl.ds(0, half), pl.ds(half, half)
    halves = (top, low)
    left = [AXES] * count
    source = list(ins)
    sent = []
    for phase in range(3):
        full = (pl.ds(0, 4),) * (2 - phase)
        tiles = 4 ** (2 - phase)
        ones = [bufs[8 * a + 3 * phase] for a in range(count)]
        twos = [bufs[8 * a + 3 * phase + 1] for a in range(count)]
        accs = [bufs[8 * a + 3 * phase + 2] if phase < 2 else outs[a] for a in range(count)]

        def spread(i):
            return (i // 4, lax.rem(i, 4)) if phase == 0 else ((i,) if phase == 1 else ())

        first, second, axes = [], [], []
        for a in range(count):
            axis = ORDERS[a % 3][phase]
            axes.append(axis)
            me, up, far, down = ring(axis)
            pair, direct = [], []
            for way, peer in enumerate((up, down)):
                mine, theirs = halves[way], halves[1 - way]
                k = (a, phase, way)
                copy = push(
                    source[a].at[pick(left[a], axis, far, full) + (mine,)],
                    ones[a].at[way],
                    send_sem.at[k + (0,)],
                    recv_sem.at[k + (0,)],
                    {axis: peer},
                )
                copy.start()
                pair.append(copy)
                copy = push(
                    source[a].at[pick(left[a], axis, peer, full) + (theirs,)],
                    twos[a].at[(way,) + full + (theirs,)],
                    send_sem.at[k + (1,)],
                    recv_sem.at[k + (1,)],
                    {axis: peer},
                )
                copy.start()
                direct.append(copy)
            first.append(pair)
            second.append(direct)
        for a in range(count):
            axis = axes[a]
            me, up, far, down = ring(axis)
            for way, peer in enumerate((up, down)):
                first[a][way].wait_recv()

                def add(i, carry, a=a, way=way, peer=peer, axis=axis):
                    there = (way,) + spread(i)
                    own = source[a][pick(left[a], axis, peer, spread(i)) + (halves[way],)]
                    total = ones[a][there].astype(F32) + own.astype(F32)
                    ones[a][there] = total.astype(BF16)
                    return carry

                lax.fori_loop(0, tiles, add, 0)
                k = (a, phase, way)
                copy = push(
                    ones[a].at[way],
                    twos[a].at[(way,) + full + (halves[way],)],
                    send_sem.at[k + (2,)],
                    recv_sem.at[k + (2,)],
                    {axis: peer},
                )
                copy.start()
                second[a].append(copy)
        for a in range(count):
            axis = axes[a]
            me, up, far, down = ring(axis)
            for copy in second[a]:
                copy.wait_recv()

            def total(i, carry, a=a, me=me, axis=axis):
                own = source[a][pick(left[a], axis, me, spread(i))].astype(F32)
                whole = own + twos[a][(0,) + spread(i)].astype(F32)
                whole = whole + twos[a][(1,) + spread(i)].astype(F32)
                accs[a][spread(i) + (slice(None), slice(None))] = whole.astype(accs[a].dtype)
                return carry

            lax.fori_loop(0, tiles, total, 0)
            sent += first[a] + second[a]
        source = accs
        left = [tuple(n for n in left[a] if n != axes[a]) for a in range(count)]
    for copy in sent:
        copy.wait_send()


def torus_scatter(parts, cid):
    count = len(parts)
    rows = parts[0].shape[0] // 64
    scratch = []
    for part in parts:
        width = part.shape[1]
        for phase in range(3):
            cube = (4,) * (2 - phase)
            scratch.append(pltpu.VMEM((2,) + cube + (rows // 2, width), BF16))
            scratch.append(pltpu.VMEM((2,) + cube + (rows, width), BF16))
            if phase < 2:
                scratch.append(pltpu.VMEM(cube + (rows, width), BF16))
    return pl.pallas_call(
        functools.partial(torus_scatter_kernel, count),
        out_shape=[jax.ShapeDtypeStruct((rows, p.shape[1]), F32) for p in parts],
        in_specs=[VM] * count,
        out_specs=[VM] * count,
        scratch_shapes=scratch + [DMA((count, 3, 2, 3)), DMA((count, 3, 2, 3))],
        compiler_params=params(cid, 56),
    )(*[p.reshape(4, 4, 4, rows, p.shape[1]) for p in parts])


def group_gather_kernel(in_ref, out_ref, send_sem, recv_sem, sib_send, sib_recv, own_sem):
    half = in_ref.shape[0] // 2
    me, up, far, down = ring("x")
    core = lax.axis_index("mp")
    other = {"mp": 1 - core}
    greet([{"x": up}, {"x": down}, other])
    top, low = pl.ds(0, half), pl.ds(half, half)
    spot = out_ref.at[me, core]
    mine = pltpu.make_async_copy(in_ref, spot, own_sem)
    mine.start()
    first = []
    for way, peer in enumerate((up, down)):
        copy = push(in_ref, spot, send_sem.at[0, way], recv_sem.at[0, way], {"x": peer})
        copy.start()
        first.append(copy)
    across = [push(in_ref, spot, sib_send.at[0], sib_recv.at[0], other)]
    across[0].start()
    second = []
    for way, (peer, origin, piece) in enumerate(((up, down, top), (down, up, low))):
        first[way].wait_recv()
        spot = out_ref.at[origin, core, piece]
        copy = push(spot, spot, send_sem.at[1, way], recv_sem.at[1, way], {"x": peer})
        copy.start()
        second.append(copy)
        whole = out_ref.at[origin, core]
        copy = push(whole, whole, sib_send.at[1 + way], sib_recv.at[1 + way], other)
        copy.start()
        across.append(copy)
    for way, piece in enumerate((top, low)):
        second[way].wait_recv()
        spot = out_ref.at[far, core, piece]
        copy = push(spot, spot, sib_send.at[3 + way], sib_recv.at[3 + way], other)
        copy.start()
        across.append(copy)
    for copy in first + second:
        copy.wait_send()
    for copy in across:
        copy.wait()
    mine.wait()


def group_gather(block, cid):
    rows, width = block.shape
    return pl.pallas_call(
        group_gather_kernel,
        out_shape=jax.ShapeDtypeStruct((4, 2, rows, width), block.dtype),
        in_specs=[VM],
        out_specs=VM,
        scratch_shapes=[DMA((2, 2)), DMA((2, 2)), DMA((5,)), DMA((5,)), DMA],
        compiler_params=params(cid, 32),
    )(block).reshape(8 * rows, width)


def group_scatter_kernel(in_ref, out_ref, got, one, two, send_sem, recv_sem, sib_send, sib_recv):
    rows = in_ref.shape[2]
    half = rows // 2
    me, up, far, down = ring("x")
    core = lax.axis_index("mp")
    other = {"mp": 1 - core}
    greet([{"x": up}, {"x": down}, other])
    across = []
    for k, chip in enumerate((far, up, down, me)):
        copy = push(in_ref.at[chip, 1 - core], got.at[chip], sib_send.at[k], sib_recv.at[k], other)
        copy.start()
        across.append(copy)

    def add(dst, src):
        dst[...] = (dst[...].astype(F32) + src[...].astype(F32)).astype(dst.dtype)

    across[0].wait_recv()
    add(got.at[far], in_ref.at[far, core])
    first = []
    for way, peer in enumerate((up, down)):
        copy = push(
            got.at[far, pl.ds(way * half, half)],
            one.at[way],
            send_sem.at[0, way],
            recv_sem.at[0, way],
            {"x": peer},
        )
        copy.start()
        first.append(copy)
    second = []
    for way, peer in enumerate((up, down)):
        across[1 + way].wait_recv()
        add(got.at[peer], in_ref.at[peer, core])
        first[way].wait_recv()
        add(got.at[peer, pl.ds(way * half, half)], one.at[way])
        copy = push(got.at[peer], two.at[way], send_sem.at[1, way], recv_sem.at[1, way], {"x": peer})
        copy.start()
        second.append(copy)
    across[3].wait_recv()
    out_ref[...] = got[me].astype(F32) + in_ref[me, core].astype(F32)
    for way in range(2):
        second[way].wait_recv()
        out_ref[...] += two[way].astype(F32)
    for copy in across + first + second:
        copy.wait_send()


def group_scatter(partial, cid):
    total, width = partial.shape
    rows = total // 8
    return pl.pallas_call(
        group_scatter_kernel,
        out_shape=jax.ShapeDtypeStruct((rows, width), F32),
        in_specs=[VM],
        out_specs=VM,
        scratch_shapes=[
            pltpu.VMEM((4, rows, width), partial.dtype),
            pltpu.VMEM((2, rows // 2, width), partial.dtype),
            pltpu.VMEM((2, rows, width), partial.dtype),
            DMA((2, 2)),
            DMA((2, 2)),
            DMA((4,)),
            DMA((4,)),
        ],
        compiler_params=params(cid, 40),
    )(partial.reshape(4, 2, rows, width))


def swap_kernel(count, *refs):
    ins, outs = refs[:count], refs[count : 2 * count]
    send_sem, recv_sem = refs[2 * count :]
    other = {"mp": 1 - lax.axis_index("mp")}
    greet([other])
    copies = [push(ins[k], outs[k], send_sem.at[k], recv_sem.at[k], other) for k in range(count)]
    for copy in copies:
        copy.start()
    for copy in copies:
        copy.wait()


def swap(blocks, cid):
    count = len(blocks)
    return pl.pallas_call(
        functools.partial(swap_kernel, count),
        out_shape=[jax.ShapeDtypeStruct(b.shape, b.dtype) for b in blocks],
        in_specs=[VM] * count,
        out_specs=[VM] * count,
        scratch_shapes=[DMA((count,)), DMA((count,))],
        compiler_params=params(cid, 32),
    )(*blocks)


def exchange_kernel(in_ref, out_ref, send_sem, recv_sem, own_sem):
    me = lax.axis_index("x")
    peers = ring("x")[1:]
    greet([{"x": peer} for peer in peers])
    mine = pltpu.make_async_copy(in_ref.at[me], out_ref.at[me], own_sem)
    mine.start()
    copies = []
    for k, peer in enumerate(peers):
        copy = push(in_ref.at[peer], out_ref.at[me], send_sem.at[k], recv_sem.at[k], {"x": peer})
        copy.start()
        copies.append(copy)
    for copy in copies:
        copy.wait()
    mine.wait()


def exchange(block, cid):
    return pl.pallas_call(
        exchange_kernel,
        out_shape=jax.ShapeDtypeStruct(block.shape, block.dtype),
        in_specs=[VM],
        out_specs=VM,
        scratch_shapes=[DMA((3,)), DMA((3,)), DMA],
        compiler_params=params(cid, 16),
    )(block)


def prefix_kernel(backward, in_ref, out_ref, slots, send_sem, recv_sem):
    axes = ("x", "y", "z")
    greet([{axis: ring(axis)[step]} for axis in axes for step in (1, 2, 3)])
    cur = (in_ref[0:1], in_ref[1:2])
    head = None
    for k, axis in enumerate(axes):
        me = lax.axis_index(axis)
        slots[k, me, 0:1] = cur[0]
        slots[k, me, 1:2] = cur[1]
        copies = []
        for step in (1, 2, 3):
            spot = slots.at[k, me]
            copy = push(
                spot,
                spot,
                send_sem.at[k, step - 1],
                recv_sem.at[k, step - 1],
                {axis: ring(axis)[step]},
            )
            copy.start()
            copies.append(copy)
        for copy in copies:
            copy.wait()
        run = (jnp.ones_like(cur[0]), jnp.zeros_like(cur[1]))
        mine = run
        for j in (3, 2, 1, 0) if backward else (0, 1, 2, 3):
            take = me == j
            mine = (jnp.where(take, run[0], mine[0]), jnp.where(take, run[1], mine[1]))
            fac, val = slots[k, j, 0:1], slots[k, j, 1:2]
            run = (run[0] * fac, val + fac * run[1])
        cur = run
        head = mine if head is None else (mine[0] * head[0], head[1] + head[0] * mine[1])
    out_ref[0:1] = head[0]
    out_ref[1:2] = head[1]


def prefix(pair, cid, backward):
    return pl.pallas_call(
        functools.partial(prefix_kernel, backward),
        out_shape=jax.ShapeDtypeStruct(pair.shape, pair.dtype),
        in_specs=[VM],
        out_specs=VM,
        scratch_shapes=[pltpu.VMEM((3, 4) + pair.shape, pair.dtype), DMA((3, 3)), DMA((3, 3))],
        compiler_params=params(cid, 16),
    )(pair)


def small_sum_kernel(in_ref, out_ref, slots, send_sem, recv_sem):
    axes = ("x", "y", "z")
    greet([{axis: ring(axis)[step]} for axis in axes for step in (1, 2, 3)])
    cur = in_ref[...]
    for k, axis in enumerate(axes):
        me = lax.axis_index(axis)
        slots[k, me] = cur
        copies = []
        for step in (1, 2, 3):
            spot = slots.at[k, me]
            copy = push(
                spot,
                spot,
                send_sem.at[k, step - 1],
                recv_sem.at[k, step - 1],
                {axis: ring(axis)[step]},
            )
            copy.start()
            copies.append(copy)
        for copy in copies:
            copy.wait()
        cur = (slots[k, 0] + slots[k, 1]) + (slots[k, 2] + slots[k, 3])
    out_ref[...] = cur


def small_sum(values, cid):
    return pl.pallas_call(
        small_sum_kernel,
        out_shape=jax.ShapeDtypeStruct(values.shape, values.dtype),
        in_specs=[VM],
        out_specs=VM,
        scratch_shapes=[pltpu.VMEM((3, 4) + values.shape, values.dtype), DMA((3, 3)), DMA((3, 3))],
        compiler_params=params(cid, 16),
    )(values)


def scan_kernel(f_ref, d_ref, cf_ref, cd_ref):
    rows, width = f_ref.shape

    def group(i, carry):
        base = pl.multiple_of(i * 8, 8)
        f, d = f_ref[pl.ds(base, 8)], d_ref[pl.ds(base, 8)]
        cf, cd = carry
        cfs, cds = [], []
        for r in range(8):
            cf = cf * f[r : r + 1]
            cd = cd * f[r : r + 1] + d[r : r + 1]
            cfs.append(cf)
            cds.append(cd)
        cf_ref[pl.ds(base, 8)] = jnp.concatenate(cfs, axis=0)
        cd_ref[pl.ds(base, 8)] = jnp.concatenate(cds, axis=0)
        return cf, cd

    zero = jnp.zeros((1, width), F32)
    lax.fori_loop(0, rows // 8, group, (zero + 1.0, zero))


def scan_back_kernel(f_ref, d_ref, cf_ref, cd_ref):
    rows, width = f_ref.shape

    def group(i, carry):
        base = pl.multiple_of(rows - 8 - i * 8, 8)
        f, d = f_ref[pl.ds(base, 8)], d_ref[pl.ds(base, 8)]
        follow, cf, cd = carry
        cfs, cds = [None] * 8, [None] * 8
        for r in (7, 6, 5, 4, 3, 2, 1, 0):
            cf = cf * follow
            cd = cd * follow + d[r : r + 1]
            cfs[r], cds[r] = cf, cd
            follow = f[r : r + 1]
        cf_ref[pl.ds(base, 8)] = jnp.concatenate(cfs, axis=0)
        cd_ref[pl.ds(base, 8)] = jnp.concatenate(cds, axis=0)
        return follow, cf, cd

    zero = jnp.zeros((1, width), F32)
    lax.fori_loop(0, rows // 8, group, (zero + 1.0, zero + 1.0, zero))


def local_scan(factors, values, backward):
    rows, width = factors.shape
    block = 256
    spec = pl.BlockSpec((rows, block), lambda i: (0, i))
    return pl.pallas_call(
        scan_back_kernel if backward else scan_kernel,
        out_shape=[jax.ShapeDtypeStruct((rows, width), F32)] * 2,
        grid=(width // block,),
        in_specs=[spec, spec],
        out_specs=[spec, spec],
    )(factors, values)


def rms_norm(values):
    mean_sq = jnp.mean(values * values, axis=-1, keepdims=True)
    inverse = lax.rsqrt(mean_sq + EPSILON)
    return values * inverse, inverse, jnp.sqrt(mean_sq[:, 0] + EPSILON)


def rms_back(grad_normed, normed, inverse, scales):
    grad_hat = grad_normed * scales
    inner_mean = jnp.mean(grad_hat * normed, axis=-1, keepdims=True)
    return inverse * (grad_hat - normed * inner_mean), jnp.sum(grad_normed * normed, axis=0)


def dot(left, right):
    return jnp.dot(left, right, preferred_element_type=F32)


def dot_t(left, right):
    return lax.dot_general(left, right, (((1,), (1,)), ((), ())), preferred_element_type=F32)


def outer(left, right):
    return lax.dot_general(left, right, (((0,), (0,)), ((), ())), preferred_element_type=F32)


def whole(half, theirs, core):
    first = jnp.where(core == 0, half, theirs)
    second = jnp.where(core == 0, theirs, half)
    return jnp.concatenate([first, second], axis=0)


def body(
    tokens,
    cotangent,
    starts,
    valid,
    w_rec,
    w_out,
    w_mlp,
    w_down,
    lru_gates,
    lru_bias,
    lam,
    conv_w,
    conv_b,
    gain_rec,
    gain_mlp,
    h_init,
    conv_state,
):
    count, width = tokens.shape
    shard, _, rec = w_rec.shape
    hidden_units = w_mlp.shape[2] // 4
    blocks, size = lru_gates.shape[1], lru_gates.shape[3]
    half = count // 2
    core = lax.axis_index("mp")
    here = lax.axis_index(SEQ)
    is_first = here == 0

    def my_half(array):
        return lax.dynamic_slice_in_dim(array, core * half, half, axis=0)

    def their_half(array):
        return lax.dynamic_slice_in_dim(array, (1 - core) * half, half, axis=0)

    down_t = w_down.T
    quarters = jnp.stack([w_mlp[:, 0], w_mlp[:, 1], down_t], axis=1)
    quarters = quarters.reshape(shard, 3, 4, hidden_units).transpose(2, 0, 1, 3)
    quarters = exchange(quarters.reshape(4, shard, 3 * hidden_units), 0)
    mlp_weights = lax.all_gather(
        quarters.reshape(4 * shard, 3 * hidden_units), ("z", "y"), axis=0, tiled=True
    )
    grad_out = my_half(cotangent).astype(F32) * my_half(valid).astype(F32)[:, None]
    grad_out_all = lax.all_gather(grad_out.astype(BF16), ("x", "mp"), axis=0, tiled=True)
    tail = lax.ppermute(tokens[count - 16 :], SEQ, [(i, (i + 1) % 64) for i in range(64)])

    w_gate, w_lin, w_back = torus_gather([w_rec[:, 0], w_rec[:, 1], w_out.T], 1, 2)

    tokens_wide = tokens.astype(F32)
    hat_rec, inverse_rec, rms_rec = rms_norm(tokens_wide)
    normed_rec = (hat_rec * gain_rec).astype(BF16)
    tail_normed = (rms_norm(tail.astype(F32))[0] * gain_rec).astype(BF16)
    gate_lin = dot(normed_rec, w_gate)
    rec_ext = dot(jnp.concatenate([tail_normed, normed_rec], axis=0), w_lin)
    rec_lin = rec_ext[16:]
    before = jnp.where(is_first, conv_state, rec_ext[16 - EDGE : 16])
    conv_in = jnp.concatenate([before, rec_lin], axis=0)
    conv_out = conv_b + sum(
        (conv_w[offset] * conv_in[offset : offset + count] for offset in range(CONV))
    )
    mixed_in = conv_out.astype(BF16)
    mixed_blocks = mixed_in.reshape(count, blocks, size)
    gate_logits = jnp.einsum("tnk,gnkj->gtnj", mixed_blocks, lru_gates, preferred_element_type=F32)
    gate_logits = gate_logits.reshape(2, count, rec) + lru_bias[:, None, :]
    reset_gate = jax.nn.sigmoid(gate_logits[0])
    input_gate = jax.nn.sigmoid(gate_logits[1])
    rates = jax.nn.softplus(-lam)
    log_decay = -8.0 * rates * reset_gate
    decays = jnp.exp(log_decay)
    scale_in = jnp.sqrt(-jnp.expm1(2.0 * log_decay))
    mixed_wide = mixed_in.astype(F32)
    driven = scale_in * input_gate * mixed_wide
    keep_mask = (1 - starts).astype(F32)[:, None]
    factors = decays * keep_mask
    cum_factor, cum_state = local_scan(factors, driven, False)
    pair = prefix(jnp.concatenate([cum_factor[-1:], cum_state[-1:]], axis=0), 2, False)
    carry_in = pair[1] + pair[0] * h_init
    states = cum_state + cum_factor * carry_in[None, :]
    gate_act, gate_pull = jax.vjp(jax.nn.gelu, gate_lin)
    branch_in = (gate_act * states).astype(BF16)

    out_part = dot_t(branch_in, w_back)
    (out_theirs,) = swap([their_half(out_part).astype(BF16)], 3)
    hidden = my_half(tokens_wide) + (my_half(out_part) + out_theirs.astype(F32))
    hat_mlp, inverse_mlp, rms_half = rms_norm(hidden)
    normed_mlp = (hat_mlp * gain_mlp).astype(BF16)
    normed_all = group_gather(normed_mlp, 4)
    gate_up = dot(normed_all, mlp_weights[:, : 2 * hidden_units])
    up_lin = gate_up[:, hidden_units:]
    mlp_act, mlp_pull = jax.vjp(jax.nn.gelu, gate_up[:, :hidden_units])
    mlp_in = (mlp_act * up_lin).astype(BF16)
    w_down_t = mlp_weights[:, 2 * hidden_units :]
    mlp_out = group_scatter(dot_t(mlp_in, w_down_t).astype(BF16), 5)
    result_half = (hidden + mlp_out).astype(BF16)

    grad_mlp_in = dot(grad_out_all, w_down_t)
    grad_gate = mlp_pull(grad_mlp_in * up_lin)[0]
    grad_up = grad_mlp_in * mlp_act
    grad_gate_up = jnp.concatenate([grad_gate, grad_up], axis=1).astype(BF16)
    normed_part = dot_t(grad_gate_up, mlp_weights[:, : 2 * hidden_units])
    grad_normed_mlp = group_scatter(normed_part.astype(BF16), 6)
    mlp_terms = jnp.concatenate(
        [outer(normed_all, grad_gate_up), outer(grad_out_all, mlp_in)], axis=1
    ).astype(BF16)
    mlp_sums = lax.psum_scatter(mlp_terms, ("z", "y"), scatter_dimension=0, tiled=True)
    grad_hidden_norm, gain_mlp_term = rms_back(grad_normed_mlp, hat_mlp, inverse_mlp, gain_mlp)
    grad_hidden = grad_out + grad_hidden_norm
    result_theirs, rms_theirs, low_theirs = swap(
        [
            result_half,
            jnp.broadcast_to(rms_half[None, :], (8, half)),
            grad_hidden.astype(BF16),
        ],
        7,
    )
    result = whole(result_half, result_theirs, core)
    rms_mlp = whole(rms_half, rms_theirs[0], core)
    grad_hidden_low = whole(grad_hidden.astype(BF16), low_theirs, core)

    grad_branch = dot(grad_hidden_low, w_back)
    grad_gate_lin = gate_pull(grad_branch * states)[0]
    grad_states = grad_branch * gate_act
    cum_back, adjoint_local = local_scan(factors, grad_states, True)
    pair = jnp.stack([factors[0] * cum_back[0], factors[0] * adjoint_local[0]])
    later = prefix(pair, 8, True)[1]
    adjoint = adjoint_local + cum_back * later[None, :]
    grad_h_term = jnp.where(is_first, factors[0] * adjoint[0], 0.0)
    prev_states = jnp.concatenate([carry_in[None, :], states[:-1]], axis=0)
    grad_scale = adjoint * input_gate * mixed_wide
    grad_input_gate = adjoint * scale_in * mixed_wide
    grad_log = adjoint * prev_states * keep_mask * decays - grad_scale * decays * decays / scale_in
    grad_lam = jnp.sum(grad_log * 8.0 * reset_gate, axis=0) * jax.nn.sigmoid(-lam)
    grad_logits = jnp.stack(
        [
            grad_log * (-8.0 * rates) * reset_gate * (1.0 - reset_gate),
            grad_input_gate * input_gate * (1.0 - input_gate),
        ],
        axis=0,
    ).astype(BF16)
    grad_bias = jnp.sum(grad_logits.astype(F32), axis=1)
    grad_blocks = grad_logits.reshape(2, count, blocks, size)
    grad_gates = jnp.einsum("tnk,gtnj->gnkj", mixed_blocks, grad_blocks, preferred_element_type=F32)
    grad_mixed = adjoint * scale_in * input_gate
    grad_mixed = grad_mixed + jnp.einsum(
        "gtnj,gnkj->tnk", grad_blocks, lru_gates, preferred_element_type=F32
    ).reshape(count, rec)
    conv_bias_gradient = jnp.sum(grad_mixed, axis=0)
    grad_conv_w = jnp.stack(
        [jnp.sum(grad_mixed * conv_in[k : k + count], axis=0) for k in range(CONV)], axis=0
    )
    grad_conv_in = jnp.zeros((count + EDGE, rec), F32)
    for offset in range(CONV):
        grad_conv_in = grad_conv_in + jnp.pad(
            conv_w[offset] * grad_mixed, ((offset, EDGE - offset), (0, 0))
        )
    edge_back = lax.ppermute(grad_conv_in[:EDGE], SEQ, [(i + 1, i) for i in range(63)])
    grad_rec_lin = grad_conv_in[EDGE:] + jnp.pad(edge_back, ((count - EDGE, 0), (0, 0)))
    conv_state_term = jnp.where(is_first, grad_conv_in[:EDGE], 0.0)
    grad_gate_low, grad_rec_low = grad_gate_lin.astype(BF16), grad_rec_lin.astype(BF16)
    normed_part = dot_t(grad_gate_low, w_gate) + dot_t(grad_rec_low, w_lin)
    (part_theirs,) = swap([their_half(normed_part).astype(BF16)], 9)
    grad_normed_rec = my_half(normed_part) + part_theirs.astype(F32)
    token_norm_gradient, gain_rec_term = rms_back(
        grad_normed_rec, my_half(hat_rec), my_half(inverse_rec), gain_rec
    )
    tokens_half = grad_hidden + token_norm_gradient
    (tokens_theirs,) = swap([tokens_half], 10)
    grad_tokens = whole(tokens_half, tokens_theirs, core)

    gate_terms = grad_gates.astype(BF16).reshape(64 * shard, -1)
    gate_terms = jnp.pad(gate_terms, ((0, 0), (0, 3 * 128 - gate_terms.shape[1])))
    sums = torus_scatter(
        [
            outer(normed_rec, grad_gate_low).astype(BF16),
            outer(normed_rec, grad_rec_low).astype(BF16),
            outer(grad_hidden_low, branch_in).astype(BF16),
            gate_terms[:, :128],
            gate_terms[:, 128:256],
            gate_terms[:, 256:],
        ],
        11,
    )
    grad_w_rec = jnp.stack([sums[0], sums[1]], axis=1)
    grad_w_out = sums[2].T
    gate_sums = jnp.concatenate(torus_gather(sums[3:], 12), axis=1)[:, : grad_gates.size // (64 * shard)]
    grad_gates = gate_sums.reshape(grad_gates.shape)

    mlp_sums = exchange(mlp_sums.astype(F32).reshape(4, shard, 3 * hidden_units), 13)
    mlp_sums = mlp_sums.reshape(4, shard, 3, hidden_units).transpose(1, 2, 0, 3)
    mlp_sums = mlp_sums.reshape(shard, 3, 4 * hidden_units)
    grad_w_mlp = mlp_sums[:, :2]
    grad_w_down = mlp_sums[:, 2].T

    pieces = (
        grad_bias,
        grad_lam,
        grad_conv_w,
        conv_bias_gradient,
        grad_h_term,
        conv_state_term,
        gain_rec_term,
        gain_mlp_term,
    )
    flat = jnp.concatenate([p.reshape(-1, 128) for p in pieces], axis=0)
    total = small_sum(flat, 14)
    summed, at = [], 0
    for piece in pieces:
        rows = piece.size // 128
        summed.append(total[at : at + rows].reshape(piece.shape))
        at += rows
    gains = total[at - 2 * width // 128 :]
    (gains_theirs,) = swap([gains], 15)
    gains = (gains + gains_theirs).reshape(2, width)
    return (
        result,
        rms_rec,
        rms_mlp,
        grad_tokens,
        grad_w_rec,
        grad_w_out,
        grad_w_mlp,
        grad_w_down,
        grad_gates,
        summed[0],
        summed[1],
        summed[2],
        summed[3],
        gains[0],
        gains[1],
        summed[4],
        summed[5],
    )


def solution(mesh):
    cube = Mesh(mesh.devices.reshape(4, 4, 4, 2), ("z", "y", "x", "mp"))
    placed = (
        P(SEQ, None),
        P(SEQ, None),
        P(SEQ),
        P(SEQ),
        P(SEQ, None, "mp"),
        P("mp", SEQ),
        P(SEQ, None, "mp"),
        P("mp", SEQ),
        P(None, "mp", None, None),
        P(None, "mp"),
        P("mp"),
        P(None, "mp"),
        P("mp"),
        P(),
        P(),
        P("mp"),
        P(None, "mp"),
    )
    return jax.shard_map(
        body,
        mesh=cube,
        in_specs=placed,
        out_specs=(
            P(SEQ, None),
            P(SEQ),
            P(SEQ),
            P(SEQ, None),
            P(SEQ, None, "mp"),
            P("mp", SEQ),
            P(SEQ, None, "mp"),
            P("mp", SEQ),
            P(None, "mp", None, None),
            P(None, "mp"),
            P("mp"),
            P(None, "mp"),
            P("mp"),
            P(),
            P(),
            P("mp"),
            P(None, "mp"),
        ),
        check_vma=False,
    )
```

```python
import functools
import jax
import jax.numpy as jnp
from jax import lax
from jax.experimental import pallas as pl
from jax.experimental.pallas import tpu as pltpu
from jax.sharding import Mesh, PartitionSpec as P

CONV = 4
EDGE = CONV - 1
BLOCK = 256
EPSILON = 1e-06
MESH = pl.DeviceIdType.MESH
ANY = pl.BlockSpec(memory_space=pl.ANY)
HBM = pl.BlockSpec(memory_space=pltpu.HBM)
VM = pl.BlockSpec(memory_space=pltpu.VMEM)
MIB = 1024 * 1024
AXES = ("z", "y", "x")
SEQ = ("z", "y", "x")
ORDERS = (("x", "y", "z"), ("y", "z", "x"), ("z", "x", "y"))
F32, BF16 = jnp.float32, jnp.bfloat16
GELU_C, GELU_A = 0.7978845608028654, 0.044715
DMA = pltpu.SemaphoreType.DMA


def dot(left, right):
    return jnp.dot(left, right, preferred_element_type=F32)


def dot_t(left, right):
    return lax.dot_general(left, right, (((1,), (1,)), ((), ())), preferred_element_type=F32)


def outer(left, right):
    return lax.dot_general(left, right, (((0,), (0,)), ((), ())), preferred_element_type=F32)


def greet(peers):
    sem = pltpu.get_barrier_semaphore()
    for peer in peers:
        pl.semaphore_signal(sem, inc=1, device_id=peer, device_id_type=MESH)
    pl.semaphore_wait(sem, len(peers))


def push(src, dst, send, recv, peer):
    return pltpu.make_async_remote_copy(
        src_ref=src, dst_ref=dst, send_sem=send, recv_sem=recv, device_id=peer, device_id_type=MESH
    )


def ring(axis):
    me = lax.axis_index(axis)
    return me, lax.rem(me + 1, 4), lax.rem(me + 2, 4), lax.rem(me + 3, 4)


def all_neighbours():
    peers = []
    for axis in AXES:
        _, up, _, down = ring(axis)
        peers += [{axis: up}, {axis: down}]
    return peers


def params(cid, mib):
    return pltpu.CompilerParams(
        collective_id=cid, has_side_effects=True, vmem_limit_bytes=mib * MIB
    )


def part_of(done, axis, index, rows, cols):
    spot = []
    for name in AXES:
        if name in done:
            spot.append(pl.ds(0, 4))
        elif name == axis:
            spot.append(index)
        else:
            spot.append(lax.axis_index(name))
    return tuple(spot) + (rows, cols)


def pick(names, axis, index, others):
    spot, rest = [], iter(others)
    for name in names:
        spot.append(index if name == axis else next(rest))
    return tuple(spot)


class Scatter:
    def __init__(self, entry, src, cols, order, cuts, bufs, out, send, recv):
        self.entry, self.src, self.order = entry, src, order
        self.start, self.width = cols
        self.cuts, self.bufs, self.out = cuts, list(bufs), out
        self.send, self.recv = send, recv
        self.left, self.sent = AXES, []
        self.direct = 0 if cuts is None else 1

    def view(self, at, rows, cols):
        start = self.start if self.phase == 0 else 0
        if rows is None:
            rows = pl.ds(0, self.src.shape[-2])
        first, width = (0, self.width) if cols is None else cols
        return at + (rows, pl.ds(start + first, width))

    def spread(self, i):
        return ((i // 4, lax.rem(i, 4)), (i,), ())[self.phase]

    def target(self, at, rows, cols):
        rows = pl.ds(0, self.src.shape[-2]) if rows is None else rows
        cols = pl.ds(0, self.width) if cols is None else pl.ds(*cols)
        return at + (rows, cols)

    def copy(self, src, dst, way, kind, peer):
        at = (self.entry, self.phase, way, kind)
        copy = push(src, dst, self.send.at[at], self.recv.at[at], {self.axis: peer})
        copy.start()
        self.sent.append(copy)
        return copy

    def begin(self, phase):
        self.phase, self.axis = phase, self.order[phase]
        self.full = (pl.ds(0, 4),) * (2 - phase)
        self.first, self.second = [], []
        if phase >= self.direct:
            self.threes = self.bufs.pop(0)
            self.acc = self.bufs.pop(0) if phase < 2 else self.out
            for step, peer in enumerate(ring(self.axis)[1:]):
                src = self.src.at[self.view(pick(self.left, self.axis, peer, self.full), None, None)]
                self.second.append(self.copy(src, self.threes.at[step], step, 0, peer))
            return
        self.ones, self.twos, self.acc = self.bufs.pop(0), self.bufs.pop(0), self.bufs.pop(0)
        _, up, far, down = ring(self.axis)
        for way, peer in enumerate((up, down)):
            src = self.src.at[self.view(pick(self.left, self.axis, far, self.full), *self.cuts[way])]
            self.first.append(self.copy(src, self.ones.at[way], way, 0, peer))
        for way, peer in enumerate((up, down)):
            cut = self.cuts[1 - way]
            src = self.src.at[self.view(pick(self.left, self.axis, peer, self.full), *cut)]
            dst = self.twos.at[self.target((way,) + self.full, *cut)]
            self.second.append(self.copy(src, dst, way, 1, peer))

    def middle(self):
        _, up, _, down = ring(self.axis)
        for way, peer in enumerate((up, down)):
            cut = self.cuts[way]
            self.first[way].wait_recv()

            def add(i, carry, way=way, peer=peer, cut=cut):
                there = (way,) + self.spread(i)
                own = self.src[self.view(pick(self.left, self.axis, peer, self.spread(i)), *cut)]
                total = self.ones[there].astype(F32) + own.astype(F32)
                self.ones[there] = total.astype(BF16)
                return carry

            lax.fori_loop(0, 4 ** (2 - self.phase), add, 0)
            dst = self.twos.at[self.target((way,) + self.full, *cut)]
            self.second.append(self.copy(self.ones.at[way], dst, way, 2, peer))

    def finish(self):
        me = lax.axis_index(self.axis)
        for copy in self.second:
            copy.wait_recv()
        if self.phase >= self.direct:
            parts = [(self.threes, 0), (self.threes, 1), (self.threes, 2)]
        else:
            parts = [(self.twos, 0), (self.twos, 1)]

        def total(i, carry):
            there = self.spread(i)
            whole = self.src[self.view(pick(self.left, self.axis, me, there), None, None)].astype(F32)
            for buf, slot in parts:
                whole = whole + buf[(slot,) + there].astype(F32)
            self.acc[there + (slice(None), slice(None))] = whole.astype(self.acc.dtype)
            return carry

        lax.fori_loop(0, 4 ** (2 - self.phase), total, 0)
        self.src = self.acc
        self.left = tuple(name for name in self.left if name != self.axis)

    def drain(self):
        for copy in self.sent:
            copy.wait_send()


def scatter_buffers(rows, width, cut):
    bufs = []
    for phase in range(3):
        cube = (4,) * (2 - phase)
        if phase == 0 and cut is not None:
            bufs.append(pltpu.VMEM((2,) + cube + cut, BF16))
            bufs.append(pltpu.VMEM((2,) + cube + (rows, width), BF16))
        else:
            bufs.append(pltpu.VMEM((3,) + cube + (rows, width), BF16))
        if phase < 2:
            bufs.append(pltpu.VMEM(cube + (rows, width), BF16))
    return bufs


class Gather:
    def __init__(self, entry, out, order, cols, send, recv, done=(), ring_rounds=()):
        self.entry, self.out, self.order, self.cols = entry, out, order, pl.ds(*cols)
        self.send, self.recv, self.sent = send, recv, []
        self.done, self.ring_rounds = done, ring_rounds

    def spot(self, origin, rows=None):
        rows = pl.ds(0, self.out.shape[3]) if rows is None else rows
        return self.out.at[part_of(self.done, self.axis, origin, rows, self.cols)]

    def copy(self, src, dst, step, way, peer):
        at = (self.entry, self.phase, step, way)
        copy = push(src, dst, self.send.at[at], self.recv.at[at], {self.axis: peer})
        copy.start()
        self.sent.append(copy)
        return copy

    def begin(self, phase, src=None):
        self.phase, self.axis = phase, self.order[phase]
        me, up, far, down = ring(self.axis)
        here = self.spot(me)
        src = here if src is None else src.at[:, self.cols]
        peers = (up, down) if phase in self.ring_rounds else (up, far, down)
        self.copies = [self.copy(src, here, 0, way, peer) for way, peer in enumerate(peers)]

    def middle(self):
        _, up, _, down = ring(self.axis)
        half = self.out.shape[3] // 2
        first, self.copies = self.copies, []
        for way, (peer, origin) in enumerate(((up, down), (down, up))):
            first[way].wait_recv()
            spot = self.spot(origin, pl.ds(way * half, half))
            self.copies.append(self.copy(spot, spot, 1, way, peer))

    def hold(self):
        for copy in self.copies:
            copy.wait_recv()

    def finish(self):
        self.hold()
        self.done = self.done + (self.axis,)

    def drain(self):
        for copy in self.sent:
            copy.wait_send()


class Rounds:
    def __init__(self, slots, send, recv, entry=0, order=("x", "y", "z")):
        self.slots, self.send, self.recv, self.sent = slots, send, recv, []
        self.entry, self.order = entry, order

    def begin(self, phase, rows):
        self.phase, axis = phase, self.order[phase]
        me = lax.axis_index(axis)
        for at, value in rows:
            self.slots[phase, me, at] = value
        self.copies = []
        for step, peer in enumerate(ring(axis)[1:]):
            spot = self.slots.at[phase, me]
            at = (self.entry, phase, step)
            copy = push(spot, spot, self.send.at[at], self.recv.at[at], {axis: peer})
            copy.start()
            self.copies.append(copy)

    def finish(self):
        for copy in self.copies:
            copy.wait_recv()
        self.sent += self.copies

    def drain(self):
        for copy in self.sent:
            copy.wait_send()


class Prefix(Rounds):
    def start(self, pair, backward):
        self.backward, self.cur, self.head = backward, pair, None
        self.share(0)

    def share(self, phase):
        self.begin(phase, [(slice(0, 1), self.cur[0]), (slice(1, 2), self.cur[1])])

    def step(self):
        self.finish()
        me = lax.axis_index(self.order[self.phase])
        run = (jnp.ones_like(self.cur[0]), jnp.zeros_like(self.cur[1]))
        mine = run
        for j in (3, 2, 1, 0) if self.backward else (0, 1, 2, 3):
            take = me == j
            mine = (jnp.where(take, run[0], mine[0]), jnp.where(take, run[1], mine[1]))
            fac, val = self.slots[self.phase, j, 0:1], self.slots[self.phase, j, 1:2]
            run = (run[0] * fac, val + fac * run[1])
        self.cur = run
        if self.head is None:
            self.head = mine
        else:
            self.head = (mine[0] * self.head[0], self.head[1] + self.head[0] * mine[1])
        if self.phase < 2:
            self.share(self.phase + 1)
        return self.head


class Total(Rounds):
    def start(self, value):
        self.begin(0, [(slice(None), value)])

    def step(self):
        self.finish()
        at = self.slots
        k = self.phase
        value = (at[k, 0] + at[k, 1]) + (at[k, 2] + at[k, 3])
        if k + 1 < len(self.order):
            self.begin(k + 1, [(slice(None), value)])
        return value


def axis_peers():
    return [{axis: ring(axis)[step]} for axis in AXES for step in (1, 2, 3)]


def along_seq(distance):
    place = lax.axis_index("z") * 16 + lax.axis_index("y") * 4 + lax.axis_index("x")
    place = lax.rem(place + distance + 64, 64)
    return {"z": place // 16, "y": lax.rem(place // 4, 4), "x": lax.rem(place, 4)}


CHUNKS = ((0, 384), (384, 512), (896, 384))
ROW_CUTS = ((pl.ds(0, 16), None), (pl.ds(16, 16), None))
HALVES = ((0, 128), (128, 128))


def gelu_parts(x):
    inner = GELU_C * (x + GELU_A * x * x * x)
    t = jnp.tanh(inner)
    slope = GELU_C * (1.0 + 3.0 * GELU_A * x * x)
    return 0.5 * x * (1.0 + t), 0.5 * (1.0 + t) + 0.5 * x * (1.0 - t * t) * slope


def mlp_kernel(
    nm_ref, go_ref, hidden_ref, inv_ref, gain_ref, go_hbm, w_hbm,
    result_ref, grad_hidden_ref, low_ref, term_ref, dw_ref,
    go, w, gathered, npart, opart, mlp_in, ggu, got, one, two, ogot, oone, otwo, low_half, result_half,
    load_sem, wsend, wrecv, gsend, grecv, gsib_send, gsib_recv,
    send_sem, recv_sem, sib_send, sib_recv, osend_sem, orecv_sem, osib_send, osib_recv, core_sem,
):
    rows, width = nm_ref.shape
    half = rows // 2
    units = mlp_in.shape[1]
    me, up, far, down = ring("x")
    core = lax.axis_index("mp")
    other = {"mp": 1 - core}
    loads = [
        pltpu.make_async_copy(go_hbm, go, load_sem.at[0]),
        pltpu.make_async_copy(nm_ref, gathered.at[me, core], load_sem.at[1]),
    ]
    wide = w.shape[4] // 2
    full, every = pl.ds(0, 4), pl.ds(0, w.shape[3])
    last = (("z", 0), ("y", wide))

    def weight_set(axis, index, at, cols):
        return ((index, full) if axis == "z" else (full, index)) + (full, at, pl.ds(cols, wide))

    for e, (axis, cols) in enumerate(last):
        here, ahead, _, behind = ring(axis)
        for k, index in enumerate((here, ahead, behind)):
            spot = weight_set(axis, index, every, cols)
            loads.append(pltpu.make_async_copy(w_hbm.at[spot], w.at[spot], load_sem.at[2 + 3 * e + k]))
    for load in loads:
        load.start()
    peers = [{"x": up}, {"x": down}, other]
    for axis in ("y", "z"):
        peers += [{axis: ring(axis)[1]}, {axis: ring(axis)[3]}]
    greet(peers)
    top, low = pl.ds(0, half), pl.ds(half, half)
    spot = gathered.at[me, core]
    first = []
    for way, peer in enumerate((up, down)):
        copy = push(nm_ref, spot, gsend.at[0, way], grecv.at[0, way], {"x": peer})
        copy.start()
        first.append(copy)
    across = [push(nm_ref, spot, gsib_send.at[0], gsib_recv.at[0], other)]
    across[0].start()
    rest = []
    for e, (axis, cols) in enumerate(last):
        _, ahead, _, behind = ring(axis)
        deep = w.shape[3] // 2
        for way, (peer, origin) in enumerate(((ahead, behind), (behind, ahead))):
            spot = weight_set(axis, origin, pl.ds(way * deep, deep), cols)
            copy = push(w_hbm.at[spot], w.at[spot], wsend.at[e, way], wrecv.at[e, way], {axis: peer})
            copy.start()
            rest.append(copy)
    second = []
    for way, (peer, origin, piece) in enumerate(((up, down, top), (down, up, low))):
        first[way].wait_recv()
        spot = gathered.at[origin, core, piece]
        copy = push(spot, spot, gsend.at[1, way], grecv.at[1, way], {"x": peer})
        copy.start()
        second.append(copy)
        spot = gathered.at[origin, core]
        copy = push(spot, spot, gsib_send.at[1 + way], gsib_recv.at[1 + way], other)
        copy.start()
        across.append(copy)
    for copy in rest:
        copy.wait_recv()
    for load in loads:
        load.wait()
    for way, piece in enumerate((top, low)):
        second[way].wait_recv()
        spot = gathered.at[far, core, piece]
        copy = push(spot, spot, gsib_send.at[3 + way], gsib_recv.at[3 + way], other)
        copy.start()
        across.append(copy)
    for copy in across:
        copy.wait_recv()

    def tile(j, start=0):
        return pl.ds(pl.multiple_of(start + j * 256, 256), 256)

    def columns(at):
        return w[:, :, :, :, at].reshape(width, 256)

    def shard_tile(i, at):
        return w[i // 2, pl.ds(2 * lax.rem(i, 2), 2), :, :, at].reshape(256, -1)

    def hidden_tile(j, carry):
        tokens_in = gathered[...].reshape(8 * rows, width)
        gate = dot(tokens_in, columns(tile(j)))
        up_lin = dot(tokens_in, columns(tile(j, units)))
        grad = dot(go[...], columns(tile(j, 2 * units)))
        act, slope = gelu_parts(gate)
        mlp_in[:, tile(j)] = (act * up_lin).astype(BF16)
        ggu[:, tile(j)] = (slope * (grad * up_lin)).astype(BF16)
        ggu[:, tile(j, units)] = (grad * act).astype(BF16)
        return carry

    lax.fori_loop(0, units // 256, hidden_tile, 0)

    def back_tile(j, carry):
        back = dot_t(ggu[...], shard_tile(j, pl.ds(0, 2 * units)))
        npart[:, :, :, tile(j)] = back.astype(BF16).reshape(4, 2, rows, 256)
        return carry

    def out_tile(j, carry):
        part = dot_t(mlp_in[...], shard_tile(j, pl.ds(2 * units, units)))
        opart[:, :, :, tile(j)] = part.astype(BF16).reshape(4, 2, rows, 256)
        return carry

    def send_across(part, got, sib_send, sib_recv):
        copies = {}
        for k, (name, chip) in enumerate((("far", far), ("up", up), ("down", down), ("me", me))):
            copy = push(part.at[chip, 1 - core], got.at[chip], sib_send.at[k], sib_recv.at[k], other)
            copy.start()
            copies[name] = copy
        return copies

    def weight_grads(lower, upper):
        def step(i, carry):
            left = gathered[:, :, :, tile(i)].reshape(8 * rows, 256)
            dw_ref[tile(i), pl.ds(0, 2 * units)] = outer(left, ggu[...]).astype(BF16)
            dw_ref[tile(i), pl.ds(2 * units, units)] = outer(go[:, tile(i)], mlp_in[...]).astype(BF16)
            return carry

        lax.fori_loop(lower, upper, step, 0)

    def add(dst, src):
        dst[...] = (dst[...].astype(F32) + src[...].astype(F32)).astype(dst.dtype)

    def far_step(sums, part, got, one, send_sem, recv_sem):
        sums["far"].wait_recv()
        add(got.at[far], part.at[far, core])
        copies = []
        for way, peer in enumerate((up, down)):
            piece = got.at[far, pl.ds(way * half, half)]
            copy = push(piece, one.at[way], send_sem.at[0, way], recv_sem.at[0, way], {"x": peer})
            copy.start()
            copies.append(copy)
        return copies

    def near_step(sums, part, got, one, two, send_sem, recv_sem, before):
        copies = []
        for way, (peer, name) in enumerate(((up, "up"), (down, "down"))):
            sums[name].wait_recv()
            add(got.at[peer], part.at[peer, core])
            before[way].wait_recv()
            add(got.at[peer, pl.ds(way * half, half)], one.at[way])
            copy = push(
                got.at[peer], two.at[way], send_sem.at[1, way], recv_sem.at[1, way], {"x": peer}
            )
            copy.start()
            copies.append(copy)
        return copies

    def last_step(sums, part, got, two, before):
        sums["me"].wait_recv()
        total = got[me].astype(F32) + part[me, core].astype(F32)
        for way in range(2):
            before[way].wait_recv()
            total = total + two[way].astype(F32)
        return total

    lax.fori_loop(0, width // 256, back_tile, 0)
    sums = send_across(npart, got, sib_send, sib_recv)
    lax.fori_loop(0, width // 256, out_tile, 0)
    third = far_step(sums, npart, got, one, send_sem, recv_sem)
    osums = send_across(opart, ogot, osib_send, osib_recv)
    weight_grads(0, 3)
    fourth = near_step(sums, npart, got, one, two, send_sem, recv_sem, third)
    fifth = far_step(osums, opart, ogot, oone, osend_sem, orecv_sem)
    weight_grads(3, 7)
    grad_normed = last_step(sums, npart, got, two, fourth)
    sixth = near_step(osums, opart, ogot, oone, otwo, osend_sem, orecv_sem, fifth)
    hat = hidden_ref[...] * inv_ref[...]
    grad_hat = grad_normed * gain_ref[...]
    inner = jnp.mean(grad_hat * hat, axis=-1, keepdims=True)
    grad_hidden = go_ref[...].astype(F32) + inv_ref[...] * (grad_hat - hat * inner)
    grad_hidden_ref[...] = grad_hidden
    term_ref[...] = jnp.sum(grad_normed * hat, axis=0, keepdims=True)
    low_half[...] = grad_hidden.astype(BF16)
    low_ref[core] = low_half[...]
    swaps = [push(low_half, low_ref.at[core], core_sem.at[0], core_sem.at[1], other)]
    swaps[0].start()
    weight_grads(7, 8)
    mlp_out = last_step(osums, opart, ogot, otwo, sixth)
    result_half[...] = (hidden_ref[...] + mlp_out).astype(BF16)
    result_ref[core] = result_half[...]
    swaps.append(push(result_half, result_ref.at[core], core_sem.at[2], core_sem.at[3], other))
    swaps[1].start()
    for copy in swaps:
        copy.wait()
    for copy in first + second + third + fourth + fifth + sixth + across + rest:
        copy.wait_send()
    for copies in (sums, osums):
        for copy in copies.values():
            copy.wait_send()


def mlp(normed, grad_out, hidden, inverse, gain, grad_out_all, weights, cid):
    rows, width = normed.shape
    units = weights.shape[4] // 3

    def block(dtype, *shape):
        return pltpu.VMEM(shape, dtype)

    return pl.pallas_call(
        mlp_kernel,
        out_shape=[
            jax.ShapeDtypeStruct((2, rows, width), BF16),
            jax.ShapeDtypeStruct((rows, width), F32),
            jax.ShapeDtypeStruct((2, rows, width), BF16),
            jax.ShapeDtypeStruct((1, width), F32),
            jax.ShapeDtypeStruct((width, 3 * units), BF16),
        ],
        in_specs=[VM] * 5 + [ANY] * 2,
        out_specs=[VM] * 5,
        scratch_shapes=[
            block(BF16, 8 * rows, width),
            block(BF16, *weights.shape),
            block(BF16, 4, 2, rows, width),
            block(BF16, 4, 2, rows, width),
            block(BF16, 4, 2, rows, width),
            block(BF16, 8 * rows, units),
            block(BF16, 8 * rows, 2 * units),
        ]
        + [block(BF16, 4, rows, width), block(BF16, 2, rows // 2, width), block(BF16, 2, rows, width)] * 2
        + [block(BF16, rows, width)] * 2
        + [DMA((8,)), DMA((2, 2)), DMA((2, 2)), DMA((2, 2)), DMA((2, 2)), DMA((5,)), DMA((5,))]
        + [DMA((2, 2)), DMA((2, 2)), DMA((4,)), DMA((4,))] * 2
        + [DMA((4,))],
        compiler_params=params(cid, 60),
    )(normed, grad_out, hidden, inverse, gain, grad_out_all, weights)


def lanes(n):
    return pl.ds(pl.multiple_of(n * BLOCK, BLOCK), BLOCK)


def minus_expm1(x):
    series = jnp.ones_like(x)
    for k in (9, 8, 7, 6, 5, 4, 3, 2):
        series = 1.0 + x * (1.0 / k) * series
    return jnp.where(x > -0.4, -x * series, 1.0 - jnp.exp(x))


CONV_W, CONV_B, RATES, BIAS, CONV_STATE, H_INIT, SLOPE = 0, 4, 5, 6, 8, 11, 12


def rec_forward_kernel(*refs):
    (
        tokens_ref, tail_ref, gain_ref, gain_mlp_ref, v_ref, keep_ref, lin_in, gate_in, back_in, quarters_ref, g_hbm,
        lin_out, gate_out, back_out, mlp_out, ext_out, act_out, mixed_out, reset_out, input_out, f_out, states_out,
        branch_out, normed_out, inv_ref, rms_ref, hidden_ref, nm_ref, inv_mlp_ref, rms_mlp_ref,
        wl, wg, wb, ext, gate_lin, mixed_v, reset_v, input_v, f_v, states, branch_v, normed, tail_in, driven, cf_v,
        part, part_low, part_in, g_v, rms_v, slots,
        tail_sem, load_sem, save_sem, own_sem, move_send, move_recv, send, recv, small_send, small_recv, core_sem,
    ) = refs
    count, width = tokens_ref.shape
    rec = f_v.shape[1]
    blocks = rec // BLOCK
    half = count // 2
    core = lax.axis_index("mp")
    other = {"mp": 1 - core}
    here = tuple(lax.axis_index(name) for name in AXES)
    load = pltpu.make_async_copy(g_hbm, g_v, load_sem)
    load.start()
    owns = [
        pltpu.make_async_copy(lin_in, wl.at[here], own_sem.at[0]),
        pltpu.make_async_copy(gate_in, wg.at[here], own_sem.at[1]),
        pltpu.make_async_copy(back_in, wb.at[here], own_sem.at[2]),
        pltpu.make_async_copy(quarters_ref.at[here[2]], mlp_out.at[here], own_sem.at[3]),
    ]
    for own in owns:
        own.start()
    greet(axis_peers() + [other, along_seq(1), along_seq(-1)])
    tail_copy = push(tail_ref, tail_in, tail_sem.at[0], tail_sem.at[1], along_seq(1))
    tail_copy.start()
    lin = [Gather(e, wl, ORDERS[e], CHUNKS[e], send, recv, ring_rounds=(2,)) for e in range(3)]
    rest = [
        Gather(3 * k + e, out, ORDERS[(e + k) % 3], CHUNKS[e], send, recv, ring_rounds=(1, 2))
        for k, out in ((1, wg), (2, wb))
        for e in range(3)
    ]
    wide = mlp_out.shape[4] // 2
    mlp_flows = [
        Gather(9 + e, mlp_out, order, (e * wide, wide), send, recv, done=("x",), ring_rounds=(1,))
        for e, order in enumerate((("y", "z"), ("z", "y")))
    ]

    def each(group, name, *args):
        for flow in group:
            getattr(flow, name)(*args)

    each(lin, "begin", 0, lin_in)
    moves = []
    for step, peer in enumerate(ring("x")[1:]):
        copy = push(
            quarters_ref.at[peer], mlp_out.at[here], move_send.at[step], move_recv.at[step], {"x": peer}
        )
        copy.start()
        moves.append(copy)
    each(rest[:3], "begin", 0, gate_in)
    each(rest[3:], "begin", 0, back_in)

    def norm(values):
        mean_sq = jnp.mean(values * values, axis=-1, keepdims=True)
        inverse = lax.rsqrt(mean_sq + EPSILON)
        return values * inverse, inverse, jnp.sqrt(mean_sq + EPSILON)

    def norm_step(i, carry):
        at = pl.ds(pl.multiple_of(i * 64, 64), 64)
        hat, inverse, rms = norm(tokens_ref[at].astype(F32))
        inv_ref[at] = inverse
        rms_ref[at] = rms
        normed[pl.ds(pl.multiple_of(16 + i * 64, 16), 64)] = (hat * gain_ref[...]).astype(BF16)
        return carry

    lax.fori_loop(0, count // 64, norm_step, 0)
    for own in owns:
        own.wait()
    each(lin, "finish")
    each(lin, "begin", 1)
    each(rest, "finish")
    tail_copy.wait_recv()
    normed[0:16] = (norm(tail_in[...].astype(F32))[0] * gain_ref[...]).astype(BF16)
    saves = []

    def save(src, dst):
        copy = pltpu.make_async_copy(src, dst, save_sem.at[len(saves)])
        copy.start()
        saves.append(copy)

    save(normed.at[pl.ds(16, count)], normed_out)
    each(lin, "finish")
    each(lin, "begin", 2)
    each(rest, "begin", 1)
    each(lin, "middle")
    each(rest, "middle")
    for copy in moves:
        copy.wait_recv()
    each(mlp_flows, "begin", 0)
    each(rest, "finish")
    each(rest, "begin", 2)
    load.wait()
    each(lin, "finish")
    save(wl, lin_out)
    is_first = (here[0] + here[1] + here[2]) == 0

    def rec_step(n, carry):
        at = lanes(n)
        ext[:, at] = dot(normed[...], wl[:, :, :, :, at].reshape(width, BLOCK))

        @pl.when(is_first)
        def _():
            ext[16 - EDGE : 16, at] = v_ref[CONV_STATE : CONV_STATE + EDGE, at]

        total = v_ref[CONV_B : CONV_B + 1, at] + jnp.zeros((count, BLOCK), F32)
        for k in range(CONV):
            total = total + v_ref[CONV_W + k : CONV_W + k + 1, at] * ext[pl.ds(16 - EDGE + k, count), at]
        mixed = total.astype(BF16)
        mixed_v[:, at] = mixed
        reset = jax.nn.sigmoid(dot(mixed, g_v[0, n]) + v_ref[BIAS : BIAS + 1, at])
        gated = jax.nn.sigmoid(dot(mixed, g_v[1, n]) + v_ref[BIAS + 1 : BIAS + 2, at])
        reset_v[:, at] = reset
        input_v[:, at] = gated
        log_decay = -8.0 * v_ref[RATES : RATES + 1, at] * reset
        f_v[:, at] = jnp.exp(log_decay) * keep_ref[...]
        driven[:, at] = jnp.sqrt(minus_expm1(2.0 * log_decay)) * gated * mixed.astype(F32)
        return carry

    lax.fori_loop(0, blocks, rec_step, 0)
    for src, dst in ((ext, ext_out), (mixed_v, mixed_out), (reset_v, reset_out), (input_v, input_out), (f_v, f_out)):
        save(src, dst)

    def group(i, carry):
        base = pl.multiple_of(i * 8, 8)
        f, d = f_v[pl.ds(base, 8)], driven[pl.ds(base, 8)]
        cf, cd = carry
        cfs, cds = [], []
        for r in range(8):
            cf = cf * f[r : r + 1]
            cd = cd * f[r : r + 1] + d[r : r + 1]
            cfs.append(cf)
            cds.append(cd)
        cf_v[pl.ds(base, 8)] = jnp.concatenate(cfs, axis=0)
        states[pl.ds(pl.multiple_of(base + 8, 8), 8)] = jnp.concatenate(cds, axis=0)
        return cf, cd

    zero = jnp.zeros((1, rec), F32)
    ends = lax.fori_loop(0, count // 8, group, (zero + 1.0, zero))
    prefix = Prefix(slots, small_send, small_recv)
    prefix.start(ends, False)
    prefix.step()
    prefix.step()
    each(rest, "middle")
    each(mlp_flows, "finish")
    each(mlp_flows, "begin", 1)
    head = prefix.step()
    carry_in = head[1] + head[0] * v_ref[H_INIT : H_INIT + 1]
    each(rest, "finish")
    save(wg, gate_out)
    save(wb, back_out)

    def gate_step(n, carry):
        gate_lin[:, lanes(n)] = dot(normed[16:], wg[:, :, :, :, lanes(n)].reshape(width, BLOCK))
        return carry

    lax.fori_loop(0, blocks, gate_step, 0)
    save(gate_lin, act_out)
    states[0:8] = jnp.broadcast_to(carry_in, (8, rec))

    def branch_step(n, carry):
        at = lanes(n)
        value = states[8:, at] + cf_v[:, at] * states[0:1, at]
        states[8:, at] = value
        branch_v[:, at] = (gelu_parts(gate_lin[:, at])[0] * value).astype(BF16)
        return carry

    lax.fori_loop(0, blocks, branch_step, 0)
    save(states, states_out)
    save(branch_v, branch_out)

    def out_step(i, carry):
        at = pl.ds(pl.multiple_of(i * 256, 256), 256)
        rows = wb[i // 2, pl.ds(2 * lax.rem(i, 2), 2)].reshape(256, rec)
        value = dot_t(branch_v[...], rows)
        part[0, :, at] = value[:half]
        part[1, :, at] = value[half:]
        return carry

    lax.fori_loop(0, width // 256, out_step, 0)
    part_low[...] = part[1 - core].astype(BF16)
    part_copy = push(part_low, part_in, core_sem.at[0], core_sem.at[1], other)
    part_copy.start()
    part_copy.wait_recv()
    mine = pl.ds(pl.multiple_of(core * half, half), half)
    hidden = tokens_ref[mine].astype(F32) + (part[core] + part_in[...].astype(F32))
    hidden_ref[...] = hidden
    hat, inverse, rms = norm(hidden)
    inv_mlp_ref[...] = inverse
    rms_v[...] = jnp.broadcast_to(rms, (half, 128))
    rms_mlp_ref[core] = rms_v[...]
    rms_copy = push(rms_v, rms_mlp_ref.at[core], core_sem.at[2], core_sem.at[3], other)
    rms_copy.start()
    nm_ref[...] = (hat * gain_mlp_ref[...]).astype(BF16)
    each(mlp_flows, "hold")
    rms_copy.wait()
    for copy in moves:
        copy.wait_send()
    for copy in saves:
        copy.wait()
    each(lin, "drain")
    each(rest, "drain")
    each(mlp_flows, "drain")
    prefix.drain()
    part_copy.wait_send()
    tail_copy.wait_send()


def rec_forward(tokens, tail, gain_rec, gain_mlp, vectors, keep, lin, gate, back, quarters, gates, cid):
    count, width = tokens.shape
    rows, rec = lin.shape
    half = count // 2

    def cube(last):
        return (4, 4, 4, rows, last)

    def sds(shape, dtype):
        return jax.ShapeDtypeStruct(shape, dtype)

    saved = [
        (cube(rec), BF16),
        (cube(rec), BF16),
        (cube(rec), BF16),
        (cube(quarters.shape[2]), BF16),
        ((count + 16, rec), F32),
        ((count, rec), F32),
        ((count, rec), BF16),
        ((count, rec), F32),
        ((count, rec), F32),
        ((count, rec), F32),
        ((count + 8, rec), F32),
        ((count, rec), BF16),
        ((count, width), BF16),
    ]
    small = [
        ((count, 1), F32),
        ((count, 1), F32),
        ((half, width), F32),
        ((half, width), BF16),
        ((half, 1), F32),
        ((2, half, 128), F32),
    ]
    scratch = saved[:3] + saved[4:12] + [((count + 16, width), BF16), (tail.shape, BF16)]
    scratch += [((count, rec), F32), ((count, rec), F32), ((2, half, width), F32)]
    scratch += [((half, width), BF16), ((half, width), BF16), (gates.shape, BF16), ((half, 128), F32), ((3, 4, 2, rec), F32)]
    return pl.pallas_call(
        rec_forward_kernel,
        out_shape=[sds(*one) for one in saved + small],
        in_specs=[VM] * 9 + [ANY] * 2,
        out_specs=[HBM] * len(saved) + [VM] * len(small),
        scratch_shapes=[pltpu.VMEM(*one) for one in scratch]
        + [
            DMA((2,)),
            DMA,
            DMA((12,)),
            DMA((4,)),
            DMA((3,)),
            DMA((3,)),
            DMA((11, 3, 2, 3)),
            DMA((11, 3, 2, 3)),
            DMA((1, 3, 3)),
            DMA((1, 3, 3)),
            DMA((4,)),
        ],
        compiler_params=params(cid, 60),
    )(tokens, tail, gain_rec[None], gain_mlp[None], vectors, keep, lin, gate, back, quarters, gates)


G_BIAS, G_LAM, G_CONV_W, G_CONV_B, G_H, G_STATE = 0, 2, 3, 7, 8, 9
GATE_ROWS = 48


def shard_rows(ref, i, value):
    value = value.reshape(2, 4, 32, value.shape[1])
    ref[i // 2, pl.ds(2 * lax.rem(i, 2), 2)] = value


def rec_back_kernel(*refs):
    (
        gh_ref, branch_ref, normed_ref, gate_ref, states_ref, f_ref, v_ref,
        wb_hbm, ext_hbm, mixed_hbm, reset_hbm, input_hbm, g_hbm,
        gate_low_ref, low_ref, small_ref, out0, out1, out2, out3, out4, out5, out6, out7,
        wb, ext, mixed_v, reset_v, input_v, g_v, cb, al, gs, gm, dw_out, dw_gate, tail, edge, edge_in, gg_ref,
    ) = refs[:40]
    bufs, refs = refs[40 : 40 + 46], refs[40 + 46 :]
    slots, load_sem, send, recv, small_send, small_recv, edge_sem = refs
    count = gate_ref.shape[0]
    rec = gate_ref.shape[1]
    blocks = rec // BLOCK
    pairs = ((wb_hbm, wb), (ext_hbm, ext), (mixed_hbm, mixed_v), (reset_hbm, reset_v), (input_hbm, input_v), (g_hbm, g_v))
    loads = [pltpu.make_async_copy(src, dst, load_sem.at[k]) for k, (src, dst) in enumerate(pairs)]
    for load in loads:
        load.start()
    ahead, behind = along_seq(1), along_seq(-1)
    greet(axis_peers() + [ahead, behind])
    place = lax.axis_index("z") * 16 + lax.axis_index("y") * 4 + lax.axis_index("x")
    is_first = jnp.where(place == 0, 1.0, 0.0)
    has_next = jnp.where(place == 63, 0.0, 1.0)
    outs = (out0, out1, out2, out3, out4, out5, out6, out7)
    flows = [
        Scatter(
            e, dw_out if e < 3 else dw_gate, CHUNKS[e % 3], ORDERS[e % 3], ROW_CUTS,
            bufs[6 * e : 6 * e + 6], outs[e], send, recv,
        )
        for e in range(6)
    ]
    gates = [
        Scatter(6 + e, gg_ref, HALVES[e], ORDERS[e], None, bufs[36 + 5 * e : 41 + 5 * e], outs[6 + e], send, recv)
        for e in range(2)
    ]
    flows += gates
    early, late = flows[:3], flows[3:6]

    def each(group, name, *args):
        for flow in group:
            getattr(flow, name)(*args)

    def weight_grad(ref, left, right):
        def step(i, carry):
            cols = pl.ds(pl.multiple_of(i * 256, 256), 256)
            shard_rows(ref, i, outer(left[:, cols], right[...]).astype(BF16))
            return carry

        lax.fori_loop(0, left.shape[1] // 256, step, 0)

    weight_grad(dw_out, gh_ref, branch_ref)
    each(early, "begin", 0)
    loads[0].wait()

    def branch_step(n, carry):
        grad = dot(gh_ref[...], wb[:, lanes(n)])
        act, slope = gelu_parts(gate_ref[:, lanes(n)])
        gate_low_ref[:, lanes(n)] = (slope * (grad * states_ref[8:, lanes(n)])).astype(BF16)
        gs[:, lanes(n)] = grad * act
        return carry

    lax.fori_loop(0, blocks, branch_step, 0)

    def group(i, carry):
        base = pl.multiple_of(count - 8 - i * 8, 8)
        f, d = f_ref[pl.ds(base, 8)], gs[pl.ds(base, 8)]
        follow, cf, cd = carry
        cfs, cds = [None] * 8, [None] * 8
        for r in (7, 6, 5, 4, 3, 2, 1, 0):
            cf = cf * follow
            cd = cd * follow + d[r : r + 1]
            cfs[r], cds[r] = cf, cd
            follow = f[r : r + 1]
        cb[pl.ds(base, 8)] = jnp.concatenate(cfs, axis=0)
        al[pl.ds(base, 8)] = jnp.concatenate(cds, axis=0)
        return follow, cf, cd

    zero = jnp.zeros((1, rec), F32)
    follow, cf, cd = lax.fori_loop(0, count // 8, group, (zero + 1.0, zero + 1.0, zero))
    prefix = Prefix(slots, small_send, small_recv)
    prefix.start((follow * cf, follow * cd), True)
    weight_grad(dw_gate, normed_ref, gate_low_ref)
    each(late, "begin", 0)
    prefix.step()
    each(early, "middle")
    prefix.step()
    for load in loads[1:]:
        load.wait()
    later = prefix.step()[1]
    al[...] = al[...] + cb[...] * later

    def grads_step(n, carry):
        at = lanes(n)
        adjoint = al[:, at]
        factors, reset, gated = f_ref[:, at], reset_v[:, at], input_v[:, at]
        mixed_low = mixed_v[:, at]
        mixed = mixed_low.astype(F32)
        rates = v_ref[RATES : RATES + 1, at]
        log_decay = -8.0 * rates * reset
        decays = jnp.exp(log_decay)
        scale_in = jnp.sqrt(minus_expm1(2.0 * log_decay))
        grad_log = adjoint * states_ref[pl.ds(7, count), at] * factors
        grad_log = grad_log - adjoint * gated * mixed * decays * decays / scale_in
        small_ref[G_LAM : G_LAM + 1, at] = (
            8.0 * jnp.sum(grad_log * reset, axis=0, keepdims=True) * v_ref[SLOPE : SLOPE + 1, at]
        )
        small_ref[G_H : G_H + 1, at] = is_first * factors[0:1] * adjoint[0:1]
        grad_reset = (grad_log * (-8.0 * rates) * reset * (1.0 - reset)).astype(BF16)
        grad_input = (adjoint * scale_in * mixed * gated * (1.0 - gated)).astype(BF16)
        for g, grad in enumerate((grad_reset, grad_input)):
            small_ref[G_BIAS + g : G_BIAS + g + 1, at] = jnp.sum(
                grad.astype(F32), axis=0, keepdims=True
            )
            b = g * blocks + n
            rows = pl.ds(pl.multiple_of(16 * lax.rem(b, 3), 16), 16)
            gg_ref[:, :, b // 3, rows, :] = outer(mixed_low, grad).astype(BF16).reshape(4, 4, 16, BLOCK)
        grad_mixed = adjoint * scale_in * gated
        grad_mixed = grad_mixed + dot_t(grad_reset, g_v[0, n]) + dot_t(grad_input, g_v[1, n])
        gm[0:8] = jnp.zeros((8, BLOCK), F32)
        gm[8 : 8 + count] = grad_mixed
        gm[8 + count :] = jnp.zeros((8, BLOCK), F32)
        small_ref[G_CONV_B : G_CONV_B + 1, at] = jnp.sum(grad_mixed, axis=0, keepdims=True)
        total = jnp.zeros((count, BLOCK), F32)
        front = jnp.zeros((8, BLOCK), F32)
        for k in range(CONV):
            small_ref[G_CONV_W + k : G_CONV_W + k + 1, at] = jnp.sum(
                grad_mixed * ext[pl.ds(16 - EDGE + k, count), at], axis=0, keepdims=True
            )
            weight = v_ref[CONV_W + k : CONV_W + k + 1, at]
            total = total + weight * gm[pl.ds(8 + EDGE - k, count)]
            front = front + weight * gm[pl.ds(8 - k, 8)]
        low_ref[:, at] = total.astype(BF16)
        tail[:, at] = total[count - 16 :]
        edge[:, at] = front
        small_ref[G_STATE : G_STATE + EDGE, at] = is_first * front[:EDGE]
        small_ref[G_STATE + EDGE :, at] = jnp.zeros((16 - G_STATE - EDGE, BLOCK), F32)
        return carry

    for x, j in ((3, 1), (3, 2)):
        gg_ref[:, :, x, 16 * j : 16 * j + 16, :] = jnp.zeros((4, 4, 16, BLOCK), BF16)
    lax.fori_loop(0, 2, grads_step, 0)
    each(early, "finish")
    each(early, "begin", 1)
    each(late, "middle")
    lax.fori_loop(2, 4, grads_step, 0)
    each(early, "finish")
    each(early, "begin", 2)
    lax.fori_loop(4, blocks, grads_step, 0)
    edge_copy = push(edge, edge_in, edge_sem.at[0], edge_sem.at[1], behind)
    edge_copy.start()
    each(gates, "begin", 0)
    each(late, "finish")
    each(late, "begin", 1)
    each(early, "finish")
    edge_copy.wait_recv()
    last = jnp.concatenate([tail[0:13], tail[13:16] + has_next * edge_in[0:EDGE]], axis=0)
    low_ref[count - 16 :] = last.astype(BF16)
    each(gates, "finish")
    each(gates, "begin", 1)
    each(late, "finish")
    each(late, "begin", 2)
    each(gates, "finish")
    each(gates, "begin", 2)
    each(late, "finish")
    each(gates, "finish")
    each(flows, "drain")
    prefix.drain()
    edge_copy.wait_send()


def rec_back(gh, branch, normed, gate_lin, states_ext, factors, vectors, w_back, ext, mixed, reset, gated, gates, cid):
    count, rec = gate_lin.shape
    blocks = rec // BLOCK
    rows = normed.shape[1] // 64

    def like(array):
        return pltpu.VMEM(array.shape, array.dtype)

    wide = pltpu.VMEM((count, rec), F32)
    cube = pltpu.VMEM((4, 4, 4, rows, rec), BF16)
    bufs = []
    for e in range(6):
        width = CHUNKS[e % 3][1]
        bufs += scatter_buffers(rows, width, (rows // 2, width))
    for _ in range(2):
        bufs += scatter_buffers(GATE_ROWS, BLOCK // 2, None)
    out = pl.pallas_call(
        rec_back_kernel,
        out_shape=[
            jax.ShapeDtypeStruct((count, rec), BF16),
            jax.ShapeDtypeStruct((count, rec), BF16),
            jax.ShapeDtypeStruct((16, rec), F32),
        ]
        + [jax.ShapeDtypeStruct((rows, CHUNKS[e % 3][1]), F32) for e in range(6)]
        + [jax.ShapeDtypeStruct((GATE_ROWS, BLOCK // 2), F32)] * 2,
        in_specs=[VM] * 7 + [ANY] * 6,
        out_specs=[VM] * 11,
        scratch_shapes=[
            like(w_back), like(ext), like(mixed), like(reset), like(gated), like(gates),
            wide, wide, wide, pltpu.VMEM((count + 16, BLOCK), F32), cube, cube,
            pltpu.VMEM((16, rec), F32), pltpu.VMEM((8, rec), F32), pltpu.VMEM((8, rec), F32),
            pltpu.VMEM((4, 4, 4, GATE_ROWS, BLOCK), BF16),
        ]
        + bufs
        + [
            pltpu.VMEM((3, 4, 2, rec), F32),
            DMA((6,)),
            DMA((8, 3, 3, 3)),
            DMA((8, 3, 3, 3)),
            DMA((1, 3, 3)),
            DMA((1, 3, 3)),
            DMA((2,)),
        ],
        compiler_params=params(cid, 62),
    )(gh, branch, normed, gate_lin, states_ext, factors, vectors, w_back, ext, mixed, reset, gated, gates)
    gates = jnp.concatenate(out[9:11], axis=1)
    return out[:3], jnp.concatenate(out[3:6], axis=1), jnp.concatenate(out[6:9], axis=1), gates


def rec_end_kernel(*refs):
    (
        gate_low_ref, low_ref, normed_ref, gg_ref, small_ref, gain_term_ref, gh_ref, tokens_in, inverse_ref, gain_ref,
        quarters_ref, wg_hbm, wl_hbm,
        tokens_ref, total_ref, gains_ref, all_gates_ref, grad_mlp_ref, grad_down_ref, out0, out1, out2,
        wg, wl, dw_lin, part, part_low, part_in, gates_ref, back, ring_gains, gains0, small0, small1, small2,
    ) = refs[:35]
    bufs, refs = refs[35 : 35 + 18], refs[35 + 18 :]
    load_sem, send, recv, gsend, grecv, small_send, small_recv, ring_send, ring_recv, core_sem, token_sem, move_send, move_recv = refs
    half, width = gh_ref.shape
    loads = [
        pltpu.make_async_copy(wg_hbm, wg, load_sem.at[0]),
        pltpu.make_async_copy(wl_hbm, wl, load_sem.at[1]),
    ]
    for load in loads:
        load.start()
    core = lax.axis_index("mp")
    other = {"mp": 1 - core}
    x_here = lax.axis_index("x")
    greet(axis_peers() + [other] + [{"x": peer, "mp": 1 - core} for peer in ring("x")[1:]])
    small = [
        Total(slots, small_send, small_recv, e, ORDERS[e])
        for e, slots in enumerate((small0, small1, small2))
    ]
    for flow, (start, wide) in zip(small, CHUNKS):
        flow.start(small_ref[:, start : start + wide])
    moves = []
    for step, peer in enumerate(ring("x")[1:]):
        copy = push(quarters_ref.at[peer], back.at[x_here], move_send.at[step], move_recv.at[step], {"x": peer})
        copy.start()
        moves.append(copy)
    back[x_here] = quarters_ref[x_here]
    outs = (out0, out1, out2)
    lin = [
        Scatter(e, dw_lin, CHUNKS[e], ORDERS[e], ROW_CUTS, bufs[6 * e : 6 * e + 6], outs[e], send, recv)
        for e in range(3)
    ]
    spread = [Gather(e, gates_ref, ORDERS[e], HALVES[e], gsend, grecv) for e in range(2)]

    def each_gate(name, *args):
        for flow in spread:
            getattr(flow, name)(*args)

    def each(name, *args):
        for flow in lin:
            getattr(flow, name)(*args)

    gates_ref[lax.axis_index("z"), lax.axis_index("y"), lax.axis_index("x")] = gg_ref[...].astype(BF16)

    def weight_grad(i, carry):
        cols = pl.ds(pl.multiple_of(i * 256, 256), 256)
        shard_rows(dw_lin, i, outer(normed_ref[:, cols], low_ref[...]).astype(BF16))
        return carry

    lax.fori_loop(0, width // 512, weight_grad, 0)
    for flow in small:
        flow.step()
    lax.fori_loop(width // 512, width // 256, weight_grad, 0)
    for flow in small:
        flow.step()
    each_gate("begin", 0)
    each("begin", 0)
    for load in loads:
        load.wait()

    def part_tile(i, carry):
        at = pl.ds(pl.multiple_of(i * 256, 256), 256)
        value = dot_t(gate_low_ref[...], wg[at, :]) + dot_t(low_ref[...], wl[at, :])
        part[0, :, at] = value[:half]
        part[1, :, at] = value[half:]
        return carry

    lax.fori_loop(0, width // 256, part_tile, 0)
    part_low[...] = part[1 - core].astype(BF16)
    part_copy = push(part_low, part_in, core_sem.at[0], core_sem.at[1], other)
    part_copy.start()
    for flow, (start, wide) in zip(small, CHUNKS):
        total_ref[:, start : start + wide] = flow.step()
    each_gate("finish")
    each_gate("begin", 1)
    part_copy.wait_recv()
    grad_normed = part[core] + part_in[...].astype(F32)
    hat = tokens_in[...].astype(F32) * inverse_ref[...]
    gain_term = jnp.sum(grad_normed * hat, axis=0, keepdims=True)
    quarter = width // 4
    for k in range(4):
        cols = slice(k * quarter, (k + 1) * quarter)
        ring_gains[x_here, core, k : k + 1] = gain_term[:, cols]
        ring_gains[x_here, core, 4 + k : 5 + k] = gain_term_ref[:, cols]
    shares = []
    spot = ring_gains.at[x_here, core]
    group = [{"x": x, "mp": c} for x in ring("x") for c in (core, 1 - core)][1:]
    for k, peer in enumerate(group):
        copy = push(spot, spot, ring_send.at[k], ring_recv.at[k], peer)
        copy.start()
        shares.append(copy)
    grad_hat = grad_normed * gain_ref[...]
    inner = jnp.mean(grad_hat * hat, axis=-1, keepdims=True)
    part[core] = gh_ref[...] + inverse_ref[...] * (grad_hat - hat * inner)
    token_copy = push(part.at[core], tokens_ref.at[core], token_sem.at[0], token_sem.at[1], other)
    token_copy.start()
    tokens_ref[core] = part[core]
    each("middle")
    for copy in shares:
        copy.wait_recv()
    gains = Total(gains0, small_send, small_recv, 3, ("y", "z"))
    sums = [ring_gains[x, 0] + ring_gains[x, 1] for x in range(4)]
    gains.start((sums[0] + sums[1]) + (sums[2] + sums[3]))
    each_gate("finish")
    each_gate("begin", 2)
    for copy in moves:
        copy.wait_recv()
    quarter = grad_down_ref.shape[1] // 4
    for q in range(4):
        value = back[q].astype(F32)
        for k in range(2):
            grad_mlp_ref[:, pl.ds((4 * k + q) * quarter, quarter)] = value[:, k * quarter : (k + 1) * quarter]
        grad_down_ref[:, pl.ds(q * quarter, quarter)] = value[:, 2 * quarter :]
    gains.step()
    each("finish")
    each("begin", 1)
    gains_ref[...] = gains.step()
    each_gate("finish")

    def unpack(b, carry):
        at = pl.ds(pl.multiple_of(16 * lax.rem(b, 3), 16), 16)
        all_gates_ref[b] = gates_ref[:, :, b // 3, at, :].reshape(BLOCK, BLOCK).astype(F32)
        return carry

    lax.fori_loop(0, all_gates_ref.shape[0], unpack, 0)
    each("finish")
    each("begin", 2)
    token_copy.wait_recv()
    each("finish")
    each("drain")
    each_gate("drain")
    gains.drain()
    for flow in small:
        flow.drain()
    for copy in shares + moves + [part_copy, token_copy]:
        copy.wait_send()


def rec_end(gate_low, low, normed, gg, small, gain_term, grad_hidden, tokens, inverse, gain, quarters, w_gate, w_lin, cid):
    count, rec = low.shape
    half, width = grad_hidden.shape
    rows = width // 64
    units = quarters.shape[2] // 3
    gate_blocks = 2 * rec // BLOCK
    bufs = []
    for e in range(3):
        bufs += scatter_buffers(rows, CHUNKS[e][1], (rows // 2, CHUNKS[e][1]))

    def sds(*shape):
        return jax.ShapeDtypeStruct(shape, F32)

    out = pl.pallas_call(
        rec_end_kernel,
        out_shape=[
            sds(2, half, width),
            sds(16, rec),
            sds(8, width // 4),
            sds(gate_blocks, BLOCK, BLOCK),
            sds(rows, 8 * units),
            sds(rows, 4 * units),
        ]
        + [sds(rows, CHUNKS[e][1]) for e in range(3)],
        in_specs=[VM] * 11 + [ANY] * 2,
        out_specs=[VM] * 9,
        scratch_shapes=[
            pltpu.VMEM(w_gate.shape, BF16),
            pltpu.VMEM(w_lin.shape, BF16),
            pltpu.VMEM((4, 4, 4, rows, rec), BF16),
            pltpu.VMEM((2, half, width), F32),
            pltpu.VMEM((half, width), BF16),
            pltpu.VMEM((half, width), BF16),
            pltpu.VMEM((4, 4, 4) + gg.shape, BF16),
            pltpu.VMEM(quarters.shape, quarters.dtype),
            pltpu.VMEM((4, 2, 8, width // 4), F32),
            pltpu.VMEM((2, 4, 8, width // 4), F32),
        ]
        + [pltpu.VMEM((3, 4, 16, wide), F32) for _, wide in CHUNKS]
        + bufs
        + [
            DMA((2,)),
            DMA((3, 3, 3, 3)),
            DMA((3, 3, 3, 3)),
            DMA((2, 3, 1, 3)),
            DMA((2, 3, 1, 3)),
            DMA((4, 3, 3)),
            DMA((4, 3, 3)),
            DMA((7,)),
            DMA((7,)),
            DMA((2,)),
            DMA((2,)),
            DMA((3,)),
            DMA((3,)),
        ],
        compiler_params=params(cid, 60),
    )(gate_low, low, normed, gg, small, gain_term, grad_hidden, tokens, inverse, gain, quarters, w_gate, w_lin)
    return (out[0].reshape(2 * half, width),) + tuple(out[1:6]) + (jnp.concatenate(out[6:9], axis=1),)


def body(
    tokens,
    cotangent,
    starts,
    valid,
    w_rec,
    w_out,
    w_mlp,
    w_down,
    lru_gates,
    lru_bias,
    lam,
    conv_w,
    conv_b,
    gain_rec,
    gain_mlp,
    h_init,
    conv_state,
):
    count, width = tokens.shape
    shard, _, rec = w_rec.shape
    hidden_units = w_mlp.shape[2] // 4
    half = count // 2
    core = lax.axis_index("mp")

    def my_half(array):
        return lax.dynamic_slice_in_dim(array, core * half, half, axis=0)

    quarters = jnp.stack([w_mlp[:, 0], w_mlp[:, 1], w_down.T], axis=1)
    quarters = quarters.reshape(shard, 3, 4, hidden_units).transpose(2, 0, 1, 3)
    quarters = quarters.reshape(4, shard, 3 * hidden_units)
    grad_out = my_half(cotangent) * my_half(valid).astype(BF16)[:, None]
    grad_out_all = lax.all_gather(grad_out, ("x", "mp"), axis=0, tiled=True)
    vectors = jnp.concatenate(
        [
            conv_w,
            conv_b[None],
            jax.nn.softplus(-lam)[None],
            lru_bias,
            conv_state,
            h_init[None],
            jax.nn.sigmoid(-lam)[None],
            jnp.zeros((3, rec), F32),
        ],
        axis=0,
    )
    (
        w_lin, w_gate, w_back, mlp_weights, ext, gate_lin, mixed, reset, gated, factors, states_ext, branch_in,
        normed_rec, inverse_rec, rms_rec, hidden, normed_mlp, inverse_mlp, rms_half,
    ) = rec_forward(
        tokens,
        tokens[count - 16 :],
        gain_rec,
        gain_mlp,
        vectors,
        (1 - starts).astype(F32)[:, None],
        w_rec[:, 1],
        w_rec[:, 0],
        w_out.T,
        quarters,
        lru_gates,
        0,
    )
    w_lin, w_gate, w_back = (w.reshape(width, rec) for w in (w_lin, w_gate, w_back))
    result, grad_hidden, grad_hidden_low, gain_mlp_term, mlp_terms = mlp(
        normed_mlp, grad_out, hidden, inverse_mlp, gain_mlp[None], grad_out_all, mlp_weights, 1
    )
    mlp_sums = lax.psum_scatter(mlp_terms, ("z", "y"), scatter_dimension=0, tiled=True)
    result = result.reshape(count, width)
    grad_hidden_low = grad_hidden_low.reshape(count, width)
    (grad_gate_low, grad_rec_low, small), out_sums, gate_sums, gate_terms = rec_back(
        grad_hidden_low,
        branch_in,
        normed_rec,
        gate_lin,
        states_ext,
        factors,
        vectors,
        w_back,
        ext,
        mixed,
        reset,
        gated,
        lru_gates,
        2,
    )
    grad_tokens, small, gains, gate_blocks, grad_w_mlp, grad_down, lin_sums = rec_end(
        grad_gate_low,
        grad_rec_low,
        normed_rec,
        gate_terms,
        small,
        gain_mlp_term,
        grad_hidden,
        my_half(tokens),
        my_half(inverse_rec),
        gain_rec[None],
        mlp_sums.reshape(4, shard, 3 * hidden_units),
        w_gate,
        w_lin,
        3,
    )
    grad_w_rec = jnp.stack([gate_sums, lin_sums], axis=1)
    grad_w_out = out_sums.T
    grad_gates = gate_blocks.reshape(lru_gates.shape)
    grad_w_mlp = grad_w_mlp.reshape(shard, 2, 4 * hidden_units)
    grad_w_down = grad_down.T
    rms_mlp = rms_half[:, :, 0].reshape(count)
    gains = gains.reshape(2, width)
    return (
        result,
        rms_rec[:, 0],
        rms_mlp,
        grad_tokens,
        grad_w_rec,
        grad_w_out,
        grad_w_mlp,
        grad_w_down,
        grad_gates,
        small[G_BIAS : G_BIAS + 2],
        small[G_LAM],
        small[G_CONV_W : G_CONV_W + CONV],
        small[G_CONV_B],
        gains[0],
        gains[1],
        small[G_H],
        small[G_STATE : G_STATE + EDGE],
    )


def solution(mesh):
    cube = Mesh(mesh.devices.reshape(4, 4, 4, 2), ("z", "y", "x", "mp"))
    placed = (
        P(SEQ, None),
        P(SEQ, None),
        P(SEQ),
        P(SEQ),
        P(SEQ, None, "mp"),
        P("mp", SEQ),
        P(SEQ, None, "mp"),
        P("mp", SEQ),
        P(None, "mp", None, None),
        P(None, "mp"),
        P("mp"),
        P(None, "mp"),
        P("mp"),
        P(),
        P(),
        P("mp"),
        P(None, "mp"),
    )
    return jax.shard_map(
        body,
        mesh=cube,
        in_specs=placed,
        out_specs=(
            P(SEQ, None),
            P(SEQ),
            P(SEQ),
            P(SEQ, None),
            P(SEQ, None, "mp"),
            P("mp", SEQ),
            P(SEQ, None, "mp"),
            P("mp", SEQ),
            P(None, "mp", None, None),
            P(None, "mp"),
            P("mp"),
            P(None, "mp"),
            P("mp"),
            P(),
            P(),
            P("mp"),
            P(None, "mp"),
        ),
        check_vma=False,
    )
```

```python
import functools
import jax
import jax.numpy as jnp
from jax import lax
from jax.experimental import pallas as pl
from jax.experimental.pallas import tpu as pltpu
from jax.sharding import Mesh, PartitionSpec as P

CONV = 4
EDGE = CONV - 1
BLOCK = 256
EPSILON = 1e-06
MESH = pl.DeviceIdType.MESH
ANY = pl.BlockSpec(memory_space=pl.ANY)
HBM = pl.BlockSpec(memory_space=pltpu.HBM)
VM = pl.BlockSpec(memory_space=pltpu.VMEM)
MIB = 1024 * 1024
AXES = ("z", "y", "x")
SEQ = ("z", "y", "x")
ORDERS = (("x", "y", "z"), ("y", "z", "x"), ("z", "x", "y"))
F32, BF16 = jnp.float32, jnp.bfloat16
GELU_C, GELU_A = 0.7978845608028654, 0.044715
DMA = pltpu.SemaphoreType.DMA


def dot(left, right):
    return jnp.dot(left, right, preferred_element_type=F32)


def dot_t(left, right):
    return lax.dot_general(left, right, (((1,), (1,)), ((), ())), preferred_element_type=F32)


def outer(left, right):
    return lax.dot_general(left, right, (((0,), (0,)), ((), ())), preferred_element_type=F32)


def greet(peers):
    sem = pltpu.get_barrier_semaphore()
    for peer in peers:
        pl.semaphore_signal(sem, inc=1, device_id=peer, device_id_type=MESH)
    pl.semaphore_wait(sem, len(peers))


def push(src, dst, send, recv, peer):
    return pltpu.make_async_remote_copy(
        src_ref=src, dst_ref=dst, send_sem=send, recv_sem=recv, device_id=peer, device_id_type=MESH
    )


def ring(axis):
    me = lax.axis_index(axis)
    return me, lax.rem(me + 1, 4), lax.rem(me + 2, 4), lax.rem(me + 3, 4)


def all_neighbours():
    peers = []
    for axis in AXES:
        _, up, _, down = ring(axis)
        peers += [{axis: up}, {axis: down}]
    return peers


def params(cid, mib):
    return pltpu.CompilerParams(
        collective_id=cid, has_side_effects=True, vmem_limit_bytes=mib * MIB
    )


def part_of(done, axis, index, rows, cols):
    spot = []
    for name in AXES:
        if name in done:
            spot.append(pl.ds(0, 4))
        elif name == axis:
            spot.append(index)
        else:
            spot.append(lax.axis_index(name))
    return tuple(spot) + (rows, cols)


def pick(names, axis, index, others):
    spot, rest = [], iter(others)
    for name in names:
        spot.append(index if name == axis else next(rest))
    return tuple(spot)


class Scatter:
    def __init__(self, entry, src, cols, order, halves, bufs, out, own_sem, send, recv, band=None):
        self.band, self.band_rows = band, src.shape[-2] if band is None else band[1]
        self.entry, self.src, self.order = entry, src, order
        self.start, self.width = cols
        self.halves, self.bufs, self.out = halves, list(bufs), out
        self.own_sem, self.send, self.recv = own_sem, send, recv
        self.left, self.sent = AXES, []

    def view(self, at, rows=None):
        if rows is None:
            first = self.band[0] if self.band is not None and self.phase == 0 else 0
            rows = pl.ds(first, self.band_rows)
        return at + (rows, pl.ds(self.start if self.phase == 0 else 0, self.width))

    def spread(self, i):
        return ((i // 4, lax.rem(i, 4)), (i,), ())[self.phase]

    def copy(self, src, dst, way, kind, peer):
        at = (self.entry, self.phase, way, kind)
        copy = push(src, dst, self.send.at[at], self.recv.at[at], {self.axis: peer})
        copy.start()
        self.sent.append(copy)
        return copy

    def load(self, index, dst, rows=None):
        src = self.src.at[self.view(pick(self.left, self.axis, index, self.full), rows)]
        copy = pltpu.make_async_copy(src, dst, self.own_sem.at[self.entry, len(self.loads)])
        copy.start()
        self.loads.append(copy)

    def begin(self, phase):
        self.phase, self.axis = phase, self.order[phase]
        self.full = (pl.ds(0, 4),) * (2 - phase)
        me, up, far, down = ring(self.axis)
        self.first, self.second, self.loads = [], [], []
        self.two_step = phase == 0 and self.halves is not None
        if self.two_step:
            self.ones, self.twos, self.near = self.bufs.pop(0), self.bufs.pop(0), self.bufs.pop(0)
            for way, peer in enumerate((up, down)):
                half = self.halves[way]
                src = self.src.at[self.view(pick(self.left, self.axis, far, self.full), half)]
                self.first.append(self.copy(src, self.ones.at[way], way, 0, peer))
            for way, peer in enumerate((up, down)):
                half = self.halves[1 - way]
                src = self.src.at[self.view(pick(self.left, self.axis, peer, self.full), half)]
                dst = self.twos.at[(way,) + self.full + (half,)]
                self.second.append(self.copy(src, dst, way, 1, peer))
            for way, peer in enumerate((up, down)):
                self.load(peer, self.near.at[way], self.halves[way])
        else:
            self.threes = self.bufs.pop(0)
            for step, peer in enumerate((up, far, down)):
                src = self.src.at[self.view(pick(self.left, self.axis, peer, self.full))]
                self.second.append(self.copy(src, self.threes.at[step], step, 0, peer))
        if phase == 0:
            self.own = self.bufs.pop(0)
            self.load(me, self.own)
        self.acc = self.bufs.pop(0) if phase < 2 else self.out

    def middle(self):
        _, up, _, down = ring(self.axis)
        for way, peer in enumerate((up, down)):
            self.first[way].wait_recv()
            self.loads[way].wait()

            def add(i, carry, way=way):
                there = (way,) + self.spread(i)
                total = self.ones[there].astype(F32) + self.near[there].astype(F32)
                self.ones[there] = total.astype(BF16)
                return carry

            lax.fori_loop(0, 16, add, 0)
            dst = self.twos.at[(way,) + self.full + (self.halves[way],)]
            self.second.append(self.copy(self.ones.at[way], dst, way, 2, peer))

    def finish(self):
        me = lax.axis_index(self.axis)
        for copy in self.second:
            copy.wait_recv()
        if self.phase == 0:
            self.loads[-1].wait()
        buf, slots = (self.twos, (0, 1)) if self.two_step else (self.threes, (0, 1, 2))

        def total(i, carry):
            there = self.spread(i)
            if self.phase == 0:
                whole = self.own[there].astype(F32)
            else:
                whole = self.src[self.view(pick(self.left, self.axis, me, there))].astype(F32)
            for slot in slots:
                whole = whole + buf[(slot,) + there].astype(F32)
            if self.phase < 2:
                self.acc[there] = whole.astype(self.acc.dtype)
            else:
                first = 0 if self.band is None else self.band[0]
                self.acc[pl.ds(first, self.band_rows), pl.ds(self.start, self.width)] = whole
            return carry

        lax.fori_loop(0, 4 ** (2 - self.phase), total, 0)
        self.src = self.acc
        self.left = tuple(name for name in self.left if name != self.axis)

    def drain(self):
        for copy in self.sent:
            copy.wait_send()


def scatter_buffers(rows, width, halved):
    bufs = []
    for phase in range(3):
        cube = (4,) * (2 - phase)
        if phase == 0 and halved:
            bufs.append(pltpu.VMEM((2,) + cube + (rows // 2, width), BF16))
            bufs.append(pltpu.VMEM((2,) + cube + (rows, width), BF16))
            bufs.append(pltpu.VMEM((2,) + cube + (rows // 2, width), BF16))
        else:
            bufs.append(pltpu.VMEM((3,) + cube + (rows, width), BF16))
        if phase == 0:
            bufs.append(pltpu.VMEM(cube + (rows, width), BF16))
        if phase < 2:
            bufs.append(pltpu.VMEM(cube + (rows, width), BF16))
    return bufs


class Gather:
    def __init__(self, entry, out, order, cols, send, recv, done=(), ring_rounds=(), band=None):
        self.band = (0, out.shape[3]) if band is None else band
        self.entry, self.out, self.order, self.cols = entry, out, order, pl.ds(*cols)
        self.send, self.recv, self.sent = send, recv, []
        self.done, self.ring_rounds = done, ring_rounds

    def spot(self, origin, rows=None):
        rows = pl.ds(*self.band) if rows is None else rows
        return self.out.at[part_of(self.done, self.axis, origin, rows, self.cols)]

    def copy(self, src, dst, step, way, peer):
        at = (self.entry, self.phase, step, way)
        copy = push(src, dst, self.send.at[at], self.recv.at[at], {self.axis: peer})
        copy.start()
        self.sent.append(copy)
        return copy

    def begin(self, phase, src=None):
        self.phase, self.axis = phase, self.order[phase]
        me, up, far, down = ring(self.axis)
        here = self.spot(me)
        src = here if src is None else src.at[:, self.cols]
        peers = (up, down) if phase in self.ring_rounds else (up, far, down)
        self.copies = [self.copy(src, here, 0, way, peer) for way, peer in enumerate(peers)]

    def middle(self):
        _, up, _, down = ring(self.axis)
        half = self.out.shape[3] // 2
        first, self.copies = self.copies, []
        for way, (peer, origin) in enumerate(((up, down), (down, up))):
            first[way].wait_recv()
            spot = self.spot(origin, pl.ds(way * half, half))
            self.copies.append(self.copy(spot, spot, 1, way, peer))

    def hold(self):
        for copy in self.copies:
            copy.wait_recv()

    def finish(self):
        self.hold()
        self.done = self.done + (self.axis,)

    def drain(self):
        for copy in self.sent:
            copy.wait_send()


class Rounds:
    def __init__(self, slots, send, recv, entry=0, order=("x", "y", "z")):
        self.slots, self.send, self.recv, self.sent = slots, send, recv, []
        self.entry, self.order = entry, order

    def begin(self, phase, rows):
        self.phase, axis = phase, self.order[phase]
        me = lax.axis_index(axis)
        for at, value in rows:
            self.slots[phase, me, at] = value
        self.copies = []
        for step, peer in enumerate(ring(axis)[1:]):
            spot = self.slots.at[phase, me]
            at = (self.entry, phase, step)
            copy = push(spot, spot, self.send.at[at], self.recv.at[at], {axis: peer})
            copy.start()
            self.copies.append(copy)

    def finish(self):
        for copy in self.copies:
            copy.wait_recv()
        self.sent += self.copies

    def drain(self):
        for copy in self.sent:
            copy.wait_send()


class Prefix(Rounds):
    def start(self, pair, backward):
        self.backward, self.cur, self.head = backward, pair, None
        self.share(0)

    def share(self, phase):
        self.begin(phase, [(slice(0, 1), self.cur[0]), (slice(1, 2), self.cur[1])])

    def step(self):
        self.finish()
        me = lax.axis_index(self.order[self.phase])
        run = (jnp.ones_like(self.cur[0]), jnp.zeros_like(self.cur[1]))
        mine = run
        for j in (3, 2, 1, 0) if self.backward else (0, 1, 2, 3):
            take = me == j
            mine = (jnp.where(take, run[0], mine[0]), jnp.where(take, run[1], mine[1]))
            fac, val = self.slots[self.phase, j, 0:1], self.slots[self.phase, j, 1:2]
            run = (run[0] * fac, val + fac * run[1])
        self.cur = run
        if self.head is None:
            self.head = mine
        else:
            self.head = (mine[0] * self.head[0], self.head[1] + self.head[0] * mine[1])
        if self.phase < 2:
            self.share(self.phase + 1)
        return self.head


class Total(Rounds):
    def start(self, value):
        self.begin(0, [(slice(None), value)])

    def step(self):
        self.finish()
        at = self.slots
        k = self.phase
        value = (at[k, 0] + at[k, 1]) + (at[k, 2] + at[k, 3])
        if k + 1 < len(self.order):
            self.begin(k + 1, [(slice(None), value)])
        return value


def axis_peers():
    return [{axis: ring(axis)[step]} for axis in AXES for step in (1, 2, 3)]


def along_seq(distance):
    place = lax.axis_index("z") * 16 + lax.axis_index("y") * 4 + lax.axis_index("x")
    place = lax.rem(place + distance + 64, 64)
    return {"z": place // 16, "y": lax.rem(place // 4, 4), "x": lax.rem(place, 4)}


CHUNKS = ((0, 384), (384, 512), (896, 384))
SUM_ORDERS = (
    (("x", "y", "z"), ("y", "z", "x"), ("z", "x", "y")),
    (("z", "y", "x"), ("x", "z", "y"), ("y", "x", "z")),
    (("y", "z", "x"), ("x", "y", "z"), ("z", "x", "y")),
)
ROW_HALVES = (pl.ds(0, 16), pl.ds(16, 16))
BANDS = ((0, 16), (16, 16), (32, 16))


def gelu_parts(x):
    inner = GELU_C * (x + GELU_A * x * x * x)
    t = jnp.tanh(inner)
    slope = GELU_C * (1.0 + 3.0 * GELU_A * x * x)
    return 0.5 * x * (1.0 + t), 0.5 * (1.0 + t) + 0.5 * x * (1.0 - t * t) * slope


FAR, UP, DOWN, ME = 0, 1, 2, 3


class RingSum:
    def __init__(self, part, got, one, two, send, recv, sib_send, sib_recv):
        self.part, self.got, self.one, self.two = part, got, one, two
        self.send, self.recv, self.sib_send, self.sib_recv = send, recv, sib_send, sib_recv
        self.core, self.sums, self.sent = lax.axis_index("mp"), {}, []

    def across(self, *slots):
        for slot in slots:
            copy = push(
                self.part.at[slot, 1 - self.core],
                self.got.at[slot],
                self.sib_send.at[slot],
                self.sib_recv.at[slot],
                {"mp": 1 - self.core},
            )
            copy.start()
            self.sums[slot] = copy

    def add(self, dst, src):
        dst[...] = (dst[...].astype(F32) + src[...].astype(F32)).astype(dst.dtype)

    def collect(self, slot):
        self.sums[slot].wait_recv()
        self.add(self.got.at[slot], self.part.at[slot, self.core])

    def far(self):
        self.collect(FAR)
        half = self.one.shape[1]
        _, up, _, down = ring("x")
        self.first = []
        for way, peer in enumerate((up, down)):
            piece = self.got.at[FAR, pl.ds(way * half, half)]
            at = (0, way)
            copy = push(piece, self.one.at[way], self.send.at[at], self.recv.at[at], {"x": peer})
            copy.start()
            self.first.append(copy)

    def near(self):
        half = self.one.shape[1]
        _, up, _, down = ring("x")
        self.second = []
        for way, (peer, slot) in enumerate(((up, UP), (down, DOWN))):
            self.collect(slot)
            self.first[way].wait_recv()
            self.add(self.got.at[slot, pl.ds(way * half, half)], self.one.at[way])
            at = (1, way)
            copy = push(self.got.at[slot], self.two.at[way], self.send.at[at], self.recv.at[at], {"x": peer})
            copy.start()
            self.second.append(copy)

    def total(self):
        self.sums[ME].wait_recv()
        total = self.got[ME].astype(F32) + self.part[ME, self.core].astype(F32)
        for way in range(2):
            self.second[way].wait_recv()
            total = total + self.two[way].astype(F32)
        return total

    def drain(self):
        for copy in self.first + self.second + list(self.sums.values()):
            copy.wait_send()


def ring_sum_scratch(rows, width):
    return [
        pltpu.VMEM((4, rows, width), BF16),
        pltpu.VMEM((2, rows // 2, width), BF16),
        pltpu.VMEM((2, rows, width), BF16),
        DMA((2, 2)),
        DMA((2, 2)),
        DMA((4,)),
        DMA((4,)),
    ]


def mlp_kernel(
    nm_ref, go_ref, hidden_ref, inv_ref, gain_ref, go_hbm, w_hbm,
    grad_hidden_ref, low_ref, term_ref, dw_ref, opart_out,
    go, w, gathered, npart, opart, mlp_in, ggu, gmi, low_half,
    load_sem, wsend, wrecv, gsend, grecv, gsib_send, gsib_recv, core_sem, *sum_refs,
):
    rows, width = nm_ref.shape
    half = rows // 2
    units = mlp_in.shape[1]
    me, up, far, down = ring("x")
    core = lax.axis_index("mp")
    other = {"mp": 1 - core}
    loads = [pltpu.make_async_copy(nm_ref, gathered.at[ME, core], load_sem.at[0])]
    wide = w.shape[4] // 2
    full, every = pl.ds(0, 4), pl.ds(0, w.shape[3])
    last = (("z", 0), ("y", wide))

    def weight_set(axis, index, at, cols):
        return ((index, full) if axis == "z" else (full, index)) + (full, at, pl.ds(cols, wide))

    for e, (axis, cols) in enumerate(last):
        here, ahead, _, behind = ring(axis)
        for k, index in enumerate((here, ahead, behind)):
            spot = weight_set(axis, index, every, cols)
            loads.append(pltpu.make_async_copy(w_hbm.at[spot], w.at[spot], load_sem.at[1 + 3 * e + k]))
    for slot, chip in ((FAR, far), (UP, up), (DOWN, down), (ME, me)):
        at = pl.ds(slot * 2 * rows, 2 * rows)
        loads.append(pltpu.make_async_copy(go_hbm.at[chip], go.at[at], load_sem.at[7 + slot]))
    for load in loads:
        load.start()
    peers = [{"x": up}, {"x": down}, other]
    for axis in ("y", "z"):
        peers += [{axis: ring(axis)[1]}, {axis: ring(axis)[3]}]
    greet(peers)
    top, low = pl.ds(0, half), pl.ds(half, half)
    first = []
    for way, (peer, slot) in enumerate(((up, DOWN), (down, UP))):
        spot = gathered.at[slot, core]
        copy = push(nm_ref, spot, gsend.at[0, way], grecv.at[0, way], {"x": peer})
        copy.start()
        first.append(copy)
    across = [push(nm_ref, gathered.at[ME, core], gsib_send.at[0], gsib_recv.at[0], other)]
    across[0].start()
    rest = []
    for e, (axis, cols) in enumerate(last):
        _, ahead, _, behind = ring(axis)
        deep = w.shape[3] // 2
        for way, (peer, origin) in enumerate(((ahead, behind), (behind, ahead))):
            spot = weight_set(axis, origin, pl.ds(way * deep, deep), cols)
            copy = push(w_hbm.at[spot], w.at[spot], wsend.at[e, way], wrecv.at[e, way], {axis: peer})
            copy.start()
            rest.append(copy)
    second = []
    for way, (peer, slot, piece) in enumerate(((up, DOWN, top), (down, UP, low))):
        first[way].wait_recv()
        spot = gathered.at[slot, core]
        copy = push(
            spot.at[piece], gathered.at[FAR, core, piece], gsend.at[1, way], grecv.at[1, way], {"x": peer}
        )
        copy.start()
        second.append(copy)
        copy = push(spot, spot, gsib_send.at[1 + way], gsib_recv.at[1 + way], other)
        copy.start()
        across.append(copy)
    for copy in rest:
        copy.wait_recv()
    for load in loads:
        load.wait()

    def tile(j, start=0):
        return pl.ds(pl.multiple_of(start + j * 256, 256), 256)

    def columns(at):
        return w[:, :, :, :, at].reshape(width, 256)

    def shard_tile(i, at):
        return w[i // 2, pl.ds(2 * lax.rem(i, 2), 2), :, :, at].reshape(256, -1)

    def grad_tile(j, carry):
        gmi[:, tile(j)] = dot(go[...], columns(tile(j, 2 * units)))
        return carry

    lax.fori_loop(0, units // 256, grad_tile, 0)
    for way, piece in enumerate((top, low)):
        second[way].wait_recv()
        spot = gathered.at[FAR, core, piece]
        copy = push(spot, spot, gsib_send.at[3 + way], gsib_recv.at[3 + way], other)
        copy.start()
        across.append(copy)

    def tokens_step(slot):
        at = pl.ds(slot * 2 * rows, 4 * rows)

        def hidden_tile(j, carry):
            tokens_in = gathered[slot : slot + 2].reshape(4 * rows, width)
            gate = dot(tokens_in, columns(tile(j)))
            up_lin = dot(tokens_in, columns(tile(j, units)))
            grad = gmi[at, tile(j)]
            act, slope = gelu_parts(gate)
            mlp_in[at, tile(j)] = (act * up_lin).astype(BF16)
            ggu[at, tile(j)] = (slope * (grad * up_lin)).astype(BF16)
            ggu[at, tile(j, units)] = (grad * act).astype(BF16)
            return carry

        lax.fori_loop(0, units // 256, hidden_tile, 0)

        def back_tile(j, carry):
            back = dot_t(ggu[at], shard_tile(j, pl.ds(0, 2 * units)))
            npart[slot : slot + 2, :, :, tile(j)] = back.astype(BF16).reshape(2, 2, rows, 256)
            return carry

        lax.fori_loop(0, width // 256, back_tile, 0)

    def out_tile(j, carry):
        part = dot_t(mlp_in[...], shard_tile(j, pl.ds(2 * units, units)))
        opart[:, :, :, tile(j)] = part.astype(BF16).reshape(4, 2, rows, 256)
        return carry

    def weight_grads(lower, upper):
        def step(i, carry):
            left = gathered[:, :, :, tile(i)].reshape(8 * rows, 256)
            dw_ref[tile(i), pl.ds(0, 2 * units)] = outer(left, ggu[...]).astype(BF16)
            dw_ref[tile(i), pl.ds(2 * units, units)] = outer(go[:, tile(i)], mlp_in[...]).astype(BF16)
            return carry

        lax.fori_loop(lower, upper, step, 0)

    sums = RingSum(npart, *sum_refs)
    for copy in across:
        copy.wait_recv()
    tokens_step(FAR)
    sums.across(FAR, UP)
    sums.far()
    tokens_step(DOWN)
    sums.across(DOWN, ME)
    sums.near()
    lax.fori_loop(0, width // 256, out_tile, 0)
    save = pltpu.make_async_copy(opart, opart_out, load_sem.at[11])
    save.start()
    weight_grads(0, 5)
    grad_normed = sums.total()
    hat = hidden_ref[...] * inv_ref[...]
    grad_hat = grad_normed * gain_ref[...]
    inner = jnp.mean(grad_hat * hat, axis=-1, keepdims=True)
    grad_hidden = go_ref[...].astype(F32) + inv_ref[...] * (grad_hat - hat * inner)
    grad_hidden_ref[...] = grad_hidden
    term_ref[...] = jnp.sum(grad_normed * hat, axis=0, keepdims=True)
    low_half[...] = grad_hidden.astype(BF16)
    low_ref[core] = low_half[...]
    swap = push(low_half, low_ref.at[core], core_sem.at[0], core_sem.at[1], other)
    swap.start()
    weight_grads(5, 8)
    swap.wait()
    save.wait()
    sums.drain()
    for copy in first + second + across + rest:
        copy.wait_send()


def mlp(normed, grad_out, hidden, inverse, gain, grad_out_all, weights, cid):
    rows, width = normed.shape
    units = weights.shape[4] // 3

    def block(dtype, *shape):
        return pltpu.VMEM(shape, dtype)

    return pl.pallas_call(
        mlp_kernel,
        out_shape=[
            jax.ShapeDtypeStruct((rows, width), F32),
            jax.ShapeDtypeStruct((2, rows, width), BF16),
            jax.ShapeDtypeStruct((1, width), F32),
            jax.ShapeDtypeStruct((width, 3 * units), BF16),
            jax.ShapeDtypeStruct((4, 2, rows, width), BF16),
        ],
        in_specs=[VM] * 5 + [ANY] * 2,
        out_specs=[VM] * 4 + [HBM],
        scratch_shapes=[
            block(BF16, 8 * rows, width),
            block(BF16, *weights.shape),
            block(BF16, 4, 2, rows, width),
            block(BF16, 4, 2, rows, width),
            block(BF16, 4, 2, rows, width),
            block(BF16, 8 * rows, units),
            block(BF16, 8 * rows, 2 * units),
            block(F32, 8 * rows, units),
            block(BF16, rows, width),
        ]
        + [DMA((12,)), DMA((2, 2)), DMA((2, 2)), DMA((2, 2)), DMA((2, 2)), DMA((5,)), DMA((5,)), DMA((2,))]
        + ring_sum_scratch(rows, width),
        compiler_params=params(cid, 60),
    )(normed, grad_out, hidden, inverse, gain, grad_out_all.reshape(4, 2 * rows, width), weights)


def lanes(n):
    return pl.ds(pl.multiple_of(n * BLOCK, BLOCK), BLOCK)


def minus_expm1(x):
    series = jnp.ones_like(x)
    for k in (9, 8, 7, 6, 5, 4, 3, 2):
        series = 1.0 + x * (1.0 / k) * series
    return jnp.where(x > -0.4, -x * series, 1.0 - jnp.exp(x))


CONV_W, CONV_B, RATES, BIAS, CONV_STATE, H_INIT, SLOPE = 0, 4, 5, 6, 8, 11, 12


def rec_forward_kernel(*refs):
    (
        tokens_ref, gain_ref, gain_mlp_ref, conv_w_ref, conv_b_ref, rates_ref, slope_ref, bias_ref, conv_state_ref,
        h_init_ref, starts_ref, valid_ref, lin_in, gate_in, back_in, mlp0, mlp1, mlp2, cot_ref, g_hbm,
        lin_out, gate_out, back_out, mlp_out, ext_out, act_out, mixed_out, reset_out, input_out, f_out, states_out,
        branch_out, normed_out, go_all, inv_ref, rms_ref, hidden_ref, nm_ref, inv_mlp_ref, rms_mlp_ref, go_ref, v_ref,
        wl, wg, wb, ext, gate_lin, mixed_v, reset_v, input_v, f_v, states, branch_v, normed, tail_in, driven, cf_v,
        part, part_low, part_in, g_v, rms_v, slots, mask_ref,
        tail_sem, load_sem, save_sem, own_sem, move_send, move_recv, send, recv, small_send, small_recv, core_sem,
        go_send, go_recv, go_sib_send, go_sib_recv,
    ) = refs
    count, width = tokens_ref.shape
    rec = f_v.shape[1]
    blocks = rec // BLOCK
    half = count // 2
    core = lax.axis_index("mp")
    other = {"mp": 1 - core}
    here = tuple(lax.axis_index(name) for name in AXES)
    load = pltpu.make_async_copy(g_hbm, g_v, load_sem)
    load.start()
    owns = [
        pltpu.make_async_copy(lin_in, wl.at[here], own_sem.at[0]),
        pltpu.make_async_copy(gate_in, wg.at[here], own_sem.at[1]),
        pltpu.make_async_copy(back_in, wb.at[here], own_sem.at[2]),
    ]
    units = mlp_out.shape[4] // 3
    every = pl.ds(0, lin_in.shape[0])

    def quarter(k, chip):
        return (mlp0, mlp1, mlp2)[k].at[every, pl.ds(pl.multiple_of(chip * units, units), units)]

    spots = [mlp_out.at[here + (every, pl.ds(k * units, units))] for k in range(3)]
    owns += [pltpu.make_async_copy(quarter(k, here[2]), spots[k], own_sem.at[3 + k]) for k in range(3)]
    for own in owns:
        own.start()
    greet(axis_peers() + [other, along_seq(1), along_seq(-1)])
    tail_copy = push(tokens_ref.at[pl.ds(count - 16, 16)], tail_in, tail_sem.at[0], tail_sem.at[1], along_seq(1))
    tail_copy.start()
    lin = [Gather(e, wl, ORDERS[e], CHUNKS[e], send, recv, ring_rounds=(2,)) for e in range(3)]
    gate = [
        Gather(3 + e, wg, ORDERS[(e + 1) % 3], CHUNKS[e], send, recv, ring_rounds=(1, 2)) for e in range(3)
    ]
    back = [
        Gather(6 + e, wb, ORDERS[(2, 1, 0)[e]], CHUNKS[e], send, recv, ring_rounds=(1, 2)) for e in range(3)
    ]
    rest = gate + back
    wide = mlp_out.shape[4] // 2
    mlp_flows = [
        Gather(9 + e, mlp_out, order, (e * wide, wide), send, recv, done=("x",), ring_rounds=(1,))
        for e, order in enumerate((("y", "z"), ("z", "y")))
    ]

    def each(group, name, *args):
        for flow in group:
            getattr(flow, name)(*args)

    each(lin, "begin", 0, lin_in)
    moves = []
    for step, peer in enumerate(ring("x")[1:]):
        for k in range(3):
            copy = push(quarter(k, peer), spots[k], move_send.at[step, k], move_recv.at[step, k], {"x": peer})
            copy.start()
            moves.append(copy)
    each(gate, "begin", 0, gate_in)
    each(back, "begin", 0, back_in)

    v_ref[CONV_W : CONV_W + CONV] = conv_w_ref[...]
    v_ref[BIAS : BIAS + 2] = bias_ref[...]
    v_ref[CONV_STATE : CONV_STATE + EDGE] = conv_state_ref[...]
    for at, ref in ((CONV_B, conv_b_ref), (RATES, rates_ref), (SLOPE, slope_ref), (H_INIT, h_init_ref)):
        v_ref[at : at + 1] = ref[...].reshape(1, rec)
    v_ref[SLOPE + 1 :] = jnp.zeros((15 - SLOPE, rec), F32)
    square = (count, count)
    diagonal = lax.broadcasted_iota(jnp.int32, square, 0) == lax.broadcasted_iota(jnp.int32, square, 1)
    for k, row in enumerate((1.0 - starts_ref[...].astype(F32), valid_ref[...].astype(F32))):
        spread = jnp.where(diagonal, jnp.broadcast_to(row.reshape(1, count), square), 0.0)
        mask_ref[:, k : k + 1] = jnp.sum(spread, axis=1, keepdims=True)

    def norm(values):
        mean_sq = jnp.mean(values * values, axis=-1, keepdims=True)
        inverse = lax.rsqrt(mean_sq + EPSILON)
        return values * inverse, inverse, jnp.sqrt(mean_sq + EPSILON)

    def norm_step(i, carry):
        at = pl.ds(pl.multiple_of(i * 64, 64), 64)
        hat, inverse, rms = norm(tokens_ref[at].astype(F32))
        inv_ref[at] = inverse
        rms_ref[at] = rms
        normed[pl.ds(pl.multiple_of(16 + i * 64, 16), 64)] = (hat * gain_ref[...]).astype(BF16)
        return carry

    lax.fori_loop(0, count // 64, norm_step, 0)
    for own in owns:
        own.wait()
    each(lin, "finish")
    each(lin, "begin", 1)
    each(rest, "finish")
    tail_copy.wait_recv()
    normed[0:16] = (norm(tail_in[...].astype(F32))[0] * gain_ref[...]).astype(BF16)
    saves = []

    def save(src, dst):
        copy = pltpu.make_async_copy(src, dst, save_sem.at[len(saves)])
        copy.start()
        saves.append(copy)

    save(normed.at[pl.ds(16, count)], normed_out)
    each(lin, "finish")
    each(lin, "begin", 2)
    each(rest, "begin", 1)
    each(lin, "middle")
    each(rest, "middle")
    for copy in moves:
        copy.wait_recv()
    each(mlp_flows, "begin", 0)
    each(rest, "finish")
    each(rest, "begin", 2)
    mine = pl.ds(pl.multiple_of(core * half, half), half)
    go_ref[...] = (cot_ref[mine].astype(F32) * mask_ref[mine, 1:2]).astype(BF16)
    load.wait()
    each(lin, "finish")
    save(wl, lin_out)
    is_first = (here[0] + here[1] + here[2]) == 0

    def rec_step(n, carry):
        at = lanes(n)
        ext[:, at] = dot(normed[...], wl[:, :, :, :, at].reshape(width, BLOCK))

        @pl.when(is_first)
        def _():
            ext[16 - EDGE : 16, at] = v_ref[CONV_STATE : CONV_STATE + EDGE, at]

        total = v_ref[CONV_B : CONV_B + 1, at] + jnp.zeros((count, BLOCK), F32)
        for k in range(CONV):
            total = total + v_ref[CONV_W + k : CONV_W + k + 1, at] * ext[pl.ds(16 - EDGE + k, count), at]
        mixed = total.astype(BF16)
        mixed_v[:, at] = mixed
        reset = jax.nn.sigmoid(dot(mixed, g_v[0, n]) + v_ref[BIAS : BIAS + 1, at])
        gated = jax.nn.sigmoid(dot(mixed, g_v[1, n]) + v_ref[BIAS + 1 : BIAS + 2, at])
        reset_v[:, at] = reset
        input_v[:, at] = gated
        log_decay = -8.0 * v_ref[RATES : RATES + 1, at] * reset
        f_v[:, at] = jnp.exp(log_decay) * mask_ref[:, 0:1]
        driven[:, at] = jnp.sqrt(minus_expm1(2.0 * log_decay)) * gated * mixed.astype(F32)
        return carry

    lax.fori_loop(0, blocks, rec_step, 0)
    for src, dst in ((ext, ext_out), (mixed_v, mixed_out), (reset_v, reset_out), (input_v, input_out), (f_v, f_out)):
        save(src, dst)

    def group(i, carry):
        base = pl.multiple_of(i * 8, 8)
        f, d = f_v[pl.ds(base, 8)], driven[pl.ds(base, 8)]
        cf, cd = carry
        cfs, cds = [], []
        for r in range(8):
            cf = cf * f[r : r + 1]
            cd = cd * f[r : r + 1] + d[r : r + 1]
            cfs.append(cf)
            cds.append(cd)
        cf_v[pl.ds(base, 8)] = jnp.concatenate(cfs, axis=0)
        states[pl.ds(pl.multiple_of(base + 8, 8), 8)] = jnp.concatenate(cds, axis=0)
        return cf, cd

    zero = jnp.zeros((1, rec), F32)
    ends = lax.fori_loop(0, count // 8, group, (zero + 1.0, zero))
    prefix = Prefix(slots, small_send, small_recv)
    prefix.start(ends, False)
    prefix.step()
    prefix.step()
    each(rest, "middle")
    each(mlp_flows, "finish")
    each(mlp_flows, "begin", 1)
    x_here, x_up, x_far, x_down = ring("x")
    spot = go_all.at[x_here, core]
    save(go_ref, spot)
    go_first = []
    for way, peer in enumerate((x_up, x_down)):
        copy = push(go_ref, spot, go_send.at[0, way], go_recv.at[0, way], {"x": peer})
        copy.start()
        go_first.append(copy)
    go_across = [push(go_ref, spot, go_sib_send.at[0], go_sib_recv.at[0], other)]
    go_across[0].start()
    head = prefix.step()
    carry_in = head[1] + head[0] * v_ref[H_INIT : H_INIT + 1]
    each(gate, "finish")
    save(wg, gate_out)

    def gate_step(n, carry):
        gate_lin[:, lanes(n)] = dot(normed[16:], wg[:, :, :, :, lanes(n)].reshape(width, BLOCK))
        return carry

    lax.fori_loop(0, blocks, gate_step, 0)
    save(gate_lin, act_out)
    states[0:8] = jnp.broadcast_to(carry_in, (8, rec))

    def branch_step(n, carry):
        at = lanes(n)
        value = states[8:, at] + cf_v[:, at] * states[0:1, at]
        states[8:, at] = value
        branch_v[:, at] = (gelu_parts(gate_lin[:, at])[0] * value).astype(BF16)
        return carry

    go_second = []
    for way, (peer, origin) in enumerate(((x_up, x_down), (x_down, x_up))):
        go_first[way].wait_recv()
        spot = go_all.at[origin, core]
        piece = spot.at[pl.ds(way * (half // 2), half // 2)]
        copy = push(piece, piece, go_send.at[1, way], go_recv.at[1, way], {"x": peer})
        copy.start()
        go_second.append(copy)
        copy = push(spot, spot, go_sib_send.at[1 + way], go_sib_recv.at[1 + way], other)
        copy.start()
        go_across.append(copy)
    lax.fori_loop(0, blocks, branch_step, 0)
    save(states, states_out)
    save(branch_v, branch_out)
    each(back, "finish")
    save(wb, back_out)

    def out_step(i, carry):
        at = pl.ds(pl.multiple_of(i * 256, 256), 256)
        rows = wb[i // 2, pl.ds(2 * lax.rem(i, 2), 2)].reshape(256, rec)
        value = dot_t(branch_v[...], rows)
        part[0, :, at] = value[:half]
        part[1, :, at] = value[half:]
        return carry

    lax.fori_loop(0, width // 256, out_step, 0)
    part_low[...] = part[1 - core].astype(BF16)
    part_copy = push(part_low, part_in, core_sem.at[0], core_sem.at[1], other)
    part_copy.start()
    for way in range(2):
        go_second[way].wait_recv()
        piece = go_all.at[x_far, core, pl.ds(way * (half // 2), half // 2)]
        copy = push(piece, piece, go_sib_send.at[3 + way], go_sib_recv.at[3 + way], other)
        copy.start()
        go_across.append(copy)
    part_copy.wait_recv()
    hidden = tokens_ref[mine].astype(F32) + (part[core] + part_in[...].astype(F32))
    hidden_ref[...] = hidden
    hat, inverse, rms = norm(hidden)
    inv_mlp_ref[...] = inverse
    rms_v[...] = jnp.broadcast_to(rms, (half, 128))
    rms_mlp_ref[core] = rms_v[...]
    rms_copy = push(rms_v, rms_mlp_ref.at[core], core_sem.at[2], core_sem.at[3], other)
    rms_copy.start()
    nm_ref[...] = (hat * gain_mlp_ref[...]).astype(BF16)
    each(mlp_flows, "hold")
    rms_copy.wait()
    for copy in go_across:
        copy.wait()
    for copy in go_first + go_second:
        copy.wait_send()
    for copy in moves:
        copy.wait_send()
    for copy in saves:
        copy.wait()
    each(lin, "drain")
    each(rest, "drain")
    each(mlp_flows, "drain")
    prefix.drain()
    part_copy.wait_send()
    tail_copy.wait_send()


def rec_forward(tokens, gain_rec, gain_mlp, vectors, masks, lin, gate, back, mlp_weights, cotangent, gates, cid):
    count, width = tokens.shape
    rows, rec = lin.shape
    half = count // 2

    def cube(last):
        return (4, 4, 4, rows, last)

    def sds(shape, dtype):
        return jax.ShapeDtypeStruct(shape, dtype)

    saved = [
        (cube(rec), BF16),
        (cube(rec), BF16),
        (cube(rec), BF16),
        (cube(3 * mlp_weights[0].shape[1] // 4), BF16),
        ((count + 16, rec), F32),
        ((count, rec), F32),
        ((count, rec), BF16),
        ((count, rec), F32),
        ((count, rec), F32),
        ((count, rec), F32),
        ((count + 8, rec), F32),
        ((count, rec), BF16),
        ((count, width), BF16),
        ((4, 2, half, width), BF16),
    ]
    small = [
        ((count, 1), F32),
        ((count, 1), F32),
        ((half, width), F32),
        ((half, width), BF16),
        ((half, 1), F32),
        ((2, half, 128), F32),
        ((half, width), BF16),
        ((16, rec), F32),
    ]
    scratch = saved[:3] + saved[4:12] + [((count + 16, width), BF16), ((16, width), BF16)]
    scratch += [((count, rec), F32), ((count, rec), F32), ((2, half, width), F32)]
    scratch += [((half, width), BF16), ((half, width), BF16), (gates.shape, BF16), ((half, 128), F32), ((3, 4, 2, rec), F32), ((count, 2), F32)]
    return pl.pallas_call(
        rec_forward_kernel,
        out_shape=[sds(*one) for one in saved + small],
        in_specs=[VM] * 19 + [ANY],
        out_specs=[HBM] * len(saved) + [VM] * len(small),
        scratch_shapes=[pltpu.VMEM(*one) for one in scratch]
        + [
            DMA((2,)),
            DMA,
            DMA((13,)),
            DMA((6,)),
            DMA((3, 3)),
            DMA((3, 3)),
            DMA((11, 3, 2, 3)),
            DMA((11, 3, 2, 3)),
            DMA((1, 3, 3)),
            DMA((1, 3, 3)),
            DMA((4,)),
            DMA((2, 2)),
            DMA((2, 2)),
            DMA((5,)),
            DMA((5,)),
        ],
        compiler_params=params(cid, 60),
    )(tokens, gain_rec[None], gain_mlp[None], *vectors, *masks, lin, gate, back, *mlp_weights, cotangent, gates)


G_BIAS, G_LAM, G_CONV_W, G_CONV_B, G_H, G_STATE = 0, 2, 3, 7, 8, 9
GATE_ROWS = 48


def shard_rows(ref, i, value):
    value = value.reshape(2, 4, 32, value.shape[1])
    ref[i // 2, pl.ds(2 * lax.rem(i, 2), 2)] = value


def rec_back_kernel(
    gh_ref, branch_ref, normed_ref, gate_ref, states_ref, f_ref, v_ref, hidden_ref,
    wb_hbm, ext_hbm, mixed_hbm, reset_hbm, input_hbm, g_hbm, wg_hbm, opart_hbm, wl_hbm,
    small_ref, part_ref, gates_out, result_ref, dw_out_hbm, dw_gate_hbm, dw_lin_hbm,
    wb, ext, mixed_v, reset_v, input_v, g_v, wg, opart, gate_low, low, cb, al, gm, dw_out, dw_gate, gg,
    tail, edge, edge_in, slots, result_half,
    *refs,
):
    bufs, refs = refs[:18], refs[18:]
    load_sem, save_sem, small_send, small_recv, edge_sem, own_sem, send, recv, core_sem = refs[:9]
    sum_refs = refs[9:]
    count, rec = gate_ref.shape
    half = count // 2
    width = gh_ref.shape[1]
    blocks = rec // BLOCK
    pairs = (
        (wb_hbm, wb), (ext_hbm, ext), (mixed_hbm, mixed_v), (reset_hbm, reset_v), (input_hbm, input_v), (g_hbm, g_v),
        (wg_hbm, wg), (opart_hbm, opart),
    )
    loads = [pltpu.make_async_copy(src, dst, load_sem.at[k]) for k, (src, dst) in enumerate(pairs)]
    for load in loads:
        load.start()
    saves = []

    def save(src, dst):
        copy = pltpu.make_async_copy(src, dst, save_sem.at[len(saves)])
        copy.start()
        saves.append(copy)

    ahead, behind = along_seq(1), along_seq(-1)
    other = {"mp": 1 - lax.axis_index("mp")}
    greet(axis_peers() + [ahead, behind, other])
    place = lax.axis_index("z") * 16 + lax.axis_index("y") * 4 + lax.axis_index("x")
    is_first = jnp.where(place == 0, 1.0, 0.0)
    has_next = jnp.where(place == 63, 0.0, 1.0)

    def weight_grad(ref, left, right):
        def step(i, carry):
            cols = pl.ds(pl.multiple_of(i * 256, 256), 256)
            shard_rows(ref, i, outer(left[:, cols], right[...]).astype(BF16))
            return carry

        lax.fori_loop(0, left.shape[1] // 256, step, 0)

    loads[0].wait()

    def branch_step(n, carry):
        grad = dot(gh_ref[...], wb[:, lanes(n)])
        act, slope = gelu_parts(gate_ref[:, lanes(n)])
        gate_low[:, lanes(n)] = (slope * (grad * states_ref[8:, lanes(n)])).astype(BF16)
        al[:, lanes(n)] = grad * act
        return carry

    lax.fori_loop(0, blocks, branch_step, 0)
    loads.append(pltpu.make_async_copy(wl_hbm, wb, load_sem.at[8]))
    loads[-1].start()
    loads[7].wait()
    sums = RingSum(opart, *sum_refs)
    sums.across(FAR, UP, DOWN, ME)

    def group(i, carry):
        base = pl.multiple_of(count - 8 - i * 8, 8)
        f, d = f_ref[pl.ds(base, 8)], al[pl.ds(base, 8)]
        follow, cf, cd = carry
        cfs, cds = [None] * 8, [None] * 8
        for r in (7, 6, 5, 4, 3, 2, 1, 0):
            cf = cf * follow
            cd = cd * follow + d[r : r + 1]
            cfs[r], cds[r] = cf, cd
            follow = f[r : r + 1]
        cb[pl.ds(base, 8)] = jnp.concatenate(cfs, axis=0)
        al[pl.ds(base, 8)] = jnp.concatenate(cds, axis=0)
        return follow, cf, cd

    zero = jnp.zeros((1, rec), F32)
    follow, cf, cd = lax.fori_loop(0, count // 8, group, (zero + 1.0, zero + 1.0, zero))
    prefix = Prefix(slots, small_send, small_recv)
    prefix.start((follow * cf, follow * cd), True)
    weight_grad(dw_out, gh_ref, branch_ref)
    save(dw_out, dw_out_hbm)
    prefix.step()
    sums.far()
    weight_grad(dw_gate, normed_ref, gate_low)
    save(dw_gate, dw_gate_hbm)
    prefix.step()
    for load in loads[1:7] + loads[8:]:
        load.wait()

    def part_tile(i, carry):
        at = pl.ds(pl.multiple_of(i * 256, 256), 256)
        value = dot_t(gate_low[...], wg[at, :])
        part_ref[0, :, at] = value[:half]
        part_ref[1, :, at] = value[half:]
        return carry

    lax.fori_loop(0, width // 256, part_tile, 0)
    later = prefix.step()[1]
    sums.near()
    al[...] = al[...] + cb[...] * later

    def grads_step(n, carry):
        at = lanes(n)
        adjoint = al[:, at]
        factors, reset, gated = f_ref[:, at], reset_v[:, at], input_v[:, at]
        mixed_low = mixed_v[:, at]
        mixed = mixed_low.astype(F32)
        rates = v_ref[RATES : RATES + 1, at]
        log_decay = -8.0 * rates * reset
        decays = jnp.exp(log_decay)
        scale_in = jnp.sqrt(minus_expm1(2.0 * log_decay))
        grad_log = adjoint * states_ref[pl.ds(7, count), at] * factors
        grad_log = grad_log - adjoint * gated * mixed * decays * decays / scale_in
        small_ref[G_LAM : G_LAM + 1, at] = (
            8.0 * jnp.sum(grad_log * reset, axis=0, keepdims=True) * v_ref[SLOPE : SLOPE + 1, at]
        )
        small_ref[G_H : G_H + 1, at] = is_first * factors[0:1] * adjoint[0:1]
        grad_reset = (grad_log * (-8.0 * rates) * reset * (1.0 - reset)).astype(BF16)
        grad_input = (adjoint * scale_in * mixed * gated * (1.0 - gated)).astype(BF16)
        for g, grad in enumerate((grad_reset, grad_input)):
            small_ref[G_BIAS + g : G_BIAS + g + 1, at] = jnp.sum(
                grad.astype(F32), axis=0, keepdims=True
            )
            b = g * blocks + n
            rows = pl.ds(pl.multiple_of(16 * lax.rem(b, 3), 16), 16)
            gg[:, :, b // 3, rows, :] = outer(mixed_low, grad).astype(BF16).reshape(4, 4, 16, BLOCK)
        grad_mixed = adjoint * scale_in * gated
        grad_mixed = grad_mixed + dot_t(grad_reset, g_v[0, n]) + dot_t(grad_input, g_v[1, n])
        gm[0:8] = jnp.zeros((8, BLOCK), F32)
        gm[8 : 8 + count] = grad_mixed
        gm[8 + count :] = jnp.zeros((8, BLOCK), F32)
        small_ref[G_CONV_B : G_CONV_B + 1, at] = jnp.sum(grad_mixed, axis=0, keepdims=True)
        total = jnp.zeros((count, BLOCK), F32)
        front = jnp.zeros((8, BLOCK), F32)
        for k in range(CONV):
            small_ref[G_CONV_W + k : G_CONV_W + k + 1, at] = jnp.sum(
                grad_mixed * ext[pl.ds(16 - EDGE + k, count), at], axis=0, keepdims=True
            )
            weight = v_ref[CONV_W + k : CONV_W + k + 1, at]
            total = total + weight * gm[pl.ds(8 + EDGE - k, count)]
            front = front + weight * gm[pl.ds(8 - k, 8)]
        low[:, at] = total.astype(BF16)
        tail[:, at] = total[count - 16 :]
        edge[:, at] = front
        small_ref[G_STATE : G_STATE + EDGE, at] = is_first * front[:EDGE]
        small_ref[G_STATE + EDGE :, at] = jnp.zeros((16 - G_STATE - EDGE, BLOCK), F32)
        return carry

    for x, j in ((3, 1), (3, 2)):
        gg[:, :, x, 16 * j : 16 * j + 16, :] = jnp.zeros((4, 4, 16, BLOCK), BF16)
    lax.fori_loop(0, blocks, grads_step, 0)
    edge_copy = push(edge, edge_in, edge_sem.at[0], edge_sem.at[1], behind)
    edge_copy.start()
    gates = [
        Scatter(
            e, gg, (0, BLOCK), ORDERS[e], None, bufs[6 * e : 6 * e + 6], gates_out, own_sem, send, recv, BANDS[e]
        )
        for e in range(3)
    ]

    def each(name, *args):
        for flow in gates:
            getattr(flow, name)(*args)

    each("begin", 0)
    saves[0].wait()
    edge_copy.wait_recv()
    last = jnp.concatenate([tail[0:13], tail[13:16] + has_next * edge_in[0:EDGE]], axis=0)
    low[count - 16 :] = last.astype(BF16)
    weight_grad(dw_out, normed_ref, low)
    save(dw_out, dw_lin_hbm)
    each("finish")
    each("begin", 1)

    def rest_tile(i, carry):
        at = pl.ds(pl.multiple_of(i * 256, 256), 256)
        value = dot_t(low[...], wb[at, :])
        part_ref[0, :, at] = part_ref[0, :, at] + value[:half]
        part_ref[1, :, at] = part_ref[1, :, at] + value[half:]
        return carry

    lax.fori_loop(0, width // 256, rest_tile, 0)
    each("finish")
    each("begin", 2)
    core = lax.axis_index("mp")
    result_half[...] = (hidden_ref[...] + sums.total()).astype(BF16)
    result_ref[core] = result_half[...]
    result_copy = push(result_half, result_ref.at[core], core_sem.at[0], core_sem.at[1], other)
    result_copy.start()
    each("finish")
    result_copy.wait()
    for copy in saves[1:]:
        copy.wait()
    each("drain")
    sums.drain()
    prefix.drain()
    edge_copy.wait_send()


def rec_back(
    gh, branch, normed, gate_lin, states_ext, factors, vectors, hidden,
    w_back, ext, mixed, reset, gated, gates, w_gate, mlp_part, w_lin, cid,
):
    count, rec = gate_lin.shape
    half, width = hidden.shape

    def like(array):
        return pltpu.VMEM(array.shape, array.dtype)

    wide, low = pltpu.VMEM((count, rec), F32), pltpu.VMEM((count, rec), BF16)
    cube = (4, 4, 4, width // 64, rec)
    bufs = []
    for _ in range(3):
        bufs += scatter_buffers(GATE_ROWS // 3, BLOCK, False)
    return pl.pallas_call(
        rec_back_kernel,
        out_shape=[
            jax.ShapeDtypeStruct((16, rec), F32),
            jax.ShapeDtypeStruct((2, half, width), F32),
            jax.ShapeDtypeStruct((GATE_ROWS, BLOCK), F32),
            jax.ShapeDtypeStruct((2, half, width), BF16),
            jax.ShapeDtypeStruct(cube, BF16),
            jax.ShapeDtypeStruct(cube, BF16),
            jax.ShapeDtypeStruct(cube, BF16),
        ],
        in_specs=[VM] * 8 + [ANY] * 9,
        out_specs=[VM] * 4 + [HBM] * 3,
        scratch_shapes=[
            like(w_back), like(ext), like(mixed), like(reset), like(gated), like(gates), like(w_gate), like(mlp_part),
            low, low, wide, wide, pltpu.VMEM((count + 16, BLOCK), F32),
            pltpu.VMEM(cube, BF16), pltpu.VMEM(cube, BF16), pltpu.VMEM((4, 4, 4, GATE_ROWS, BLOCK), BF16),
            pltpu.VMEM((16, rec), F32), pltpu.VMEM((8, rec), F32), pltpu.VMEM((8, rec), F32),
            pltpu.VMEM((3, 4, 2, rec), F32), pltpu.VMEM((half, width), BF16),
        ]
        + bufs
        + [
            DMA((9,)),
            DMA((3,)),
            DMA((1, 3, 3)),
            DMA((1, 3, 3)),
            DMA((2,)),
            DMA((3, 3)),
            DMA((3, 3, 3, 3)),
            DMA((3, 3, 3, 3)),
            DMA((2,)),
        ]
        + ring_sum_scratch(half, width),
        compiler_params=params(cid, 61),
    )(
        gh, branch, normed, gate_lin, states_ext, factors, vectors, hidden,
        w_back, ext, mixed, reset, gated, gates, w_gate, mlp_part, w_lin,
    )


def rec_end_kernel(
    part, small_ref, gain_term_ref, gh_ref, tokens_in, inverse_ref, gain_ref, gates_in,
    dw0, dw1, dw2,
    total_ref, gains_ref, all_gates_ref, out0, out1, out2, tokens_hbm,
    *refs,
):
    bufs, refs = refs[: 9 * 8], refs[9 * 8 :]
    (
        part_low, part_in, tokens_v, gates_ref, ring_gains, gains0, small0, small1, small2,
        load_sem, own_sem, send, recv, gsend, grecv, small_send, small_recv, ring_send, ring_recv, core_sem,
    ) = refs
    half, width = gh_ref.shape
    core = lax.axis_index("mp")
    other = {"mp": 1 - core}
    x_here = lax.axis_index("x")
    greet(axis_peers() + [other] + [{"x": peer, "mp": 1 - core} for peer in ring("x")[1:]])
    small = [
        Total(slots, small_send, small_recv, e, ORDERS[e])
        for e, slots in enumerate((small0, small1, small2))
    ]
    for flow, (start, wide) in zip(small, CHUNKS):
        flow.start(small_ref[:, start : start + wide])
    part_low[...] = part[1 - core].astype(BF16)
    part_copy = push(part_low, part_in, core_sem.at[0], core_sem.at[1], other)
    part_copy.start()
    flows = [
        Scatter(
            e, (dw0, dw1, dw2)[e // 3], CHUNKS[e % 3], SUM_ORDERS[e // 3][e % 3], ROW_HALVES,
            bufs[8 * e : 8 * e + 8], (out0, out1, out2)[e // 3], own_sem, send, recv,
        )
        for e in range(9)
    ]
    one, two, three = flows[:3], flows[3:6], flows[6:]
    spread = [Gather(e, gates_ref, ORDERS[e], (0, BLOCK), gsend, grecv, band=BANDS[e]) for e in range(3)]

    def each(group, name, *args):
        for flow in group:
            getattr(flow, name)(*args)

    gates_ref[lax.axis_index("z"), lax.axis_index("y"), x_here] = gates_in[...].astype(BF16)
    each(spread, "begin", 0)
    each(one, "begin", 0)
    part_copy.wait_recv()
    grad_normed = part[core] + part_in[...].astype(F32)
    hat = tokens_in[...].astype(F32) * inverse_ref[...]
    gain_term = jnp.sum(grad_normed * hat, axis=0, keepdims=True)
    quarter = width // 4
    for k in range(4):
        cols = slice(k * quarter, (k + 1) * quarter)
        ring_gains[x_here, core, k : k + 1] = gain_term[:, cols]
        ring_gains[x_here, core, 4 + k : 5 + k] = gain_term_ref[:, cols]
    shares = []
    spot = ring_gains.at[x_here, core]
    group = [{"x": x, "mp": c} for x in ring("x") for c in (core, 1 - core)][1:]
    for k, peer in enumerate(group):
        copy = push(spot, spot, ring_send.at[k], ring_recv.at[k], peer)
        copy.start()
        shares.append(copy)
    each(two, "begin", 0)
    grad_hat = grad_normed * gain_ref[...]
    inner = jnp.mean(grad_hat * hat, axis=-1, keepdims=True)
    tokens_v[...] = gh_ref[...] + inverse_ref[...] * (grad_hat - hat * inner)
    token_copy = push(tokens_v, tokens_hbm.at[core], core_sem.at[2], core_sem.at[3], other)
    token_copy.start()
    token_save = pltpu.make_async_copy(tokens_v, tokens_hbm.at[core], load_sem.at[1])
    token_save.start()
    for flow in small:
        flow.step()
    each(spread, "finish")
    each(spread, "begin", 1)
    each(one, "middle")
    for copy in shares:
        copy.wait_recv()
    gains = Total(gains0, small_send, small_recv, 3, ("y", "z"))
    halves = [ring_gains[x, 0] + ring_gains[x, 1] for x in range(4)]
    gains.start((halves[0] + halves[1]) + (halves[2] + halves[3]))
    each(three, "begin", 0)
    each(two, "middle")
    for flow in small:
        flow.step()
    each(spread, "finish")
    each(spread, "begin", 2)
    gains.step()
    each(one, "finish")
    each(one, "begin", 1)
    each(three, "middle")
    each(two, "finish")
    each(two, "begin", 1)
    each(one, "finish")
    each(one, "begin", 2)
    for flow, (start, wide) in zip(small, CHUNKS):
        total_ref[:, start : start + wide] = flow.step()
    gains_ref[...] = gains.step()
    each(spread, "finish")

    def unpack(b, carry):
        at = pl.ds(pl.multiple_of(16 * lax.rem(b, 3), 16), 16)
        all_gates_ref[b] = gates_ref[:, :, b // 3, at, :].reshape(BLOCK, BLOCK).astype(F32)
        return carry

    lax.fori_loop(0, all_gates_ref.shape[0], unpack, 0)
    each(three, "finish")
    each(three, "begin", 1)
    each(two, "finish")
    each(two, "begin", 2)
    each(one, "finish")
    each(three, "finish")
    each(three, "begin", 2)
    each(two, "finish")
    each(three, "finish")
    for copy in (token_copy, token_save):
        copy.wait()
    each(flows + spread + small, "drain")
    gains.drain()
    for copy in shares + [part_copy]:
        copy.wait_send()


def rec_end(part, small, gain_term, grad_hidden, tokens, inverse, gain, gates, weights, cid):
    half, width = grad_hidden.shape
    rows, rec = weights[0].shape[3:]
    gate_blocks = 2 * rec // BLOCK

    def sds(*shape):
        return jax.ShapeDtypeStruct(shape, F32)

    bufs = []
    for e in range(9):
        bufs += scatter_buffers(rows, CHUNKS[e % 3][1], True)
    return pl.pallas_call(
        rec_end_kernel,
        out_shape=[
            sds(16, rec),
            sds(8, width // 4),
            sds(gate_blocks, BLOCK, BLOCK),
            sds(rows, rec),
            sds(rows, rec),
            sds(rows, rec),
            sds(2, half, width),
        ],
        in_specs=[VM] * 8 + [ANY] * 3,
        out_specs=[VM] * 6 + [HBM],
        scratch_shapes=bufs
        + [
            pltpu.VMEM((half, width), BF16),
            pltpu.VMEM((half, width), BF16),
            pltpu.VMEM((half, width), F32),
            pltpu.VMEM((4, 4, 4) + gates.shape, BF16),
            pltpu.VMEM((4, 2, 8, width // 4), F32),
            pltpu.VMEM((2, 4, 8, width // 4), F32),
        ]
        + [pltpu.VMEM((3, 4, 16, wide), F32) for _, wide in CHUNKS]
        + [
            DMA((2,)),
            DMA((9, 3)),
            DMA((9, 3, 3, 3)),
            DMA((9, 3, 3, 3)),
            DMA((3, 3, 1, 3)),
            DMA((3, 3, 1, 3)),
            DMA((4, 3, 3)),
            DMA((4, 3, 3)),
            DMA((7,)),
            DMA((7,)),
            DMA((4,)),
        ],
        compiler_params=params(cid, 60),
    )(part, small, gain_term, grad_hidden, tokens, inverse, gain, gates, *weights)


def mlp_end_kernel(in_ref, back, send, recv):
    x_here = lax.axis_index("x")
    peers = ring("x")[1:]
    greet([{"x": peer} for peer in peers])
    moves = []
    for step, peer in enumerate(peers):
        copy = push(in_ref.at[peer], back.at[x_here], send.at[step], recv.at[step], {"x": peer})
        copy.start()
        moves.append(copy)
    back[x_here] = in_ref[x_here]
    for copy in moves:
        copy.wait()


def mlp_end(quarters, cid):
    return pl.pallas_call(
        mlp_end_kernel,
        out_shape=jax.ShapeDtypeStruct(quarters.shape, quarters.dtype),
        in_specs=[VM],
        out_specs=VM,
        scratch_shapes=[DMA((3,)), DMA((3,))],
        compiler_params=params(cid, 61),
    )(quarters)


def finish_kernel(
    small_hbm, gains_hbm, out_hbm, gate_hbm, lin_hbm, back_hbm, result_in, tokens_in, gates_in,
    result_ref, tokens_ref, gates_ref, rec_ref, out_ref, mlp_ref, down_ref, bias_ref, lam_ref, conv_w_ref, conv_b_ref,
    gain_rec_ref, gain_mlp_ref, h_ref, state_ref,
    small_ref, gains_ref, out_sums, gate_sums, lin_sums, back, result_v, tokens_v, gates_v, sem, out_sem,
):
    pairs = (
        (result_in, result_v), (tokens_in, tokens_v), (gates_in, gates_v),
        (small_hbm, small_ref), (gains_hbm, gains_ref), (out_hbm, out_sums), (gate_hbm, gate_sums),
        (lin_hbm, lin_sums), (back_hbm, back),
    )
    loads = [pltpu.make_async_copy(src, dst, sem.at[k]) for k, (src, dst) in enumerate(pairs)]
    for load in loads:
        load.start()
    copies = []
    for k, (src, dst) in enumerate(((result_v, result_ref), (tokens_v, tokens_ref), (gates_v, gates_ref))):
        loads[k].wait()
        copies.append(pltpu.make_async_copy(src, dst, out_sem.at[k]))
        copies[k].start()
    for load in loads[3:]:
        load.wait()
    rec_ref[:, 0, :] = gate_sums[...]
    rec_ref[:, 1, :] = lin_sums[...]
    out_ref[...] = out_sums[...]
    units = down_ref.shape[1] // 4
    for q in range(4):
        value = back[q].astype(F32)
        at = pl.ds(q * units, units)
        for k in range(2):
            mlp_ref[:, k, at] = value[:, k * units : (k + 1) * units]
        down_ref[:, at] = value[:, 2 * units :]
    bias_ref[...] = small_ref[G_BIAS : G_BIAS + 2]
    lam_ref[...] = small_ref[G_LAM]
    conv_w_ref[...] = small_ref[G_CONV_W : G_CONV_W + CONV]
    conv_b_ref[...] = small_ref[G_CONV_B]
    h_ref[...] = small_ref[G_H]
    state_ref[...] = small_ref[G_STATE : G_STATE + EDGE]
    quarter = gains_ref.shape[1]
    for k in range(4):
        at = pl.ds(k * quarter, quarter)
        gain_rec_ref[at] = gains_ref[k]
        gain_mlp_ref[at] = gains_ref[4 + k]
    for copy in copies:
        copy.wait()


def finish(small, gains, sums, back, result, tokens, gates):
    rec = small.shape[1]
    rows = back.shape[1]
    units = back.shape[2] // 3
    width = gains.size // 2

    def sds(*shape):
        return jax.ShapeDtypeStruct(shape, F32)

    return pl.pallas_call(
        finish_kernel,
        out_shape=[
            jax.ShapeDtypeStruct(result.shape, result.dtype),
            sds(*tokens.shape),
            sds(*gates.shape),
            sds(rows, 2, rec),
            sds(rows, rec),
            sds(rows, 2, 4 * units),
            sds(rows, 4 * units),
            sds(2, rec),
            sds(rec),
            sds(CONV, rec),
            sds(rec),
            sds(width),
            sds(width),
            sds(rec),
            sds(EDGE, rec),
        ],
        in_specs=[HBM] * 9,
        out_specs=[HBM] * 3 + [VM] * 12,
        scratch_shapes=[pltpu.VMEM(a.shape, a.dtype) for a in (small, gains, *sums, back, result, tokens, gates)]
        + [DMA((9,)), DMA((3,))],
        compiler_params=pltpu.CompilerParams(vmem_limit_bytes=61 * MIB),
    )(small, gains, *sums, back, result, tokens, gates)


def body(
    tokens,
    cotangent,
    starts,
    valid,
    w_rec,
    w_out,
    w_mlp,
    w_down,
    lru_gates,
    lru_bias,
    lam,
    conv_w,
    conv_b,
    gain_rec,
    gain_mlp,
    h_init,
    conv_state,
):
    count, width = tokens.shape
    shard, _, rec = w_rec.shape
    hidden_units = w_mlp.shape[2] // 4
    half = count // 2
    core = lax.axis_index("mp")

    def my_half(array):
        return lax.dynamic_slice_in_dim(array, core * half, half, axis=0)

    (
        w_lin, w_gate, w_back, mlp_weights, ext, gate_lin, mixed, reset, gated, factors, states_ext, branch_in,
        normed_rec, grad_out_all, inverse_rec, rms_rec, hidden, normed_mlp, inverse_mlp, rms_half, grad_out, vectors,
    ) = rec_forward(
        tokens,
        gain_rec,
        gain_mlp,
        (conv_w, conv_b, jax.nn.softplus(-lam), jax.nn.sigmoid(-lam), lru_bias, conv_state, h_init),
        (starts, valid),
        w_rec[:, 1],
        w_rec[:, 0],
        w_out.T,
        (w_mlp[:, 0], w_mlp[:, 1], w_down.T),
        cotangent,
        lru_gates,
        0,
    )
    w_lin, w_gate, w_back = (w.reshape(width, rec) for w in (w_lin, w_gate, w_back))
    grad_hidden, grad_hidden_low, gain_mlp_term, mlp_terms, mlp_part = mlp(
        normed_mlp, grad_out, hidden, inverse_mlp, gain_mlp[None], grad_out_all, mlp_weights, 1
    )
    mlp_sums = lax.psum_scatter(mlp_terms, ("z", "y"), scatter_dimension=0, tiled=True)
    grad_hidden_low = grad_hidden_low.reshape(count, width)
    small, normed_part, gate_terms, result, *weight_terms = rec_back(
        grad_hidden_low,
        branch_in,
        normed_rec,
        gate_lin,
        states_ext,
        factors,
        vectors,
        hidden,
        w_back,
        ext,
        mixed,
        reset,
        gated,
        lru_gates,
        w_gate,
        mlp_part,
        w_lin,
        2,
    )
    small, gains, gate_blocks, out_sums, gate_sums, lin_sums, grad_tokens = rec_end(
        normed_part,
        small,
        gain_mlp_term,
        grad_hidden,
        my_half(tokens),
        my_half(inverse_rec),
        gain_rec[None],
        gate_terms,
        weight_terms,
        3,
    )
    back = mlp_end(mlp_sums.reshape(4, shard, 3 * hidden_units), 4)
    (
        result, grad_tokens, grad_gates, grad_w_rec, grad_out_t, grad_w_mlp, grad_down_t, grad_bias, grad_lam,
        grad_conv_w, conv_bias_gradient, grad_gain_rec, grad_gain_mlp, grad_h_init, grad_conv_state,
    ) = finish(
        small,
        gains,
        (out_sums, gate_sums, lin_sums),
        back,
        result.reshape(count, width),
        grad_tokens.reshape(count, width),
        gate_blocks.reshape(lru_gates.shape),
    )
    return (
        result,
        rms_rec[:, 0],
        rms_half[:, :, 0].reshape(count),
        grad_tokens,
        grad_w_rec,
        grad_out_t.T,
        grad_w_mlp,
        grad_down_t.T,
        grad_gates,
        grad_bias,
        grad_lam,
        grad_conv_w,
        conv_bias_gradient,
        grad_gain_rec,
        grad_gain_mlp,
        grad_h_init,
        grad_conv_state,
    )


def solution(mesh):
    cube = Mesh(mesh.devices.reshape(4, 4, 4, 2), ("z", "y", "x", "mp"))
    placed = (
        P(SEQ, None),
        P(SEQ, None),
        P(SEQ),
        P(SEQ),
        P(SEQ, None, "mp"),
        P("mp", SEQ),
        P(SEQ, None, "mp"),
        P("mp", SEQ),
        P(None, "mp", None, None),
        P(None, "mp"),
        P("mp"),
        P(None, "mp"),
        P("mp"),
        P(),
        P(),
        P("mp"),
        P(None, "mp"),
    )
    return jax.shard_map(
        body,
        mesh=cube,
        in_specs=placed,
        out_specs=(
            P(SEQ, None),
            P(SEQ),
            P(SEQ),
            P(SEQ, None),
            P(SEQ, None, "mp"),
            P("mp", SEQ),
            P(SEQ, None, "mp"),
            P("mp", SEQ),
            P(None, "mp", None, None),
            P(None, "mp"),
            P("mp"),
            P(None, "mp"),
            P("mp"),
            P(),
            P(),
            P("mp"),
            P(None, "mp"),
        ),
        check_vma=False,
    )
```

```python
import functools
import jax
import jax.numpy as jnp
from jax import lax
from jax.experimental import pallas as pl
from jax.experimental.pallas import tpu as pltpu
from jax.sharding import Mesh, PartitionSpec as P

CONV = 4
EDGE = CONV - 1
BLOCK = 256
EPSILON = 1e-06
MESH = pl.DeviceIdType.MESH
ANY = pl.BlockSpec(memory_space=pl.ANY)
HBM = pl.BlockSpec(memory_space=pltpu.HBM)
VM = pl.BlockSpec(memory_space=pltpu.VMEM)
MIB = 1024 * 1024
AXES = ("z", "y", "x")
SEQ = ("z", "y", "x")
ORDERS = (("x", "y", "z"), ("y", "z", "x"), ("z", "x", "y"))
F32, BF16 = jnp.float32, jnp.bfloat16
GELU_C, GELU_A = 0.7978845608028654, 0.044715
DMA = pltpu.SemaphoreType.DMA


def loop(lower, upper, step, batch):
    main = lower + (upper - lower) // batch * batch

    def several(k, carry):
        for i in range(batch):
            step(lower + k * batch + i, 0)
        return carry

    if main > lower:
        lax.fori_loop(0, (main - lower) // batch, several, 0)
    for i in range(main, upper):
        step(i, 0)


def dot(left, right):
    return jnp.dot(left, right, preferred_element_type=F32)


def dot_t(left, right):
    return lax.dot_general(left, right, (((1,), (1,)), ((), ())), preferred_element_type=F32)


def outer(left, right):
    return lax.dot_general(left, right, (((0,), (0,)), ((), ())), preferred_element_type=F32)


def greet(peers):
    sem = pltpu.get_barrier_semaphore()
    for peer in peers:
        pl.semaphore_signal(sem, inc=1, device_id=peer, device_id_type=MESH)
    pl.semaphore_wait(sem, len(peers))


def push(src, dst, send, recv, peer):
    return pltpu.make_async_remote_copy(
        src_ref=src, dst_ref=dst, send_sem=send, recv_sem=recv, device_id=peer, device_id_type=MESH
    )


def ring(axis):
    me = lax.axis_index(axis)
    return me, lax.rem(me + 1, 4), lax.rem(me + 2, 4), lax.rem(me + 3, 4)


def all_neighbours():
    peers = []
    for axis in AXES:
        _, up, _, down = ring(axis)
        peers += [{axis: up}, {axis: down}]
    return peers


def params(cid, mib):
    return pltpu.CompilerParams(
        collective_id=cid, has_side_effects=True, vmem_limit_bytes=mib * MIB
    )


def part_of(done, axis, index, rows, cols):
    spot = []
    for name in AXES:
        if name in done:
            spot.append(pl.ds(0, 4))
        elif name == axis:
            spot.append(index)
        else:
            spot.append(lax.axis_index(name))
    return tuple(spot) + (rows, cols)


def pick(names, axis, index, others):
    spot, rest = [], iter(others)
    for name in names:
        spot.append(index if name == axis else next(rest))
    return tuple(spot)


class Scatter:
    def __init__(self, entry, src, cols, order, halves, bufs, out, own_sem, send, recv, band=None):
        self.band, self.band_rows = band, src.shape[-2] if band is None else band[1]
        self.entry, self.src, self.order = entry, src, order
        self.start, self.width = cols
        self.halves, self.bufs, self.out = halves, list(bufs), out
        self.own_sem, self.send, self.recv = own_sem, send, recv
        self.left, self.sent = AXES, []

    def view(self, at, rows=None):
        if rows is None:
            first = self.band[0] if self.band is not None and self.phase == 0 else 0
            rows = pl.ds(first, self.band_rows)
        return at + (rows, pl.ds(self.start if self.phase == 0 else 0, self.width))

    def spread(self, i):
        return ((i // 4, lax.rem(i, 4)), (i,), ())[self.phase]

    def copy(self, src, dst, way, kind, peer):
        at = (self.entry, self.phase, way, kind)
        copy = push(src, dst, self.send.at[at], self.recv.at[at], {self.axis: peer})
        copy.start()
        self.sent.append(copy)
        return copy

    def load(self, index, dst, rows=None):
        src = self.src.at[self.view(pick(self.left, self.axis, index, self.full), rows)]
        copy = pltpu.make_async_copy(src, dst, self.own_sem.at[self.entry, len(self.loads)])
        copy.start()
        self.loads.append(copy)

    def begin(self, phase):
        self.phase, self.axis = phase, self.order[phase]
        self.full = (pl.ds(0, 4),) * (2 - phase)
        me, up, far, down = ring(self.axis)
        self.first, self.second, self.loads = [], [], []
        self.two_step = phase == 0 and self.halves is not None
        if self.two_step:
            self.ones, self.twos, self.near = self.bufs.pop(0), self.bufs.pop(0), self.bufs.pop(0)
            for way, peer in enumerate((up, down)):
                half = self.halves[way]
                src = self.src.at[self.view(pick(self.left, self.axis, far, self.full), half)]
                self.first.append(self.copy(src, self.ones.at[way], way, 0, peer))
            for way, peer in enumerate((up, down)):
                half = self.halves[1 - way]
                src = self.src.at[self.view(pick(self.left, self.axis, peer, self.full), half)]
                dst = self.twos.at[(way,) + self.full + (half,)]
                self.second.append(self.copy(src, dst, way, 1, peer))
            for way, peer in enumerate((up, down)):
                self.load(peer, self.near.at[way], self.halves[way])
        else:
            self.threes = self.bufs.pop(0)
            for step, peer in enumerate((up, far, down)):
                src = self.src.at[self.view(pick(self.left, self.axis, peer, self.full))]
                self.second.append(self.copy(src, self.threes.at[step], step, 0, peer))
        if phase == 0:
            self.own = self.bufs.pop(0)
            self.load(me, self.own)
        self.acc = self.bufs.pop(0) if phase < 2 else self.out

    def middle(self):
        _, up, _, down = ring(self.axis)
        for way, peer in enumerate((up, down)):
            self.first[way].wait_recv()
            self.loads[way].wait()

            def add(i, carry, way=way):
                there = (way,) + self.spread(i)
                total = self.ones[there].astype(F32) + self.near[there].astype(F32)
                self.ones[there] = total.astype(BF16)
                return carry

            lax.fori_loop(0, 16, add, 0)
            dst = self.twos.at[(way,) + self.full + (self.halves[way],)]
            self.second.append(self.copy(self.ones.at[way], dst, way, 2, peer))

    def finish(self):
        me = lax.axis_index(self.axis)
        for copy in self.second:
            copy.wait_recv()
        if self.phase == 0:
            self.loads[-1].wait()
        buf, slots = (self.twos, (0, 1)) if self.two_step else (self.threes, (0, 1, 2))

        def total(i, carry):
            there = self.spread(i)
            if self.phase == 0:
                whole = self.own[there].astype(F32)
            else:
                whole = self.src[self.view(pick(self.left, self.axis, me, there))].astype(F32)
            for slot in slots:
                whole = whole + buf[(slot,) + there].astype(F32)
            if self.phase < 2:
                self.acc[there] = whole.astype(self.acc.dtype)
            else:
                first = 0 if self.band is None else self.band[0]
                self.acc[pl.ds(first, self.band_rows), pl.ds(self.start, self.width)] = whole
            return carry

        lax.fori_loop(0, 4 ** (2 - self.phase), total, 0)
        self.src = self.acc
        self.left = tuple(name for name in self.left if name != self.axis)

    def drain(self):
        for copy in self.sent:
            copy.wait_send()


def scatter_buffers(rows, width, halved):
    bufs = []
    for phase in range(3):
        cube = (4,) * (2 - phase)
        if phase == 0 and halved:
            bufs.append(pltpu.VMEM((2,) + cube + (rows // 2, width), BF16))
            bufs.append(pltpu.VMEM((2,) + cube + (rows, width), BF16))
            bufs.append(pltpu.VMEM((2,) + cube + (rows // 2, width), BF16))
        else:
            bufs.append(pltpu.VMEM((3,) + cube + (rows, width), BF16))
        if phase == 0:
            bufs.append(pltpu.VMEM(cube + (rows, width), BF16))
        if phase < 2:
            bufs.append(pltpu.VMEM(cube + (rows, width), BF16))
    return bufs


class Gather:
    def __init__(self, entry, out, order, cols, send, recv, done=(), ring_rounds=(), band=None):
        self.band = (0, out.shape[3]) if band is None else band
        self.entry, self.out, self.order, self.cols = entry, out, order, pl.ds(*cols)
        self.send, self.recv, self.sent = send, recv, []
        self.done, self.ring_rounds = done, ring_rounds

    def spot(self, origin, rows=None):
        rows = pl.ds(*self.band) if rows is None else rows
        return self.out.at[part_of(self.done, self.axis, origin, rows, self.cols)]

    def copy(self, src, dst, step, way, peer):
        at = (self.entry, self.phase, step, way)
        copy = push(src, dst, self.send.at[at], self.recv.at[at], {self.axis: peer})
        copy.start()
        self.sent.append(copy)
        return copy

    def begin(self, phase, src=None):
        self.phase, self.axis = phase, self.order[phase]
        me, up, far, down = ring(self.axis)
        here = self.spot(me)
        src = here if src is None else src.at[:, self.cols]
        peers = (up, down) if phase in self.ring_rounds else (up, far, down)
        self.copies = [self.copy(src, here, 0, way, peer) for way, peer in enumerate(peers)]

    def middle(self):
        _, up, _, down = ring(self.axis)
        half = self.out.shape[3] // 2
        first, self.copies = self.copies, []
        for way, (peer, origin) in enumerate(((up, down), (down, up))):
            first[way].wait_recv()
            spot = self.spot(origin, pl.ds(way * half, half))
            self.copies.append(self.copy(spot, spot, 1, way, peer))

    def hold(self):
        for copy in self.copies:
            copy.wait_recv()

    def finish(self):
        self.hold()
        self.done = self.done + (self.axis,)

    def drain(self):
        for copy in self.sent:
            copy.wait_send()


class Rounds:
    def __init__(self, slots, send, recv, entry=0, order=("x", "y", "z")):
        self.slots, self.send, self.recv, self.sent = slots, send, recv, []
        self.entry, self.order = entry, order

    def begin(self, phase, rows):
        self.phase, axis = phase, self.order[phase]
        me = lax.axis_index(axis)
        for at, value in rows:
            self.slots[phase, me, at] = value
        self.copies = []
        for step, peer in enumerate(ring(axis)[1:]):
            spot = self.slots.at[phase, me]
            at = (self.entry, phase, step)
            copy = push(spot, spot, self.send.at[at], self.recv.at[at], {axis: peer})
            copy.start()
            self.copies.append(copy)

    def finish(self):
        for copy in self.copies:
            copy.wait_recv()
        self.sent += self.copies

    def drain(self):
        for copy in self.sent:
            copy.wait_send()


class Prefix(Rounds):
    def start(self, pair, backward):
        self.backward, self.cur, self.head = backward, pair, None
        self.share(0)

    def share(self, phase):
        self.begin(phase, [(slice(0, 1), self.cur[0]), (slice(1, 2), self.cur[1])])

    def step(self):
        self.finish()
        me = lax.axis_index(self.order[self.phase])
        run = (jnp.ones_like(self.cur[0]), jnp.zeros_like(self.cur[1]))
        mine = run
        for j in (3, 2, 1, 0) if self.backward else (0, 1, 2, 3):
            take = me == j
            mine = (jnp.where(take, run[0], mine[0]), jnp.where(take, run[1], mine[1]))
            fac, val = self.slots[self.phase, j, 0:1], self.slots[self.phase, j, 1:2]
            run = (run[0] * fac, val + fac * run[1])
        self.cur = run
        if self.head is None:
            self.head = mine
        else:
            self.head = (mine[0] * self.head[0], self.head[1] + self.head[0] * mine[1])
        if self.phase < 2:
            self.share(self.phase + 1)
        return self.head


class Total(Rounds):
    def start(self, value):
        self.begin(0, [(slice(None), value)])

    def step(self):
        self.finish()
        at = self.slots
        k = self.phase
        value = (at[k, 0] + at[k, 1]) + (at[k, 2] + at[k, 3])
        if k + 1 < len(self.order):
            self.begin(k + 1, [(slice(None), value)])
        return value


def axis_peers():
    return [{axis: ring(axis)[step]} for axis in AXES for step in (1, 2, 3)]


def along_seq(distance):
    place = lax.axis_index("z") * 16 + lax.axis_index("y") * 4 + lax.axis_index("x")
    place = lax.rem(place + distance + 64, 64)
    return {"z": place // 16, "y": lax.rem(place // 4, 4), "x": lax.rem(place, 4)}


CHUNKS = ((0, 384), (384, 512), (896, 384))
SUM_ORDERS = (
    (("y", "z", "x"), ("x", "y", "z"), ("z", "y", "x")),
    (("z", "x", "y"), ("x", "z", "y"), ("y", "x", "z")),
    (("y", "z", "x"), ("x", "y", "z"), ("z", "x", "y")),
)
ROW_HALVES = (pl.ds(0, 16), pl.ds(16, 16))
BANDS = ((0, 16), (16, 16), (32, 16))


def gelu_parts(x):
    inner = GELU_C * (x + GELU_A * x * x * x)
    t = jnp.tanh(inner)
    slope = GELU_C * (1.0 + 3.0 * GELU_A * x * x)
    return 0.5 * x * (1.0 + t), 0.5 * (1.0 + t) + 0.5 * x * (1.0 - t * t) * slope


FAR, UP, DOWN, ME = 0, 1, 2, 3


class RingSum:
    def __init__(self, part, got, one, two, send, recv, sib_send, sib_recv):
        self.part, self.got, self.one, self.two = part, got, one, two
        self.send, self.recv, self.sib_send, self.sib_recv = send, recv, sib_send, sib_recv
        self.core, self.sums, self.sent = lax.axis_index("mp"), {}, []

    def across(self, *slots):
        for slot in slots:
            copy = push(
                self.part.at[slot, 1 - self.core],
                self.got.at[slot],
                self.sib_send.at[slot],
                self.sib_recv.at[slot],
                {"mp": 1 - self.core},
            )
            copy.start()
            self.sums[slot] = copy

    def add(self, dst, src):
        dst[...] = (dst[...].astype(F32) + src[...].astype(F32)).astype(dst.dtype)

    def collect(self, slot):
        self.sums[slot].wait_recv()
        self.add(self.got.at[slot], self.part.at[slot, self.core])

    def far(self):
        self.collect(FAR)
        half = self.one.shape[1]
        _, up, _, down = ring("x")
        self.first = []
        for way, peer in enumerate((up, down)):
            piece = self.got.at[FAR, pl.ds(way * half, half)]
            at = (0, way)
            copy = push(piece, self.one.at[way], self.send.at[at], self.recv.at[at], {"x": peer})
            copy.start()
            self.first.append(copy)

    def near(self):
        half = self.one.shape[1]
        _, up, _, down = ring("x")
        self.second = []
        for way, (peer, slot) in enumerate(((up, UP), (down, DOWN))):
            self.collect(slot)
            self.first[way].wait_recv()
            self.add(self.got.at[slot, pl.ds(way * half, half)], self.one.at[way])
            at = (1, way)
            copy = push(self.got.at[slot], self.two.at[way], self.send.at[at], self.recv.at[at], {"x": peer})
            copy.start()
            self.second.append(copy)

    def total(self):
        self.sums[ME].wait_recv()
        total = self.got[ME].astype(F32) + self.part[ME, self.core].astype(F32)
        for way in range(2):
            self.second[way].wait_recv()
            total = total + self.two[way].astype(F32)
        return total

    def drain(self):
        for copy in self.first + self.second + list(self.sums.values()):
            copy.wait_send()


def ring_sum_scratch(rows, width):
    return [
        pltpu.VMEM((4, rows, width), BF16),
        pltpu.VMEM((2, rows // 2, width), BF16),
        pltpu.VMEM((2, rows, width), BF16),
        DMA((2, 2)),
        DMA((2, 2)),
        DMA((4,)),
        DMA((4,)),
    ]


def mlp_kernel(
    nm_ref, go_ref, hidden_ref, inv_ref, gain_ref, go_hbm, w_hbm,
    grad_hidden_ref, low_ref, term_ref, dw_ref, opart_out,
    go, w, gathered, npart, opart, mlp_in, ggu, gmi, low_half,
    load_sem, wsend, wrecv, gsend, grecv, gsib_send, gsib_recv, core_sem, *sum_refs,
):
    rows, width = nm_ref.shape
    half = rows // 2
    units = mlp_in.shape[1]
    me, up, far, down = ring("x")
    core = lax.axis_index("mp")
    other = {"mp": 1 - core}
    loads = [pltpu.make_async_copy(nm_ref, gathered.at[ME, core], load_sem.at[0])]
    wide = w.shape[4] // 2
    full, every = pl.ds(0, 4), pl.ds(0, w.shape[3])
    last = (("z", 0), ("y", wide))

    def weight_set(axis, index, at, cols):
        return ((index, full) if axis == "z" else (full, index)) + (full, at, pl.ds(cols, wide))

    for e, (axis, cols) in enumerate(last):
        here, ahead, _, behind = ring(axis)
        for k, index in enumerate((here, ahead, behind)):
            spot = weight_set(axis, index, every, cols)
            loads.append(pltpu.make_async_copy(w_hbm.at[spot], w.at[spot], load_sem.at[1 + 3 * e + k]))
    for slot, chip in ((FAR, far), (UP, up), (DOWN, down), (ME, me)):
        at = pl.ds(slot * 2 * rows, 2 * rows)
        loads.append(pltpu.make_async_copy(go_hbm.at[chip], go.at[at], load_sem.at[7 + slot]))
    for load in loads:
        load.start()
    peers = [{"x": up}, {"x": down}, other]
    for axis in ("y", "z"):
        peers += [{axis: ring(axis)[1]}, {axis: ring(axis)[3]}]
    greet(peers)
    top, low = pl.ds(0, half), pl.ds(half, half)
    first = []
    for way, (peer, slot) in enumerate(((up, DOWN), (down, UP))):
        spot = gathered.at[slot, core]
        copy = push(nm_ref, spot, gsend.at[0, way], grecv.at[0, way], {"x": peer})
        copy.start()
        first.append(copy)
    across = [push(nm_ref, gathered.at[ME, core], gsib_send.at[0], gsib_recv.at[0], other)]
    across[0].start()
    rest = []
    for e, (axis, cols) in enumerate(last):
        _, ahead, _, behind = ring(axis)
        deep = w.shape[3] // 2
        for way, (peer, origin) in enumerate(((ahead, behind), (behind, ahead))):
            spot = weight_set(axis, origin, pl.ds(way * deep, deep), cols)
            copy = push(w_hbm.at[spot], w.at[spot], wsend.at[e, way], wrecv.at[e, way], {axis: peer})
            copy.start()
            rest.append(copy)
    second = []
    for way, (peer, slot, piece) in enumerate(((up, DOWN, top), (down, UP, low))):
        first[way].wait_recv()
        spot = gathered.at[slot, core]
        copy = push(
            spot.at[piece], gathered.at[FAR, core, piece], gsend.at[1, way], grecv.at[1, way], {"x": peer}
        )
        copy.start()
        second.append(copy)
        copy = push(spot, spot, gsib_send.at[1 + way], gsib_recv.at[1 + way], other)
        copy.start()
        across.append(copy)
    for copy in rest:
        copy.wait_recv()
    for load in loads:
        load.wait()

    def tile(j, start=0):
        return pl.ds(pl.multiple_of(start + j * 256, 256), 256)

    def columns(at):
        return w[:, :, :, :, at].reshape(width, 256)

    def shard_tile(i, at):
        return w[i // 2, pl.ds(2 * lax.rem(i, 2), 2), :, :, at].reshape(256, -1)

    def grad_tile(j, carry):
        gmi[:, tile(j)] = dot(go[...], columns(tile(j, 2 * units)))
        return carry

    loop(0, units // 256, grad_tile, 3)
    for way, piece in enumerate((top, low)):
        second[way].wait_recv()
        spot = gathered.at[FAR, core, piece]
        copy = push(spot, spot, gsib_send.at[3 + way], gsib_recv.at[3 + way], other)
        copy.start()
        across.append(copy)

    def tokens_step(slot):
        at = pl.ds(slot * 2 * rows, 4 * rows)

        def hidden_tile(j, carry):
            tokens_in = gathered[slot : slot + 2].reshape(4 * rows, width)
            gate = dot(tokens_in, columns(tile(j)))
            up_lin = dot(tokens_in, columns(tile(j, units)))
            grad = gmi[at, tile(j)]
            act, slope = gelu_parts(gate)
            mlp_in[at, tile(j)] = (act * up_lin).astype(BF16)
            ggu[at, tile(j)] = (slope * (grad * up_lin)).astype(BF16)
            ggu[at, tile(j, units)] = (grad * act).astype(BF16)
            return carry

        loop(0, units // 256, hidden_tile, 3)

        def back_tile(j, carry):
            back = dot_t(ggu[at], shard_tile(j, pl.ds(0, 2 * units)))
            npart[slot : slot + 2, :, :, tile(j)] = back.astype(BF16).reshape(2, 2, rows, 256)
            return carry

        loop(0, width // 256, back_tile, 2)

    def out_tile(j, carry):
        part = dot_t(mlp_in[...], shard_tile(j, pl.ds(2 * units, units)))
        opart[:, :, :, tile(j)] = part.astype(BF16).reshape(4, 2, rows, 256)
        return carry

    def weight_grads(lower, upper):
        def step(i, carry):
            left = gathered[:, :, :, tile(i)].reshape(8 * rows, 256)
            dw_ref[tile(i), pl.ds(0, 2 * units)] = outer(left, ggu[...]).astype(BF16)
            dw_ref[tile(i), pl.ds(2 * units, units)] = outer(go[:, tile(i)], mlp_in[...]).astype(BF16)
            return carry

        loop(lower, upper, step, 2)

    sums = RingSum(npart, *sum_refs)
    for copy in across:
        copy.wait_recv()
    tokens_step(FAR)
    sums.across(FAR, UP)
    sums.far()
    tokens_step(DOWN)
    sums.across(DOWN, ME)
    sums.near()
    loop(0, width // 256, out_tile, 2)
    save = pltpu.make_async_copy(opart, opart_out, load_sem.at[11])
    save.start()
    weight_grads(0, 5)
    grad_normed = sums.total()
    hat = hidden_ref[...] * inv_ref[...]
    grad_hat = grad_normed * gain_ref[...]
    inner = jnp.mean(grad_hat * hat, axis=-1, keepdims=True)
    grad_hidden = go_ref[...].astype(F32) + inv_ref[...] * (grad_hat - hat * inner)
    grad_hidden_ref[...] = grad_hidden
    term_ref[...] = jnp.sum(grad_normed * hat, axis=0, keepdims=True)
    low_half[...] = grad_hidden.astype(BF16)
    low_ref[core] = low_half[...]
    swap = push(low_half, low_ref.at[core], core_sem.at[0], core_sem.at[1], other)
    swap.start()
    weight_grads(5, 8)
    swap.wait()
    save.wait()
    sums.drain()
    for copy in first + second + across + rest:
        copy.wait_send()


def mlp(normed, grad_out, hidden, inverse, gain, grad_out_all, weights, cid):
    rows, width = normed.shape
    units = weights.shape[4] // 3

    def block(dtype, *shape):
        return pltpu.VMEM(shape, dtype)

    return pl.pallas_call(
        mlp_kernel,
        out_shape=[
            jax.ShapeDtypeStruct((rows, width), F32),
            jax.ShapeDtypeStruct((2, rows, width), BF16),
            jax.ShapeDtypeStruct((1, width), F32),
            jax.ShapeDtypeStruct((width, 3 * units), BF16),
            jax.ShapeDtypeStruct((4, 2, rows, width), BF16),
        ],
        in_specs=[VM] * 5 + [ANY] * 2,
        out_specs=[VM] * 4 + [HBM],
        scratch_shapes=[
            block(BF16, 8 * rows, width),
            block(BF16, *weights.shape),
            block(BF16, 4, 2, rows, width),
            block(BF16, 4, 2, rows, width),
            block(BF16, 4, 2, rows, width),
            block(BF16, 8 * rows, units),
            block(BF16, 8 * rows, 2 * units),
            block(F32, 8 * rows, units),
            block(BF16, rows, width),
        ]
        + [DMA((12,)), DMA((2, 2)), DMA((2, 2)), DMA((2, 2)), DMA((2, 2)), DMA((5,)), DMA((5,)), DMA((2,))]
        + ring_sum_scratch(rows, width),
        compiler_params=params(cid, 60),
    )(normed, grad_out, hidden, inverse, gain, grad_out_all.reshape(4, 2 * rows, width), weights)


def lanes(n):
    return pl.ds(pl.multiple_of(n * BLOCK, BLOCK), BLOCK)


def minus_expm1(x):
    series = jnp.ones_like(x)
    for k in (9, 8, 7, 6, 5, 4, 3, 2):
        series = 1.0 + x * (1.0 / k) * series
    return jnp.where(x > -0.4, -x * series, 1.0 - jnp.exp(x))


CONV_W, CONV_B, RATES, BIAS, CONV_STATE, H_INIT, SLOPE = 0, 4, 5, 6, 8, 11, 12


def rec_forward_kernel(*refs):
    (
        tokens_ref, gain_ref, gain_mlp_ref, conv_w_ref, conv_b_ref, rates_ref, slope_ref, bias_ref, conv_state_ref,
        h_init_ref, starts_ref, valid_ref, rec_in, back_in, mlp_in, down_in, cot_ref, g_hbm,
        lin_out, gate_out, back_out, mlp_out, ext_out, act_out, mixed_out, reset_out, input_out, f_out, states_out,
        branch_out, normed_out, go_all, inv_ref, rms_ref, hidden_ref, nm_ref, inv_mlp_ref, rms_mlp_ref, go_ref, v_ref,
        wl, wg, wb, ext, gate_lin, mixed_v, reset_v, input_v, f_v, states, branch_v, normed, tail_in, driven, cf_v,
        part, part_low, part_in, g_v, rms_v, slots, mask_ref,
        tail_sem, load_sem, save_sem, own_sem, move_send, move_recv, send, recv, small_send, small_recv, core_sem,
        go_send, go_recv, go_sib_send, go_sib_recv,
    ) = refs
    count, width = tokens_ref.shape
    rec = f_v.shape[1]
    gate_in, lin_in = rec_in.at[:, pl.ds(0, rec)], rec_in.at[:, pl.ds(rec, rec)]
    blocks = rec // BLOCK
    half = count // 2
    core = lax.axis_index("mp")
    other = {"mp": 1 - core}
    here = tuple(lax.axis_index(name) for name in AXES)
    load = pltpu.make_async_copy(g_hbm, g_v, load_sem)
    load.start()
    owns = [
        pltpu.make_async_copy(lin_in, wl.at[here], own_sem.at[0]),
        pltpu.make_async_copy(gate_in, wg.at[here], own_sem.at[1]),
        pltpu.make_async_copy(back_in, wb.at[here], own_sem.at[2]),
    ]
    units = mlp_out.shape[4] // 3
    every = pl.ds(0, rec_in.shape[0])

    def quarter(k, chip):
        if k == 2:
            return down_in.at[every, pl.ds(pl.multiple_of(chip * units, units), units)]
        return mlp_in.at[every, pl.ds(pl.multiple_of((4 * k + chip) * units, units), units)]

    spots = [mlp_out.at[here + (every, pl.ds(k * units, units))] for k in range(3)]
    owns += [pltpu.make_async_copy(quarter(k, here[2]), spots[k], own_sem.at[3 + k]) for k in range(3)]
    for own in owns:
        own.start()
    greet(axis_peers() + [other, along_seq(1), along_seq(-1)])
    tail_copy = push(tokens_ref.at[pl.ds(count - 16, 16)], tail_in, tail_sem.at[0], tail_sem.at[1], along_seq(1))
    tail_copy.start()
    lin = [Gather(e, wl, ORDERS[e], CHUNKS[e], send, recv, ring_rounds=(2,)) for e in range(3)]
    gate = [
        Gather(3 + e, wg, ORDERS[(e + 1) % 3], CHUNKS[e], send, recv, ring_rounds=(1, 2)) for e in range(3)
    ]
    back = [
        Gather(6 + e, wb, ORDERS[(2, 1, 0)[e]], CHUNKS[e], send, recv, ring_rounds=(1, 2)) for e in range(3)
    ]
    rest = gate + back
    wide = mlp_out.shape[4] // 2
    mlp_flows = [
        Gather(9 + e, mlp_out, order, (e * wide, wide), send, recv, done=("x",), ring_rounds=(1,))
        for e, order in enumerate((("y", "z"), ("z", "y")))
    ]

    def each(group, name, *args):
        for flow in group:
            getattr(flow, name)(*args)

    each(lin, "begin", 0, lin_in)
    moves = []
    for step, peer in enumerate(ring("x")[1:]):
        for k in range(3):
            copy = push(quarter(k, peer), spots[k], move_send.at[step, k], move_recv.at[step, k], {"x": peer})
            copy.start()
            moves.append(copy)
    each(gate, "begin", 0, gate_in)
    each(back, "begin", 0, back_in)

    v_ref[CONV_W : CONV_W + CONV] = conv_w_ref[...]
    v_ref[BIAS : BIAS + 2] = bias_ref[...]
    v_ref[CONV_STATE : CONV_STATE + EDGE] = conv_state_ref[...]
    for at, ref in ((CONV_B, conv_b_ref), (RATES, rates_ref), (SLOPE, slope_ref), (H_INIT, h_init_ref)):
        v_ref[at : at + 1] = ref[...].reshape(1, rec)
    v_ref[SLOPE + 1 :] = jnp.zeros((15 - SLOPE, rec), F32)
    square = (count, count)
    diagonal = lax.broadcasted_iota(jnp.int32, square, 0) == lax.broadcasted_iota(jnp.int32, square, 1)
    for k, row in enumerate((1.0 - starts_ref[...].astype(F32), valid_ref[...].astype(F32))):
        spread = jnp.where(diagonal, jnp.broadcast_to(row.reshape(1, count), square), 0.0)
        mask_ref[:, k : k + 1] = jnp.sum(spread, axis=1, keepdims=True)

    def norm(values):
        mean_sq = jnp.mean(values * values, axis=-1, keepdims=True)
        inverse = lax.rsqrt(mean_sq + EPSILON)
        return values * inverse, inverse, jnp.sqrt(mean_sq + EPSILON)

    def norm_step(i, carry):
        at = pl.ds(pl.multiple_of(i * 64, 64), 64)
        hat, inverse, rms = norm(tokens_ref[at].astype(F32))
        inv_ref[at] = inverse
        rms_ref[at] = rms
        normed[pl.ds(pl.multiple_of(16 + i * 64, 16), 64)] = (hat * gain_ref[...]).astype(BF16)
        return carry

    lax.fori_loop(0, count // 64, norm_step, 0)
    for own in owns:
        own.wait()
    each(lin, "finish")
    each(lin, "begin", 1)
    each(rest, "finish")
    each(rest, "begin", 1)
    tail_copy.wait_recv()
    normed[0:16] = (norm(tail_in[...].astype(F32))[0] * gain_ref[...]).astype(BF16)
    saves = []

    def save(src, dst):
        copy = pltpu.make_async_copy(src, dst, save_sem.at[len(saves)])
        copy.start()
        saves.append(copy)

    save(normed.at[pl.ds(16, count)], normed_out)
    each(lin, "finish")
    each(lin, "begin", 2)
    for copy in moves:
        copy.wait_recv()
    each(mlp_flows, "begin", 0)
    each(rest, "middle")
    each(lin, "middle")
    each(rest, "finish")
    each(rest, "begin", 2)
    mine = pl.ds(pl.multiple_of(core * half, half), half)
    go_ref[...] = (cot_ref[mine].astype(F32) * mask_ref[mine, 1:2]).astype(BF16)
    load.wait()
    each(lin, "finish")
    save(wl, lin_out)
    is_first = (here[0] + here[1] + here[2]) == 0

    def rec_step(n, carry):
        at = lanes(n)
        ext[:, at] = dot(normed[...], wl[:, :, :, :, at].reshape(width, BLOCK))

        @pl.when(is_first)
        def _():
            ext[16 - EDGE : 16, at] = v_ref[CONV_STATE : CONV_STATE + EDGE, at]

        total = v_ref[CONV_B : CONV_B + 1, at] + jnp.zeros((count, BLOCK), F32)
        for k in range(CONV):
            total = total + v_ref[CONV_W + k : CONV_W + k + 1, at] * ext[pl.ds(16 - EDGE + k, count), at]
        mixed = total.astype(BF16)
        mixed_v[:, at] = mixed
        reset = jax.nn.sigmoid(dot(mixed, g_v[0, n]) + v_ref[BIAS : BIAS + 1, at])
        gated = jax.nn.sigmoid(dot(mixed, g_v[1, n]) + v_ref[BIAS + 1 : BIAS + 2, at])
        reset_v[:, at] = reset
        input_v[:, at] = gated
        log_decay = -8.0 * v_ref[RATES : RATES + 1, at] * reset
        f_v[:, at] = jnp.exp(log_decay) * mask_ref[:, 0:1]
        driven[:, at] = jnp.sqrt(minus_expm1(2.0 * log_decay)) * gated * mixed.astype(F32)
        return carry

    lax.fori_loop(0, blocks, rec_step, 0)
    for src, dst in ((ext, ext_out), (mixed_v, mixed_out), (reset_v, reset_out), (input_v, input_out), (f_v, f_out)):
        save(src, dst)

    def group(i, carry):
        base = pl.multiple_of(i * 8, 8)
        f, d = f_v[pl.ds(base, 8)], driven[pl.ds(base, 8)]
        cf, cd = carry
        cfs, cds = [], []
        for r in range(8):
            cf = cf * f[r : r + 1]
            cd = cd * f[r : r + 1] + d[r : r + 1]
            cfs.append(cf)
            cds.append(cd)
        cf_v[pl.ds(base, 8)] = jnp.concatenate(cfs, axis=0)
        states[pl.ds(pl.multiple_of(base + 8, 8), 8)] = jnp.concatenate(cds, axis=0)
        return cf, cd

    zero = jnp.zeros((1, rec), F32)
    ends = lax.fori_loop(0, count // 8, group, (zero + 1.0, zero))
    prefix = Prefix(slots, small_send, small_recv)
    prefix.start(ends, False)
    by_axis = {axis: [flow for flow in rest if flow.axis == axis] for axis in AXES}
    each(by_axis["x"], "middle")
    prefix.step()
    each(by_axis["y"], "middle")
    each(mlp_flows, "finish")
    mlp_flows[1].begin(1)
    prefix.step()
    each(by_axis["z"], "middle")
    mlp_flows[0].begin(1)
    x_here, x_up, x_far, x_down = ring("x")
    spot = go_all.at[x_here, core]
    save(go_ref, spot)
    go_first = []
    for way, peer in enumerate((x_up, x_down)):
        copy = push(go_ref, spot, go_send.at[0, way], go_recv.at[0, way], {"x": peer})
        copy.start()
        go_first.append(copy)
    go_across = [push(go_ref, spot, go_sib_send.at[0], go_sib_recv.at[0], other)]
    go_across[0].start()
    head = prefix.step()
    carry_in = head[1] + head[0] * v_ref[H_INIT : H_INIT + 1]
    each(gate, "finish")
    save(wg, gate_out)

    def gate_step(n, carry):
        gate_lin[:, lanes(n)] = dot(normed[16:], wg[:, :, :, :, lanes(n)].reshape(width, BLOCK))
        return carry

    lax.fori_loop(0, blocks, gate_step, 0)
    save(gate_lin, act_out)
    states[0:8] = jnp.broadcast_to(carry_in, (8, rec))

    def branch_step(n, carry):
        at = lanes(n)
        value = states[8:, at] + cf_v[:, at] * states[0:1, at]
        states[8:, at] = value
        branch_v[:, at] = (gelu_parts(gate_lin[:, at])[0] * value).astype(BF16)
        return carry

    lax.fori_loop(0, blocks, branch_step, 0)
    save(states, states_out)
    save(branch_v, branch_out)
    each(back, "finish")
    save(wb, back_out)

    def out_step(i, carry):
        at = pl.ds(pl.multiple_of(i * 256, 256), 256)
        rows = wb[i // 2, pl.ds(2 * lax.rem(i, 2), 2)].reshape(256, rec)
        value = dot_t(branch_v[...], rows)
        part[0, :, at] = value[:half]
        part[1, :, at] = value[half:]
        return carry

    lax.fori_loop(0, width // 256, out_step, 0)
    part_low[...] = part[1 - core].astype(BF16)
    part_copy = push(part_low, part_in, core_sem.at[0], core_sem.at[1], other)
    part_copy.start()
    go_second = []
    for way, (peer, origin) in enumerate(((x_up, x_down), (x_down, x_up))):
        go_first[way].wait_recv()
        spot = go_all.at[origin, core]
        piece = spot.at[pl.ds(way * (half // 2), half // 2)]
        copy = push(piece, piece, go_send.at[1, way], go_recv.at[1, way], {"x": peer})
        copy.start()
        go_second.append(copy)
        copy = push(spot, spot, go_sib_send.at[1 + way], go_sib_recv.at[1 + way], other)
        copy.start()
        go_across.append(copy)
    part_copy.wait_recv()
    hidden = tokens_ref[mine].astype(F32) + (part[core] + part_in[...].astype(F32))
    hidden_ref[...] = hidden
    hat, inverse, rms = norm(hidden)
    inv_mlp_ref[...] = inverse
    rms_v[...] = jnp.broadcast_to(rms, (half, 128))
    rms_mlp_ref[core] = rms_v[...]
    rms_copy = push(rms_v, rms_mlp_ref.at[core], core_sem.at[2], core_sem.at[3], other)
    rms_copy.start()
    nm_ref[...] = (hat * gain_mlp_ref[...]).astype(BF16)
    for way in range(2):
        go_second[way].wait_recv()
        piece = go_all.at[x_far, core, pl.ds(way * (half // 2), half // 2)]
        copy = push(piece, piece, go_sib_send.at[3 + way], go_sib_recv.at[3 + way], other)
        copy.start()
        go_across.append(copy)
    each(mlp_flows, "hold")
    rms_copy.wait()
    for copy in go_across:
        copy.wait()
    for copy in go_first + go_second:
        copy.wait_send()
    for copy in moves:
        copy.wait_send()
    for copy in saves:
        copy.wait()
    each(lin, "drain")
    each(rest, "drain")
    each(mlp_flows, "drain")
    prefix.drain()
    part_copy.wait_send()
    tail_copy.wait_send()


def rec_forward(tokens, gain_rec, gain_mlp, vectors, masks, w_rec, back, w_mlp, down, cotangent, gates, cid):
    count, width = tokens.shape
    rows, rec = back.shape
    half = count // 2

    def cube(last):
        return (4, 4, 4, rows, last)

    def sds(shape, dtype):
        return jax.ShapeDtypeStruct(shape, dtype)

    saved = [
        (cube(rec), BF16),
        (cube(rec), BF16),
        (cube(rec), BF16),
        (cube(3 * down.shape[1] // 4), BF16),
        ((count + 16, rec), F32),
        ((count, rec), F32),
        ((count, rec), BF16),
        ((count, rec), F32),
        ((count, rec), F32),
        ((count, rec), F32),
        ((count + 8, rec), F32),
        ((count, rec), BF16),
        ((count, width), BF16),
        ((4, 2, half, width), BF16),
    ]
    small = [
        ((count, 1), F32),
        ((count, 1), F32),
        ((half, width), F32),
        ((half, width), BF16),
        ((half, 1), F32),
        ((2, half, 128), F32),
        ((half, width), BF16),
        ((16, rec), F32),
    ]
    scratch = saved[:3] + saved[4:12] + [((count + 16, width), BF16), ((16, width), BF16)]
    scratch += [((count, rec), F32), ((count, rec), F32), ((2, half, width), F32)]
    scratch += [((half, width), BF16), ((half, width), BF16), (gates.shape, BF16), ((half, 128), F32), ((3, 4, 2, rec), F32), ((count, 2), F32)]
    return pl.pallas_call(
        rec_forward_kernel,
        out_shape=[sds(*one) for one in saved + small],
        in_specs=[VM] * 17 + [ANY],
        out_specs=[HBM] * len(saved) + [VM] * len(small),
        scratch_shapes=[pltpu.VMEM(*one) for one in scratch]
        + [
            DMA((2,)),
            DMA,
            DMA((13,)),
            DMA((6,)),
            DMA((3, 3)),
            DMA((3, 3)),
            DMA((11, 3, 2, 3)),
            DMA((11, 3, 2, 3)),
            DMA((1, 3, 3)),
            DMA((1, 3, 3)),
            DMA((4,)),
            DMA((2, 2)),
            DMA((2, 2)),
            DMA((5,)),
            DMA((5,)),
        ],
        compiler_params=params(cid, 60),
    )(tokens, gain_rec[None], gain_mlp[None], *vectors, *masks, w_rec, back, w_mlp, down, cotangent, gates)


G_BIAS, G_LAM, G_CONV_W, G_CONV_B, G_H, G_STATE = 0, 2, 3, 7, 8, 9
GATE_ROWS = 48


def shard_rows(ref, i, value):
    value = value.reshape(2, 4, 32, value.shape[1])
    ref[i // 2, pl.ds(2 * lax.rem(i, 2), 2)] = value


def rec_back_kernel(
    gh_ref, branch_ref, normed_ref, gate_ref, states_ref, f_ref, v_ref, hidden_ref,
    wb_hbm, ext_hbm, mixed_hbm, reset_hbm, input_hbm, g_hbm, wg_hbm, opart_hbm,
    small_ref, part_ref, low, result_ref, dw_out_hbm, dw_gate_hbm, gg_hbm,
    wb, ext, mixed_v, reset_v, input_v, g_v, wg, opart, gate_low, cb, al, gm, dw_out, dw_gate, gg,
    tail, edge, edge_in, slots, result_half,
    *refs,
):
    load_sem, save_sem, small_send, small_recv, edge_sem, core_sem = refs[:6]
    sum_refs = refs[6:]
    count, rec = gate_ref.shape
    half = count // 2
    width = gh_ref.shape[1]
    blocks = rec // BLOCK
    pairs = (
        (wb_hbm, wb), (ext_hbm, ext), (mixed_hbm, mixed_v), (reset_hbm, reset_v), (input_hbm, input_v), (g_hbm, g_v),
        (wg_hbm, wg), (opart_hbm, opart),
    )
    loads = [pltpu.make_async_copy(src, dst, load_sem.at[k]) for k, (src, dst) in enumerate(pairs)]
    for load in loads:
        load.start()
    saves = []

    def save(src, dst):
        copy = pltpu.make_async_copy(src, dst, save_sem.at[len(saves)])
        copy.start()
        saves.append(copy)

    ahead, behind = along_seq(1), along_seq(-1)
    other = {"mp": 1 - lax.axis_index("mp")}
    greet(axis_peers() + [ahead, behind, other])
    place = lax.axis_index("z") * 16 + lax.axis_index("y") * 4 + lax.axis_index("x")
    is_first = jnp.where(place == 0, 1.0, 0.0)
    has_next = jnp.where(place == 63, 0.0, 1.0)

    def weight_grad(ref, left, right):
        def step(i, carry):
            cols = pl.ds(pl.multiple_of(i * 256, 256), 256)
            shard_rows(ref, i, outer(left[:, cols], right[...]).astype(BF16))
            return carry

        loop(0, left.shape[1] // 256, step, 2)

    loads[0].wait()

    def branch_step(n, carry):
        grad = dot(gh_ref[...], wb[:, lanes(n)])
        act, slope = gelu_parts(gate_ref[:, lanes(n)])
        gate_low[:, lanes(n)] = (slope * (grad * states_ref[8:, lanes(n)])).astype(BF16)
        al[:, lanes(n)] = grad * act
        return carry

    loop(0, blocks, branch_step, 5)
    loads[7].wait()
    sums = RingSum(opart, *sum_refs)
    sums.across(FAR, UP, DOWN, ME)

    def group(i, carry):
        base = pl.multiple_of(count - 8 - i * 8, 8)
        f, d = f_ref[pl.ds(base, 8)], al[pl.ds(base, 8)]
        follow, cf, cd = carry
        cfs, cds = [None] * 8, [None] * 8
        for r in (7, 6, 5, 4, 3, 2, 1, 0):
            cf = cf * follow
            cd = cd * follow + d[r : r + 1]
            cfs[r], cds[r] = cf, cd
            follow = f[r : r + 1]
        cb[pl.ds(base, 8)] = jnp.concatenate(cfs, axis=0)
        al[pl.ds(base, 8)] = jnp.concatenate(cds, axis=0)
        return follow, cf, cd

    zero = jnp.zeros((1, rec), F32)
    follow, cf, cd = lax.fori_loop(0, count // 8, group, (zero + 1.0, zero + 1.0, zero))
    prefix = Prefix(slots, small_send, small_recv)
    prefix.start((follow * cf, follow * cd), True)
    weight_grad(dw_out, gh_ref, branch_ref)
    save(dw_out, dw_out_hbm)
    prefix.step()
    sums.far()
    weight_grad(dw_gate, normed_ref, gate_low)
    save(dw_gate, dw_gate_hbm)
    prefix.step()
    for load in loads[1:7]:
        load.wait()

    def part_tile(i, carry):
        at = pl.ds(pl.multiple_of(i * 256, 256), 256)
        value = dot_t(gate_low[...], wg[at, :])
        part_ref[0, :, at] = value[:half]
        part_ref[1, :, at] = value[half:]
        return carry

    lax.fori_loop(0, width // 256, part_tile, 0)
    later = prefix.step()[1]
    sums.near()
    al[...] = al[...] + cb[...] * later

    def grads_step(n, carry):
        at = lanes(n)
        adjoint = al[:, at]
        factors, reset, gated = f_ref[:, at], reset_v[:, at], input_v[:, at]
        mixed_low = mixed_v[:, at]
        mixed = mixed_low.astype(F32)
        rates = v_ref[RATES : RATES + 1, at]
        log_decay = -8.0 * rates * reset
        decays = jnp.exp(log_decay)
        scale_in = jnp.sqrt(minus_expm1(2.0 * log_decay))
        grad_log = adjoint * states_ref[pl.ds(7, count), at] * factors
        grad_log = grad_log - adjoint * gated * mixed * decays * decays / scale_in
        small_ref[G_LAM : G_LAM + 1, at] = (
            8.0 * jnp.sum(grad_log * reset, axis=0, keepdims=True) * v_ref[SLOPE : SLOPE + 1, at]
        )
        small_ref[G_H : G_H + 1, at] = is_first * factors[0:1] * adjoint[0:1]
        grad_reset = (grad_log * (-8.0 * rates) * reset * (1.0 - reset)).astype(BF16)
        grad_input = (adjoint * scale_in * mixed * gated * (1.0 - gated)).astype(BF16)
        for g, grad in enumerate((grad_reset, grad_input)):
            small_ref[G_BIAS + g : G_BIAS + g + 1, at] = jnp.sum(
                grad.astype(F32), axis=0, keepdims=True
            )
            b = g * blocks + n
            rows = pl.ds(pl.multiple_of(16 * lax.rem(b, 3), 16), 16)
            gg[:, :, b // 3, rows, :] = outer(mixed_low, grad).astype(BF16).reshape(4, 4, 16, BLOCK)
        grad_mixed = adjoint * scale_in * gated
        grad_mixed = grad_mixed + dot_t(grad_reset, g_v[0, n]) + dot_t(grad_input, g_v[1, n])
        gm[0:8] = jnp.zeros((8, BLOCK), F32)
        gm[8 : 8 + count] = grad_mixed
        gm[8 + count :] = jnp.zeros((8, BLOCK), F32)
        small_ref[G_CONV_B : G_CONV_B + 1, at] = jnp.sum(grad_mixed, axis=0, keepdims=True)
        total = jnp.zeros((count, BLOCK), F32)
        front = jnp.zeros((8, BLOCK), F32)
        for k in range(CONV):
            small_ref[G_CONV_W + k : G_CONV_W + k + 1, at] = jnp.sum(
                grad_mixed * ext[pl.ds(16 - EDGE + k, count), at], axis=0, keepdims=True
            )
            weight = v_ref[CONV_W + k : CONV_W + k + 1, at]
            total = total + weight * gm[pl.ds(8 + EDGE - k, count)]
            front = front + weight * gm[pl.ds(8 - k, 8)]
        low[:, at] = total.astype(BF16)
        tail[:, at] = total[count - 16 :]
        edge[:, at] = front
        small_ref[G_STATE : G_STATE + EDGE, at] = is_first * front[:EDGE]
        small_ref[G_STATE + EDGE :, at] = jnp.zeros((16 - G_STATE - EDGE, BLOCK), F32)
        return carry

    for x, j in ((3, 1), (3, 2)):
        gg[:, :, x, 16 * j : 16 * j + 16, :] = jnp.zeros((4, 4, 16, BLOCK), BF16)
    loop(0, blocks, grads_step, 5)
    edge_copy = push(edge, edge_in, edge_sem.at[0], edge_sem.at[1], behind)
    edge_copy.start()
    save(gg, gg_hbm)
    core = lax.axis_index("mp")
    result_half[...] = (hidden_ref[...] + sums.total()).astype(BF16)
    result_ref[core] = result_half[...]
    result_copy = push(result_half, result_ref.at[core], core_sem.at[0], core_sem.at[1], other)
    result_copy.start()
    edge_copy.wait_recv()
    last = jnp.concatenate([tail[0:13], tail[13:16] + has_next * edge_in[0:EDGE]], axis=0)
    low[count - 16 :] = last.astype(BF16)
    result_copy.wait()
    for copy in saves:
        copy.wait()
    sums.drain()
    prefix.drain()
    edge_copy.wait_send()


def rec_back(
    gh, branch, normed, gate_lin, states_ext, factors, vectors, hidden,
    w_back, ext, mixed, reset, gated, gates, w_gate, mlp_part, cid,
):
    count, rec = gate_lin.shape
    half, width = hidden.shape

    def like(array):
        return pltpu.VMEM(array.shape, array.dtype)

    wide, low = pltpu.VMEM((count, rec), F32), pltpu.VMEM((count, rec), BF16)
    cube, gate_cube = (4, 4, 4, width // 64, rec), (4, 4, 4, GATE_ROWS, BLOCK)
    return pl.pallas_call(
        rec_back_kernel,
        out_shape=[
            jax.ShapeDtypeStruct((16, rec), F32),
            jax.ShapeDtypeStruct((2, half, width), F32),
            jax.ShapeDtypeStruct((count, rec), BF16),
            jax.ShapeDtypeStruct((2, half, width), BF16),
            jax.ShapeDtypeStruct(cube, BF16),
            jax.ShapeDtypeStruct(cube, BF16),
            jax.ShapeDtypeStruct(gate_cube, BF16),
        ],
        in_specs=[VM] * 8 + [ANY] * 8,
        out_specs=[VM] * 4 + [HBM] * 3,
        scratch_shapes=[
            like(w_back), like(ext), like(mixed), like(reset), like(gated), like(gates), like(w_gate), like(mlp_part),
            low, wide, wide, pltpu.VMEM((count + 16, BLOCK), F32),
            pltpu.VMEM(cube, BF16), pltpu.VMEM(cube, BF16), pltpu.VMEM(gate_cube, BF16),
            pltpu.VMEM((16, rec), F32), pltpu.VMEM((8, rec), F32), pltpu.VMEM((8, rec), F32),
            pltpu.VMEM((3, 4, 2, rec), F32), pltpu.VMEM((half, width), BF16),
            DMA((8,)),
            DMA((3,)),
            DMA((1, 3, 3)),
            DMA((1, 3, 3)),
            DMA((2,)),
            DMA((2,)),
        ]
        + ring_sum_scratch(half, width),
        compiler_params=params(cid, 61),
    )(
        gh, branch, normed, gate_lin, states_ext, factors, vectors, hidden,
        w_back, ext, mixed, reset, gated, gates, w_gate, mlp_part,
    )


def rec_end_kernel(
    part_in_ref, small_ref, gain_term_ref, gh_ref, tokens_in, inverse_ref, gain_ref, normed_ref, low_ref,
    dw0, dw1, gg_hbm, wl_hbm,
    total_ref, gains_ref, all_gates_ref, out0, out1, out2, tokens_hbm,
    *refs,
):
    bufs, refs = refs[: 9 * 8 + 3 * 6], refs[9 * 8 + 3 * 6 :]
    (
        part, dw2, wl, gates_out, part_low, part_in, tokens_v, gates_ref, ring_gains, gains0, small0, small1, small2,
        load_sem, own_sem, send, recv, gsend, grecv, small_send, small_recv, ring_send, ring_recv, core_sem,
    ) = refs
    half, width = gh_ref.shape
    load = pltpu.make_async_copy(wl_hbm, wl, load_sem.at[0])
    load.start()
    core = lax.axis_index("mp")
    other = {"mp": 1 - core}
    x_here = lax.axis_index("x")
    greet(axis_peers() + [other] + [{"x": peer, "mp": 1 - core} for peer in ring("x")[1:]])
    small = [
        Total(slots, small_send, small_recv, e, ORDERS[e])
        for e, slots in enumerate((small0, small1, small2))
    ]
    for flow, (start, wide) in zip(small, CHUNKS):
        flow.start(small_ref[:, start : start + wide])
    gates = [
        Scatter(
            9 + e, gg_hbm, (0, BLOCK), ORDERS[e], None, bufs[72 + 6 * e : 78 + 6 * e], gates_out,
            own_sem, send, recv, BANDS[e],
        )
        for e in range(3)
    ]
    flows = [
        Scatter(
            e, (dw0, dw1, dw2)[e // 3], CHUNKS[e % 3], SUM_ORDERS[e // 3][e % 3], ROW_HALVES,
            bufs[8 * e : 8 * e + 8], (out0, out1, out2)[e // 3], own_sem, send, recv,
        )
        for e in range(9)
    ]
    one, two, three = flows[:3], flows[3:6], flows[6:]
    spread = [Gather(e, gates_ref, ORDERS[e], (0, BLOCK), gsend, grecv, band=BANDS[e]) for e in range(3)]

    def each(group, name, *args):
        for flow in group:
            getattr(flow, name)(*args)

    each(gates, "begin", 0)
    each(one, "begin", 0)
    each(two, "begin", 0)

    def weight_grad(i, carry):
        cols = pl.ds(pl.multiple_of(i * 256, 256), 256)
        shard_rows(dw2, i, outer(normed_ref[:, cols], low_ref[...]).astype(BF16))
        return carry

    lax.fori_loop(0, width // 256, weight_grad, 0)
    each(three, "begin", 0)
    each(gates, "finish")
    each(gates, "begin", 1)
    for flow in small:
        flow.step()
    load.wait()

    def part_tile(i, carry):
        at = pl.ds(pl.multiple_of(i * 256, 256), 256)
        value = dot_t(low_ref[...], wl[at, :])
        part[0, :, at] = part_in_ref[0, :, at] + value[:half]
        part[1, :, at] = part_in_ref[1, :, at] + value[half:]
        return carry

    lax.fori_loop(0, width // 256, part_tile, 0)
    part_low[...] = part[1 - core].astype(BF16)
    part_copy = push(part_low, part_in, core_sem.at[0], core_sem.at[1], other)
    part_copy.start()
    each(one, "middle")
    part_copy.wait_recv()
    grad_normed = part[core] + part_in[...].astype(F32)
    hat = tokens_in[...].astype(F32) * inverse_ref[...]
    gain_term = jnp.sum(grad_normed * hat, axis=0, keepdims=True)
    quarter = width // 4
    for k in range(4):
        cols = slice(k * quarter, (k + 1) * quarter)
        ring_gains[x_here, core, k : k + 1] = gain_term[:, cols]
        ring_gains[x_here, core, 4 + k : 5 + k] = gain_term_ref[:, cols]
    shares = []
    spot = ring_gains.at[x_here, core]
    group = [{"x": x, "mp": c} for x in ring("x") for c in (core, 1 - core)][1:]
    for k, peer in enumerate(group):
        copy = push(spot, spot, ring_send.at[k], ring_recv.at[k], peer)
        copy.start()
        shares.append(copy)
    grad_hat = grad_normed * gain_ref[...]
    inner = jnp.mean(grad_hat * hat, axis=-1, keepdims=True)
    tokens_v[...] = gh_ref[...] + inverse_ref[...] * (grad_hat - hat * inner)
    token_copy = push(tokens_v, tokens_hbm.at[core], core_sem.at[2], core_sem.at[3], other)
    token_copy.start()
    token_save = pltpu.make_async_copy(tokens_v, tokens_hbm.at[core], load_sem.at[1])
    token_save.start()
    each(two, "middle")
    each(gates, "finish")
    each(gates, "begin", 2)
    for flow in small:
        flow.step()
    each(one, "finish")
    each(one, "begin", 1)
    for copy in shares:
        copy.wait_recv()
    gains = Total(gains0, small_send, small_recv, 3, ("y", "z"))
    halves = [ring_gains[x, 0] + ring_gains[x, 1] for x in range(4)]
    gains.start((halves[0] + halves[1]) + (halves[2] + halves[3]))
    each(three, "middle")
    each(gates, "finish")
    gates_ref[lax.axis_index("z"), lax.axis_index("y"), x_here] = gates_out[...].astype(BF16)
    each(spread, "begin", 0)
    for flow, (start, wide) in zip(small, CHUNKS):
        total_ref[:, start : start + wide] = flow.step()
    each(two, "finish")
    each(two, "begin", 1)
    gains.step()
    each(one, "finish")
    each(one, "begin", 2)
    each(spread, "finish")
    each(spread, "begin", 1)
    each(three, "finish")
    each(three, "begin", 1)
    gains_ref[...] = gains.step()
    each(spread, "finish")
    each(spread, "begin", 2)
    each(two, "finish")
    each(two, "begin", 2)
    each(one, "finish")
    each(three, "finish")
    each(three, "begin", 2)
    each(two, "finish")
    each(spread, "finish")

    def unpack(b, carry):
        at = pl.ds(pl.multiple_of(16 * lax.rem(b, 3), 16), 16)
        all_gates_ref[b] = gates_ref[:, :, b // 3, at, :].reshape(BLOCK, BLOCK).astype(F32)
        return carry

    lax.fori_loop(0, all_gates_ref.shape[0], unpack, 0)
    each(three, "finish")
    for copy in (token_copy, token_save):
        copy.wait()
    each(flows + gates + spread + small, "drain")
    gains.drain()
    for copy in shares + [part_copy]:
        copy.wait_send()


def rec_end(part, small, gain_term, grad_hidden, tokens, inverse, gain, normed, low, weights, gates, w_lin, cid):
    half, width = grad_hidden.shape
    rows, rec = weights[0].shape[3:]
    gate_blocks = 2 * rec // BLOCK

    def sds(*shape):
        return jax.ShapeDtypeStruct(shape, F32)

    bufs = []
    for e in range(9):
        bufs += scatter_buffers(rows, CHUNKS[e % 3][1], True)
    for _ in range(3):
        bufs += scatter_buffers(GATE_ROWS // 3, BLOCK, False)
    return pl.pallas_call(
        rec_end_kernel,
        out_shape=[
            sds(16, rec),
            sds(8, width // 4),
            sds(gate_blocks, BLOCK, BLOCK),
            sds(rows, rec),
            sds(rows, rec),
            sds(rows, rec),
            sds(2, half, width),
        ],
        in_specs=[VM] * 9 + [ANY] * 4,
        out_specs=[VM] * 6 + [HBM],
        scratch_shapes=bufs
        + [
            pltpu.VMEM(part.shape, F32),
            pltpu.VMEM(weights[0].shape, BF16),
            pltpu.VMEM(w_lin.shape, BF16),
            pltpu.VMEM((GATE_ROWS, BLOCK), F32),
            pltpu.VMEM((half, width), BF16),
            pltpu.VMEM((half, width), BF16),
            pltpu.VMEM((half, width), F32),
            pltpu.VMEM(gates.shape, BF16),
            pltpu.VMEM((4, 2, 8, width // 4), F32),
            pltpu.VMEM((2, 4, 8, width // 4), F32),
        ]
        + [pltpu.VMEM((3, 4, 16, wide), F32) for _, wide in CHUNKS]
        + [
            DMA((2,)),
            DMA((12, 3)),
            DMA((12, 3, 3, 3)),
            DMA((12, 3, 3, 3)),
            DMA((3, 3, 1, 3)),
            DMA((3, 3, 1, 3)),
            DMA((4, 3, 3)),
            DMA((4, 3, 3)),
            DMA((7,)),
            DMA((7,)),
            DMA((4,)),
        ],
        compiler_params=params(cid, 60),
    )(part, small, gain_term, grad_hidden, tokens, inverse, gain, normed, low, *weights, gates, w_lin)


def mlp_end_kernel(in_ref, back, send, recv):
    x_here = lax.axis_index("x")
    peers = ring("x")[1:]
    greet([{"x": peer} for peer in peers])
    moves = []
    for step, peer in enumerate(peers):
        copy = push(in_ref.at[peer], back.at[x_here], send.at[step], recv.at[step], {"x": peer})
        copy.start()
        moves.append(copy)
    back[x_here] = in_ref[x_here]
    for copy in moves:
        copy.wait()


def mlp_end(quarters, cid):
    return pl.pallas_call(
        mlp_end_kernel,
        out_shape=jax.ShapeDtypeStruct(quarters.shape, quarters.dtype),
        in_specs=[VM],
        out_specs=VM,
        scratch_shapes=[DMA((3,)), DMA((3,))],
        compiler_params=params(cid, 61),
    )(quarters)


def finish_kernel(
    small_hbm, gains_hbm, out_hbm, gate_hbm, lin_hbm, back_hbm, result_in, tokens_in, gates_in,
    result_ref, tokens_ref, gates_ref, rec_ref, out_ref, mlp_ref, down_ref, bias_ref, lam_ref, conv_w_ref, conv_b_ref,
    gain_rec_ref, gain_mlp_ref, h_ref, state_ref,
    small_ref, gains_ref, out_sums, gate_sums, lin_sums, back, result_v, tokens_v, gates_v, sem, out_sem,
):
    pairs = (
        (result_in, result_v), (tokens_in, tokens_v), (gates_in, gates_v),
        (small_hbm, small_ref), (gains_hbm, gains_ref), (out_hbm, out_sums), (gate_hbm, gate_sums),
        (lin_hbm, lin_sums), (back_hbm, back),
    )
    loads = [pltpu.make_async_copy(src, dst, sem.at[k]) for k, (src, dst) in enumerate(pairs)]
    for load in loads:
        load.start()
    copies = []
    for k, (src, dst) in enumerate(((result_v, result_ref), (tokens_v, tokens_ref), (gates_v, gates_ref))):
        loads[k].wait()
        copies.append(pltpu.make_async_copy(src, dst, out_sem.at[k]))
        copies[k].start()
    for load in loads[3:]:
        load.wait()
    rec_ref[:, 0, :] = gate_sums[...]
    rec_ref[:, 1, :] = lin_sums[...]
    out_ref[...] = out_sums[...]
    units = down_ref.shape[1] // 4
    for q in range(4):
        value = back[q].astype(F32)
        at = pl.ds(q * units, units)
        for k in range(2):
            mlp_ref[:, k, at] = value[:, k * units : (k + 1) * units]
        down_ref[:, at] = value[:, 2 * units :]
    bias_ref[...] = small_ref[G_BIAS : G_BIAS + 2]
    lam_ref[...] = small_ref[G_LAM]
    conv_w_ref[...] = small_ref[G_CONV_W : G_CONV_W + CONV]
    conv_b_ref[...] = small_ref[G_CONV_B]
    h_ref[...] = small_ref[G_H]
    state_ref[...] = small_ref[G_STATE : G_STATE + EDGE]
    quarter = gains_ref.shape[1]
    for k in range(4):
        at = pl.ds(k * quarter, quarter)
        gain_rec_ref[at] = gains_ref[k]
        gain_mlp_ref[at] = gains_ref[4 + k]
    for copy in copies:
        copy.wait()


def finish(small, gains, sums, back, result, tokens, gates):
    rec = small.shape[1]
    rows = back.shape[1]
    units = back.shape[2] // 3
    width = gains.size // 2

    def sds(*shape):
        return jax.ShapeDtypeStruct(shape, F32)

    return pl.pallas_call(
        finish_kernel,
        out_shape=[
            jax.ShapeDtypeStruct(result.shape, result.dtype),
            sds(*tokens.shape),
            sds(*gates.shape),
            sds(rows, 2, rec),
            sds(rows, rec),
            sds(rows, 2, 4 * units),
            sds(rows, 4 * units),
            sds(2, rec),
            sds(rec),
            sds(CONV, rec),
            sds(rec),
            sds(width),
            sds(width),
            sds(rec),
            sds(EDGE, rec),
        ],
        in_specs=[HBM] * 9,
        out_specs=[HBM] * 3 + [VM] * 12,
        scratch_shapes=[pltpu.VMEM(a.shape, a.dtype) for a in (small, gains, *sums, back, result, tokens, gates)]
        + [DMA((9,)), DMA((3,))],
        compiler_params=pltpu.CompilerParams(vmem_limit_bytes=61 * MIB),
    )(small, gains, *sums, back, result, tokens, gates)


def body(
    tokens,
    cotangent,
    starts,
    valid,
    w_rec,
    w_out,
    w_mlp,
    w_down,
    lru_gates,
    lru_bias,
    lam,
    conv_w,
    conv_b,
    gain_rec,
    gain_mlp,
    h_init,
    conv_state,
):
    count, width = tokens.shape
    shard, _, rec = w_rec.shape
    hidden_units = w_mlp.shape[2] // 4
    half = count // 2
    core = lax.axis_index("mp")

    def my_half(array):
        return lax.dynamic_slice_in_dim(array, core * half, half, axis=0)

    (
        w_lin, w_gate, w_back, mlp_weights, ext, gate_lin, mixed, reset, gated, factors, states_ext, branch_in,
        normed_rec, grad_out_all, inverse_rec, rms_rec, hidden, normed_mlp, inverse_mlp, rms_half, grad_out, vectors,
    ) = rec_forward(
        tokens,
        gain_rec,
        gain_mlp,
        (conv_w, conv_b, jax.nn.softplus(-lam), jax.nn.sigmoid(-lam), lru_bias, conv_state, h_init),
        (starts, valid),
        w_rec.reshape(shard, 2 * rec),
        w_out.T,
        w_mlp.reshape(shard, 8 * hidden_units),
        w_down.T,
        cotangent,
        lru_gates,
        0,
    )
    w_lin, w_gate, w_back = (w.reshape(width, rec) for w in (w_lin, w_gate, w_back))
    grad_hidden, grad_hidden_low, gain_mlp_term, mlp_terms, mlp_part = mlp(
        normed_mlp, grad_out, hidden, inverse_mlp, gain_mlp[None], grad_out_all, mlp_weights, 1
    )
    mlp_sums = lax.psum_scatter(mlp_terms, ("z", "y"), scatter_dimension=0, tiled=True)
    grad_hidden_low = grad_hidden_low.reshape(count, width)
    small, normed_part, grad_rec_low, result, *weight_terms, gate_terms = rec_back(
        grad_hidden_low,
        branch_in,
        normed_rec,
        gate_lin,
        states_ext,
        factors,
        vectors,
        hidden,
        w_back,
        ext,
        mixed,
        reset,
        gated,
        lru_gates,
        w_gate,
        mlp_part,
        2,
    )
    small, gains, gate_blocks, out_sums, gate_sums, lin_sums, grad_tokens = rec_end(
        normed_part,
        small,
        gain_mlp_term,
        grad_hidden,
        my_half(tokens),
        my_half(inverse_rec),
        gain_rec[None],
        normed_rec,
        grad_rec_low,
        weight_terms,
        gate_terms,
        w_lin,
        3,
    )
    back = mlp_end(mlp_sums.reshape(4, shard, 3 * hidden_units), 4)
    (
        result, grad_tokens, grad_gates, grad_w_rec, grad_out_t, grad_w_mlp, grad_down_t, grad_bias, grad_lam,
        grad_conv_w, conv_bias_gradient, grad_gain_rec, grad_gain_mlp, grad_h_init, grad_conv_state,
    ) = finish(
        small,
        gains,
        (out_sums, gate_sums, lin_sums),
        back,
        result.reshape(count, width),
        grad_tokens.reshape(count, width),
        gate_blocks.reshape(lru_gates.shape),
    )
    return (
        result,
        rms_rec[:, 0],
        rms_half[:, :, 0].reshape(count),
        grad_tokens,
        grad_w_rec,
        grad_out_t.T,
        grad_w_mlp,
        grad_down_t.T,
        grad_gates,
        grad_bias,
        grad_lam,
        grad_conv_w,
        conv_bias_gradient,
        grad_gain_rec,
        grad_gain_mlp,
        grad_h_init,
        grad_conv_state,
    )


def solution(mesh):
    cube = Mesh(mesh.devices.reshape(4, 4, 4, 2), ("z", "y", "x", "mp"))
    placed = (
        P(SEQ, None),
        P(SEQ, None),
        P(SEQ),
        P(SEQ),
        P(SEQ, None, "mp"),
        P("mp", SEQ),
        P(SEQ, None, "mp"),
        P("mp", SEQ),
        P(None, "mp", None, None),
        P(None, "mp"),
        P("mp"),
        P(None, "mp"),
        P("mp"),
        P(),
        P(),
        P("mp"),
        P(None, "mp"),
    )
    return jax.shard_map(
        body,
        mesh=cube,
        in_specs=placed,
        out_specs=(
            P(SEQ, None),
            P(SEQ),
            P(SEQ),
            P(SEQ, None),
            P(SEQ, None, "mp"),
            P("mp", SEQ),
            P(SEQ, None, "mp"),
            P("mp", SEQ),
            P(None, "mp", None, None),
            P(None, "mp"),
            P("mp"),
            P(None, "mp"),
            P("mp"),
            P(),
            P(),
            P("mp"),
            P(None, "mp"),
        ),
        check_vma=False,
    )
```

```python
import functools
import jax
import jax.numpy as jnp
from jax import lax
from jax.experimental import pallas as pl
from jax.experimental.pallas import tpu as pltpu
from jax.sharding import Mesh, PartitionSpec as P

CONV = 4
EDGE = CONV - 1
BLOCK = 256
EPSILON = 1e-06
MESH = pl.DeviceIdType.MESH
ANY = pl.BlockSpec(memory_space=pl.ANY)
HBM = pl.BlockSpec(memory_space=pltpu.HBM)
VM = pl.BlockSpec(memory_space=pltpu.VMEM)
MIB = 1024 * 1024
AXES = ("z", "y", "x")
SEQ = ("z", "y", "x")
ORDERS = (("x", "y", "z"), ("y", "z", "x"), ("z", "x", "y"))
F32, BF16 = jnp.float32, jnp.bfloat16
GELU_C, GELU_A = 0.7978845608028654, 0.044715
DMA = pltpu.SemaphoreType.DMA


def loop(lower, upper, step, batch):
    main = lower + (upper - lower) // batch * batch

    def several(k, carry):
        for i in range(batch):
            step(lower + k * batch + i, 0)
        return carry

    if main > lower:
        lax.fori_loop(0, (main - lower) // batch, several, 0)
    for i in range(main, upper):
        step(i, 0)


def dot(left, right):
    return jnp.dot(left, right, preferred_element_type=F32)


def dot_t(left, right):
    return lax.dot_general(left, right, (((1,), (1,)), ((), ())), preferred_element_type=F32)


def outer(left, right):
    return lax.dot_general(left, right, (((0,), (0,)), ((), ())), preferred_element_type=F32)


def greet(peers):
    sem = pltpu.get_barrier_semaphore()
    for peer in peers:
        pl.semaphore_signal(sem, inc=1, device_id=peer, device_id_type=MESH)
    pl.semaphore_wait(sem, len(peers))


def push(src, dst, send, recv, peer):
    return pltpu.make_async_remote_copy(
        src_ref=src, dst_ref=dst, send_sem=send, recv_sem=recv, device_id=peer, device_id_type=MESH
    )


def ring(axis):
    me = lax.axis_index(axis)
    return me, lax.rem(me + 1, 4), lax.rem(me + 2, 4), lax.rem(me + 3, 4)


def all_neighbours():
    peers = []
    for axis in AXES:
        _, up, _, down = ring(axis)
        peers += [{axis: up}, {axis: down}]
    return peers


def params(cid, mib):
    return pltpu.CompilerParams(
        collective_id=cid, has_side_effects=True, vmem_limit_bytes=mib * MIB
    )


def part_of(done, axis, index, rows, cols):
    spot = []
    for name in AXES:
        if name in done:
            spot.append(pl.ds(0, 4))
        elif name == axis:
            spot.append(index)
        else:
            spot.append(lax.axis_index(name))
    return tuple(spot) + (rows, cols)


def pick(names, axis, index, others):
    spot, rest = [], iter(others)
    for name in names:
        spot.append(index if name == axis else next(rest))
    return tuple(spot)


class Scatter:
    def __init__(self, entry, src, cols, order, halves, bufs, out, own_sem, send, recv, band=None, rings=1):
        self.rings = 0 if halves is None else rings
        self.band, self.band_rows = band, src.shape[-2] if band is None else band[1]
        self.entry, self.src, self.order = entry, src, order
        self.start, self.width = cols
        self.halves, self.bufs, self.out = halves, list(bufs), out
        self.own_sem, self.send, self.recv = own_sem, send, recv
        self.left, self.sent = AXES, []

    def view(self, at, rows=None):
        if rows is None:
            first = self.band[0] if self.band is not None and self.phase == 0 else 0
            rows = pl.ds(first, self.band_rows)
        return at + (rows, pl.ds(self.start if self.phase == 0 else 0, self.width))

    def spread(self, i):
        return ((i // 4, lax.rem(i, 4)), (i,), ())[self.phase]

    def copy(self, src, dst, way, kind, peer):
        at = (self.entry, self.phase, way, kind)
        copy = push(src, dst, self.send.at[at], self.recv.at[at], {self.axis: peer})
        copy.start()
        self.sent.append(copy)
        return copy

    def load(self, index, dst, rows=None):
        src = self.src.at[self.view(pick(self.left, self.axis, index, self.full), rows)]
        copy = pltpu.make_async_copy(src, dst, self.own_sem.at[self.entry, len(self.loads)])
        copy.start()
        self.loads.append(copy)

    def begin(self, phase):
        self.phase, self.axis = phase, self.order[phase]
        self.full = (pl.ds(0, 4),) * (2 - phase)
        me, up, far, down = ring(self.axis)
        self.first, self.second, self.loads = [], [], []
        self.two_step = phase < self.rings
        if self.two_step:
            self.ones, self.twos = self.bufs.pop(0), self.bufs.pop(0)
            self.near = self.bufs.pop(0) if phase == 0 else None
            for way, peer in enumerate((up, down)):
                half = self.halves[way]
                src = self.src.at[self.view(pick(self.left, self.axis, far, self.full), half)]
                self.first.append(self.copy(src, self.ones.at[way], way, 0, peer))
            for way, peer in enumerate((up, down)):
                half = self.halves[1 - way]
                src = self.src.at[self.view(pick(self.left, self.axis, peer, self.full), half)]
                dst = self.twos.at[(way,) + self.full + (half,)]
                self.second.append(self.copy(src, dst, way, 1, peer))
            for way, peer in enumerate((up, down)):
                if phase == 0:
                    self.load(peer, self.near.at[way], self.halves[way])
        else:
            self.threes = self.bufs.pop(0)
            for step, peer in enumerate((up, far, down)):
                src = self.src.at[self.view(pick(self.left, self.axis, peer, self.full))]
                self.second.append(self.copy(src, self.threes.at[step], step, 0, peer))
        if phase == 0:
            self.own = self.bufs.pop(0)
            self.load(me, self.own)
        self.acc = self.bufs.pop(0) if phase < 2 else self.out

    def middle(self):
        _, up, _, down = ring(self.axis)
        for way, peer in enumerate((up, down)):
            self.first[way].wait_recv()
            if self.phase == 0:
                self.loads[way].wait()

            def add(i, carry, way=way, peer=peer):
                there = (way,) + self.spread(i)
                if self.phase == 0:
                    own = self.near[there]
                else:
                    at = pick(self.left, self.axis, peer, self.spread(i))
                    own = self.src[self.view(at, self.halves[way])]
                total = self.ones[there].astype(F32) + own.astype(F32)
                self.ones[there] = total.astype(BF16)
                return carry

            lax.fori_loop(0, 4 ** (2 - self.phase), add, 0)
            dst = self.twos.at[(way,) + self.full + (self.halves[way],)]
            self.second.append(self.copy(self.ones.at[way], dst, way, 2, peer))

    def finish(self):
        me = lax.axis_index(self.axis)
        for copy in self.second:
            copy.wait_recv()
        if self.phase == 0:
            self.loads[-1].wait()
        buf, slots = (self.twos, (0, 1)) if self.two_step else (self.threes, (0, 1, 2))

        def total(i, carry):
            there = self.spread(i)
            if self.phase == 0:
                whole = self.own[there].astype(F32)
            else:
                whole = self.src[self.view(pick(self.left, self.axis, me, there))].astype(F32)
            for slot in slots:
                whole = whole + buf[(slot,) + there].astype(F32)
            if self.phase < 2:
                self.acc[there] = whole.astype(self.acc.dtype)
            else:
                first = 0 if self.band is None else self.band[0]
                self.acc[pl.ds(first, self.band_rows), pl.ds(self.start, self.width)] = whole
            return carry

        lax.fori_loop(0, 4 ** (2 - self.phase), total, 0)
        self.src = self.acc
        self.left = tuple(name for name in self.left if name != self.axis)

    def drain(self):
        for copy in self.sent:
            copy.wait_send()


def scatter_buffers(rows, width, rings):
    bufs = []
    for phase in range(3):
        cube = (4,) * (2 - phase)
        if phase < rings:
            bufs.append(pltpu.VMEM((2,) + cube + (rows // 2, width), BF16))
            bufs.append(pltpu.VMEM((2,) + cube + (rows, width), BF16))
            if phase == 0:
                bufs.append(pltpu.VMEM((2,) + cube + (rows // 2, width), BF16))
        else:
            bufs.append(pltpu.VMEM((3,) + cube + (rows, width), BF16))
        if phase == 0:
            bufs.append(pltpu.VMEM(cube + (rows, width), BF16))
        if phase < 2:
            bufs.append(pltpu.VMEM(cube + (rows, width), BF16))
    return bufs


class Gather:
    def __init__(self, entry, out, order, cols, send, recv, done=(), ring_rounds=(), band=None):
        self.band = (0, out.shape[3]) if band is None else band
        self.entry, self.out, self.order, self.cols = entry, out, order, pl.ds(*cols)
        self.send, self.recv, self.sent = send, recv, []
        self.done, self.ring_rounds = done, ring_rounds

    def spot(self, origin, rows=None):
        rows = pl.ds(*self.band) if rows is None else rows
        return self.out.at[part_of(self.done, self.axis, origin, rows, self.cols)]

    def copy(self, src, dst, step, way, peer):
        at = (self.entry, self.phase, step, way)
        copy = push(src, dst, self.send.at[at], self.recv.at[at], {self.axis: peer})
        copy.start()
        self.sent.append(copy)
        return copy

    def begin(self, phase, src=None):
        self.phase, self.axis = phase, self.order[phase]
        me, up, far, down = ring(self.axis)
        here = self.spot(me)
        src = here if src is None else src.at[:, self.cols]
        peers = (up, down) if phase in self.ring_rounds else (up, far, down)
        self.copies = [self.copy(src, here, 0, way, peer) for way, peer in enumerate(peers)]

    def middle(self):
        _, up, _, down = ring(self.axis)
        half = self.out.shape[3] // 2
        first, self.copies = self.copies, []
        for way, (peer, origin) in enumerate(((up, down), (down, up))):
            first[way].wait_recv()
            spot = self.spot(origin, pl.ds(way * half, half))
            self.copies.append(self.copy(spot, spot, 1, way, peer))

    def hold(self):
        for copy in self.copies:
            copy.wait_recv()

    def finish(self):
        self.hold()
        self.done = self.done + (self.axis,)

    def drain(self):
        for copy in self.sent:
            copy.wait_send()


class Rounds:
    def __init__(self, slots, send, recv, entry=0, order=("x", "y", "z")):
        self.slots, self.send, self.recv, self.sent = slots, send, recv, []
        self.entry, self.order = entry, order

    def begin(self, phase, rows):
        self.phase, axis = phase, self.order[phase]
        me = lax.axis_index(axis)
        for at, value in rows:
            self.slots[phase, me, at] = value
        self.copies = []
        for step, peer in enumerate(ring(axis)[1:]):
            spot = self.slots.at[phase, me]
            at = (self.entry, phase, step)
            copy = push(spot, spot, self.send.at[at], self.recv.at[at], {axis: peer})
            copy.start()
            self.copies.append(copy)

    def finish(self):
        for copy in self.copies:
            copy.wait_recv()
        self.sent += self.copies

    def drain(self):
        for copy in self.sent:
            copy.wait_send()


class Prefix(Rounds):
    def start(self, pair, backward):
        self.backward, self.cur, self.head = backward, pair, None
        self.share(0)

    def share(self, phase):
        self.begin(phase, [(slice(0, 1), self.cur[0]), (slice(1, 2), self.cur[1])])

    def step(self):
        self.finish()
        me = lax.axis_index(self.order[self.phase])
        run = (jnp.ones_like(self.cur[0]), jnp.zeros_like(self.cur[1]))
        mine = run
        for j in (3, 2, 1, 0) if self.backward else (0, 1, 2, 3):
            take = me == j
            mine = (jnp.where(take, run[0], mine[0]), jnp.where(take, run[1], mine[1]))
            fac, val = self.slots[self.phase, j, 0:1], self.slots[self.phase, j, 1:2]
            run = (run[0] * fac, val + fac * run[1])
        self.cur = run
        if self.head is None:
            self.head = mine
        else:
            self.head = (mine[0] * self.head[0], self.head[1] + self.head[0] * mine[1])
        if self.phase < 2:
            self.share(self.phase + 1)
        return self.head


class Total(Rounds):
    def start(self, value):
        self.begin(0, [(slice(None), value)])

    def step(self):
        self.finish()
        at = self.slots
        k = self.phase
        value = (at[k, 0] + at[k, 1]) + (at[k, 2] + at[k, 3])
        if k + 1 < len(self.order):
            self.begin(k + 1, [(slice(None), value)])
        return value


def axis_peers():
    return [{axis: ring(axis)[step]} for axis in AXES for step in (1, 2, 3)]


def along_seq(distance):
    place = lax.axis_index("z") * 16 + lax.axis_index("y") * 4 + lax.axis_index("x")
    place = lax.rem(place + distance + 64, 64)
    return {"z": place // 16, "y": lax.rem(place // 4, 4), "x": lax.rem(place, 4)}


CHUNKS = ((0, 384), (384, 512), (896, 384))
SUM_ORDERS = (
    (("y", "z", "x"), ("x", "y", "z"), ("z", "y", "x")),
    (("z", "x", "y"), ("x", "z", "y"), ("y", "x", "z")),
    (("y", "z", "x"), ("x", "y", "z"), ("z", "x", "y")),
)
ROW_HALVES = (pl.ds(0, 16), pl.ds(16, 16))
BANDS = ((0, 16), (16, 16), (32, 16))


def gelu_parts(x):
    inner = GELU_C * (x + GELU_A * x * x * x)
    t = jnp.tanh(inner)
    slope = GELU_C * (1.0 + 3.0 * GELU_A * x * x)
    return 0.5 * x * (1.0 + t), 0.5 * (1.0 + t) + 0.5 * x * (1.0 - t * t) * slope


FAR, UP, DOWN, ME = 0, 1, 2, 3


class RingSum:
    def __init__(self, part, got, one, two, send, recv, sib_send, sib_recv):
        self.part, self.got, self.one, self.two = part, got, one, two
        self.send, self.recv, self.sib_send, self.sib_recv = send, recv, sib_send, sib_recv
        self.core, self.sums, self.sent = lax.axis_index("mp"), {}, []

    def across(self, *slots):
        for slot in slots:
            copy = push(
                self.part.at[slot, 1 - self.core],
                self.got.at[slot],
                self.sib_send.at[slot],
                self.sib_recv.at[slot],
                {"mp": 1 - self.core},
            )
            copy.start()
            self.sums[slot] = copy

    def add(self, dst, src):
        dst[...] = (dst[...].astype(F32) + src[...].astype(F32)).astype(dst.dtype)

    def collect(self, slot):
        self.sums[slot].wait_recv()
        self.add(self.got.at[slot], self.part.at[slot, self.core])

    def far(self):
        self.collect(FAR)
        half = self.one.shape[1]
        _, up, _, down = ring("x")
        self.first = []
        for way, peer in enumerate((up, down)):
            piece = self.got.at[FAR, pl.ds(way * half, half)]
            at = (0, way)
            copy = push(piece, self.one.at[way], self.send.at[at], self.recv.at[at], {"x": peer})
            copy.start()
            self.first.append(copy)

    def near(self):
        half = self.one.shape[1]
        _, up, _, down = ring("x")
        self.second = []
        for way, (peer, slot) in enumerate(((up, UP), (down, DOWN))):
            self.collect(slot)
            self.first[way].wait_recv()
            self.add(self.got.at[slot, pl.ds(way * half, half)], self.one.at[way])
            at = (1, way)
            copy = push(self.got.at[slot], self.two.at[way], self.send.at[at], self.recv.at[at], {"x": peer})
            copy.start()
            self.second.append(copy)

    def total(self):
        self.sums[ME].wait_recv()
        total = self.got[ME].astype(F32) + self.part[ME, self.core].astype(F32)
        for way in range(2):
            self.second[way].wait_recv()
            total = total + self.two[way].astype(F32)
        return total

    def drain(self):
        for copy in self.first + self.second + list(self.sums.values()):
            copy.wait_send()


def ring_sum_scratch(rows, width):
    return [
        pltpu.VMEM((4, rows, width), BF16),
        pltpu.VMEM((2, rows // 2, width), BF16),
        pltpu.VMEM((2, rows, width), BF16),
        DMA((2, 2)),
        DMA((2, 2)),
        DMA((4,)),
        DMA((4,)),
    ]


def mlp_kernel(
    nm_ref, go_ref, hidden_ref, inv_ref, gain_ref, go_hbm, w_hbm,
    grad_hidden_ref, low_ref, term_ref, dw_ref, opart_out,
    go, w, gathered, npart, opart, mlp_in, ggu, gmi, low_half,
    load_sem, wsend, wrecv, gsend, grecv, gsib_send, gsib_recv, core_sem, *sum_refs,
):
    rows, width = nm_ref.shape
    half = rows // 2
    units = mlp_in.shape[1]
    me, up, far, down = ring("x")
    core = lax.axis_index("mp")
    other = {"mp": 1 - core}
    loads = [pltpu.make_async_copy(nm_ref, gathered.at[ME, core], load_sem.at[0])]
    wide = w.shape[4] // 2
    full, every = pl.ds(0, 4), pl.ds(0, w.shape[3])
    last = (("z", 0), ("y", wide))

    def weight_set(axis, index, at, cols):
        return ((index, full) if axis == "z" else (full, index)) + (full, at, pl.ds(cols, wide))

    for e, (axis, cols) in enumerate(last):
        here, ahead, _, behind = ring(axis)
        for k, index in enumerate((here, ahead, behind)):
            spot = weight_set(axis, index, every, cols)
            loads.append(pltpu.make_async_copy(w_hbm.at[spot], w.at[spot], load_sem.at[1 + 3 * e + k]))
    for slot, chip in ((FAR, far), (UP, up), (DOWN, down), (ME, me)):
        at = pl.ds(slot * 2 * rows, 2 * rows)
        loads.append(pltpu.make_async_copy(go_hbm.at[chip], go.at[at], load_sem.at[7 + slot]))
    for load in loads:
        load.start()
    peers = [{"x": up}, {"x": down}, other]
    for axis in ("y", "z"):
        peers += [{axis: ring(axis)[1]}, {axis: ring(axis)[3]}]
    greet(peers)
    top, low = pl.ds(0, half), pl.ds(half, half)
    first = []
    for way, (peer, slot) in enumerate(((up, DOWN), (down, UP))):
        spot = gathered.at[slot, core]
        copy = push(nm_ref, spot, gsend.at[0, way], grecv.at[0, way], {"x": peer})
        copy.start()
        first.append(copy)
    across = [push(nm_ref, gathered.at[ME, core], gsib_send.at[0], gsib_recv.at[0], other)]
    across[0].start()
    rest = []
    for e, (axis, cols) in enumerate(last):
        _, ahead, _, behind = ring(axis)
        deep = w.shape[3] // 2
        for way, (peer, origin) in enumerate(((ahead, behind), (behind, ahead))):
            spot = weight_set(axis, origin, pl.ds(way * deep, deep), cols)
            copy = push(w_hbm.at[spot], w.at[spot], wsend.at[e, way], wrecv.at[e, way], {axis: peer})
            copy.start()
            rest.append(copy)
    second = []
    for way, (peer, slot, piece) in enumerate(((up, DOWN, top), (down, UP, low))):
        first[way].wait_recv()
        spot = gathered.at[slot, core]
        copy = push(
            spot.at[piece], gathered.at[FAR, core, piece], gsend.at[1, way], grecv.at[1, way], {"x": peer}
        )
        copy.start()
        second.append(copy)
        copy = push(spot, spot, gsib_send.at[1 + way], gsib_recv.at[1 + way], other)
        copy.start()
        across.append(copy)
    for copy in rest:
        copy.wait_recv()
    for load in loads:
        load.wait()

    def tile(j, start=0):
        return pl.ds(pl.multiple_of(start + j * 256, 256), 256)

    def columns(at):
        return w[:, :, :, :, at].reshape(width, 256)

    def shard_tile(i, at):
        return w[i // 2, pl.ds(2 * lax.rem(i, 2), 2), :, :, at].reshape(256, -1)

    def grad_tile(j, carry):
        gmi[:, tile(j)] = dot(go[...], columns(tile(j, 2 * units)))
        return carry

    loop(0, units // 256, grad_tile, 3)
    for way, piece in enumerate((top, low)):
        second[way].wait_recv()
        spot = gathered.at[FAR, core, piece]
        copy = push(spot, spot, gsib_send.at[3 + way], gsib_recv.at[3 + way], other)
        copy.start()
        across.append(copy)

    def tokens_step(slot):
        at = pl.ds(slot * 2 * rows, 4 * rows)

        def hidden_tile(j, carry):
            tokens_in = gathered[slot : slot + 2].reshape(4 * rows, width)
            gate = dot(tokens_in, columns(tile(j)))
            up_lin = dot(tokens_in, columns(tile(j, units)))
            grad = gmi[at, tile(j)]
            act, slope = gelu_parts(gate)
            mlp_in[at, tile(j)] = (act * up_lin).astype(BF16)
            ggu[at, tile(j)] = (slope * (grad * up_lin)).astype(BF16)
            ggu[at, tile(j, units)] = (grad * act).astype(BF16)
            return carry

        loop(0, units // 256, hidden_tile, 3)

        def back_tile(j, carry):
            back = dot_t(ggu[at], shard_tile(j, pl.ds(0, 2 * units)))
            npart[slot : slot + 2, :, :, tile(j)] = back.astype(BF16).reshape(2, 2, rows, 256)
            return carry

        loop(0, width // 256, back_tile, 2)

    def out_tile(j, carry):
        part = dot_t(mlp_in[...], shard_tile(j, pl.ds(2 * units, units)))
        opart[:, :, :, tile(j)] = part.astype(BF16).reshape(4, 2, rows, 256)
        return carry

    def weight_grads(lower, upper):
        def step(i, carry):
            left = gathered[:, :, :, tile(i)].reshape(8 * rows, 256)
            dw_ref[tile(i), pl.ds(0, 2 * units)] = outer(left, ggu[...]).astype(BF16)
            dw_ref[tile(i), pl.ds(2 * units, units)] = outer(go[:, tile(i)], mlp_in[...]).astype(BF16)
            return carry

        loop(lower, upper, step, 2)

    sums = RingSum(npart, *sum_refs)
    for copy in across:
        copy.wait_recv()
    tokens_step(FAR)
    sums.across(FAR, UP)
    sums.far()
    tokens_step(DOWN)
    sums.across(DOWN, ME)
    sums.near()
    loop(0, width // 256, out_tile, 2)
    save = pltpu.make_async_copy(opart, opart_out, load_sem.at[11])
    save.start()
    weight_grads(0, 5)
    grad_normed = sums.total()
    hat = hidden_ref[...] * inv_ref[...]
    grad_hat = grad_normed * gain_ref[...]
    inner = jnp.mean(grad_hat * hat, axis=-1, keepdims=True)
    grad_hidden = go_ref[...].astype(F32) + inv_ref[...] * (grad_hat - hat * inner)
    grad_hidden_ref[...] = grad_hidden
    term_ref[...] = jnp.sum(grad_normed * hat, axis=0, keepdims=True)
    low_half[...] = grad_hidden.astype(BF16)
    low_ref[core] = low_half[...]
    swap = push(low_half, low_ref.at[core], core_sem.at[0], core_sem.at[1], other)
    swap.start()
    weight_grads(5, 8)
    swap.wait()
    save.wait()
    sums.drain()
    for copy in first + second + across + rest:
        copy.wait_send()


def mlp(normed, grad_out, hidden, inverse, gain, grad_out_all, weights, cid):
    rows, width = normed.shape
    units = weights.shape[4] // 3

    def block(dtype, *shape):
        return pltpu.VMEM(shape, dtype)

    return pl.pallas_call(
        mlp_kernel,
        out_shape=[
            jax.ShapeDtypeStruct((rows, width), F32),
            jax.ShapeDtypeStruct((2, rows, width), BF16),
            jax.ShapeDtypeStruct((1, width), F32),
            jax.ShapeDtypeStruct((width, 3 * units), BF16),
            jax.ShapeDtypeStruct((4, 2, rows, width), BF16),
        ],
        in_specs=[VM] * 5 + [ANY] * 2,
        out_specs=[VM] * 4 + [HBM],
        scratch_shapes=[
            block(BF16, 8 * rows, width),
            block(BF16, *weights.shape),
            block(BF16, 4, 2, rows, width),
            block(BF16, 4, 2, rows, width),
            block(BF16, 4, 2, rows, width),
            block(BF16, 8 * rows, units),
            block(BF16, 8 * rows, 2 * units),
            block(F32, 8 * rows, units),
            block(BF16, rows, width),
        ]
        + [DMA((12,)), DMA((2, 2)), DMA((2, 2)), DMA((2, 2)), DMA((2, 2)), DMA((5,)), DMA((5,)), DMA((2,))]
        + ring_sum_scratch(rows, width),
        compiler_params=params(cid, 60),
    )(normed, grad_out, hidden, inverse, gain, grad_out_all.reshape(4, 2 * rows, width), weights)


def lanes(n):
    return pl.ds(pl.multiple_of(n * BLOCK, BLOCK), BLOCK)


def minus_expm1(x):
    series = jnp.ones_like(x)
    for k in (9, 8, 7, 6, 5, 4, 3, 2):
        series = 1.0 + x * (1.0 / k) * series
    return jnp.where(x > -0.4, -x * series, 1.0 - jnp.exp(x))


def log1p(x):
    series = jnp.zeros_like(x)
    for k in (7, 6, 5, 4, 3, 2, 1):
        series = 1.0 / k - x * series
    return jnp.where(x < 0.05, x * series, jnp.log(1.0 + x))


CONV_W, CONV_B, RATES, BIAS, CONV_STATE, H_INIT, SLOPE = 0, 4, 5, 6, 8, 11, 12


def rec_forward_kernel(*refs):
    (
        tokens_ref, gain_ref, gain_mlp_ref, conv_w_ref, conv_b_ref, lam_ref, bias_ref, conv_state_ref,
        h_init_ref, starts_ref, valid_ref, rec_raw, back_in, mlp_raw, down_in, cot_ref, g_hbm,
        lin_out, gate_out, back_out, mlp_out, ext_out, act_out, mixed_out, reset_out, input_out, f_out, states_out,
        branch_out, normed_out, go_all, inv_ref, rms_ref, hidden_ref, nm_ref, inv_mlp_ref, rms_mlp_ref, go_ref, v_ref,
        wl, wg, wb, ext, gate_lin, mixed_v, reset_v, input_v, f_v, states, branch_v, normed, tail_in, driven, cf_v,
        part, part_low, part_in, g_v, rms_v, slots, mask_ref, rec_in, mlp_in,
        tail_sem, load_sem, save_sem, own_sem, move_send, move_recv, send, recv, small_send, small_recv, core_sem,
        go_send, go_recv, go_sib_send, go_sib_recv,
    ) = refs
    count, width = tokens_ref.shape
    rec = f_v.shape[1]
    for k in range(2):
        rec_in[:, k * rec : (k + 1) * rec] = rec_raw[:, k, :]
        mlp_in[:, k * mlp_raw.shape[2] : (k + 1) * mlp_raw.shape[2]] = mlp_raw[:, k, :]
    gate_in, lin_in = rec_in.at[:, pl.ds(0, rec)], rec_in.at[:, pl.ds(rec, rec)]
    blocks = rec // BLOCK
    half = count // 2
    core = lax.axis_index("mp")
    other = {"mp": 1 - core}
    here = tuple(lax.axis_index(name) for name in AXES)
    load = pltpu.make_async_copy(g_hbm, g_v, load_sem)
    load.start()
    owns = [
        pltpu.make_async_copy(lin_in, wl.at[here], own_sem.at[0]),
        pltpu.make_async_copy(gate_in, wg.at[here], own_sem.at[1]),
        pltpu.make_async_copy(back_in, wb.at[here], own_sem.at[2]),
    ]
    units = mlp_out.shape[4] // 3
    every = pl.ds(0, rec_in.shape[0])

    def quarter(k, chip):
        if k == 2:
            return down_in.at[every, pl.ds(pl.multiple_of(chip * units, units), units)]
        return mlp_in.at[every, pl.ds(pl.multiple_of((4 * k + chip) * units, units), units)]

    spots = [mlp_out.at[here + (every, pl.ds(k * units, units))] for k in range(3)]
    owns += [pltpu.make_async_copy(quarter(k, here[2]), spots[k], own_sem.at[3 + k]) for k in range(3)]
    for own in owns:
        own.start()
    greet(axis_peers() + [other, along_seq(1), along_seq(-1)])
    tail_copy = push(tokens_ref.at[pl.ds(count - 16, 16)], tail_in, tail_sem.at[0], tail_sem.at[1], along_seq(1))
    tail_copy.start()
    lin = [Gather(e, wl, ORDERS[e], CHUNKS[e], send, recv, ring_rounds=(2,)) for e in range(3)]
    gate = [
        Gather(3 + e, wg, ORDERS[(e + 1) % 3], CHUNKS[e], send, recv, ring_rounds=(1, 2)) for e in range(3)
    ]
    back = [
        Gather(6 + e, wb, ORDERS[(2, 1, 0)[e]], CHUNKS[e], send, recv, ring_rounds=(1, 2)) for e in range(3)
    ]
    rest = gate + back
    wide = mlp_out.shape[4] // 2
    mlp_flows = [
        Gather(9 + e, mlp_out, order, (e * wide, wide), send, recv, done=("x",), ring_rounds=(1,))
        for e, order in enumerate((("y", "z"), ("z", "y")))
    ]

    def each(group, name, *args):
        for flow in group:
            getattr(flow, name)(*args)

    each(lin, "begin", 0, lin_in)
    moves = []
    for step, peer in enumerate(ring("x")[1:]):
        for k in range(3):
            copy = push(quarter(k, peer), spots[k], move_send.at[step, k], move_recv.at[step, k], {"x": peer})
            copy.start()
            moves.append(copy)
    each(gate, "begin", 0, gate_in)
    each(back, "begin", 0, back_in)

    v_ref[CONV_W : CONV_W + CONV] = conv_w_ref[...]
    v_ref[BIAS : BIAS + 2] = bias_ref[...]
    v_ref[CONV_STATE : CONV_STATE + EDGE] = conv_state_ref[...]
    for at, ref in ((CONV_B, conv_b_ref), (H_INIT, h_init_ref)):
        v_ref[at : at + 1] = ref[...].reshape(1, rec)
    lam = lam_ref[...].reshape(1, rec)
    v_ref[RATES : RATES + 1] = jnp.maximum(-lam, 0.0) + log1p(jnp.exp(-jnp.abs(lam)))
    v_ref[SLOPE : SLOPE + 1] = 1.0 / (1.0 + jnp.exp(lam))
    v_ref[SLOPE + 1 :] = jnp.zeros((15 - SLOPE, rec), F32)
    square = (count, count)
    diagonal = lax.broadcasted_iota(jnp.int32, square, 0) == lax.broadcasted_iota(jnp.int32, square, 1)
    for k, row in enumerate((1.0 - starts_ref[...].astype(F32), valid_ref[...].astype(F32))):
        spread = jnp.where(diagonal, jnp.broadcast_to(row.reshape(1, count), square), 0.0)
        mask_ref[:, k : k + 1] = jnp.sum(spread, axis=1, keepdims=True)

    def norm(values):
        mean_sq = jnp.mean(values * values, axis=-1, keepdims=True)
        inverse = lax.rsqrt(mean_sq + EPSILON)
        return values * inverse, inverse, jnp.sqrt(mean_sq + EPSILON)

    def norm_step(i, carry):
        at = pl.ds(pl.multiple_of(i * 64, 64), 64)
        hat, inverse, rms = norm(tokens_ref[at].astype(F32))
        inv_ref[at] = inverse
        rms_ref[at] = rms
        normed[pl.ds(pl.multiple_of(16 + i * 64, 16), 64)] = (hat * gain_ref[...]).astype(BF16)
        return carry

    lax.fori_loop(0, count // 64, norm_step, 0)
    for own in owns:
        own.wait()
    each(lin, "finish")
    each(lin, "begin", 1)
    each(rest, "finish")
    each(rest, "begin", 1)
    tail_copy.wait_recv()
    normed[0:16] = (norm(tail_in[...].astype(F32))[0] * gain_ref[...]).astype(BF16)
    saves = []

    def save(src, dst):
        copy = pltpu.make_async_copy(src, dst, save_sem.at[len(saves)])
        copy.start()
        saves.append(copy)

    save(normed.at[pl.ds(16, count)], normed_out)
    each(lin, "finish")
    each(lin, "begin", 2)
    for copy in moves:
        copy.wait_recv()
    each(mlp_flows, "begin", 0)
    each(rest, "middle")
    each(lin, "middle")
    each(rest, "finish")
    each(rest, "begin", 2)
    mine = pl.ds(pl.multiple_of(core * half, half), half)
    go_ref[...] = (cot_ref[mine].astype(F32) * mask_ref[mine, 1:2]).astype(BF16)
    load.wait()
    each(lin, "finish")
    save(wl, lin_out)
    is_first = (here[0] + here[1] + here[2]) == 0

    def rec_step(n, carry):
        at = lanes(n)
        ext[:, at] = dot(normed[...], wl[:, :, :, :, at].reshape(width, BLOCK))

        @pl.when(is_first)
        def _():
            ext[16 - EDGE : 16, at] = v_ref[CONV_STATE : CONV_STATE + EDGE, at]

        total = v_ref[CONV_B : CONV_B + 1, at] + jnp.zeros((count, BLOCK), F32)
        for k in range(CONV):
            total = total + v_ref[CONV_W + k : CONV_W + k + 1, at] * ext[pl.ds(16 - EDGE + k, count), at]
        mixed = total.astype(BF16)
        mixed_v[:, at] = mixed
        reset = jax.nn.sigmoid(dot(mixed, g_v[0, n]) + v_ref[BIAS : BIAS + 1, at])
        gated = jax.nn.sigmoid(dot(mixed, g_v[1, n]) + v_ref[BIAS + 1 : BIAS + 2, at])
        reset_v[:, at] = reset
        input_v[:, at] = gated
        log_decay = -8.0 * v_ref[RATES : RATES + 1, at] * reset
        f_v[:, at] = jnp.exp(log_decay) * mask_ref[:, 0:1]
        driven[:, at] = jnp.sqrt(minus_expm1(2.0 * log_decay)) * gated * mixed.astype(F32)
        return carry

    lax.fori_loop(0, blocks, rec_step, 0)
    for src, dst in ((ext, ext_out), (mixed_v, mixed_out), (reset_v, reset_out), (input_v, input_out), (f_v, f_out)):
        save(src, dst)

    def group(i, carry):
        base = pl.multiple_of(i * 8, 8)
        f, d = f_v[pl.ds(base, 8)], driven[pl.ds(base, 8)]
        cf, cd = carry
        cfs, cds = [], []
        for r in range(8):
            cf = cf * f[r : r + 1]
            cd = cd * f[r : r + 1] + d[r : r + 1]
            cfs.append(cf)
            cds.append(cd)
        cf_v[pl.ds(base, 8)] = jnp.concatenate(cfs, axis=0)
        states[pl.ds(pl.multiple_of(base + 8, 8), 8)] = jnp.concatenate(cds, axis=0)
        return cf, cd

    zero = jnp.zeros((1, rec), F32)
    ends = lax.fori_loop(0, count // 8, group, (zero + 1.0, zero))
    prefix = Prefix(slots, small_send, small_recv)
    prefix.start(ends, False)
    by_axis = {axis: [flow for flow in rest if flow.axis == axis] for axis in AXES}
    each(by_axis["x"], "middle")
    prefix.step()
    each(by_axis["y"], "middle")
    each(mlp_flows, "finish")
    mlp_flows[1].begin(1)
    prefix.step()
    each(by_axis["z"], "middle")
    mlp_flows[0].begin(1)
    x_here, x_up, x_far, x_down = ring("x")
    spot = go_all.at[x_here, core]
    save(go_ref, spot)
    go_first = []
    for way, peer in enumerate((x_up, x_down)):
        copy = push(go_ref, spot, go_send.at[0, way], go_recv.at[0, way], {"x": peer})
        copy.start()
        go_first.append(copy)
    go_across = [push(go_ref, spot, go_sib_send.at[0], go_sib_recv.at[0], other)]
    go_across[0].start()
    head = prefix.step()
    carry_in = head[1] + head[0] * v_ref[H_INIT : H_INIT + 1]
    each(gate, "finish")
    save(wg, gate_out)

    def gate_step(n, carry):
        gate_lin[:, lanes(n)] = dot(normed[16:], wg[:, :, :, :, lanes(n)].reshape(width, BLOCK))
        return carry

    lax.fori_loop(0, blocks, gate_step, 0)
    save(gate_lin, act_out)
    states[0:8] = jnp.broadcast_to(carry_in, (8, rec))

    def branch_step(n, carry):
        at = lanes(n)
        value = states[8:, at] + cf_v[:, at] * states[0:1, at]
        states[8:, at] = value
        branch_v[:, at] = (gelu_parts(gate_lin[:, at])[0] * value).astype(BF16)
        return carry

    lax.fori_loop(0, blocks, branch_step, 0)
    save(states, states_out)
    save(branch_v, branch_out)
    each(back, "finish")
    save(wb, back_out)

    def out_step(i, carry):
        at = pl.ds(pl.multiple_of(i * 256, 256), 256)
        rows = wb[i // 2, pl.ds(2 * lax.rem(i, 2), 2)].reshape(256, rec)
        value = dot_t(branch_v[...], rows)
        part[0, :, at] = value[:half]
        part[1, :, at] = value[half:]
        return carry

    lax.fori_loop(0, width // 256, out_step, 0)
    part_low[...] = part[1 - core].astype(BF16)
    part_copy = push(part_low, part_in, core_sem.at[0], core_sem.at[1], other)
    part_copy.start()
    go_second = []
    for way, (peer, origin) in enumerate(((x_up, x_down), (x_down, x_up))):
        go_first[way].wait_recv()
        spot = go_all.at[origin, core]
        piece = spot.at[pl.ds(way * (half // 2), half // 2)]
        copy = push(piece, piece, go_send.at[1, way], go_recv.at[1, way], {"x": peer})
        copy.start()
        go_second.append(copy)
        copy = push(spot, spot, go_sib_send.at[1 + way], go_sib_recv.at[1 + way], other)
        copy.start()
        go_across.append(copy)
    part_copy.wait_recv()
    hidden = tokens_ref[mine].astype(F32) + (part[core] + part_in[...].astype(F32))
    hidden_ref[...] = hidden
    hat, inverse, rms = norm(hidden)
    inv_mlp_ref[...] = inverse
    rms_v[...] = jnp.broadcast_to(rms, (half, 128))
    rms_mlp_ref[core] = rms_v[...]
    rms_copy = push(rms_v, rms_mlp_ref.at[core], core_sem.at[2], core_sem.at[3], other)
    rms_copy.start()
    nm_ref[...] = (hat * gain_mlp_ref[...]).astype(BF16)
    for way in range(2):
        go_second[way].wait_recv()
        piece = go_all.at[x_far, core, pl.ds(way * (half // 2), half // 2)]
        copy = push(piece, piece, go_sib_send.at[3 + way], go_sib_recv.at[3 + way], other)
        copy.start()
        go_across.append(copy)
    each(mlp_flows, "hold")
    rms_copy.wait()
    for copy in go_across:
        copy.wait()
    for copy in go_first + go_second:
        copy.wait_send()
    for copy in moves:
        copy.wait_send()
    for copy in saves:
        copy.wait()
    each(lin, "drain")
    each(rest, "drain")
    each(mlp_flows, "drain")
    prefix.drain()
    part_copy.wait_send()
    tail_copy.wait_send()


def rec_forward(tokens, gain_rec, gain_mlp, vectors, masks, w_rec, back, w_mlp, down, cotangent, gates, cid):
    count, width = tokens.shape
    rows, rec = back.shape
    half = count // 2

    def cube(last):
        return (4, 4, 4, rows, last)

    def sds(shape, dtype):
        return jax.ShapeDtypeStruct(shape, dtype)

    saved = [
        (cube(rec), BF16),
        (cube(rec), BF16),
        (cube(rec), BF16),
        (cube(3 * down.shape[1] // 4), BF16),
        ((count + 16, rec), F32),
        ((count, rec), F32),
        ((count, rec), BF16),
        ((count, rec), F32),
        ((count, rec), F32),
        ((count, rec), F32),
        ((count + 8, rec), F32),
        ((count, rec), BF16),
        ((count, width), BF16),
        ((4, 2, half, width), BF16),
    ]
    small = [
        ((count, 1), F32),
        ((count, 1), F32),
        ((half, width), F32),
        ((half, width), BF16),
        ((half, 1), F32),
        ((2, half, 128), F32),
        ((half, width), BF16),
        ((16, rec), F32),
    ]
    scratch = saved[:3] + saved[4:12] + [((count + 16, width), BF16), ((16, width), BF16)]
    scratch += [((count, rec), F32), ((count, rec), F32), ((2, half, width), F32)]
    scratch += [((half, width), BF16), ((half, width), BF16), (gates.shape, BF16), ((half, 128), F32), ((3, 4, 2, rec), F32), ((count, 2), F32)]
    scratch += [((rows, 2 * rec), BF16), ((rows, 2 * w_mlp.shape[2]), BF16)]
    return pl.pallas_call(
        rec_forward_kernel,
        out_shape=[sds(*one) for one in saved + small],
        in_specs=[VM] * 16 + [ANY],
        out_specs=[HBM] * len(saved) + [VM] * len(small),
        scratch_shapes=[pltpu.VMEM(*one) for one in scratch]
        + [
            DMA((2,)),
            DMA,
            DMA((13,)),
            DMA((6,)),
            DMA((3, 3)),
            DMA((3, 3)),
            DMA((11, 3, 2, 3)),
            DMA((11, 3, 2, 3)),
            DMA((1, 3, 3)),
            DMA((1, 3, 3)),
            DMA((4,)),
            DMA((2, 2)),
            DMA((2, 2)),
            DMA((5,)),
            DMA((5,)),
        ],
        compiler_params=params(cid, 60),
    )(tokens, gain_rec[None], gain_mlp[None], *vectors, *masks, w_rec, back, w_mlp, down, cotangent, gates)


G_BIAS, G_LAM, G_CONV_W, G_CONV_B, G_H, G_STATE = 0, 2, 3, 7, 8, 9
GATE_ROWS = 48


def shard_rows(ref, i, value):
    value = value.reshape(2, 4, 32, value.shape[1])
    ref[i // 2, pl.ds(2 * lax.rem(i, 2), 2)] = value


def rec_back_kernel(
    gh_ref, branch_ref, normed_ref, gate_ref, states_ref, f_ref, v_ref, hidden_ref,
    wb_hbm, ext_hbm, mixed_hbm, reset_hbm, input_hbm, g_hbm, wg_hbm, opart_hbm,
    small_ref, part_ref, low, result_ref, dw_out_hbm, dw_gate_hbm, gg_hbm,
    wb, ext, mixed_v, reset_v, input_v, g_v, wg, opart, gate_low, cb, al, gm, dw_out, dw_gate, gg,
    tail, edge, edge_in, slots, result_half,
    *refs,
):
    load_sem, save_sem, small_send, small_recv, edge_sem, core_sem = refs[:6]
    sum_refs = refs[6:]
    count, rec = gate_ref.shape
    half = count // 2
    width = gh_ref.shape[1]
    blocks = rec // BLOCK
    pairs = (
        (wb_hbm, wb), (ext_hbm, ext), (mixed_hbm, mixed_v), (reset_hbm, reset_v), (input_hbm, input_v), (g_hbm, g_v),
        (wg_hbm, wg), (opart_hbm, opart),
    )
    loads = [pltpu.make_async_copy(src, dst, load_sem.at[k]) for k, (src, dst) in enumerate(pairs)]
    for load in loads:
        load.start()
    saves = []

    def save(src, dst):
        copy = pltpu.make_async_copy(src, dst, save_sem.at[len(saves)])
        copy.start()
        saves.append(copy)

    ahead, behind = along_seq(1), along_seq(-1)
    other = {"mp": 1 - lax.axis_index("mp")}
    greet(axis_peers() + [ahead, behind, other])
    place = lax.axis_index("z") * 16 + lax.axis_index("y") * 4 + lax.axis_index("x")
    is_first = jnp.where(place == 0, 1.0, 0.0)
    has_next = jnp.where(place == 63, 0.0, 1.0)

    def weight_grad(ref, left, right):
        def step(i, carry):
            cols = pl.ds(pl.multiple_of(i * 256, 256), 256)
            shard_rows(ref, i, outer(left[:, cols], right[...]).astype(BF16))
            return carry

        loop(0, left.shape[1] // 256, step, 2)

    loads[0].wait()

    def branch_step(n, carry):
        grad = dot(gh_ref[...], wb[:, lanes(n)])
        act, slope = gelu_parts(gate_ref[:, lanes(n)])
        gate_low[:, lanes(n)] = (slope * (grad * states_ref[8:, lanes(n)])).astype(BF16)
        al[:, lanes(n)] = grad * act
        return carry

    loop(0, blocks, branch_step, 5)
    loads[7].wait()
    sums = RingSum(opart, *sum_refs)
    sums.across(FAR, UP, DOWN, ME)

    def group(i, carry):
        base = pl.multiple_of(count - 8 - i * 8, 8)
        f, d = f_ref[pl.ds(base, 8)], al[pl.ds(base, 8)]
        follow, cf, cd = carry
        cfs, cds = [None] * 8, [None] * 8
        for r in (7, 6, 5, 4, 3, 2, 1, 0):
            cf = cf * follow
            cd = cd * follow + d[r : r + 1]
            cfs[r], cds[r] = cf, cd
            follow = f[r : r + 1]
        cb[pl.ds(base, 8)] = jnp.concatenate(cfs, axis=0)
        al[pl.ds(base, 8)] = jnp.concatenate(cds, axis=0)
        return follow, cf, cd

    zero = jnp.zeros((1, rec), F32)
    follow, cf, cd = lax.fori_loop(0, count // 8, group, (zero + 1.0, zero + 1.0, zero))
    prefix = Prefix(slots, small_send, small_recv)
    prefix.start((follow * cf, follow * cd), True)
    weight_grad(dw_out, gh_ref, branch_ref)
    save(dw_out, dw_out_hbm)
    prefix.step()
    sums.far()
    weight_grad(dw_gate, normed_ref, gate_low)
    save(dw_gate, dw_gate_hbm)
    prefix.step()
    for load in loads[1:7]:
        load.wait()

    def part_tile(i, carry):
        at = pl.ds(pl.multiple_of(i * 256, 256), 256)
        value = dot_t(gate_low[...], wg[at, :])
        part_ref[0, :, at] = value[:half]
        part_ref[1, :, at] = value[half:]
        return carry

    lax.fori_loop(0, width // 256, part_tile, 0)
    later = prefix.step()[1]
    sums.near()
    al[...] = al[...] + cb[...] * later

    def grads_step(n, carry):
        at = lanes(n)
        adjoint = al[:, at]
        factors, reset, gated = f_ref[:, at], reset_v[:, at], input_v[:, at]
        mixed_low = mixed_v[:, at]
        mixed = mixed_low.astype(F32)
        rates = v_ref[RATES : RATES + 1, at]
        log_decay = -8.0 * rates * reset
        decays = jnp.exp(log_decay)
        scale_in = jnp.sqrt(minus_expm1(2.0 * log_decay))
        grad_log = adjoint * states_ref[pl.ds(7, count), at] * factors
        grad_log = grad_log - adjoint * gated * mixed * decays * decays / scale_in
        small_ref[G_LAM : G_LAM + 1, at] = (
            8.0 * jnp.sum(grad_log * reset, axis=0, keepdims=True) * v_ref[SLOPE : SLOPE + 1, at]
        )
        small_ref[G_H : G_H + 1, at] = is_first * factors[0:1] * adjoint[0:1]
        grad_reset = (grad_log * (-8.0 * rates) * reset * (1.0 - reset)).astype(BF16)
        grad_input = (adjoint * scale_in * mixed * gated * (1.0 - gated)).astype(BF16)
        for g, grad in enumerate((grad_reset, grad_input)):
            small_ref[G_BIAS + g : G_BIAS + g + 1, at] = jnp.sum(
                grad.astype(F32), axis=0, keepdims=True
            )
            b = g * blocks + n
            rows = pl.ds(pl.multiple_of(16 * lax.rem(b, 3), 16), 16)
            gg[:, :, b // 3, rows, :] = outer(mixed_low, grad).astype(BF16).reshape(4, 4, 16, BLOCK)
        grad_mixed = adjoint * scale_in * gated
        grad_mixed = grad_mixed + dot_t(grad_reset, g_v[0, n]) + dot_t(grad_input, g_v[1, n])
        gm[0:8] = jnp.zeros((8, BLOCK), F32)
        gm[8 : 8 + count] = grad_mixed
        gm[8 + count :] = jnp.zeros((8, BLOCK), F32)
        small_ref[G_CONV_B : G_CONV_B + 1, at] = jnp.sum(grad_mixed, axis=0, keepdims=True)
        total = jnp.zeros((count, BLOCK), F32)
        front = jnp.zeros((8, BLOCK), F32)
        for k in range(CONV):
            small_ref[G_CONV_W + k : G_CONV_W + k + 1, at] = jnp.sum(
                grad_mixed * ext[pl.ds(16 - EDGE + k, count), at], axis=0, keepdims=True
            )
            weight = v_ref[CONV_W + k : CONV_W + k + 1, at]
            total = total + weight * gm[pl.ds(8 + EDGE - k, count)]
            front = front + weight * gm[pl.ds(8 - k, 8)]
        low[:, at] = total.astype(BF16)
        tail[:, at] = total[count - 16 :]
        edge[:, at] = front
        small_ref[G_STATE : G_STATE + EDGE, at] = is_first * front[:EDGE]
        small_ref[G_STATE + EDGE :, at] = jnp.zeros((16 - G_STATE - EDGE, BLOCK), F32)
        return carry

    for x, j in ((3, 1), (3, 2)):
        gg[:, :, x, 16 * j : 16 * j + 16, :] = jnp.zeros((4, 4, 16, BLOCK), BF16)
    loop(0, blocks, grads_step, 5)
    edge_copy = push(edge, edge_in, edge_sem.at[0], edge_sem.at[1], behind)
    edge_copy.start()
    save(gg, gg_hbm)
    core = lax.axis_index("mp")
    result_half[...] = (hidden_ref[...] + sums.total()).astype(BF16)
    result_ref[core] = result_half[...]
    result_copy = push(result_half, result_ref.at[core], core_sem.at[0], core_sem.at[1], other)
    result_copy.start()
    edge_copy.wait_recv()
    last = jnp.concatenate([tail[0:13], tail[13:16] + has_next * edge_in[0:EDGE]], axis=0)
    low[count - 16 :] = last.astype(BF16)
    result_copy.wait()
    for copy in saves:
        copy.wait()
    sums.drain()
    prefix.drain()
    edge_copy.wait_send()


def rec_back(
    gh, branch, normed, gate_lin, states_ext, factors, vectors, hidden,
    w_back, ext, mixed, reset, gated, gates, w_gate, mlp_part, cid,
):
    count, rec = gate_lin.shape
    half, width = hidden.shape

    def like(array):
        return pltpu.VMEM(array.shape, array.dtype)

    wide, low = pltpu.VMEM((count, rec), F32), pltpu.VMEM((count, rec), BF16)
    cube, gate_cube = (4, 4, 4, width // 64, rec), (4, 4, 4, GATE_ROWS, BLOCK)
    return pl.pallas_call(
        rec_back_kernel,
        out_shape=[
            jax.ShapeDtypeStruct((16, rec), F32),
            jax.ShapeDtypeStruct((2, half, width), F32),
            jax.ShapeDtypeStruct((count, rec), BF16),
            jax.ShapeDtypeStruct((2, half, width), BF16),
            jax.ShapeDtypeStruct(cube, BF16),
            jax.ShapeDtypeStruct(cube, BF16),
            jax.ShapeDtypeStruct(gate_cube, BF16),
        ],
        in_specs=[VM] * 8 + [ANY] * 8,
        out_specs=[VM] * 4 + [HBM] * 3,
        scratch_shapes=[
            like(w_back), like(ext), like(mixed), like(reset), like(gated), like(gates), like(w_gate), like(mlp_part),
            low, wide, wide, pltpu.VMEM((count + 16, BLOCK), F32),
            pltpu.VMEM(cube, BF16), pltpu.VMEM(cube, BF16), pltpu.VMEM(gate_cube, BF16),
            pltpu.VMEM((16, rec), F32), pltpu.VMEM((8, rec), F32), pltpu.VMEM((8, rec), F32),
            pltpu.VMEM((3, 4, 2, rec), F32), pltpu.VMEM((half, width), BF16),
            DMA((8,)),
            DMA((3,)),
            DMA((1, 3, 3)),
            DMA((1, 3, 3)),
            DMA((2,)),
            DMA((2,)),
        ]
        + ring_sum_scratch(half, width),
        compiler_params=params(cid, 61),
    )(
        gh, branch, normed, gate_lin, states_ext, factors, vectors, hidden,
        w_back, ext, mixed, reset, gated, gates, w_gate, mlp_part,
    )


def rec_end_kernel(
    part_in_ref, small_ref, gain_term_ref, gh_ref, tokens_in, inverse_ref, gain_ref, normed_ref, low_ref,
    dw0, dw1, gg_hbm, wl_hbm,
    total_ref, gains_ref, all_gates_ref, out0, out1, out2, tokens_hbm,
    *refs,
):
    bufs, refs = refs[: 78 + 3 * 6], refs[78 + 3 * 6 :]
    (
        part, dw2, wl, gates_out, part_low, part_in, tokens_v, gates_ref, ring_gains, gains0, small0, small1, small2,
        load_sem, own_sem, send, recv, gsend, grecv, small_send, small_recv, ring_send, ring_recv, core_sem,
    ) = refs
    half, width = gh_ref.shape
    load = pltpu.make_async_copy(wl_hbm, wl, load_sem.at[0])
    load.start()
    core = lax.axis_index("mp")
    other = {"mp": 1 - core}
    x_here = lax.axis_index("x")
    greet(axis_peers() + [other] + [{"x": peer, "mp": 1 - core} for peer in ring("x")[1:]])
    small = [
        Total(slots, small_send, small_recv, e, ORDERS[e])
        for e, slots in enumerate((small0, small1, small2))
    ]
    for flow, (start, wide) in zip(small, CHUNKS):
        flow.start(small_ref[:, start : start + wide])
    gates = [
        Scatter(
            9 + e, gg_hbm, (0, BLOCK), ORDERS[e], None, bufs[78 + 6 * e : 84 + 6 * e], gates_out,
            own_sem, send, recv, BANDS[e],
        )
        for e in range(3)
    ]
    flows = [
        Scatter(
            e, (dw0, dw1, dw2)[e // 3], CHUNKS[e % 3], SUM_ORDERS[e // 3][e % 3], ROW_HALVES,
            bufs[9 * e : 9 * e + 9] if e < 6 else bufs[8 * e + 6 : 8 * e + 14], (out0, out1, out2)[e // 3],
            own_sem, send, recv, rings=2 if e < 6 else 1,
        )
        for e in range(9)
    ]
    one, two, three = flows[:3], flows[3:6], flows[6:]
    spread = [Gather(e, gates_ref, ORDERS[e], (0, BLOCK), gsend, grecv, band=BANDS[e]) for e in range(3)]

    def each(group, name, *args):
        for flow in group:
            getattr(flow, name)(*args)

    each(gates, "begin", 0)
    each(one, "begin", 0)
    each(two, "begin", 0)

    def weight_grad(i, carry):
        cols = pl.ds(pl.multiple_of(i * 256, 256), 256)
        shard_rows(dw2, i, outer(normed_ref[:, cols], low_ref[...]).astype(BF16))
        return carry

    lax.fori_loop(0, width // 256, weight_grad, 0)
    each(three, "begin", 0)
    each(gates, "finish")
    each(gates, "begin", 1)
    for flow in small:
        flow.step()
    load.wait()

    def part_tile(i, carry):
        at = pl.ds(pl.multiple_of(i * 256, 256), 256)
        value = dot_t(low_ref[...], wl[at, :])
        part[0, :, at] = part_in_ref[0, :, at] + value[:half]
        part[1, :, at] = part_in_ref[1, :, at] + value[half:]
        return carry

    lax.fori_loop(0, width // 256, part_tile, 0)
    part_low[...] = part[1 - core].astype(BF16)
    part_copy = push(part_low, part_in, core_sem.at[0], core_sem.at[1], other)
    part_copy.start()
    each(one, "middle")
    part_copy.wait_recv()
    grad_normed = part[core] + part_in[...].astype(F32)
    mine = pl.ds(pl.multiple_of(core * half, half), half)
    inverse = inverse_ref[mine]
    hat = tokens_in[mine].astype(F32) * inverse
    gain_term = jnp.sum(grad_normed * hat, axis=0, keepdims=True)
    quarter = width // 4
    for k in range(4):
        cols = slice(k * quarter, (k + 1) * quarter)
        ring_gains[x_here, core, k : k + 1] = gain_term[:, cols]
        ring_gains[x_here, core, 4 + k : 5 + k] = gain_term_ref[:, cols]
    shares = []
    spot = ring_gains.at[x_here, core]
    group = [{"x": x, "mp": c} for x in ring("x") for c in (core, 1 - core)][1:]
    for k, peer in enumerate(group):
        copy = push(spot, spot, ring_send.at[k], ring_recv.at[k], peer)
        copy.start()
        shares.append(copy)
    grad_hat = grad_normed * gain_ref[...]
    inner = jnp.mean(grad_hat * hat, axis=-1, keepdims=True)
    tokens_v[...] = gh_ref[...] + inverse * (grad_hat - hat * inner)
    token_copy = push(tokens_v, tokens_hbm.at[core], core_sem.at[2], core_sem.at[3], other)
    token_copy.start()
    token_save = pltpu.make_async_copy(tokens_v, tokens_hbm.at[core], load_sem.at[1])
    token_save.start()
    each(two, "middle")
    each(gates, "finish")
    each(gates, "begin", 2)
    for flow in small:
        flow.step()
    each(one, "finish")
    each(one, "begin", 1)
    for copy in shares:
        copy.wait_recv()
    gains = Total(gains0, small_send, small_recv, 3, ("y", "z"))
    halves = [ring_gains[x, 0] + ring_gains[x, 1] for x in range(4)]
    gains.start((halves[0] + halves[1]) + (halves[2] + halves[3]))
    each(three, "middle")
    each(gates, "finish")
    gates_ref[lax.axis_index("z"), lax.axis_index("y"), x_here] = gates_out[...].astype(BF16)
    each(spread, "begin", 0)
    for flow, (start, wide) in zip(small, CHUNKS):
        total_ref[:, start : start + wide] = flow.step()
    each(two, "finish")
    each(two, "begin", 1)
    gains.step()
    each(one, "middle")
    each(spread, "finish")
    each(spread, "begin", 1)
    each(three, "finish")
    each(three, "begin", 1)
    each(two, "middle")
    each(one, "finish")
    each(one, "begin", 2)
    gains_ref[...] = gains.step()
    each(spread, "finish")
    each(spread, "begin", 2)
    each(two, "finish")
    each(two, "begin", 2)
    each(one, "finish")
    each(three, "finish")
    each(three, "begin", 2)
    each(two, "finish")
    each(spread, "finish")

    def unpack(b, carry):
        at = pl.ds(pl.multiple_of(16 * lax.rem(b, 3), 16), 16)
        all_gates_ref[b] = gates_ref[:, :, b // 3, at, :].reshape(BLOCK, BLOCK).astype(F32)
        return carry

    lax.fori_loop(0, all_gates_ref.shape[0], unpack, 0)
    each(three, "finish")
    for copy in (token_copy, token_save):
        copy.wait()
    each(flows + gates + spread + small, "drain")
    gains.drain()
    for copy in shares + [part_copy]:
        copy.wait_send()


def rec_end(part, small, gain_term, grad_hidden, tokens, inverse, gain, normed, low, weights, gates, w_lin, cid):
    half, width = grad_hidden.shape
    rows, rec = weights[0].shape[3:]
    gate_blocks = 2 * rec // BLOCK

    def sds(*shape):
        return jax.ShapeDtypeStruct(shape, F32)

    bufs = []
    for e in range(9):
        bufs += scatter_buffers(rows, CHUNKS[e % 3][1], 2 if e < 6 else 1)
    for _ in range(3):
        bufs += scatter_buffers(GATE_ROWS // 3, BLOCK, 0)
    return pl.pallas_call(
        rec_end_kernel,
        out_shape=[
            sds(16, rec),
            sds(8, width // 4),
            sds(gate_blocks, BLOCK, BLOCK),
            sds(rows, rec),
            sds(rows, rec),
            sds(rows, rec),
            sds(2, half, width),
        ],
        in_specs=[VM] * 9 + [ANY] * 4,
        out_specs=[VM] * 6 + [HBM],
        scratch_shapes=bufs
        + [
            pltpu.VMEM(part.shape, F32),
            pltpu.VMEM(weights[0].shape, BF16),
            pltpu.VMEM(w_lin.shape, BF16),
            pltpu.VMEM((GATE_ROWS, BLOCK), F32),
            pltpu.VMEM((half, width), BF16),
            pltpu.VMEM((half, width), BF16),
            pltpu.VMEM((half, width), F32),
            pltpu.VMEM(gates.shape, BF16),
            pltpu.VMEM((4, 2, 8, width // 4), F32),
            pltpu.VMEM((2, 4, 8, width // 4), F32),
        ]
        + [pltpu.VMEM((3, 4, 16, wide), F32) for _, wide in CHUNKS]
        + [
            DMA((2,)),
            DMA((12, 3)),
            DMA((12, 3, 3, 3)),
            DMA((12, 3, 3, 3)),
            DMA((3, 3, 1, 3)),
            DMA((3, 3, 1, 3)),
            DMA((4, 3, 3)),
            DMA((4, 3, 3)),
            DMA((7,)),
            DMA((7,)),
            DMA((4,)),
        ],
        compiler_params=params(cid, 60),
    )(part, small, gain_term, grad_hidden, tokens, inverse, gain, normed, low, *weights, gates, w_lin)


def mlp_end_kernel(in_ref, back, send, recv):
    x_here = lax.axis_index("x")
    peers = ring("x")[1:]
    greet([{"x": peer} for peer in peers])
    moves = []
    for step, peer in enumerate(peers):
        copy = push(in_ref.at[peer], back.at[x_here], send.at[step], recv.at[step], {"x": peer})
        copy.start()
        moves.append(copy)
    back[x_here] = in_ref[x_here]
    for copy in moves:
        copy.wait()


def mlp_end(quarters, cid):
    return pl.pallas_call(
        mlp_end_kernel,
        out_shape=jax.ShapeDtypeStruct(quarters.shape, quarters.dtype),
        in_specs=[VM],
        out_specs=VM,
        scratch_shapes=[DMA((3,)), DMA((3,))],
        compiler_params=params(cid, 61),
    )(quarters)


def finish_kernel(
    small_hbm, gains_hbm, out_hbm, gate_hbm, lin_hbm, back_hbm, rms_hbm, rms_mlp_hbm, result_in, tokens_in, gates_in,
    result_ref, tokens_ref, gates_ref, rec_ref, out_ref, mlp_ref, down_ref, bias_ref, lam_ref, conv_w_ref, conv_b_ref,
    gain_rec_ref, gain_mlp_ref, h_ref, state_ref, rms_ref, rms_mlp_ref,
    small_ref, gains_ref, out_sums, gate_sums, lin_sums, back, rms_v, rms_mlp_v, result_v, tokens_v, gates_v, sem, out_sem,
):
    pairs = (
        (result_in, result_v), (tokens_in, tokens_v), (gates_in, gates_v),
        (small_hbm, small_ref), (gains_hbm, gains_ref), (out_hbm, out_sums), (gate_hbm, gate_sums),
        (lin_hbm, lin_sums), (back_hbm, back), (rms_hbm, rms_v), (rms_mlp_hbm, rms_mlp_v),
    )
    loads = [pltpu.make_async_copy(src, dst, sem.at[k]) for k, (src, dst) in enumerate(pairs)]
    for load in loads:
        load.start()
    copies = []
    for k, (src, dst) in enumerate(((result_v, result_ref), (tokens_v, tokens_ref), (gates_v, gates_ref))):
        loads[k].wait()
        copies.append(pltpu.make_async_copy(src, dst, out_sem.at[k]))
        copies[k].start()
    for load in loads[3:]:
        load.wait()
    rec_ref[:, 0, :] = gate_sums[...]
    rec_ref[:, 1, :] = lin_sums[...]
    out_ref[...] = out_sums[...]
    units = down_ref.shape[1] // 4
    for q in range(4):
        value = back[q].astype(F32)
        at = pl.ds(q * units, units)
        for k in range(2):
            mlp_ref[:, k, at] = value[:, k * units : (k + 1) * units]
        down_ref[:, at] = value[:, 2 * units :]
    bias_ref[...] = small_ref[G_BIAS : G_BIAS + 2]
    lam_ref[...] = small_ref[G_LAM]
    conv_w_ref[...] = small_ref[G_CONV_W : G_CONV_W + CONV]
    conv_b_ref[...] = small_ref[G_CONV_B]
    h_ref[...] = small_ref[G_H]
    state_ref[...] = small_ref[G_STATE : G_STATE + EDGE]
    quarter = gains_ref.shape[1]
    for k in range(4):
        at = pl.ds(k * quarter, quarter)
        gain_rec_ref[at] = gains_ref[k]
        gain_mlp_ref[at] = gains_ref[4 + k]
    half = rms_mlp_v.shape[1]
    square = (half, half)
    diagonal = lax.broadcasted_iota(jnp.int32, square, 0) == lax.broadcasted_iota(jnp.int32, square, 1)
    for core in range(2):
        at = pl.ds(core * half, half)
        for ref, column in ((rms_ref, rms_v[at, 0:1]), (rms_mlp_ref, rms_mlp_v[core, :, 0:1])):
            spread = jnp.where(diagonal, jnp.broadcast_to(column, square), 0.0)
            ref[at] = jnp.sum(spread, axis=0)
    for copy in copies:
        copy.wait()


def finish(small, gains, sums, back, rms, rms_mlp, result, tokens, gates):
    rec = small.shape[1]
    rows = back.shape[1]
    units = back.shape[2] // 3
    width = gains.size // 2

    def sds(*shape):
        return jax.ShapeDtypeStruct(shape, F32)

    return pl.pallas_call(
        finish_kernel,
        out_shape=[
            jax.ShapeDtypeStruct(result.shape, result.dtype),
            sds(*tokens.shape),
            sds(*gates.shape),
            sds(rows, 2, rec),
            sds(rows, rec),
            sds(rows, 2, 4 * units),
            sds(rows, 4 * units),
            sds(2, rec),
            sds(rec),
            sds(CONV, rec),
            sds(rec),
            sds(width),
            sds(width),
            sds(rec),
            sds(EDGE, rec),
            sds(rms.shape[0]),
            sds(rms.shape[0]),
        ],
        in_specs=[HBM] * 11,
        out_specs=[HBM] * 3 + [VM] * 14,
        scratch_shapes=[pltpu.VMEM(a.shape, a.dtype) for a in (small, gains, *sums, back, rms, rms_mlp, result, tokens, gates)]
        + [DMA((11,)), DMA((3,))],
        compiler_params=pltpu.CompilerParams(vmem_limit_bytes=61 * MIB),
    )(small, gains, *sums, back, rms, rms_mlp, result, tokens, gates)


def body(
    tokens,
    cotangent,
    starts,
    valid,
    w_rec,
    w_out,
    w_mlp,
    w_down,
    lru_gates,
    lru_bias,
    lam,
    conv_w,
    conv_b,
    gain_rec,
    gain_mlp,
    h_init,
    conv_state,
):
    count, width = tokens.shape
    shard, _, rec = w_rec.shape
    hidden_units = w_mlp.shape[2] // 4
    half = count // 2
    core = lax.axis_index("mp")

    (
        w_lin, w_gate, w_back, mlp_weights, ext, gate_lin, mixed, reset, gated, factors, states_ext, branch_in,
        normed_rec, grad_out_all, inverse_rec, rms_rec, hidden, normed_mlp, inverse_mlp, rms_half, grad_out, vectors,
    ) = rec_forward(
        tokens,
        gain_rec,
        gain_mlp,
        (conv_w, conv_b, lam, lru_bias, conv_state, h_init),
        (starts, valid),
        w_rec,
        w_out.T,
        w_mlp,
        w_down.T,
        cotangent,
        lru_gates,
        0,
    )
    w_lin, w_gate, w_back = (w.reshape(width, rec) for w in (w_lin, w_gate, w_back))
    grad_hidden, grad_hidden_low, gain_mlp_term, mlp_terms, mlp_part = mlp(
        normed_mlp, grad_out, hidden, inverse_mlp, gain_mlp[None], grad_out_all, mlp_weights, 1
    )
    mlp_sums = lax.psum_scatter(mlp_terms, ("z", "y"), scatter_dimension=0, tiled=True)
    grad_hidden_low = grad_hidden_low.reshape(count, width)
    small, normed_part, grad_rec_low, result, *weight_terms, gate_terms = rec_back(
        grad_hidden_low,
        branch_in,
        normed_rec,
        gate_lin,
        states_ext,
        factors,
        vectors,
        hidden,
        w_back,
        ext,
        mixed,
        reset,
        gated,
        lru_gates,
        w_gate,
        mlp_part,
        2,
    )
    small, gains, gate_blocks, out_sums, gate_sums, lin_sums, grad_tokens = rec_end(
        normed_part,
        small,
        gain_mlp_term,
        grad_hidden,
        tokens,
        inverse_rec,
        gain_rec[None],
        normed_rec,
        grad_rec_low,
        weight_terms,
        gate_terms,
        w_lin,
        3,
    )
    back = mlp_end(mlp_sums.reshape(4, shard, 3 * hidden_units), 4)
    (
        result, grad_tokens, grad_gates, grad_w_rec, grad_out_t, grad_w_mlp, grad_down_t, grad_bias, grad_lam,
        grad_conv_w, conv_bias_gradient, grad_gain_rec, grad_gain_mlp, grad_h_init, grad_conv_state, rms_rec, rms_mlp,
    ) = finish(
        small,
        gains,
        (out_sums, gate_sums, lin_sums),
        back,
        rms_rec,
        rms_half,
        result.reshape(count, width),
        grad_tokens.reshape(count, width),
        gate_blocks.reshape(lru_gates.shape),
    )
    return (
        result,
        rms_rec,
        rms_mlp,
        grad_tokens,
        grad_w_rec,
        grad_out_t.T,
        grad_w_mlp,
        grad_down_t.T,
        grad_gates,
        grad_bias,
        grad_lam,
        grad_conv_w,
        conv_bias_gradient,
        grad_gain_rec,
        grad_gain_mlp,
        grad_h_init,
        grad_conv_state,
    )


def solution(mesh):
    cube = Mesh(mesh.devices.reshape(4, 4, 4, 2), ("z", "y", "x", "mp"))
    placed = (
        P(SEQ, None),
        P(SEQ, None),
        P(SEQ),
        P(SEQ),
        P(SEQ, None, "mp"),
        P("mp", SEQ),
        P(SEQ, None, "mp"),
        P("mp", SEQ),
        P(None, "mp", None, None),
        P(None, "mp"),
        P("mp"),
        P(None, "mp"),
        P("mp"),
        P(),
        P(),
        P("mp"),
        P(None, "mp"),
    )
    return jax.shard_map(
        body,
        mesh=cube,
        in_specs=placed,
        out_specs=(
            P(SEQ, None),
            P(SEQ),
            P(SEQ),
            P(SEQ, None),
            P(SEQ, None, "mp"),
            P("mp", SEQ),
            P(SEQ, None, "mp"),
            P("mp", SEQ),
            P(None, "mp", None, None),
            P(None, "mp"),
            P("mp"),
            P(None, "mp"),
            P("mp"),
            P(),
            P(),
            P("mp"),
            P(None, "mp"),
        ),
        check_vma=False,
    )
```

```python
import functools
import jax
import jax.numpy as jnp
from jax import lax
from jax.experimental import pallas as pl
from jax.experimental.pallas import tpu as pltpu
from jax.sharding import Mesh, PartitionSpec as P

CONV = 4
EDGE = CONV - 1
BLOCK = 256
EPSILON = 1e-06
MESH = pl.DeviceIdType.MESH
ANY = pl.BlockSpec(memory_space=pl.ANY)
HBM = pl.BlockSpec(memory_space=pltpu.HBM)
VM = pl.BlockSpec(memory_space=pltpu.VMEM)
MIB = 1024 * 1024
AXES = ("z", "y", "x")
SEQ = ("z", "y", "x")
ORDERS = (("x", "y", "z"), ("y", "z", "x"), ("z", "x", "y"))
F32, BF16 = jnp.float32, jnp.bfloat16
GELU_C, GELU_A = 0.7978845608028654, 0.044715
DMA = pltpu.SemaphoreType.DMA


def loop(lower, upper, step, batch):
    main = lower + (upper - lower) // batch * batch

    def several(k, carry):
        for i in range(batch):
            step(lower + k * batch + i, 0)
        return carry

    if main > lower:
        lax.fori_loop(0, (main - lower) // batch, several, 0)
    for i in range(main, upper):
        step(i, 0)


def dot(left, right):
    return jnp.dot(left, right, preferred_element_type=F32)


def dot_t(left, right):
    return lax.dot_general(left, right, (((1,), (1,)), ((), ())), preferred_element_type=F32)


def outer(left, right):
    return lax.dot_general(left, right, (((0,), (0,)), ((), ())), preferred_element_type=F32)


def greet(peers):
    sem = pltpu.get_barrier_semaphore()
    for peer in peers:
        pl.semaphore_signal(sem, inc=1, device_id=peer, device_id_type=MESH)
    pl.semaphore_wait(sem, len(peers))


def push(src, dst, send, recv, peer):
    return pltpu.make_async_remote_copy(
        src_ref=src, dst_ref=dst, send_sem=send, recv_sem=recv, device_id=peer, device_id_type=MESH
    )


def ring(axis):
    me = lax.axis_index(axis)
    return me, lax.rem(me + 1, 4), lax.rem(me + 2, 4), lax.rem(me + 3, 4)


def all_neighbours():
    peers = []
    for axis in AXES:
        _, up, _, down = ring(axis)
        peers += [{axis: up}, {axis: down}]
    return peers


def params(cid, mib):
    return pltpu.CompilerParams(
        collective_id=cid, has_side_effects=True, vmem_limit_bytes=mib * MIB
    )


def part_of(done, axis, index, rows, cols):
    spot = []
    for name in AXES:
        if name in done:
            spot.append(pl.ds(0, 4))
        elif name == axis:
            spot.append(index)
        else:
            spot.append(lax.axis_index(name))
    return tuple(spot) + (rows, cols)


def pick(names, axis, index, others):
    spot, rest = [], iter(others)
    for name in names:
        spot.append(index if name == axis else next(rest))
    return tuple(spot)


class Scatter:
    def __init__(self, entry, src, cols, order, halves, bufs, out, own_sem, send, recv, band=None, rings=1):
        self.rings = 0 if halves is None else rings
        self.band, self.band_rows = band, src.shape[-2] if band is None else band[1]
        self.entry, self.src, self.order = entry, src, order
        self.start, self.width = cols
        self.halves, self.bufs, self.out = halves, list(bufs), out
        self.own_sem, self.send, self.recv = own_sem, send, recv
        self.left, self.sent = AXES, []

    def view(self, at, rows=None):
        if rows is None:
            first = self.band[0] if self.band is not None and self.phase == 0 else 0
            rows = pl.ds(first, self.band_rows)
        return at + (rows, pl.ds(self.start if self.phase == 0 else 0, self.width))

    def spread(self, i):
        return ((i // 4, lax.rem(i, 4)), (i,), ())[self.phase]

    def copy(self, src, dst, way, kind, peer):
        at = (self.entry, self.phase, way, kind)
        copy = push(src, dst, self.send.at[at], self.recv.at[at], {self.axis: peer})
        copy.start()
        self.sent.append(copy)
        return copy

    def load(self, index, dst, rows=None):
        src = self.src.at[self.view(pick(self.left, self.axis, index, self.full), rows)]
        copy = pltpu.make_async_copy(src, dst, self.own_sem.at[self.entry, len(self.loads)])
        copy.start()
        self.loads.append(copy)

    def begin(self, phase):
        self.phase, self.axis = phase, self.order[phase]
        self.full = (pl.ds(0, 4),) * (2 - phase)
        me, up, far, down = ring(self.axis)
        self.first, self.second, self.loads = [], [], []
        self.two_step = phase < self.rings
        if self.two_step:
            self.ones, self.twos = self.bufs.pop(0), self.bufs.pop(0)
            self.near = self.bufs.pop(0) if phase == 0 else None
            for way, peer in enumerate((up, down)):
                half = self.halves[way]
                src = self.src.at[self.view(pick(self.left, self.axis, far, self.full), half)]
                self.first.append(self.copy(src, self.ones.at[way], way, 0, peer))
            for way, peer in enumerate((up, down)):
                half = self.halves[1 - way]
                src = self.src.at[self.view(pick(self.left, self.axis, peer, self.full), half)]
                dst = self.twos.at[(way,) + self.full + (half,)]
                self.second.append(self.copy(src, dst, way, 1, peer))
            for way, peer in enumerate((up, down)):
                if phase == 0:
                    self.load(peer, self.near.at[way], self.halves[way])
        else:
            self.threes = self.bufs.pop(0)
            for step, peer in enumerate((up, far, down)):
                src = self.src.at[self.view(pick(self.left, self.axis, peer, self.full))]
                self.second.append(self.copy(src, self.threes.at[step], step, 0, peer))
        if phase == 0:
            self.own = self.bufs.pop(0)
            self.load(me, self.own)
        self.acc = self.bufs.pop(0) if phase < 2 else self.out

    def middle(self):
        _, up, _, down = ring(self.axis)
        for way, peer in enumerate((up, down)):
            self.first[way].wait_recv()
            if self.phase == 0:
                self.loads[way].wait()

            def add(i, carry, way=way, peer=peer):
                there = (way,) + self.spread(i)
                if self.phase == 0:
                    own = self.near[there]
                else:
                    at = pick(self.left, self.axis, peer, self.spread(i))
                    own = self.src[self.view(at, self.halves[way])]
                total = self.ones[there].astype(F32) + own.astype(F32)
                self.ones[there] = total.astype(BF16)
                return carry

            lax.fori_loop(0, 4 ** (2 - self.phase), add, 0)
            dst = self.twos.at[(way,) + self.full + (self.halves[way],)]
            self.second.append(self.copy(self.ones.at[way], dst, way, 2, peer))

    def finish(self):
        me = lax.axis_index(self.axis)
        for copy in self.second:
            copy.wait_recv()
        if self.phase == 0:
            self.loads[-1].wait()
        buf, slots = (self.twos, (0, 1)) if self.two_step else (self.threes, (0, 1, 2))

        def total(i, carry):
            there = self.spread(i)
            if self.phase == 0:
                whole = self.own[there].astype(F32)
            else:
                whole = self.src[self.view(pick(self.left, self.axis, me, there))].astype(F32)
            for slot in slots:
                whole = whole + buf[(slot,) + there].astype(F32)
            if self.phase < 2:
                self.acc[there] = whole.astype(self.acc.dtype)
            else:
                first = 0 if self.band is None else self.band[0]
                self.acc[pl.ds(first, self.band_rows), pl.ds(self.start, self.width)] = whole
            return carry

        lax.fori_loop(0, 4 ** (2 - self.phase), total, 0)
        self.src = self.acc
        self.left = tuple(name for name in self.left if name != self.axis)

    def drain(self):
        for copy in self.sent:
            copy.wait_send()


def scatter_buffers(rows, width, rings):
    bufs = []
    for phase in range(3):
        cube = (4,) * (2 - phase)
        if phase < rings:
            bufs.append(pltpu.VMEM((2,) + cube + (rows // 2, width), BF16))
            bufs.append(pltpu.VMEM((2,) + cube + (rows, width), BF16))
            if phase == 0:
                bufs.append(pltpu.VMEM((2,) + cube + (rows // 2, width), BF16))
        else:
            bufs.append(pltpu.VMEM((3,) + cube + (rows, width), BF16))
        if phase == 0:
            bufs.append(pltpu.VMEM(cube + (rows, width), BF16))
        if phase < 2:
            bufs.append(pltpu.VMEM(cube + (rows, width), BF16))
    return bufs


class Gather:
    def __init__(self, entry, out, order, cols, send, recv, done=(), ring_rounds=(), band=None):
        self.band = (0, out.shape[3]) if band is None else band
        self.entry, self.out, self.order, self.cols = entry, out, order, pl.ds(*cols)
        self.send, self.recv, self.sent = send, recv, []
        self.done, self.ring_rounds = done, ring_rounds

    def spot(self, origin, rows=None):
        rows = pl.ds(*self.band) if rows is None else rows
        return self.out.at[part_of(self.done, self.axis, origin, rows, self.cols)]

    def copy(self, src, dst, step, way, peer):
        at = (self.entry, self.phase, step, way)
        copy = push(src, dst, self.send.at[at], self.recv.at[at], {self.axis: peer})
        copy.start()
        self.sent.append(copy)
        return copy

    def begin(self, phase, src=None):
        self.phase, self.axis = phase, self.order[phase]
        me, up, far, down = ring(self.axis)
        here = self.spot(me)
        src = here if src is None else src.at[:, self.cols]
        peers = (up, down) if phase in self.ring_rounds else (up, far, down)
        self.copies = [self.copy(src, here, 0, way, peer) for way, peer in enumerate(peers)]

    def middle(self):
        _, up, _, down = ring(self.axis)
        half = self.out.shape[3] // 2
        first, self.copies = self.copies, []
        for way, (peer, origin) in enumerate(((up, down), (down, up))):
            first[way].wait_recv()
            spot = self.spot(origin, pl.ds(way * half, half))
            self.copies.append(self.copy(spot, spot, 1, way, peer))

    def hold(self):
        for copy in self.copies:
            copy.wait_recv()

    def finish(self):
        self.hold()
        self.done = self.done + (self.axis,)

    def drain(self):
        for copy in self.sent:
            copy.wait_send()


class Rounds:
    def __init__(self, slots, send, recv, entry=0, order=("x", "y", "z")):
        self.slots, self.send, self.recv, self.sent = slots, send, recv, []
        self.entry, self.order = entry, order

    def begin(self, phase, rows):
        self.phase, axis = phase, self.order[phase]
        me = lax.axis_index(axis)
        for at, value in rows:
            self.slots[phase, me, at] = value
        self.copies = []
        for step, peer in enumerate(ring(axis)[1:]):
            spot = self.slots.at[phase, me]
            at = (self.entry, phase, step)
            copy = push(spot, spot, self.send.at[at], self.recv.at[at], {axis: peer})
            copy.start()
            self.copies.append(copy)

    def finish(self):
        for copy in self.copies:
            copy.wait_recv()
        self.sent += self.copies

    def drain(self):
        for copy in self.sent:
            copy.wait_send()


class Prefix(Rounds):
    def start(self, pair, backward):
        self.backward, self.cur, self.head = backward, pair, None
        self.share(0)

    def share(self, phase):
        self.begin(phase, [(slice(0, 1), self.cur[0]), (slice(1, 2), self.cur[1])])

    def step(self):
        self.finish()
        me = lax.axis_index(self.order[self.phase])
        run = (jnp.ones_like(self.cur[0]), jnp.zeros_like(self.cur[1]))
        mine = run
        for j in (3, 2, 1, 0) if self.backward else (0, 1, 2, 3):
            take = me == j
            mine = (jnp.where(take, run[0], mine[0]), jnp.where(take, run[1], mine[1]))
            fac, val = self.slots[self.phase, j, 0:1], self.slots[self.phase, j, 1:2]
            run = (run[0] * fac, val + fac * run[1])
        self.cur = run
        if self.head is None:
            self.head = mine
        else:
            self.head = (mine[0] * self.head[0], self.head[1] + self.head[0] * mine[1])
        if self.phase < 2:
            self.share(self.phase + 1)
        return self.head


class Total(Rounds):
    def start(self, value):
        self.begin(0, [(slice(None), value)])

    def step(self):
        self.finish()
        at = self.slots
        k = self.phase
        value = (at[k, 0] + at[k, 1]) + (at[k, 2] + at[k, 3])
        if k + 1 < len(self.order):
            self.begin(k + 1, [(slice(None), value)])
        return value


def axis_peers():
    return [{axis: ring(axis)[step]} for axis in AXES for step in (1, 2, 3)]


def along_seq(distance):
    place = lax.axis_index("z") * 16 + lax.axis_index("y") * 4 + lax.axis_index("x")
    place = lax.rem(place + distance + 64, 64)
    return {"z": place // 16, "y": lax.rem(place // 4, 4), "x": lax.rem(place, 4)}


CHUNKS = ((0, 384), (384, 512), (896, 384))
SUM_ORDERS = (
    (("y", "z", "x"), ("x", "y", "z"), ("z", "y", "x")),
    (("z", "x", "y"), ("x", "z", "y"), ("y", "x", "z")),
    (("y", "z", "x"), ("x", "y", "z"), ("z", "x", "y")),
)
ROW_HALVES = (pl.ds(0, 16), pl.ds(16, 16))
BANDS = ((0, 16), (16, 16), (32, 16))


def gelu_parts(x):
    inner = GELU_C * (x + GELU_A * x * x * x)
    t = jnp.tanh(inner)
    slope = GELU_C * (1.0 + 3.0 * GELU_A * x * x)
    return 0.5 * x * (1.0 + t), 0.5 * (1.0 + t) + 0.5 * x * (1.0 - t * t) * slope


FAR, UP, DOWN, ME = 0, 1, 2, 3


class RingSum:
    def __init__(self, part, got, one, two, send, recv, sib_send, sib_recv):
        self.part, self.got, self.one, self.two = part, got, one, two
        self.send, self.recv, self.sib_send, self.sib_recv = send, recv, sib_send, sib_recv
        self.core, self.sums, self.sent = lax.axis_index("mp"), {}, []

    def across(self, *slots):
        for slot in slots:
            copy = push(
                self.part.at[slot, 1 - self.core],
                self.got.at[slot],
                self.sib_send.at[slot],
                self.sib_recv.at[slot],
                {"mp": 1 - self.core},
            )
            copy.start()
            self.sums[slot] = copy

    def add(self, dst, src):
        dst[...] = (dst[...].astype(F32) + src[...].astype(F32)).astype(dst.dtype)

    def collect(self, slot):
        self.sums[slot].wait_recv()
        self.add(self.got.at[slot], self.part.at[slot, self.core])

    def far(self):
        self.collect(FAR)
        half = self.one.shape[1]
        _, up, _, down = ring("x")
        self.first = []
        for way, peer in enumerate((up, down)):
            piece = self.got.at[FAR, pl.ds(way * half, half)]
            at = (0, way)
            copy = push(piece, self.one.at[way], self.send.at[at], self.recv.at[at], {"x": peer})
            copy.start()
            self.first.append(copy)

    def near(self):
        half = self.one.shape[1]
        _, up, _, down = ring("x")
        self.second = []
        for way, (peer, slot) in enumerate(((up, UP), (down, DOWN))):
            self.collect(slot)
            self.first[way].wait_recv()
            self.add(self.got.at[slot, pl.ds(way * half, half)], self.one.at[way])
            at = (1, way)
            copy = push(self.got.at[slot], self.two.at[way], self.send.at[at], self.recv.at[at], {"x": peer})
            copy.start()
            self.second.append(copy)

    def total(self):
        self.sums[ME].wait_recv()
        total = self.got[ME].astype(F32) + self.part[ME, self.core].astype(F32)
        for way in range(2):
            self.second[way].wait_recv()
            total = total + self.two[way].astype(F32)
        return total

    def drain(self):
        for copy in self.first + self.second + list(self.sums.values()):
            copy.wait_send()


def ring_sum_scratch(rows, width):
    return [
        pltpu.VMEM((4, rows, width), BF16),
        pltpu.VMEM((2, rows // 2, width), BF16),
        pltpu.VMEM((2, rows, width), BF16),
        DMA((2, 2)),
        DMA((2, 2)),
        DMA((4,)),
        DMA((4,)),
    ]


def mlp_kernel(
    nm_ref, go_ref, hidden_ref, inv_ref, gain_ref, go_hbm, w_hbm,
    grad_hidden_ref, low_ref, term_ref, dw_ref, opart_out,
    go, w, gathered, npart, opart, mlp_in, ggu, gmi, low_half,
    load_sem, wsend, wrecv, gsend, grecv, gsib_send, gsib_recv, core_sem, *sum_refs,
):
    rows, width = nm_ref.shape
    half = rows // 2
    units = mlp_in.shape[1]
    me, up, far, down = ring("x")
    core = lax.axis_index("mp")
    other = {"mp": 1 - core}
    loads = [pltpu.make_async_copy(nm_ref, gathered.at[ME, core], load_sem.at[0])]
    wide = w.shape[4] // 2
    full, every = pl.ds(0, 4), pl.ds(0, w.shape[3])
    last = (("z", 0), ("y", wide))

    def weight_set(axis, index, at, cols):
        return ((index, full) if axis == "z" else (full, index)) + (full, at, pl.ds(cols, wide))

    for e, (axis, cols) in enumerate(last):
        here, ahead, _, behind = ring(axis)
        for k, index in enumerate((here, ahead, behind)):
            spot = weight_set(axis, index, every, cols)
            loads.append(pltpu.make_async_copy(w_hbm.at[spot], w.at[spot], load_sem.at[1 + 3 * e + k]))
    for slot, chip in ((FAR, far), (UP, up), (DOWN, down), (ME, me)):
        at = pl.ds(slot * 2 * rows, 2 * rows)
        loads.append(pltpu.make_async_copy(go_hbm.at[chip], go.at[at], load_sem.at[7 + slot]))
    for load in loads:
        load.start()
    peers = [{"x": up}, {"x": down}, other]
    for axis in ("y", "z"):
        peers += [{axis: ring(axis)[1]}, {axis: ring(axis)[3]}]
    greet(peers)
    top, low = pl.ds(0, half), pl.ds(half, half)
    first = []
    for way, (peer, slot) in enumerate(((up, DOWN), (down, UP))):
        spot = gathered.at[slot, core]
        copy = push(nm_ref, spot, gsend.at[0, way], grecv.at[0, way], {"x": peer})
        copy.start()
        first.append(copy)
    across = [push(nm_ref, gathered.at[ME, core], gsib_send.at[0], gsib_recv.at[0], other)]
    across[0].start()
    rest = []
    for e, (axis, cols) in enumerate(last):
        _, ahead, _, behind = ring(axis)
        deep = w.shape[3] // 2
        for way, (peer, origin) in enumerate(((ahead, behind), (behind, ahead))):
            spot = weight_set(axis, origin, pl.ds(way * deep, deep), cols)
            copy = push(w_hbm.at[spot], w.at[spot], wsend.at[e, way], wrecv.at[e, way], {axis: peer})
            copy.start()
            rest.append(copy)
    second = []
    for way, (peer, slot, piece) in enumerate(((up, DOWN, top), (down, UP, low))):
        first[way].wait_recv()
        spot = gathered.at[slot, core]
        copy = push(
            spot.at[piece], gathered.at[FAR, core, piece], gsend.at[1, way], grecv.at[1, way], {"x": peer}
        )
        copy.start()
        second.append(copy)
        copy = push(spot, spot, gsib_send.at[1 + way], gsib_recv.at[1 + way], other)
        copy.start()
        across.append(copy)
    for copy in rest:
        copy.wait_recv()
    for load in loads:
        load.wait()

    def tile(j, start=0):
        return pl.ds(pl.multiple_of(start + j * 256, 256), 256)

    def columns(at):
        return w[:, :, :, :, at].reshape(width, 256)

    def shard_tile(i, at):
        return w[i // 2, pl.ds(2 * lax.rem(i, 2), 2), :, :, at].reshape(256, -1)

    def grad_tile(j, carry):
        gmi[:, tile(j)] = dot(go[...], columns(tile(j, 2 * units)))
        return carry

    loop(0, units // 256, grad_tile, 1)
    for way, piece in enumerate((top, low)):
        second[way].wait_recv()
        spot = gathered.at[FAR, core, piece]
        copy = push(spot, spot, gsib_send.at[3 + way], gsib_recv.at[3 + way], other)
        copy.start()
        across.append(copy)

    def tokens_step(slot):
        at = pl.ds(slot * 2 * rows, 4 * rows)

        def hidden_tile(j, carry):
            tokens_in = gathered[slot : slot + 2].reshape(4 * rows, width)
            gate = dot(tokens_in, columns(tile(j)))
            up_lin = dot(tokens_in, columns(tile(j, units)))
            grad = gmi[at, tile(j)]
            act, slope = gelu_parts(gate)
            mlp_in[at, tile(j)] = (act * up_lin).astype(BF16)
            ggu[at, tile(j)] = (slope * (grad * up_lin)).astype(BF16)
            ggu[at, tile(j, units)] = (grad * act).astype(BF16)
            return carry

        loop(0, units // 256, hidden_tile, 1)

        def back_tile(j, carry):
            back = dot_t(ggu[at], shard_tile(j, pl.ds(0, 2 * units)))
            npart[slot : slot + 2, :, :, tile(j)] = back.astype(BF16).reshape(2, 2, rows, 256)
            return carry

        loop(0, width // 256, back_tile, 1)

    def out_tile(j, carry):
        part = dot_t(mlp_in[...], shard_tile(j, pl.ds(2 * units, units)))
        opart[:, :, :, tile(j)] = part.astype(BF16).reshape(4, 2, rows, 256)
        return carry

    def weight_grads(lower, upper):
        def step(i, carry):
            left = gathered[:, :, :, tile(i)].reshape(8 * rows, 256)
            dw_ref[tile(i), pl.ds(0, 2 * units)] = outer(left, ggu[...]).astype(BF16)
            dw_ref[tile(i), pl.ds(2 * units, units)] = outer(go[:, tile(i)], mlp_in[...]).astype(BF16)
            return carry

        loop(lower, upper, step, 1)

    sums = RingSum(npart, *sum_refs)
    for copy in across:
        copy.wait_recv()
    tokens_step(FAR)
    sums.across(FAR, UP)
    sums.far()
    tokens_step(DOWN)
    sums.across(DOWN, ME)
    sums.near()
    loop(0, width // 256, out_tile, 1)
    save = pltpu.make_async_copy(opart, opart_out, load_sem.at[11])
    save.start()
    weight_grads(0, 5)
    grad_normed = sums.total()
    hat = hidden_ref[...] * inv_ref[...]
    grad_hat = grad_normed * gain_ref[...]
    inner = jnp.mean(grad_hat * hat, axis=-1, keepdims=True)
    grad_hidden = go_ref[...].astype(F32) + inv_ref[...] * (grad_hat - hat * inner)
    grad_hidden_ref[...] = grad_hidden
    term_ref[...] = jnp.sum(grad_normed * hat, axis=0, keepdims=True)
    low_half[...] = grad_hidden.astype(BF16)
    low_ref[core] = low_half[...]
    swap = push(low_half, low_ref.at[core], core_sem.at[0], core_sem.at[1], other)
    swap.start()
    weight_grads(5, 8)
    swap.wait()
    save.wait()
    sums.drain()
    for copy in first + second + across + rest:
        copy.wait_send()


def mlp(normed, grad_out, hidden, inverse, gain, grad_out_all, weights, cid):
    rows, width = normed.shape
    units = weights.shape[4] // 3

    def block(dtype, *shape):
        return pltpu.VMEM(shape, dtype)

    return pl.pallas_call(
        mlp_kernel,
        out_shape=[
            jax.ShapeDtypeStruct((rows, width), F32),
            jax.ShapeDtypeStruct((2, rows, width), BF16),
            jax.ShapeDtypeStruct((1, width), F32),
            jax.ShapeDtypeStruct((width, 3 * units), BF16),
            jax.ShapeDtypeStruct((4, 2, rows, width), BF16),
        ],
        in_specs=[VM] * 5 + [ANY] * 2,
        out_specs=[VM] * 4 + [HBM],
        scratch_shapes=[
            block(BF16, 8 * rows, width),
            block(BF16, *weights.shape),
            block(BF16, 4, 2, rows, width),
            block(BF16, 4, 2, rows, width),
            block(BF16, 4, 2, rows, width),
            block(BF16, 8 * rows, units),
            block(BF16, 8 * rows, 2 * units),
            block(F32, 8 * rows, units),
            block(BF16, rows, width),
        ]
        + [DMA((12,)), DMA((2, 2)), DMA((2, 2)), DMA((2, 2)), DMA((2, 2)), DMA((5,)), DMA((5,)), DMA((2,))]
        + ring_sum_scratch(rows, width),
        compiler_params=params(cid, 60),
    )(normed, grad_out, hidden, inverse, gain, grad_out_all.reshape(4, 2 * rows, width), weights)


def lanes(n):
    return pl.ds(pl.multiple_of(n * BLOCK, BLOCK), BLOCK)


def minus_expm1(x):
    series = jnp.ones_like(x)
    for k in (9, 8, 7, 6, 5, 4, 3, 2):
        series = 1.0 + x * (1.0 / k) * series
    return jnp.where(x > -0.4, -x * series, 1.0 - jnp.exp(x))


def log1p(x):
    series = jnp.zeros_like(x)
    for k in (7, 6, 5, 4, 3, 2, 1):
        series = 1.0 / k - x * series
    return jnp.where(x < 0.05, x * series, jnp.log(1.0 + x))


CONV_W, CONV_B, RATES, BIAS, CONV_STATE, H_INIT, SLOPE = 0, 4, 5, 6, 8, 11, 12


def rec_forward_kernel(*refs):
    (
        tokens_ref, gain_ref, gain_mlp_ref, conv_w_ref, conv_b_ref, lam_ref, bias_ref, conv_state_ref,
        h_init_ref, starts_ref, valid_ref, rec_raw, back_in, mlp_raw, down_in, cot_ref, g_hbm,
        lin_out, gate_out, back_out, mlp_out, ext_out, act_out, mixed_out, reset_out, input_out, f_out, states_out,
        branch_out, normed_out, go_all, inv_ref, rms_ref, hidden_ref, nm_ref, inv_mlp_ref, rms_mlp_ref, go_ref, v_ref,
        wl, wg, wb, ext, gate_lin, mixed_v, reset_v, input_v, f_v, states, branch_v, normed, tail_in, driven, cf_v,
        part, part_low, part_in, g_v, rms_v, slots, mask_ref, rec_in, mlp_in,
        tail_sem, load_sem, save_sem, own_sem, move_send, move_recv, send, recv, small_send, small_recv, core_sem,
        go_send, go_recv, go_sib_send, go_sib_recv,
    ) = refs
    count, width = tokens_ref.shape
    rec = f_v.shape[1]
    for k in range(2):
        rec_in[:, k * rec : (k + 1) * rec] = rec_raw[:, k, :]
        mlp_in[:, k * mlp_raw.shape[2] : (k + 1) * mlp_raw.shape[2]] = mlp_raw[:, k, :]
    gate_in, lin_in = rec_in.at[:, pl.ds(0, rec)], rec_in.at[:, pl.ds(rec, rec)]
    blocks = rec // BLOCK
    half = count // 2
    core = lax.axis_index("mp")
    other = {"mp": 1 - core}
    here = tuple(lax.axis_index(name) for name in AXES)
    load = pltpu.make_async_copy(g_hbm, g_v, load_sem)
    load.start()
    owns = [
        pltpu.make_async_copy(lin_in, wl.at[here], own_sem.at[0]),
        pltpu.make_async_copy(gate_in, wg.at[here], own_sem.at[1]),
        pltpu.make_async_copy(back_in, wb.at[here], own_sem.at[2]),
    ]
    units = mlp_out.shape[4] // 3
    every = pl.ds(0, rec_in.shape[0])

    def quarter(k, chip):
        if k == 2:
            return down_in.at[every, pl.ds(pl.multiple_of(chip * units, units), units)]
        return mlp_in.at[every, pl.ds(pl.multiple_of((4 * k + chip) * units, units), units)]

    spots = [mlp_out.at[here + (every, pl.ds(k * units, units))] for k in range(3)]
    owns += [pltpu.make_async_copy(quarter(k, here[2]), spots[k], own_sem.at[3 + k]) for k in range(3)]
    for own in owns:
        own.start()
    greet(axis_peers() + [other, along_seq(1), along_seq(-1)])
    tail_copy = push(tokens_ref.at[pl.ds(count - 16, 16)], tail_in, tail_sem.at[0], tail_sem.at[1], along_seq(1))
    tail_copy.start()
    lin = [Gather(e, wl, ORDERS[e], CHUNKS[e], send, recv, ring_rounds=(2,)) for e in range(3)]
    gate = [
        Gather(3 + e, wg, ORDERS[(e + 1) % 3], CHUNKS[e], send, recv, ring_rounds=(1, 2)) for e in range(3)
    ]
    back = [
        Gather(6 + e, wb, ORDERS[(2, 1, 0)[e]], CHUNKS[e], send, recv, ring_rounds=(1, 2)) for e in range(3)
    ]
    rest = gate + back
    wide = mlp_out.shape[4] // 2
    mlp_flows = [
        Gather(9 + e, mlp_out, order, (e * wide, wide), send, recv, done=("x",), ring_rounds=(1,))
        for e, order in enumerate((("y", "z"), ("z", "y")))
    ]

    def each(group, name, *args):
        for flow in group:
            getattr(flow, name)(*args)

    each(lin, "begin", 0, lin_in)
    moves = []
    for step, peer in enumerate(ring("x")[1:]):
        for k in range(3):
            copy = push(quarter(k, peer), spots[k], move_send.at[step, k], move_recv.at[step, k], {"x": peer})
            copy.start()
            moves.append(copy)
    each(gate, "begin", 0, gate_in)
    each(back, "begin", 0, back_in)

    v_ref[CONV_W : CONV_W + CONV] = conv_w_ref[...]
    v_ref[BIAS : BIAS + 2] = bias_ref[...]
    v_ref[CONV_STATE : CONV_STATE + EDGE] = conv_state_ref[...]
    for at, ref in ((CONV_B, conv_b_ref), (H_INIT, h_init_ref)):
        v_ref[at : at + 1] = ref[...].reshape(1, rec)
    lam = lam_ref[...].reshape(1, rec)
    v_ref[RATES : RATES + 1] = jnp.maximum(-lam, 0.0) + log1p(jnp.exp(-jnp.abs(lam)))
    v_ref[SLOPE : SLOPE + 1] = 1.0 / (1.0 + jnp.exp(lam))
    v_ref[SLOPE + 1 :] = jnp.zeros((15 - SLOPE, rec), F32)
    square = (count, count)
    diagonal = lax.broadcasted_iota(jnp.int32, square, 0) == lax.broadcasted_iota(jnp.int32, square, 1)
    for k, row in enumerate((1.0 - starts_ref[...].astype(F32), valid_ref[...].astype(F32))):
        spread = jnp.where(diagonal, jnp.broadcast_to(row.reshape(1, count), square), 0.0)
        mask_ref[:, k : k + 1] = jnp.sum(spread, axis=1, keepdims=True)

    def norm(values):
        mean_sq = jnp.mean(values * values, axis=-1, keepdims=True)
        inverse = lax.rsqrt(mean_sq + EPSILON)
        return values * inverse, inverse, jnp.sqrt(mean_sq + EPSILON)

    def norm_step(i, carry):
        at = pl.ds(pl.multiple_of(i * 64, 64), 64)
        hat, inverse, rms = norm(tokens_ref[at].astype(F32))
        inv_ref[at] = inverse
        rms_ref[at] = rms
        normed[pl.ds(pl.multiple_of(16 + i * 64, 16), 64)] = (hat * gain_ref[...]).astype(BF16)
        return carry

    lax.fori_loop(0, count // 64, norm_step, 0)
    for own in owns:
        own.wait()
    each(lin, "finish")
    each(lin, "begin", 1)
    each(rest, "finish")
    each(rest, "begin", 1)
    tail_copy.wait_recv()
    normed[0:16] = (norm(tail_in[...].astype(F32))[0] * gain_ref[...]).astype(BF16)
    saves = []

    def save(src, dst):
        copy = pltpu.make_async_copy(src, dst, save_sem.at[len(saves)])
        copy.start()
        saves.append(copy)

    save(normed.at[pl.ds(16, count)], normed_out)
    each(lin, "finish")
    each(lin, "begin", 2)
    for copy in moves:
        copy.wait_recv()
    each(mlp_flows, "begin", 0)
    each(rest, "middle")
    each(lin, "middle")
    each(rest, "finish")
    each(rest, "begin", 2)
    mine = pl.ds(pl.multiple_of(core * half, half), half)
    go_ref[...] = (cot_ref[mine].astype(F32) * mask_ref[mine, 1:2]).astype(BF16)
    load.wait()
    each(lin, "finish")
    save(wl, lin_out)
    is_first = (here[0] + here[1] + here[2]) == 0

    def rec_step(n, carry):
        at = lanes(n)
        ext[:, at] = dot(normed[...], wl[:, :, :, :, at].reshape(width, BLOCK))

        @pl.when(is_first)
        def _():
            ext[16 - EDGE : 16, at] = v_ref[CONV_STATE : CONV_STATE + EDGE, at]

        total = v_ref[CONV_B : CONV_B + 1, at] + jnp.zeros((count, BLOCK), F32)
        for k in range(CONV):
            total = total + v_ref[CONV_W + k : CONV_W + k + 1, at] * ext[pl.ds(16 - EDGE + k, count), at]
        mixed = total.astype(BF16)
        mixed_v[:, at] = mixed
        reset = jax.nn.sigmoid(dot(mixed, g_v[0, n]) + v_ref[BIAS : BIAS + 1, at])
        gated = jax.nn.sigmoid(dot(mixed, g_v[1, n]) + v_ref[BIAS + 1 : BIAS + 2, at])
        reset_v[:, at] = reset
        input_v[:, at] = gated
        log_decay = -8.0 * v_ref[RATES : RATES + 1, at] * reset
        f_v[:, at] = jnp.exp(log_decay) * mask_ref[:, 0:1]
        driven[:, at] = jnp.sqrt(minus_expm1(2.0 * log_decay)) * gated * mixed.astype(F32)
        return carry

    lax.fori_loop(0, blocks, rec_step, 0)
    for src, dst in ((ext, ext_out), (mixed_v, mixed_out), (reset_v, reset_out), (input_v, input_out), (f_v, f_out)):
        save(src, dst)

    def group(i, carry):
        base = pl.multiple_of(i * 8, 8)
        f, d = f_v[pl.ds(base, 8)], driven[pl.ds(base, 8)]
        cf, cd = carry
        cfs, cds = [], []
        for r in range(8):
            cf = cf * f[r : r + 1]
            cd = cd * f[r : r + 1] + d[r : r + 1]
            cfs.append(cf)
            cds.append(cd)
        cf_v[pl.ds(base, 8)] = jnp.concatenate(cfs, axis=0)
        states[pl.ds(pl.multiple_of(base + 8, 8), 8)] = jnp.concatenate(cds, axis=0)
        return cf, cd

    zero = jnp.zeros((1, rec), F32)
    ends = lax.fori_loop(0, count // 8, group, (zero + 1.0, zero))
    prefix = Prefix(slots, small_send, small_recv)
    prefix.start(ends, False)
    by_axis = {axis: [flow for flow in rest if flow.axis == axis] for axis in AXES}
    each(by_axis["x"], "middle")
    prefix.step()
    each(by_axis["y"], "middle")
    each(mlp_flows, "finish")
    mlp_flows[1].begin(1)
    prefix.step()
    each(by_axis["z"], "middle")
    mlp_flows[0].begin(1)
    x_here, x_up, x_far, x_down = ring("x")
    spot = go_all.at[x_here, core]
    save(go_ref, spot)
    go_first = []
    for way, peer in enumerate((x_up, x_down)):
        copy = push(go_ref, spot, go_send.at[0, way], go_recv.at[0, way], {"x": peer})
        copy.start()
        go_first.append(copy)
    go_across = [push(go_ref, spot, go_sib_send.at[0], go_sib_recv.at[0], other)]
    go_across[0].start()
    head = prefix.step()
    carry_in = head[1] + head[0] * v_ref[H_INIT : H_INIT + 1]
    each(gate, "finish")
    save(wg, gate_out)

    def gate_step(n, carry):
        gate_lin[:, lanes(n)] = dot(normed[16:], wg[:, :, :, :, lanes(n)].reshape(width, BLOCK))
        return carry

    lax.fori_loop(0, blocks, gate_step, 0)
    save(gate_lin, act_out)
    states[0:8] = jnp.broadcast_to(carry_in, (8, rec))

    def branch_step(n, carry):
        at = lanes(n)
        value = states[8:, at] + cf_v[:, at] * states[0:1, at]
        states[8:, at] = value
        branch_v[:, at] = (gelu_parts(gate_lin[:, at])[0] * value).astype(BF16)
        return carry

    lax.fori_loop(0, blocks, branch_step, 0)
    save(states, states_out)
    save(branch_v, branch_out)
    each(back, "finish")
    save(wb, back_out)

    def out_step(i, carry):
        at = pl.ds(pl.multiple_of(i * 256, 256), 256)
        rows = wb[i // 2, pl.ds(2 * lax.rem(i, 2), 2)].reshape(256, rec)
        value = dot_t(branch_v[...], rows)
        part[0, :, at] = value[:half]
        part[1, :, at] = value[half:]
        return carry

    lax.fori_loop(0, width // 256, out_step, 0)
    part_low[...] = part[1 - core].astype(BF16)
    part_copy = push(part_low, part_in, core_sem.at[0], core_sem.at[1], other)
    part_copy.start()
    go_second = []
    for way, (peer, origin) in enumerate(((x_up, x_down), (x_down, x_up))):
        go_first[way].wait_recv()
        spot = go_all.at[origin, core]
        piece = spot.at[pl.ds(way * (half // 2), half // 2)]
        copy = push(piece, piece, go_send.at[1, way], go_recv.at[1, way], {"x": peer})
        copy.start()
        go_second.append(copy)
        copy = push(spot, spot, go_sib_send.at[1 + way], go_sib_recv.at[1 + way], other)
        copy.start()
        go_across.append(copy)
    part_copy.wait_recv()
    hidden = tokens_ref[mine].astype(F32) + (part[core] + part_in[...].astype(F32))
    hidden_ref[...] = hidden
    hat, inverse, rms = norm(hidden)
    inv_mlp_ref[...] = inverse
    rms_v[...] = jnp.broadcast_to(rms, (half, 128))
    rms_mlp_ref[core] = rms_v[...]
    rms_copy = push(rms_v, rms_mlp_ref.at[core], core_sem.at[2], core_sem.at[3], other)
    rms_copy.start()
    nm_ref[...] = (hat * gain_mlp_ref[...]).astype(BF16)
    for way in range(2):
        go_second[way].wait_recv()
        piece = go_all.at[x_far, core, pl.ds(way * (half // 2), half // 2)]
        copy = push(piece, piece, go_sib_send.at[3 + way], go_sib_recv.at[3 + way], other)
        copy.start()
        go_across.append(copy)
    each(mlp_flows, "hold")
    rms_copy.wait()
    for copy in go_across:
        copy.wait()
    for copy in go_first + go_second:
        copy.wait_send()
    for copy in moves:
        copy.wait_send()
    for copy in saves:
        copy.wait()
    each(lin, "drain")
    each(rest, "drain")
    each(mlp_flows, "drain")
    prefix.drain()
    part_copy.wait_send()
    tail_copy.wait_send()


def rec_forward(tokens, gain_rec, gain_mlp, vectors, masks, w_rec, back, w_mlp, down, cotangent, gates, cid):
    count, width = tokens.shape
    rows, rec = back.shape
    half = count // 2

    def cube(last):
        return (4, 4, 4, rows, last)

    def sds(shape, dtype):
        return jax.ShapeDtypeStruct(shape, dtype)

    saved = [
        (cube(rec), BF16),
        (cube(rec), BF16),
        (cube(rec), BF16),
        (cube(3 * down.shape[1] // 4), BF16),
        ((count + 16, rec), F32),
        ((count, rec), F32),
        ((count, rec), BF16),
        ((count, rec), F32),
        ((count, rec), F32),
        ((count, rec), F32),
        ((count + 8, rec), F32),
        ((count, rec), BF16),
        ((count, width), BF16),
        ((4, 2, half, width), BF16),
    ]
    small = [
        ((count, 1), F32),
        ((count, 1), F32),
        ((half, width), F32),
        ((half, width), BF16),
        ((half, 1), F32),
        ((2, half, 128), F32),
        ((half, width), BF16),
        ((16, rec), F32),
    ]
    scratch = saved[:3] + saved[4:12] + [((count + 16, width), BF16), ((16, width), BF16)]
    scratch += [((count, rec), F32), ((count, rec), F32), ((2, half, width), F32)]
    scratch += [((half, width), BF16), ((half, width), BF16), (gates.shape, BF16), ((half, 128), F32), ((3, 4, 2, rec), F32), ((count, 2), F32)]
    scratch += [((rows, 2 * rec), BF16), ((rows, 2 * w_mlp.shape[2]), BF16)]
    return pl.pallas_call(
        rec_forward_kernel,
        out_shape=[sds(*one) for one in saved + small],
        in_specs=[VM] * 16 + [ANY],
        out_specs=[HBM] * len(saved) + [VM] * len(small),
        scratch_shapes=[pltpu.VMEM(*one) for one in scratch]
        + [
            DMA((2,)),
            DMA,
            DMA((13,)),
            DMA((6,)),
            DMA((3, 3)),
            DMA((3, 3)),
            DMA((11, 3, 2, 3)),
            DMA((11, 3, 2, 3)),
            DMA((1, 3, 3)),
            DMA((1, 3, 3)),
            DMA((4,)),
            DMA((2, 2)),
            DMA((2, 2)),
            DMA((5,)),
            DMA((5,)),
        ],
        compiler_params=params(cid, 60),
    )(tokens, gain_rec[None], gain_mlp[None], *vectors, *masks, w_rec, back, w_mlp, down, cotangent, gates)


G_BIAS, G_LAM, G_CONV_W, G_CONV_B, G_H, G_STATE = 0, 2, 3, 7, 8, 9
GATE_ROWS = 48


def shard_rows(ref, i, value):
    value = value.reshape(2, 4, 32, value.shape[1])
    ref[i // 2, pl.ds(2 * lax.rem(i, 2), 2)] = value


def rec_back_kernel(
    gh_ref, branch_ref, normed_ref, gate_ref, states_ref, f_ref, v_ref, hidden_ref,
    wb_hbm, ext_hbm, mixed_hbm, reset_hbm, input_hbm, g_hbm, wg_hbm, opart_hbm,
    small_ref, part_ref, low, result_ref, dw_out_hbm, dw_gate_hbm, gg_hbm,
    wb, ext, mixed_v, reset_v, input_v, g_v, wg, opart, gate_low, cb, al, gm, dw_out, dw_gate, gg,
    tail, edge, edge_in, slots, result_half,
    *refs,
):
    load_sem, save_sem, small_send, small_recv, edge_sem, core_sem = refs[:6]
    sum_refs = refs[6:]
    count, rec = gate_ref.shape
    half = count // 2
    width = gh_ref.shape[1]
    blocks = rec // BLOCK
    pairs = (
        (wb_hbm, wb), (ext_hbm, ext), (mixed_hbm, mixed_v), (reset_hbm, reset_v), (input_hbm, input_v), (g_hbm, g_v),
        (wg_hbm, wg), (opart_hbm, opart),
    )
    loads = [pltpu.make_async_copy(src, dst, load_sem.at[k]) for k, (src, dst) in enumerate(pairs)]
    for load in loads:
        load.start()
    saves = []

    def save(src, dst):
        copy = pltpu.make_async_copy(src, dst, save_sem.at[len(saves)])
        copy.start()
        saves.append(copy)

    ahead, behind = along_seq(1), along_seq(-1)
    other = {"mp": 1 - lax.axis_index("mp")}
    greet(axis_peers() + [ahead, behind, other])
    place = lax.axis_index("z") * 16 + lax.axis_index("y") * 4 + lax.axis_index("x")
    is_first = jnp.where(place == 0, 1.0, 0.0)
    has_next = jnp.where(place == 63, 0.0, 1.0)

    def weight_grad(ref, left, right):
        def step(i, carry):
            cols = pl.ds(pl.multiple_of(i * 256, 256), 256)
            shard_rows(ref, i, outer(left[:, cols], right[...]).astype(BF16))
            return carry

        loop(0, left.shape[1] // 256, step, 1)

    loads[0].wait()

    def branch_step(n, carry):
        grad = dot(gh_ref[...], wb[:, lanes(n)])
        act, slope = gelu_parts(gate_ref[:, lanes(n)])
        gate_low[:, lanes(n)] = (slope * (grad * states_ref[8:, lanes(n)])).astype(BF16)
        al[:, lanes(n)] = grad * act
        return carry

    loop(0, blocks, branch_step, 1)
    loads[7].wait()
    sums = RingSum(opart, *sum_refs)
    sums.across(FAR, UP, DOWN, ME)

    def group(i, carry):
        base = pl.multiple_of(count - 8 - i * 8, 8)
        f, d = f_ref[pl.ds(base, 8)], al[pl.ds(base, 8)]
        follow, cf, cd = carry
        cfs, cds = [None] * 8, [None] * 8
        for r in (7, 6, 5, 4, 3, 2, 1, 0):
            cf = cf * follow
            cd = cd * follow + d[r : r + 1]
            cfs[r], cds[r] = cf, cd
            follow = f[r : r + 1]
        cb[pl.ds(base, 8)] = jnp.concatenate(cfs, axis=0)
        al[pl.ds(base, 8)] = jnp.concatenate(cds, axis=0)
        return follow, cf, cd

    zero = jnp.zeros((1, rec), F32)
    follow, cf, cd = lax.fori_loop(0, count // 8, group, (zero + 1.0, zero + 1.0, zero))
    prefix = Prefix(slots, small_send, small_recv)
    prefix.start((follow * cf, follow * cd), True)
    weight_grad(dw_out, gh_ref, branch_ref)
    save(dw_out, dw_out_hbm)
    prefix.step()
    sums.far()
    weight_grad(dw_gate, normed_ref, gate_low)
    save(dw_gate, dw_gate_hbm)
    prefix.step()
    for load in loads[1:7]:
        load.wait()

    def part_tile(i, carry):
        at = pl.ds(pl.multiple_of(i * 256, 256), 256)
        value = dot_t(gate_low[...], wg[at, :])
        part_ref[0, :, at] = value[:half]
        part_ref[1, :, at] = value[half:]
        return carry

    lax.fori_loop(0, width // 256, part_tile, 0)
    later = prefix.step()[1]
    sums.near()
    al[...] = al[...] + cb[...] * later

    def grads_step(n, carry):
        at = lanes(n)
        adjoint = al[:, at]
        factors, reset, gated = f_ref[:, at], reset_v[:, at], input_v[:, at]
        mixed_low = mixed_v[:, at]
        mixed = mixed_low.astype(F32)
        rates = v_ref[RATES : RATES + 1, at]
        log_decay = -8.0 * rates * reset
        decays = jnp.exp(log_decay)
        scale_in = jnp.sqrt(minus_expm1(2.0 * log_decay))
        grad_log = adjoint * states_ref[pl.ds(7, count), at] * factors
        grad_log = grad_log - adjoint * gated * mixed * decays * decays / scale_in
        small_ref[G_LAM : G_LAM + 1, at] = (
            8.0 * jnp.sum(grad_log * reset, axis=0, keepdims=True) * v_ref[SLOPE : SLOPE + 1, at]
        )
        small_ref[G_H : G_H + 1, at] = is_first * factors[0:1] * adjoint[0:1]
        grad_reset = (grad_log * (-8.0 * rates) * reset * (1.0 - reset)).astype(BF16)
        grad_input = (adjoint * scale_in * mixed * gated * (1.0 - gated)).astype(BF16)
        for g, grad in enumerate((grad_reset, grad_input)):
            small_ref[G_BIAS + g : G_BIAS + g + 1, at] = jnp.sum(
                grad.astype(F32), axis=0, keepdims=True
            )
            b = g * blocks + n
            rows = pl.ds(pl.multiple_of(16 * lax.rem(b, 3), 16), 16)
            gg[:, :, b // 3, rows, :] = outer(mixed_low, grad).astype(BF16).reshape(4, 4, 16, BLOCK)
        grad_mixed = adjoint * scale_in * gated
        grad_mixed = grad_mixed + dot_t(grad_reset, g_v[0, n]) + dot_t(grad_input, g_v[1, n])
        gm[0:8] = jnp.zeros((8, BLOCK), F32)
        gm[8 : 8 + count] = grad_mixed
        gm[8 + count :] = jnp.zeros((8, BLOCK), F32)
        small_ref[G_CONV_B : G_CONV_B + 1, at] = jnp.sum(grad_mixed, axis=0, keepdims=True)
        total = jnp.zeros((count, BLOCK), F32)
        front = jnp.zeros((8, BLOCK), F32)
        for k in range(CONV):
            small_ref[G_CONV_W + k : G_CONV_W + k + 1, at] = jnp.sum(
                grad_mixed * ext[pl.ds(16 - EDGE + k, count), at], axis=0, keepdims=True
            )
            weight = v_ref[CONV_W + k : CONV_W + k + 1, at]
            total = total + weight * gm[pl.ds(8 + EDGE - k, count)]
            front = front + weight * gm[pl.ds(8 - k, 8)]
        low[:, at] = total.astype(BF16)
        tail[:, at] = total[count - 16 :]
        edge[:, at] = front
        small_ref[G_STATE : G_STATE + EDGE, at] = is_first * front[:EDGE]
        small_ref[G_STATE + EDGE :, at] = jnp.zeros((16 - G_STATE - EDGE, BLOCK), F32)
        return carry

    for x, j in ((3, 1), (3, 2)):
        gg[:, :, x, 16 * j : 16 * j + 16, :] = jnp.zeros((4, 4, 16, BLOCK), BF16)
    loop(0, blocks, grads_step, 1)
    edge_copy = push(edge, edge_in, edge_sem.at[0], edge_sem.at[1], behind)
    edge_copy.start()
    save(gg, gg_hbm)
    core = lax.axis_index("mp")
    result_half[...] = (hidden_ref[...] + sums.total()).astype(BF16)
    result_ref[core] = result_half[...]
    result_copy = push(result_half, result_ref.at[core], core_sem.at[0], core_sem.at[1], other)
    result_copy.start()
    edge_copy.wait_recv()
    last = jnp.concatenate([tail[0:13], tail[13:16] + has_next * edge_in[0:EDGE]], axis=0)
    low[count - 16 :] = last.astype(BF16)
    result_copy.wait()
    for copy in saves:
        copy.wait()
    sums.drain()
    prefix.drain()
    edge_copy.wait_send()


def rec_back(
    gh, branch, normed, gate_lin, states_ext, factors, vectors, hidden,
    w_back, ext, mixed, reset, gated, gates, w_gate, mlp_part, cid,
):
    count, rec = gate_lin.shape
    half, width = hidden.shape

    def like(array):
        return pltpu.VMEM(array.shape, array.dtype)

    wide, low = pltpu.VMEM((count, rec), F32), pltpu.VMEM((count, rec), BF16)
    cube, gate_cube = (4, 4, 4, width // 64, rec), (4, 4, 4, GATE_ROWS, BLOCK)
    return pl.pallas_call(
        rec_back_kernel,
        out_shape=[
            jax.ShapeDtypeStruct((16, rec), F32),
            jax.ShapeDtypeStruct((2, half, width), F32),
            jax.ShapeDtypeStruct((count, rec), BF16),
            jax.ShapeDtypeStruct((2, half, width), BF16),
            jax.ShapeDtypeStruct(cube, BF16),
            jax.ShapeDtypeStruct(cube, BF16),
            jax.ShapeDtypeStruct(gate_cube, BF16),
        ],
        in_specs=[VM] * 8 + [ANY] * 8,
        out_specs=[VM] * 4 + [HBM] * 3,
        scratch_shapes=[
            like(w_back), like(ext), like(mixed), like(reset), like(gated), like(gates), like(w_gate), like(mlp_part),
            low, wide, wide, pltpu.VMEM((count + 16, BLOCK), F32),
            pltpu.VMEM(cube, BF16), pltpu.VMEM(cube, BF16), pltpu.VMEM(gate_cube, BF16),
            pltpu.VMEM((16, rec), F32), pltpu.VMEM((8, rec), F32), pltpu.VMEM((8, rec), F32),
            pltpu.VMEM((3, 4, 2, rec), F32), pltpu.VMEM((half, width), BF16),
            DMA((8,)),
            DMA((3,)),
            DMA((1, 3, 3)),
            DMA((1, 3, 3)),
            DMA((2,)),
            DMA((2,)),
        ]
        + ring_sum_scratch(half, width),
        compiler_params=params(cid, 61),
    )(
        gh, branch, normed, gate_lin, states_ext, factors, vectors, hidden,
        w_back, ext, mixed, reset, gated, gates, w_gate, mlp_part,
    )


def rec_end_kernel(
    part_in_ref, small_ref, gain_term_ref, gh_ref, tokens_in, inverse_ref, gain_ref, normed_ref, low_ref,
    dw0, dw1, gg_hbm, wl_hbm,
    total_ref, gains_ref, all_gates_ref, out0, out1, out2, tokens_hbm,
    *refs,
):
    bufs, refs = refs[: 78 + 3 * 6], refs[78 + 3 * 6 :]
    (
        part, dw2, wl, gates_out, part_low, part_in, tokens_v, gates_ref, ring_gains, gains0, small0, small1, small2,
        load_sem, own_sem, send, recv, gsend, grecv, small_send, small_recv, ring_send, ring_recv, core_sem,
    ) = refs
    half, width = gh_ref.shape
    load = pltpu.make_async_copy(wl_hbm, wl, load_sem.at[0])
    load.start()
    core = lax.axis_index("mp")
    other = {"mp": 1 - core}
    x_here = lax.axis_index("x")
    greet(axis_peers() + [other] + [{"x": peer, "mp": 1 - core} for peer in ring("x")[1:]])
    small = [
        Total(slots, small_send, small_recv, e, ORDERS[e])
        for e, slots in enumerate((small0, small1, small2))
    ]
    for flow, (start, wide) in zip(small, CHUNKS):
        flow.start(small_ref[:, start : start + wide])
    gates = [
        Scatter(
            9 + e, gg_hbm, (0, BLOCK), ORDERS[e], None, bufs[78 + 6 * e : 84 + 6 * e], gates_out,
            own_sem, send, recv, BANDS[e],
        )
        for e in range(3)
    ]
    flows = [
        Scatter(
            e, (dw0, dw1, dw2)[e // 3], CHUNKS[e % 3], SUM_ORDERS[e // 3][e % 3], ROW_HALVES,
            bufs[9 * e : 9 * e + 9] if e < 6 else bufs[8 * e + 6 : 8 * e + 14], (out0, out1, out2)[e // 3],
            own_sem, send, recv, rings=2 if e < 6 else 1,
        )
        for e in range(9)
    ]
    one, two, three = flows[:3], flows[3:6], flows[6:]
    spread = [Gather(e, gates_ref, ORDERS[e], (0, BLOCK), gsend, grecv, band=BANDS[e]) for e in range(3)]

    def each(group, name, *args):
        for flow in group:
            getattr(flow, name)(*args)

    each(gates, "begin", 0)
    each(one, "begin", 0)
    each(two, "begin", 0)

    def weight_grad(i, carry):
        cols = pl.ds(pl.multiple_of(i * 256, 256), 256)
        shard_rows(dw2, i, outer(normed_ref[:, cols], low_ref[...]).astype(BF16))
        return carry

    lax.fori_loop(0, width // 256, weight_grad, 0)
    each(three, "begin", 0)
    each(gates, "finish")
    each(gates, "begin", 1)
    for flow in small:
        flow.step()
    load.wait()

    def part_tile(i, carry):
        at = pl.ds(pl.multiple_of(i * 256, 256), 256)
        value = dot_t(low_ref[...], wl[at, :])
        part[0, :, at] = part_in_ref[0, :, at] + value[:half]
        part[1, :, at] = part_in_ref[1, :, at] + value[half:]
        return carry

    lax.fori_loop(0, width // 256, part_tile, 0)
    part_low[...] = part[1 - core].astype(BF16)
    part_copy = push(part_low, part_in, core_sem.at[0], core_sem.at[1], other)
    part_copy.start()
    each(one, "middle")
    part_copy.wait_recv()
    grad_normed = part[core] + part_in[...].astype(F32)
    mine = pl.ds(pl.multiple_of(core * half, half), half)
    inverse = inverse_ref[mine]
    hat = tokens_in[mine].astype(F32) * inverse
    gain_term = jnp.sum(grad_normed * hat, axis=0, keepdims=True)
    quarter = width // 4
    for k in range(4):
        cols = slice(k * quarter, (k + 1) * quarter)
        ring_gains[x_here, core, k : k + 1] = gain_term[:, cols]
        ring_gains[x_here, core, 4 + k : 5 + k] = gain_term_ref[:, cols]
    shares = []
    spot = ring_gains.at[x_here, core]
    group = [{"x": x, "mp": c} for x in ring("x") for c in (core, 1 - core)][1:]
    for k, peer in enumerate(group):
        copy = push(spot, spot, ring_send.at[k], ring_recv.at[k], peer)
        copy.start()
        shares.append(copy)
    grad_hat = grad_normed * gain_ref[...]
    inner = jnp.mean(grad_hat * hat, axis=-1, keepdims=True)
    tokens_v[...] = gh_ref[...] + inverse * (grad_hat - hat * inner)
    token_copy = push(tokens_v, tokens_hbm.at[core], core_sem.at[2], core_sem.at[3], other)
    token_copy.start()
    token_save = pltpu.make_async_copy(tokens_v, tokens_hbm.at[core], load_sem.at[1])
    token_save.start()
    each(two, "middle")
    each(gates, "finish")
    each(gates, "begin", 2)
    for flow in small:
        flow.step()
    each(one, "finish")
    each(one, "begin", 1)
    for copy in shares:
        copy.wait_recv()
    gains = Total(gains0, small_send, small_recv, 3, ("y", "z"))
    halves = [ring_gains[x, 0] + ring_gains[x, 1] for x in range(4)]
    gains.start((halves[0] + halves[1]) + (halves[2] + halves[3]))
    each(three, "middle")
    each(gates, "finish")
    gates_ref[lax.axis_index("z"), lax.axis_index("y"), x_here] = gates_out[...].astype(BF16)
    each(spread, "begin", 0)
    for flow, (start, wide) in zip(small, CHUNKS):
        total_ref[:, start : start + wide] = flow.step()
    each(two, "finish")
    each(two, "begin", 1)
    gains.step()
    each(one, "middle")
    each(spread, "finish")
    each(spread, "begin", 1)
    each(three, "finish")
    each(three, "begin", 1)
    each(two, "middle")
    each(one, "finish")
    each(one, "begin", 2)
    gains_ref[...] = gains.step()
    each(spread, "finish")
    each(spread, "begin", 2)
    each(two, "finish")
    each(two, "begin", 2)
    each(one, "finish")
    each(three, "finish")
    each(three, "begin", 2)
    each(two, "finish")
    each(spread, "finish")

    def unpack(b, carry):
        at = pl.ds(pl.multiple_of(16 * lax.rem(b, 3), 16), 16)
        all_gates_ref[b] = gates_ref[:, :, b // 3, at, :].reshape(BLOCK, BLOCK).astype(F32)
        return carry

    lax.fori_loop(0, all_gates_ref.shape[0], unpack, 0)
    each(three, "finish")
    for copy in (token_copy, token_save):
        copy.wait()
    each(flows + gates + spread + small, "drain")
    gains.drain()
    for copy in shares + [part_copy]:
        copy.wait_send()


def rec_end(part, small, gain_term, grad_hidden, tokens, inverse, gain, normed, low, weights, gates, w_lin, cid):
    half, width = grad_hidden.shape
    rows, rec = weights[0].shape[3:]
    gate_blocks = 2 * rec // BLOCK

    def sds(*shape):
        return jax.ShapeDtypeStruct(shape, F32)

    bufs = []
    for e in range(9):
        bufs += scatter_buffers(rows, CHUNKS[e % 3][1], 2 if e < 6 else 1)
    for _ in range(3):
        bufs += scatter_buffers(GATE_ROWS // 3, BLOCK, 0)
    return pl.pallas_call(
        rec_end_kernel,
        out_shape=[
            sds(16, rec),
            sds(8, width // 4),
            sds(gate_blocks, BLOCK, BLOCK),
            sds(rows, rec),
            sds(rows, rec),
            sds(rows, rec),
            sds(2, half, width),
        ],
        in_specs=[VM] * 9 + [ANY] * 4,
        out_specs=[VM] * 6 + [HBM],
        scratch_shapes=bufs
        + [
            pltpu.VMEM(part.shape, F32),
            pltpu.VMEM(weights[0].shape, BF16),
            pltpu.VMEM(w_lin.shape, BF16),
            pltpu.VMEM((GATE_ROWS, BLOCK), F32),
            pltpu.VMEM((half, width), BF16),
            pltpu.VMEM((half, width), BF16),
            pltpu.VMEM((half, width), F32),
            pltpu.VMEM(gates.shape, BF16),
            pltpu.VMEM((4, 2, 8, width // 4), F32),
            pltpu.VMEM((2, 4, 8, width // 4), F32),
        ]
        + [pltpu.VMEM((3, 4, 16, wide), F32) for _, wide in CHUNKS]
        + [
            DMA((2,)),
            DMA((12, 3)),
            DMA((12, 3, 3, 3)),
            DMA((12, 3, 3, 3)),
            DMA((3, 3, 1, 3)),
            DMA((3, 3, 1, 3)),
            DMA((4, 3, 3)),
            DMA((4, 3, 3)),
            DMA((7,)),
            DMA((7,)),
            DMA((4,)),
        ],
        compiler_params=params(cid, 60),
    )(part, small, gain_term, grad_hidden, tokens, inverse, gain, normed, low, *weights, gates, w_lin)


def mlp_end_kernel(in_ref, back, send, recv):
    x_here = lax.axis_index("x")
    peers = ring("x")[1:]
    greet([{"x": peer} for peer in peers])
    moves = []
    for step, peer in enumerate(peers):
        copy = push(in_ref.at[peer], back.at[x_here], send.at[step], recv.at[step], {"x": peer})
        copy.start()
        moves.append(copy)
    back[x_here] = in_ref[x_here]
    for copy in moves:
        copy.wait()


def mlp_end(quarters, cid):
    return pl.pallas_call(
        mlp_end_kernel,
        out_shape=jax.ShapeDtypeStruct(quarters.shape, quarters.dtype),
        in_specs=[VM],
        out_specs=VM,
        scratch_shapes=[DMA((3,)), DMA((3,))],
        compiler_params=params(cid, 61),
    )(quarters)


def finish_kernel(
    small_hbm, gains_hbm, out_hbm, gate_hbm, lin_hbm, back_hbm, rms_hbm, rms_mlp_hbm, result_in, tokens_in, gates_in,
    result_ref, tokens_ref, gates_ref, rec_ref, out_ref, mlp_ref, down_ref, bias_ref, lam_ref, conv_w_ref, conv_b_ref,
    gain_rec_ref, gain_mlp_ref, h_ref, state_ref, rms_ref, rms_mlp_ref,
    small_ref, gains_ref, out_sums, gate_sums, lin_sums, back, rms_v, rms_mlp_v, result_v, tokens_v, gates_v, sem, out_sem,
):
    pairs = (
        (result_in, result_v), (tokens_in, tokens_v), (gates_in, gates_v),
        (small_hbm, small_ref), (gains_hbm, gains_ref), (out_hbm, out_sums), (gate_hbm, gate_sums),
        (lin_hbm, lin_sums), (back_hbm, back), (rms_hbm, rms_v), (rms_mlp_hbm, rms_mlp_v),
    )
    loads = [pltpu.make_async_copy(src, dst, sem.at[k]) for k, (src, dst) in enumerate(pairs)]
    for load in loads:
        load.start()
    copies = []
    for k, (src, dst) in enumerate(((result_v, result_ref), (tokens_v, tokens_ref), (gates_v, gates_ref))):
        loads[k].wait()
        copies.append(pltpu.make_async_copy(src, dst, out_sem.at[k]))
        copies[k].start()
    for load in loads[3:]:
        load.wait()
    rec_ref[:, 0, :] = gate_sums[...]
    rec_ref[:, 1, :] = lin_sums[...]
    out_ref[...] = out_sums[...]
    units = down_ref.shape[1] // 4
    for q in range(4):
        value = back[q].astype(F32)
        at = pl.ds(q * units, units)
        for k in range(2):
            mlp_ref[:, k, at] = value[:, k * units : (k + 1) * units]
        down_ref[:, at] = value[:, 2 * units :]
    bias_ref[...] = small_ref[G_BIAS : G_BIAS + 2]
    lam_ref[...] = small_ref[G_LAM]
    conv_w_ref[...] = small_ref[G_CONV_W : G_CONV_W + CONV]
    conv_b_ref[...] = small_ref[G_CONV_B]
    h_ref[...] = small_ref[G_H]
    state_ref[...] = small_ref[G_STATE : G_STATE + EDGE]
    quarter = gains_ref.shape[1]
    for k in range(4):
        at = pl.ds(k * quarter, quarter)
        gain_rec_ref[at] = gains_ref[k]
        gain_mlp_ref[at] = gains_ref[4 + k]
    half = rms_mlp_v.shape[1]
    square = (half, half)
    diagonal = lax.broadcasted_iota(jnp.int32, square, 0) == lax.broadcasted_iota(jnp.int32, square, 1)
    for core in range(2):
        at = pl.ds(core * half, half)
        for ref, column in ((rms_ref, rms_v[at, 0:1]), (rms_mlp_ref, rms_mlp_v[core, :, 0:1])):
            spread = jnp.where(diagonal, jnp.broadcast_to(column, square), 0.0)
            ref[at] = jnp.sum(spread, axis=0)
    for copy in copies:
        copy.wait()


def finish(small, gains, sums, back, rms, rms_mlp, result, tokens, gates):
    rec = small.shape[1]
    rows = back.shape[1]
    units = back.shape[2] // 3
    width = gains.size // 2

    def sds(*shape):
        return jax.ShapeDtypeStruct(shape, F32)

    return pl.pallas_call(
        finish_kernel,
        out_shape=[
            jax.ShapeDtypeStruct(result.shape, result.dtype),
            sds(*tokens.shape),
            sds(*gates.shape),
            sds(rows, 2, rec),
            sds(rows, rec),
            sds(rows, 2, 4 * units),
            sds(rows, 4 * units),
            sds(2, rec),
            sds(rec),
            sds(CONV, rec),
            sds(rec),
            sds(width),
            sds(width),
            sds(rec),
            sds(EDGE, rec),
            sds(rms.shape[0]),
            sds(rms.shape[0]),
        ],
        in_specs=[HBM] * 11,
        out_specs=[HBM] * 3 + [VM] * 14,
        scratch_shapes=[pltpu.VMEM(a.shape, a.dtype) for a in (small, gains, *sums, back, rms, rms_mlp, result, tokens, gates)]
        + [DMA((11,)), DMA((3,))],
        compiler_params=pltpu.CompilerParams(vmem_limit_bytes=61 * MIB),
    )(small, gains, *sums, back, rms, rms_mlp, result, tokens, gates)


def body(
    tokens,
    cotangent,
    starts,
    valid,
    w_rec,
    w_out,
    w_mlp,
    w_down,
    lru_gates,
    lru_bias,
    lam,
    conv_w,
    conv_b,
    gain_rec,
    gain_mlp,
    h_init,
    conv_state,
):
    count, width = tokens.shape
    shard, _, rec = w_rec.shape
    hidden_units = w_mlp.shape[2] // 4
    half = count // 2
    core = lax.axis_index("mp")

    (
        w_lin, w_gate, w_back, mlp_weights, ext, gate_lin, mixed, reset, gated, factors, states_ext, branch_in,
        normed_rec, grad_out_all, inverse_rec, rms_rec, hidden, normed_mlp, inverse_mlp, rms_half, grad_out, vectors,
    ) = rec_forward(
        tokens,
        gain_rec,
        gain_mlp,
        (conv_w, conv_b, lam, lru_bias, conv_state, h_init),
        (starts, valid),
        w_rec,
        w_out.T,
        w_mlp,
        w_down.T,
        cotangent,
        lru_gates,
        0,
    )
    w_lin, w_gate, w_back = (w.reshape(width, rec) for w in (w_lin, w_gate, w_back))
    grad_hidden, grad_hidden_low, gain_mlp_term, mlp_terms, mlp_part = mlp(
        normed_mlp, grad_out, hidden, inverse_mlp, gain_mlp[None], grad_out_all, mlp_weights, 1
    )
    mlp_sums = lax.psum_scatter(mlp_terms, ("z", "y"), scatter_dimension=0, tiled=True)
    grad_hidden_low = grad_hidden_low.reshape(count, width)
    small, normed_part, grad_rec_low, result, *weight_terms, gate_terms = rec_back(
        grad_hidden_low,
        branch_in,
        normed_rec,
        gate_lin,
        states_ext,
        factors,
        vectors,
        hidden,
        w_back,
        ext,
        mixed,
        reset,
        gated,
        lru_gates,
        w_gate,
        mlp_part,
        2,
    )
    small, gains, gate_blocks, out_sums, gate_sums, lin_sums, grad_tokens = rec_end(
        normed_part,
        small,
        gain_mlp_term,
        grad_hidden,
        tokens,
        inverse_rec,
        gain_rec[None],
        normed_rec,
        grad_rec_low,
        weight_terms,
        gate_terms,
        w_lin,
        3,
    )
    back = mlp_end(mlp_sums.reshape(4, shard, 3 * hidden_units), 4)
    (
        result, grad_tokens, grad_gates, grad_w_rec, grad_out_t, grad_w_mlp, grad_down_t, grad_bias, grad_lam,
        grad_conv_w, conv_bias_gradient, grad_gain_rec, grad_gain_mlp, grad_h_init, grad_conv_state, rms_rec, rms_mlp,
    ) = finish(
        small,
        gains,
        (out_sums, gate_sums, lin_sums),
        back,
        rms_rec,
        rms_half,
        result.reshape(count, width),
        grad_tokens.reshape(count, width),
        gate_blocks.reshape(lru_gates.shape),
    )
    return (
        result,
        rms_rec,
        rms_mlp,
        grad_tokens,
        grad_w_rec,
        grad_out_t.T,
        grad_w_mlp,
        grad_down_t.T,
        grad_gates,
        grad_bias,
        grad_lam,
        grad_conv_w,
        conv_bias_gradient,
        grad_gain_rec,
        grad_gain_mlp,
        grad_h_init,
        grad_conv_state,
    )


def solution(mesh):
    cube = Mesh(mesh.devices.reshape(4, 4, 4, 2), ("z", "y", "x", "mp"))
    placed = (
        P(SEQ, None),
        P(SEQ, None),
        P(SEQ),
        P(SEQ),
        P(SEQ, None, "mp"),
        P("mp", SEQ),
        P(SEQ, None, "mp"),
        P("mp", SEQ),
        P(None, "mp", None, None),
        P(None, "mp"),
        P("mp"),
        P(None, "mp"),
        P("mp"),
        P(),
        P(),
        P("mp"),
        P(None, "mp"),
    )
    return jax.shard_map(
        body,
        mesh=cube,
        in_specs=placed,
        out_specs=(
            P(SEQ, None),
            P(SEQ),
            P(SEQ),
            P(SEQ, None),
            P(SEQ, None, "mp"),
            P("mp", SEQ),
            P(SEQ, None, "mp"),
            P("mp", SEQ),
            P(None, "mp", None, None),
            P(None, "mp"),
            P("mp"),
            P(None, "mp"),
            P("mp"),
            P(),
            P(),
            P("mp"),
            P(None, "mp"),
        ),
        check_vma=False,
    )
```

```python
import functools
import jax
import jax.numpy as jnp
from jax import lax
from jax.experimental import pallas as pl
from jax.experimental.pallas import tpu as pltpu
from jax.sharding import Mesh, PartitionSpec as P

CONV = 4
EDGE = CONV - 1
BLOCK = 256
EPSILON = 1e-06
MESH = pl.DeviceIdType.MESH
ANY = pl.BlockSpec(memory_space=pl.ANY)
HBM = pl.BlockSpec(memory_space=pltpu.HBM)
VM = pl.BlockSpec(memory_space=pltpu.VMEM)
MIB = 1024 * 1024
AXES = ("z", "y", "x")
SEQ = ("z", "y", "x")
ORDERS = (("x", "y", "z"), ("y", "z", "x"), ("z", "x", "y"))
F32, BF16 = jnp.float32, jnp.bfloat16
GELU_C, GELU_A = 0.7978845608028654, 0.044715
DMA = pltpu.SemaphoreType.DMA


def loop(lower, upper, step, batch):
    main = lower + (upper - lower) // batch * batch

    def several(k, carry):
        for i in range(batch):
            step(lower + k * batch + i, 0)
        return carry

    if main > lower:
        lax.fori_loop(0, (main - lower) // batch, several, 0)
    for i in range(main, upper):
        step(i, 0)


def dot(left, right):
    return jnp.dot(left, right, preferred_element_type=F32)


def dot_t(left, right):
    return lax.dot_general(left, right, (((1,), (1,)), ((), ())), preferred_element_type=F32)


def outer(left, right):
    return lax.dot_general(left, right, (((0,), (0,)), ((), ())), preferred_element_type=F32)


def greet(peers):
    sem = pltpu.get_barrier_semaphore()
    for peer in peers:
        pl.semaphore_signal(sem, inc=1, device_id=peer, device_id_type=MESH)
    pl.semaphore_wait(sem, len(peers))


def push(src, dst, send, recv, peer):
    return pltpu.make_async_remote_copy(
        src_ref=src, dst_ref=dst, send_sem=send, recv_sem=recv, device_id=peer, device_id_type=MESH
    )


def ring(axis):
    me = lax.axis_index(axis)
    return me, lax.rem(me + 1, 4), lax.rem(me + 2, 4), lax.rem(me + 3, 4)


def all_neighbours():
    peers = []
    for axis in AXES:
        _, up, _, down = ring(axis)
        peers += [{axis: up}, {axis: down}]
    return peers


def params(cid, mib):
    return pltpu.CompilerParams(
        collective_id=cid, has_side_effects=True, vmem_limit_bytes=mib * MIB
    )


def part_of(done, axis, index, rows, cols):
    spot = []
    for name in AXES:
        if name in done:
            spot.append(pl.ds(0, 4))
        elif name == axis:
            spot.append(index)
        else:
            spot.append(lax.axis_index(name))
    return tuple(spot) + (rows, cols)


def pick(names, axis, index, others):
    spot, rest = [], iter(others)
    for name in names:
        spot.append(index if name == axis else next(rest))
    return tuple(spot)


class Scatter:
    def __init__(self, entry, src, cols, order, halves, bufs, out, own_sem, send, recv, band=None, rings=1):
        self.rings = 0 if halves is None else rings
        self.band, self.band_rows = band, src.shape[-2] if band is None else band[1]
        self.entry, self.src, self.order = entry, src, order
        self.start, self.width = cols
        self.halves, self.bufs, self.out = halves, list(bufs), out
        self.own_sem, self.send, self.recv = own_sem, send, recv
        self.left, self.sent = AXES, []

    def view(self, at, rows=None):
        if rows is None:
            first = self.band[0] if self.band is not None and self.phase == 0 else 0
            rows = pl.ds(first, self.band_rows)
        return at + (rows, pl.ds(self.start if self.phase == 0 else 0, self.width))

    def spread(self, i):
        return ((i // 4, lax.rem(i, 4)), (i,), ())[self.phase]

    def copy(self, src, dst, way, kind, peer):
        at = (self.entry, self.phase, way, kind)
        copy = push(src, dst, self.send.at[at], self.recv.at[at], {self.axis: peer})
        copy.start()
        self.sent.append(copy)
        return copy

    def load(self, index, dst, rows=None):
        src = self.src.at[self.view(pick(self.left, self.axis, index, self.full), rows)]
        copy = pltpu.make_async_copy(src, dst, self.own_sem.at[self.entry, len(self.loads)])
        copy.start()
        self.loads.append(copy)

    def begin(self, phase):
        self.phase, self.axis = phase, self.order[phase]
        self.full = (pl.ds(0, 4),) * (2 - phase)
        me, up, far, down = ring(self.axis)
        self.first, self.second, self.loads = [], [], []
        self.two_step = phase < self.rings
        if self.two_step:
            self.ones, self.twos = self.bufs.pop(0), self.bufs.pop(0)
            self.near = self.bufs.pop(0) if phase == 0 else None
            for way, peer in enumerate((up, down)):
                half = self.halves[way]
                src = self.src.at[self.view(pick(self.left, self.axis, far, self.full), half)]
                self.first.append(self.copy(src, self.ones.at[way], way, 0, peer))
            for way, peer in enumerate((up, down)):
                half = self.halves[1 - way]
                src = self.src.at[self.view(pick(self.left, self.axis, peer, self.full), half)]
                dst = self.twos.at[(way,) + self.full + (half,)]
                self.second.append(self.copy(src, dst, way, 1, peer))
            for way, peer in enumerate((up, down)):
                if phase == 0:
                    self.load(peer, self.near.at[way], self.halves[way])
        else:
            self.threes = self.bufs.pop(0)
            for step, peer in enumerate((up, far, down)):
                src = self.src.at[self.view(pick(self.left, self.axis, peer, self.full))]
                self.second.append(self.copy(src, self.threes.at[step], step, 0, peer))
        if phase == 0:
            self.own = self.bufs.pop(0)
            self.load(me, self.own)
        self.acc = self.bufs.pop(0) if phase < 2 else self.out

    def middle(self):
        _, up, _, down = ring(self.axis)
        for way, peer in enumerate((up, down)):
            self.first[way].wait_recv()
            if self.phase == 0:
                self.loads[way].wait()

            def add(i, carry, way=way, peer=peer):
                there = (way,) + self.spread(i)
                if self.phase == 0:
                    own = self.near[there]
                else:
                    at = pick(self.left, self.axis, peer, self.spread(i))
                    own = self.src[self.view(at, self.halves[way])]
                total = self.ones[there].astype(F32) + own.astype(F32)
                self.ones[there] = total.astype(BF16)
                return carry

            lax.fori_loop(0, 4 ** (2 - self.phase), add, 0)
            dst = self.twos.at[(way,) + self.full + (self.halves[way],)]
            self.second.append(self.copy(self.ones.at[way], dst, way, 2, peer))

    def finish(self):
        me = lax.axis_index(self.axis)
        for copy in self.second:
            copy.wait_recv()
        if self.phase == 0:
            self.loads[-1].wait()
        buf, slots = (self.twos, (0, 1)) if self.two_step else (self.threes, (0, 1, 2))

        def total(i, carry):
            there = self.spread(i)
            if self.phase == 0:
                whole = self.own[there].astype(F32)
            else:
                whole = self.src[self.view(pick(self.left, self.axis, me, there))].astype(F32)
            for slot in slots:
                whole = whole + buf[(slot,) + there].astype(F32)
            if self.phase < 2:
                self.acc[there] = whole.astype(self.acc.dtype)
            else:
                first = 0 if self.band is None else self.band[0]
                self.acc[pl.ds(first, self.band_rows), pl.ds(self.start, self.width)] = whole
            return carry

        lax.fori_loop(0, 4 ** (2 - self.phase), total, 0)
        self.src = self.acc
        self.left = tuple(name for name in self.left if name != self.axis)

    def drain(self):
        for copy in self.sent:
            copy.wait_send()


def scatter_buffers(rows, width, rings):
    bufs = []
    for phase in range(3):
        cube = (4,) * (2 - phase)
        if phase < rings:
            bufs.append(pltpu.VMEM((2,) + cube + (rows // 2, width), BF16))
            bufs.append(pltpu.VMEM((2,) + cube + (rows, width), BF16))
            if phase == 0:
                bufs.append(pltpu.VMEM((2,) + cube + (rows // 2, width), BF16))
        else:
            bufs.append(pltpu.VMEM((3,) + cube + (rows, width), BF16))
        if phase == 0:
            bufs.append(pltpu.VMEM(cube + (rows, width), BF16))
        if phase < 2:
            bufs.append(pltpu.VMEM(cube + (rows, width), BF16))
    return bufs


class Gather:
    def __init__(self, entry, out, order, cols, send, recv, done=(), ring_rounds=(), band=None):
        self.band = (0, out.shape[3]) if band is None else band
        self.entry, self.out, self.order, self.cols = entry, out, order, pl.ds(*cols)
        self.send, self.recv, self.sent = send, recv, []
        self.done, self.ring_rounds = done, ring_rounds

    def spot(self, origin, rows=None):
        rows = pl.ds(*self.band) if rows is None else rows
        return self.out.at[part_of(self.done, self.axis, origin, rows, self.cols)]

    def copy(self, src, dst, step, way, peer):
        at = (self.entry, self.phase, step, way)
        copy = push(src, dst, self.send.at[at], self.recv.at[at], {self.axis: peer})
        copy.start()
        self.sent.append(copy)
        return copy

    def begin(self, phase, src=None):
        self.phase, self.axis = phase, self.order[phase]
        me, up, far, down = ring(self.axis)
        here = self.spot(me)
        src = here if src is None else src.at[:, self.cols]
        peers = (up, down) if phase in self.ring_rounds else (up, far, down)
        self.copies = [self.copy(src, here, 0, way, peer) for way, peer in enumerate(peers)]

    def middle(self):
        _, up, _, down = ring(self.axis)
        half = self.out.shape[3] // 2
        first, self.copies = self.copies, []
        for way, (peer, origin) in enumerate(((up, down), (down, up))):
            first[way].wait_recv()
            spot = self.spot(origin, pl.ds(way * half, half))
            self.copies.append(self.copy(spot, spot, 1, way, peer))

    def hold(self):
        for copy in self.copies:
            copy.wait_recv()

    def finish(self):
        self.hold()
        self.done = self.done + (self.axis,)

    def drain(self):
        for copy in self.sent:
            copy.wait_send()


class Rounds:
    def __init__(self, slots, send, recv, entry=0, order=("x", "y", "z")):
        self.slots, self.send, self.recv, self.sent = slots, send, recv, []
        self.entry, self.order = entry, order

    def begin(self, phase, rows):
        self.phase, axis = phase, self.order[phase]
        me = lax.axis_index(axis)
        for at, value in rows:
            self.slots[phase, me, at] = value
        self.copies = []
        for step, peer in enumerate(ring(axis)[1:]):
            spot = self.slots.at[phase, me]
            at = (self.entry, phase, step)
            copy = push(spot, spot, self.send.at[at], self.recv.at[at], {axis: peer})
            copy.start()
            self.copies.append(copy)

    def finish(self):
        for copy in self.copies:
            copy.wait_recv()
        self.sent += self.copies

    def drain(self):
        for copy in self.sent:
            copy.wait_send()


class Prefix(Rounds):
    def start(self, pair, backward):
        self.backward, self.cur, self.head = backward, pair, None
        self.share(0)

    def share(self, phase):
        self.begin(phase, [(slice(0, 1), self.cur[0]), (slice(1, 2), self.cur[1])])

    def step(self):
        self.finish()
        me = lax.axis_index(self.order[self.phase])
        run = (jnp.ones_like(self.cur[0]), jnp.zeros_like(self.cur[1]))
        mine = run
        for j in (3, 2, 1, 0) if self.backward else (0, 1, 2, 3):
            take = me == j
            mine = (jnp.where(take, run[0], mine[0]), jnp.where(take, run[1], mine[1]))
            fac, val = self.slots[self.phase, j, 0:1], self.slots[self.phase, j, 1:2]
            run = (run[0] * fac, val + fac * run[1])
        self.cur = run
        if self.head is None:
            self.head = mine
        else:
            self.head = (mine[0] * self.head[0], self.head[1] + self.head[0] * mine[1])
        if self.phase < 2:
            self.share(self.phase + 1)
        return self.head


class Total(Rounds):
    def start(self, value):
        self.begin(0, [(slice(None), value)])

    def step(self):
        self.finish()
        at = self.slots
        k = self.phase
        value = (at[k, 0] + at[k, 1]) + (at[k, 2] + at[k, 3])
        if k + 1 < len(self.order):
            self.begin(k + 1, [(slice(None), value)])
        return value


def axis_peers():
    return [{axis: ring(axis)[step]} for axis in AXES for step in (1, 2, 3)]


def along_seq(distance):
    place = lax.axis_index("z") * 16 + lax.axis_index("y") * 4 + lax.axis_index("x")
    place = lax.rem(place + distance + 64, 64)
    return {"z": place // 16, "y": lax.rem(place // 4, 4), "x": lax.rem(place, 4)}


CHUNKS = ((0, 384), (384, 512), (896, 384))
SUM_ORDERS = (
    (("y", "z", "x"), ("x", "y", "z"), ("z", "y", "x")),
    (("z", "x", "y"), ("x", "z", "y"), ("y", "x", "z")),
    (("y", "z", "x"), ("x", "y", "z"), ("z", "x", "y")),
)
ROW_HALVES = (pl.ds(0, 16), pl.ds(16, 16))
BANDS = ((0, 16), (16, 16), (32, 16))


def gelu_parts(x):
    inner = GELU_C * (x + GELU_A * x * x * x)
    t = jnp.tanh(inner)
    slope = GELU_C * (1.0 + 3.0 * GELU_A * x * x)
    return 0.5 * x * (1.0 + t), 0.5 * (1.0 + t) + 0.5 * x * (1.0 - t * t) * slope


FAR, UP, DOWN, ME = 0, 1, 2, 3


class RingSum:
    def __init__(self, part, got, one, two, send, recv, sib_send, sib_recv):
        self.part, self.got, self.one, self.two = part, got, one, two
        self.send, self.recv, self.sib_send, self.sib_recv = send, recv, sib_send, sib_recv
        self.core, self.sums, self.sent = lax.axis_index("mp"), {}, []

    def across(self, *slots):
        for slot in slots:
            copy = push(
                self.part.at[slot, 1 - self.core],
                self.got.at[slot],
                self.sib_send.at[slot],
                self.sib_recv.at[slot],
                {"mp": 1 - self.core},
            )
            copy.start()
            self.sums[slot] = copy

    def add(self, dst, src):
        dst[...] = (dst[...].astype(F32) + src[...].astype(F32)).astype(dst.dtype)

    def collect(self, slot):
        self.sums[slot].wait_recv()
        self.add(self.got.at[slot], self.part.at[slot, self.core])

    def far(self):
        self.collect(FAR)
        half = self.one.shape[1]
        _, up, _, down = ring("x")
        self.first = []
        for way, peer in enumerate((up, down)):
            piece = self.got.at[FAR, pl.ds(way * half, half)]
            at = (0, way)
            copy = push(piece, self.one.at[way], self.send.at[at], self.recv.at[at], {"x": peer})
            copy.start()
            self.first.append(copy)

    def near(self):
        half = self.one.shape[1]
        _, up, _, down = ring("x")
        self.second = []
        for way, (peer, slot) in enumerate(((up, UP), (down, DOWN))):
            self.collect(slot)
            self.first[way].wait_recv()
            self.add(self.got.at[slot, pl.ds(way * half, half)], self.one.at[way])
            at = (1, way)
            copy = push(self.got.at[slot], self.two.at[way], self.send.at[at], self.recv.at[at], {"x": peer})
            copy.start()
            self.second.append(copy)

    def total(self):
        self.sums[ME].wait_recv()
        total = self.got[ME].astype(F32) + self.part[ME, self.core].astype(F32)
        for way in range(2):
            self.second[way].wait_recv()
            total = total + self.two[way].astype(F32)
        return total

    def drain(self):
        for copy in self.first + self.second + list(self.sums.values()):
            copy.wait_send()


def ring_sum_scratch(rows, width):
    return [
        pltpu.VMEM((4, rows, width), BF16),
        pltpu.VMEM((2, rows // 2, width), BF16),
        pltpu.VMEM((2, rows, width), BF16),
        DMA((2, 2)),
        DMA((2, 2)),
        DMA((4,)),
        DMA((4,)),
    ]


def mlp_kernel(
    nm_ref, go_ref, hidden_ref, inv_ref, gain_ref, go_hbm, w_hbm,
    grad_hidden_ref, low_ref, term_ref, dw_ref, opart_out,
    go, w, gathered, npart, opart, mlp_in, ggu, gmi, low_half,
    load_sem, wsend, wrecv, gsend, grecv, gsib_send, gsib_recv, core_sem, *sum_refs,
):
    rows, width = nm_ref.shape
    half = rows // 2
    units = mlp_in.shape[1]
    me, up, far, down = ring("x")
    core = lax.axis_index("mp")
    other = {"mp": 1 - core}
    loads = [pltpu.make_async_copy(nm_ref, gathered.at[ME, core], load_sem.at[0])]
    wide = w.shape[4] // 2
    full, every = pl.ds(0, 4), pl.ds(0, w.shape[3])
    last = (("z", 0), ("y", wide))

    def weight_set(axis, index, at, cols):
        return ((index, full) if axis == "z" else (full, index)) + (full, at, pl.ds(cols, wide))

    for e, (axis, cols) in enumerate(last):
        here, ahead, _, behind = ring(axis)
        for k, index in enumerate((here, ahead, behind)):
            spot = weight_set(axis, index, every, cols)
            loads.append(pltpu.make_async_copy(w_hbm.at[spot], w.at[spot], load_sem.at[1 + 3 * e + k]))
    for slot, chip in ((FAR, far), (UP, up), (DOWN, down), (ME, me)):
        at = pl.ds(slot * 2 * rows, 2 * rows)
        loads.append(pltpu.make_async_copy(go_hbm.at[chip], go.at[at], load_sem.at[7 + slot]))
    for load in loads:
        load.start()
    peers = [{"x": up}, {"x": down}, other]
    for axis in ("y", "z"):
        peers += [{axis: ring(axis)[1]}, {axis: ring(axis)[3]}]
    greet(peers)
    top, low = pl.ds(0, half), pl.ds(half, half)
    first = []
    for way, (peer, slot) in enumerate(((up, DOWN), (down, UP))):
        spot = gathered.at[slot, core]
        copy = push(nm_ref, spot, gsend.at[0, way], grecv.at[0, way], {"x": peer})
        copy.start()
        first.append(copy)
    across = [push(nm_ref, gathered.at[ME, core], gsib_send.at[0], gsib_recv.at[0], other)]
    across[0].start()
    rest = []
    for e, (axis, cols) in enumerate(last):
        _, ahead, _, behind = ring(axis)
        deep = w.shape[3] // 2
        for way, (peer, origin) in enumerate(((ahead, behind), (behind, ahead))):
            spot = weight_set(axis, origin, pl.ds(way * deep, deep), cols)
            copy = push(w_hbm.at[spot], w.at[spot], wsend.at[e, way], wrecv.at[e, way], {axis: peer})
            copy.start()
            rest.append(copy)
    second = []
    for way, (peer, slot, piece) in enumerate(((up, DOWN, top), (down, UP, low))):
        first[way].wait_recv()
        spot = gathered.at[slot, core]
        copy = push(
            spot.at[piece], gathered.at[FAR, core, piece], gsend.at[1, way], grecv.at[1, way], {"x": peer}
        )
        copy.start()
        second.append(copy)
        copy = push(spot, spot, gsib_send.at[1 + way], gsib_recv.at[1 + way], other)
        copy.start()
        across.append(copy)
    for copy in rest:
        copy.wait_recv()
    for load in loads:
        load.wait()

    def tile(j, start=0):
        return pl.ds(pl.multiple_of(start + j * 256, 256), 256)

    def columns(at):
        return w[:, :, :, :, at].reshape(width, 256)

    def shard_tile(i, at):
        return w[i // 2, pl.ds(2 * lax.rem(i, 2), 2), :, :, at].reshape(256, -1)

    def grad_tile(j, carry):
        gmi[:, tile(j)] = dot(go[...], columns(tile(j, 2 * units)))
        return carry

    loop(0, units // 256, grad_tile, 1)
    for way, piece in enumerate((top, low)):
        second[way].wait_recv()
        spot = gathered.at[FAR, core, piece]
        copy = push(spot, spot, gsib_send.at[3 + way], gsib_recv.at[3 + way], other)
        copy.start()
        across.append(copy)

    def tokens_step(slot):
        at = pl.ds(slot * 2 * rows, 4 * rows)

        def hidden_tile(j, carry):
            tokens_in = gathered[slot : slot + 2].reshape(4 * rows, width)
            gate = dot(tokens_in, columns(tile(j)))
            up_lin = dot(tokens_in, columns(tile(j, units)))
            grad = gmi[at, tile(j)]
            act, slope = gelu_parts(gate)
            mlp_in[at, tile(j)] = (act * up_lin).astype(BF16)
            ggu[at, tile(j)] = (slope * (grad * up_lin)).astype(BF16)
            ggu[at, tile(j, units)] = (grad * act).astype(BF16)
            return carry

        loop(0, units // 256, hidden_tile, 1)

        def back_tile(j, carry):
            back = dot_t(ggu[at], shard_tile(j, pl.ds(0, 2 * units)))
            npart[slot : slot + 2, :, :, tile(j)] = back.astype(BF16).reshape(2, 2, rows, 256)
            return carry

        loop(0, width // 256, back_tile, 1)

    def out_tile(j, carry):
        part = dot_t(mlp_in[...], shard_tile(j, pl.ds(2 * units, units)))
        opart[:, :, :, tile(j)] = part.astype(BF16).reshape(4, 2, rows, 256)
        return carry

    def weight_grads(lower, upper):
        def step(i, carry):
            left = gathered[:, :, :, tile(i)].reshape(8 * rows, 256)
            dw_ref[tile(i), pl.ds(0, 2 * units)] = outer(left, ggu[...]).astype(BF16)
            dw_ref[tile(i), pl.ds(2 * units, units)] = outer(go[:, tile(i)], mlp_in[...]).astype(BF16)
            return carry

        loop(lower, upper, step, 2)

    sums = RingSum(npart, *sum_refs)
    for copy in across:
        copy.wait_recv()
    tokens_step(FAR)
    sums.across(FAR, UP)
    sums.far()
    tokens_step(DOWN)
    sums.across(DOWN, ME)
    sums.near()
    loop(0, width // 256, out_tile, 1)
    save = pltpu.make_async_copy(opart, opart_out, load_sem.at[11])
    save.start()
    weight_grads(0, 5)
    grad_normed = sums.total()
    hat = hidden_ref[...] * inv_ref[...]
    grad_hat = grad_normed * gain_ref[...]
    inner = jnp.mean(grad_hat * hat, axis=-1, keepdims=True)
    grad_hidden = go_ref[...].astype(F32) + inv_ref[...] * (grad_hat - hat * inner)
    grad_hidden_ref[...] = grad_hidden
    term_ref[...] = jnp.sum(grad_normed * hat, axis=0, keepdims=True)
    low_half[...] = grad_hidden.astype(BF16)
    low_ref[core] = low_half[...]
    swap = push(low_half, low_ref.at[core], core_sem.at[0], core_sem.at[1], other)
    swap.start()
    weight_grads(5, 8)
    swap.wait()
    save.wait()
    sums.drain()
    for copy in first + second + across + rest:
        copy.wait_send()


def mlp(normed, grad_out, hidden, inverse, gain, grad_out_all, weights, cid):
    rows, width = normed.shape
    units = weights.shape[4] // 3

    def block(dtype, *shape):
        return pltpu.VMEM(shape, dtype)

    return pl.pallas_call(
        mlp_kernel,
        out_shape=[
            jax.ShapeDtypeStruct((rows, width), F32),
            jax.ShapeDtypeStruct((2, rows, width), BF16),
            jax.ShapeDtypeStruct((1, width), F32),
            jax.ShapeDtypeStruct((width, 3 * units), BF16),
            jax.ShapeDtypeStruct((4, 2, rows, width), BF16),
        ],
        in_specs=[VM] * 5 + [ANY] * 2,
        out_specs=[VM] * 4 + [HBM],
        scratch_shapes=[
            block(BF16, 8 * rows, width),
            block(BF16, *weights.shape),
            block(BF16, 4, 2, rows, width),
            block(BF16, 4, 2, rows, width),
            block(BF16, 4, 2, rows, width),
            block(BF16, 8 * rows, units),
            block(BF16, 8 * rows, 2 * units),
            block(F32, 8 * rows, units),
            block(BF16, rows, width),
        ]
        + [DMA((12,)), DMA((2, 2)), DMA((2, 2)), DMA((2, 2)), DMA((2, 2)), DMA((5,)), DMA((5,)), DMA((2,))]
        + ring_sum_scratch(rows, width),
        compiler_params=params(cid, 60),
    )(normed, grad_out, hidden, inverse, gain, grad_out_all.reshape(4, 2 * rows, width), weights)


def lanes(n):
    return pl.ds(pl.multiple_of(n * BLOCK, BLOCK), BLOCK)


def minus_expm1(x):
    series = jnp.ones_like(x)
    for k in (9, 8, 7, 6, 5, 4, 3, 2):
        series = 1.0 + x * (1.0 / k) * series
    return jnp.where(x > -0.4, -x * series, 1.0 - jnp.exp(x))


def log1p(x):
    series = jnp.zeros_like(x)
    for k in (7, 6, 5, 4, 3, 2, 1):
        series = 1.0 / k - x * series
    return jnp.where(x < 0.05, x * series, jnp.log(1.0 + x))


CONV_W, CONV_B, RATES, BIAS, CONV_STATE, H_INIT, SLOPE = 0, 4, 5, 6, 8, 11, 12


def rec_forward_kernel(*refs):
    (
        tokens_ref, gain_ref, gain_mlp_ref, conv_w_ref, conv_b_ref, lam_ref, bias_ref, conv_state_ref,
        h_init_ref, starts_ref, valid_ref, rec_raw, back_in, mlp_raw, down_in, cot_ref, g_hbm,
        lin_out, gate_out, back_out, mlp_out, ext_out, act_out, mixed_out, reset_out, input_out, f_out, states_out,
        branch_out, normed_out, go_all, inv_ref, rms_ref, hidden_ref, nm_ref, inv_mlp_ref, rms_mlp_ref, go_ref, v_ref,
        wl, wg, wb, ext, gate_lin, mixed_v, reset_v, input_v, f_v, states, branch_v, normed, tail_in, driven, cf_v,
        part, part_low, part_in, g_v, rms_v, slots, mask_ref, rec_in, mlp_in,
        tail_sem, load_sem, save_sem, own_sem, move_send, move_recv, send, recv, small_send, small_recv, core_sem,
        go_send, go_recv, go_sib_send, go_sib_recv,
    ) = refs
    count, width = tokens_ref.shape
    rec = f_v.shape[1]
    for k in range(2):
        rec_in[:, k * rec : (k + 1) * rec] = rec_raw[:, k, :]
        mlp_in[:, k * mlp_raw.shape[2] : (k + 1) * mlp_raw.shape[2]] = mlp_raw[:, k, :]
    gate_in, lin_in = rec_in.at[:, pl.ds(0, rec)], rec_in.at[:, pl.ds(rec, rec)]
    blocks = rec // BLOCK
    half = count // 2
    core = lax.axis_index("mp")
    other = {"mp": 1 - core}
    here = tuple(lax.axis_index(name) for name in AXES)
    load = pltpu.make_async_copy(g_hbm, g_v, load_sem)
    load.start()
    owns = [
        pltpu.make_async_copy(lin_in, wl.at[here], own_sem.at[0]),
        pltpu.make_async_copy(gate_in, wg.at[here], own_sem.at[1]),
        pltpu.make_async_copy(back_in, wb.at[here], own_sem.at[2]),
    ]
    units = mlp_out.shape[4] // 3
    every = pl.ds(0, rec_in.shape[0])

    def quarter(k, chip):
        if k == 2:
            return down_in.at[every, pl.ds(pl.multiple_of(chip * units, units), units)]
        return mlp_in.at[every, pl.ds(pl.multiple_of((4 * k + chip) * units, units), units)]

    spots = [mlp_out.at[here + (every, pl.ds(k * units, units))] for k in range(3)]
    owns += [pltpu.make_async_copy(quarter(k, here[2]), spots[k], own_sem.at[3 + k]) for k in range(3)]
    for own in owns:
        own.start()
    greet(axis_peers() + [other, along_seq(1), along_seq(-1)])
    tail_copy = push(tokens_ref.at[pl.ds(count - 16, 16)], tail_in, tail_sem.at[0], tail_sem.at[1], along_seq(1))
    tail_copy.start()
    lin = [Gather(e, wl, ORDERS[e], CHUNKS[e], send, recv, ring_rounds=(2,)) for e in range(3)]
    gate = [
        Gather(3 + e, wg, ORDERS[(e + 1) % 3], CHUNKS[e], send, recv, ring_rounds=(1, 2)) for e in range(3)
    ]
    back = [
        Gather(6 + e, wb, ORDERS[(2, 1, 0)[e]], CHUNKS[e], send, recv, ring_rounds=(1, 2)) for e in range(3)
    ]
    rest = gate + back
    wide = mlp_out.shape[4] // 2
    mlp_flows = [
        Gather(9 + e, mlp_out, order, (e * wide, wide), send, recv, done=("x",), ring_rounds=(1,))
        for e, order in enumerate((("y", "z"), ("z", "y")))
    ]

    def each(group, name, *args):
        for flow in group:
            getattr(flow, name)(*args)

    each(lin, "begin", 0, lin_in)
    moves = []
    for step, peer in enumerate(ring("x")[1:]):
        for k in range(3):
            copy = push(quarter(k, peer), spots[k], move_send.at[step, k], move_recv.at[step, k], {"x": peer})
            copy.start()
            moves.append(copy)
    each(gate, "begin", 0, gate_in)
    each(back, "begin", 0, back_in)

    v_ref[CONV_W : CONV_W + CONV] = conv_w_ref[...]
    v_ref[BIAS : BIAS + 2] = bias_ref[...]
    v_ref[CONV_STATE : CONV_STATE + EDGE] = conv_state_ref[...]
    for at, ref in ((CONV_B, conv_b_ref), (H_INIT, h_init_ref)):
        v_ref[at : at + 1] = ref[...].reshape(1, rec)
    lam = lam_ref[...].reshape(1, rec)
    v_ref[RATES : RATES + 1] = jnp.maximum(-lam, 0.0) + log1p(jnp.exp(-jnp.abs(lam)))
    v_ref[SLOPE : SLOPE + 1] = 1.0 / (1.0 + jnp.exp(lam))
    v_ref[SLOPE + 1 :] = jnp.zeros((15 - SLOPE, rec), F32)
    square = (count, count)
    diagonal = lax.broadcasted_iota(jnp.int32, square, 0) == lax.broadcasted_iota(jnp.int32, square, 1)
    for k, row in enumerate((1.0 - starts_ref[...].astype(F32), valid_ref[...].astype(F32))):
        spread = jnp.where(diagonal, jnp.broadcast_to(row.reshape(1, count), square), 0.0)
        mask_ref[:, k : k + 1] = jnp.sum(spread, axis=1, keepdims=True)

    def norm(values):
        mean_sq = jnp.mean(values * values, axis=-1, keepdims=True)
        inverse = lax.rsqrt(mean_sq + EPSILON)
        return values * inverse, inverse, jnp.sqrt(mean_sq + EPSILON)

    def norm_step(i, carry):
        at = pl.ds(pl.multiple_of(i * 64, 64), 64)
        hat, inverse, rms = norm(tokens_ref[at].astype(F32))
        inv_ref[at] = inverse
        rms_ref[at] = rms
        normed[pl.ds(pl.multiple_of(16 + i * 64, 16), 64)] = (hat * gain_ref[...]).astype(BF16)
        return carry

    lax.fori_loop(0, count // 64, norm_step, 0)
    for own in owns:
        own.wait()
    each(lin, "finish")
    each(lin, "begin", 1)
    each(rest, "finish")
    each(rest, "begin", 1)
    tail_copy.wait_recv()
    normed[0:16] = (norm(tail_in[...].astype(F32))[0] * gain_ref[...]).astype(BF16)
    saves = []

    def save(src, dst):
        copy = pltpu.make_async_copy(src, dst, save_sem.at[len(saves)])
        copy.start()
        saves.append(copy)

    save(normed.at[pl.ds(16, count)], normed_out)
    each(lin, "finish")
    each(lin, "begin", 2)
    for copy in moves:
        copy.wait_recv()
    each(mlp_flows, "begin", 0)
    each(rest, "middle")
    each(lin, "middle")
    each(rest, "finish")
    each(rest, "begin", 2)
    mine = pl.ds(pl.multiple_of(core * half, half), half)
    go_ref[...] = (cot_ref[mine].astype(F32) * mask_ref[mine, 1:2]).astype(BF16)
    load.wait()
    each(lin, "finish")
    save(wl, lin_out)
    is_first = (here[0] + here[1] + here[2]) == 0

    def rec_step(n, carry):
        at = lanes(n)
        ext[:, at] = dot(normed[...], wl[:, :, :, :, at].reshape(width, BLOCK))

        @pl.when(is_first)
        def _():
            ext[16 - EDGE : 16, at] = v_ref[CONV_STATE : CONV_STATE + EDGE, at]

        total = v_ref[CONV_B : CONV_B + 1, at] + jnp.zeros((count, BLOCK), F32)
        for k in range(CONV):
            total = total + v_ref[CONV_W + k : CONV_W + k + 1, at] * ext[pl.ds(16 - EDGE + k, count), at]
        mixed = total.astype(BF16)
        mixed_v[:, at] = mixed
        reset = jax.nn.sigmoid(dot(mixed, g_v[0, n]) + v_ref[BIAS : BIAS + 1, at])
        gated = jax.nn.sigmoid(dot(mixed, g_v[1, n]) + v_ref[BIAS + 1 : BIAS + 2, at])
        reset_v[:, at] = reset
        input_v[:, at] = gated
        log_decay = -8.0 * v_ref[RATES : RATES + 1, at] * reset
        f_v[:, at] = jnp.exp(log_decay) * mask_ref[:, 0:1]
        driven[:, at] = jnp.sqrt(minus_expm1(2.0 * log_decay)) * gated * mixed.astype(F32)
        return carry

    lax.fori_loop(0, blocks, rec_step, 0)
    for src, dst in ((ext, ext_out), (mixed_v, mixed_out), (reset_v, reset_out), (input_v, input_out), (f_v, f_out)):
        save(src, dst)

    def group(i, carry):
        base = pl.multiple_of(i * 8, 8)
        f, d = f_v[pl.ds(base, 8)], driven[pl.ds(base, 8)]
        cf, cd = carry
        cfs, cds = [], []
        for r in range(8):
            cf = cf * f[r : r + 1]
            cd = cd * f[r : r + 1] + d[r : r + 1]
            cfs.append(cf)
            cds.append(cd)
        cf_v[pl.ds(base, 8)] = jnp.concatenate(cfs, axis=0)
        states[pl.ds(pl.multiple_of(base + 8, 8), 8)] = jnp.concatenate(cds, axis=0)
        return cf, cd

    zero = jnp.zeros((1, rec), F32)
    ends = lax.fori_loop(0, count // 8, group, (zero + 1.0, zero))
    prefix = Prefix(slots, small_send, small_recv)
    prefix.start(ends, False)
    by_axis = {axis: [flow for flow in rest if flow.axis == axis] for axis in AXES}
    each(by_axis["x"], "middle")
    prefix.step()
    each(by_axis["y"], "middle")
    each(mlp_flows, "finish")
    mlp_flows[1].begin(1)
    prefix.step()
    each(by_axis["z"], "middle")
    mlp_flows[0].begin(1)
    x_here, x_up, x_far, x_down = ring("x")
    spot = go_all.at[x_here, core]
    save(go_ref, spot)
    go_first = []
    for way, peer in enumerate((x_up, x_down)):
        copy = push(go_ref, spot, go_send.at[0, way], go_recv.at[0, way], {"x": peer})
        copy.start()
        go_first.append(copy)
    go_across = [push(go_ref, spot, go_sib_send.at[0], go_sib_recv.at[0], other)]
    go_across[0].start()
    head = prefix.step()
    carry_in = head[1] + head[0] * v_ref[H_INIT : H_INIT + 1]
    each(gate, "finish")
    save(wg, gate_out)

    def gate_step(n, carry):
        gate_lin[:, lanes(n)] = dot(normed[16:], wg[:, :, :, :, lanes(n)].reshape(width, BLOCK))
        return carry

    lax.fori_loop(0, blocks, gate_step, 0)
    save(gate_lin, act_out)
    states[0:8] = jnp.broadcast_to(carry_in, (8, rec))

    def branch_step(n, carry):
        at = lanes(n)
        value = states[8:, at] + cf_v[:, at] * states[0:1, at]
        states[8:, at] = value
        branch_v[:, at] = (gelu_parts(gate_lin[:, at])[0] * value).astype(BF16)
        return carry

    lax.fori_loop(0, blocks, branch_step, 0)
    save(states, states_out)
    save(branch_v, branch_out)
    each(back, "finish")
    save(wb, back_out)

    def out_step(i, carry):
        at = pl.ds(pl.multiple_of(i * 256, 256), 256)
        rows = wb[i // 2, pl.ds(2 * lax.rem(i, 2), 2)].reshape(256, rec)
        value = dot_t(branch_v[...], rows)
        part[0, :, at] = value[:half]
        part[1, :, at] = value[half:]
        return carry

    lax.fori_loop(0, width // 256, out_step, 0)
    part_low[...] = part[1 - core].astype(BF16)
    part_copy = push(part_low, part_in, core_sem.at[0], core_sem.at[1], other)
    part_copy.start()
    go_second = []
    for way, (peer, origin) in enumerate(((x_up, x_down), (x_down, x_up))):
        go_first[way].wait_recv()
        spot = go_all.at[origin, core]
        piece = spot.at[pl.ds(way * (half // 2), half // 2)]
        copy = push(piece, piece, go_send.at[1, way], go_recv.at[1, way], {"x": peer})
        copy.start()
        go_second.append(copy)
        copy = push(spot, spot, go_sib_send.at[1 + way], go_sib_recv.at[1 + way], other)
        copy.start()
        go_across.append(copy)
    part_copy.wait_recv()
    hidden = tokens_ref[mine].astype(F32) + (part[core] + part_in[...].astype(F32))
    hidden_ref[...] = hidden
    hat, inverse, rms = norm(hidden)
    inv_mlp_ref[...] = inverse
    rms_v[...] = jnp.broadcast_to(rms, (half, 128))
    rms_mlp_ref[core] = rms_v[...]
    rms_copy = push(rms_v, rms_mlp_ref.at[core], core_sem.at[2], core_sem.at[3], other)
    rms_copy.start()
    nm_ref[...] = (hat * gain_mlp_ref[...]).astype(BF16)
    for way in range(2):
        go_second[way].wait_recv()
        piece = go_all.at[x_far, core, pl.ds(way * (half // 2), half // 2)]
        copy = push(piece, piece, go_sib_send.at[3 + way], go_sib_recv.at[3 + way], other)
        copy.start()
        go_across.append(copy)
    each(mlp_flows, "hold")
    rms_copy.wait()
    for copy in go_across:
        copy.wait()
    for copy in go_first + go_second:
        copy.wait_send()
    for copy in moves:
        copy.wait_send()
    for copy in saves:
        copy.wait()
    each(lin, "drain")
    each(rest, "drain")
    each(mlp_flows, "drain")
    prefix.drain()
    part_copy.wait_send()
    tail_copy.wait_send()


def rec_forward(tokens, gain_rec, gain_mlp, vectors, masks, w_rec, back, w_mlp, down, cotangent, gates, cid):
    count, width = tokens.shape
    rows, rec = back.shape
    half = count // 2

    def cube(last):
        return (4, 4, 4, rows, last)

    def sds(shape, dtype):
        return jax.ShapeDtypeStruct(shape, dtype)

    saved = [
        (cube(rec), BF16),
        (cube(rec), BF16),
        (cube(rec), BF16),
        (cube(3 * down.shape[1] // 4), BF16),
        ((count + 16, rec), F32),
        ((count, rec), F32),
        ((count, rec), BF16),
        ((count, rec), F32),
        ((count, rec), F32),
        ((count, rec), F32),
        ((count + 8, rec), F32),
        ((count, rec), BF16),
        ((count, width), BF16),
        ((4, 2, half, width), BF16),
    ]
    small = [
        ((count, 1), F32),
        ((count, 1), F32),
        ((half, width), F32),
        ((half, width), BF16),
        ((half, 1), F32),
        ((2, half, 128), F32),
        ((half, width), BF16),
        ((16, rec), F32),
    ]
    scratch = saved[:3] + saved[4:12] + [((count + 16, width), BF16), ((16, width), BF16)]
    scratch += [((count, rec), F32), ((count, rec), F32), ((2, half, width), F32)]
    scratch += [((half, width), BF16), ((half, width), BF16), (gates.shape, BF16), ((half, 128), F32), ((3, 4, 2, rec), F32), ((count, 2), F32)]
    scratch += [((rows, 2 * rec), BF16), ((rows, 2 * w_mlp.shape[2]), BF16)]
    return pl.pallas_call(
        rec_forward_kernel,
        out_shape=[sds(*one) for one in saved + small],
        in_specs=[VM] * 16 + [ANY],
        out_specs=[HBM] * len(saved) + [VM] * len(small),
        scratch_shapes=[pltpu.VMEM(*one) for one in scratch]
        + [
            DMA((2,)),
            DMA,
            DMA((13,)),
            DMA((6,)),
            DMA((3, 3)),
            DMA((3, 3)),
            DMA((11, 3, 2, 3)),
            DMA((11, 3, 2, 3)),
            DMA((1, 3, 3)),
            DMA((1, 3, 3)),
            DMA((4,)),
            DMA((2, 2)),
            DMA((2, 2)),
            DMA((5,)),
            DMA((5,)),
        ],
        compiler_params=params(cid, 60),
    )(tokens, gain_rec[None], gain_mlp[None], *vectors, *masks, w_rec, back, w_mlp, down, cotangent, gates)


G_BIAS, G_LAM, G_CONV_W, G_CONV_B, G_H, G_STATE = 0, 2, 3, 7, 8, 9
GATE_ROWS = 48


def shard_rows(ref, i, value):
    value = value.reshape(2, 4, 32, value.shape[1])
    ref[i // 2, pl.ds(2 * lax.rem(i, 2), 2)] = value


def rec_back_kernel(
    gh_ref, branch_ref, normed_ref, gate_ref, states_ref, f_ref, v_ref, hidden_ref,
    wb_hbm, ext_hbm, mixed_hbm, reset_hbm, input_hbm, g_hbm, wg_hbm, opart_hbm,
    small_ref, part_ref, low, result_ref, dw_out_hbm, dw_gate_hbm, gg_hbm,
    wb, ext, mixed_v, reset_v, input_v, g_v, wg, opart, gate_low, cb, al, gm, dw_out, dw_gate, gg,
    tail, edge, edge_in, slots, result_half,
    *refs,
):
    load_sem, save_sem, small_send, small_recv, edge_sem, core_sem = refs[:6]
    sum_refs = refs[6:]
    count, rec = gate_ref.shape
    half = count // 2
    width = gh_ref.shape[1]
    blocks = rec // BLOCK
    pairs = (
        (wb_hbm, wb), (ext_hbm, ext), (mixed_hbm, mixed_v), (reset_hbm, reset_v), (input_hbm, input_v), (g_hbm, g_v),
        (wg_hbm, wg), (opart_hbm, opart),
    )
    loads = [pltpu.make_async_copy(src, dst, load_sem.at[k]) for k, (src, dst) in enumerate(pairs)]
    for load in loads:
        load.start()
    saves = []

    def save(src, dst):
        copy = pltpu.make_async_copy(src, dst, save_sem.at[len(saves)])
        copy.start()
        saves.append(copy)

    ahead, behind = along_seq(1), along_seq(-1)
    other = {"mp": 1 - lax.axis_index("mp")}
    greet(axis_peers() + [ahead, behind, other])
    place = lax.axis_index("z") * 16 + lax.axis_index("y") * 4 + lax.axis_index("x")
    is_first = jnp.where(place == 0, 1.0, 0.0)
    has_next = jnp.where(place == 63, 0.0, 1.0)

    def weight_grad(ref, left, right):
        def step(i, carry):
            cols = pl.ds(pl.multiple_of(i * 256, 256), 256)
            shard_rows(ref, i, outer(left[:, cols], right[...]).astype(BF16))
            return carry

        loop(0, left.shape[1] // 256, step, 1)

    loads[0].wait()

    def branch_step(n, carry):
        grad = dot(gh_ref[...], wb[:, lanes(n)])
        act, slope = gelu_parts(gate_ref[:, lanes(n)])
        gate_low[:, lanes(n)] = (slope * (grad * states_ref[8:, lanes(n)])).astype(BF16)
        al[:, lanes(n)] = grad * act
        return carry

    loop(0, blocks, branch_step, 1)
    loads[7].wait()
    sums = RingSum(opart, *sum_refs)
    sums.across(FAR, UP, DOWN, ME)

    def group(i, carry):
        base = pl.multiple_of(count - 8 - i * 8, 8)
        f, d = f_ref[pl.ds(base, 8)], al[pl.ds(base, 8)]
        follow, cf, cd = carry
        cfs, cds = [None] * 8, [None] * 8
        for r in (7, 6, 5, 4, 3, 2, 1, 0):
            cf = cf * follow
            cd = cd * follow + d[r : r + 1]
            cfs[r], cds[r] = cf, cd
            follow = f[r : r + 1]
        cb[pl.ds(base, 8)] = jnp.concatenate(cfs, axis=0)
        al[pl.ds(base, 8)] = jnp.concatenate(cds, axis=0)
        return follow, cf, cd

    zero = jnp.zeros((1, rec), F32)
    follow, cf, cd = lax.fori_loop(0, count // 8, group, (zero + 1.0, zero + 1.0, zero))
    prefix = Prefix(slots, small_send, small_recv)
    prefix.start((follow * cf, follow * cd), True)
    weight_grad(dw_out, gh_ref, branch_ref)
    save(dw_out, dw_out_hbm)
    prefix.step()
    sums.far()
    weight_grad(dw_gate, normed_ref, gate_low)
    save(dw_gate, dw_gate_hbm)
    prefix.step()
    for load in loads[1:7]:
        load.wait()

    def part_tile(i, carry):
        at = pl.ds(pl.multiple_of(i * 256, 256), 256)
        value = dot_t(gate_low[...], wg[at, :])
        part_ref[0, :, at] = value[:half]
        part_ref[1, :, at] = value[half:]
        return carry

    lax.fori_loop(0, width // 256, part_tile, 0)
    later = prefix.step()[1]
    sums.near()
    al[...] = al[...] + cb[...] * later

    def grads_step(n, carry):
        at = lanes(n)
        adjoint = al[:, at]
        factors, reset, gated = f_ref[:, at], reset_v[:, at], input_v[:, at]
        mixed_low = mixed_v[:, at]
        mixed = mixed_low.astype(F32)
        rates = v_ref[RATES : RATES + 1, at]
        log_decay = -8.0 * rates * reset
        decays = jnp.exp(log_decay)
        scale_in = jnp.sqrt(minus_expm1(2.0 * log_decay))
        grad_log = adjoint * states_ref[pl.ds(7, count), at] * factors
        grad_log = grad_log - adjoint * gated * mixed * decays * decays / scale_in
        small_ref[G_LAM : G_LAM + 1, at] = (
            8.0 * jnp.sum(grad_log * reset, axis=0, keepdims=True) * v_ref[SLOPE : SLOPE + 1, at]
        )
        small_ref[G_H : G_H + 1, at] = is_first * factors[0:1] * adjoint[0:1]
        grad_reset = (grad_log * (-8.0 * rates) * reset * (1.0 - reset)).astype(BF16)
        grad_input = (adjoint * scale_in * mixed * gated * (1.0 - gated)).astype(BF16)
        for g, grad in enumerate((grad_reset, grad_input)):
            small_ref[G_BIAS + g : G_BIAS + g + 1, at] = jnp.sum(
                grad.astype(F32), axis=0, keepdims=True
            )
            b = g * blocks + n
            rows = pl.ds(pl.multiple_of(16 * lax.rem(b, 3), 16), 16)
            gg[:, :, b // 3, rows, :] = outer(mixed_low, grad).astype(BF16).reshape(4, 4, 16, BLOCK)
        grad_mixed = adjoint * scale_in * gated
        grad_mixed = grad_mixed + dot_t(grad_reset, g_v[0, n]) + dot_t(grad_input, g_v[1, n])
        gm[0:8] = jnp.zeros((8, BLOCK), F32)
        gm[8 : 8 + count] = grad_mixed
        gm[8 + count :] = jnp.zeros((8, BLOCK), F32)
        small_ref[G_CONV_B : G_CONV_B + 1, at] = jnp.sum(grad_mixed, axis=0, keepdims=True)
        total = jnp.zeros((count, BLOCK), F32)
        front = jnp.zeros((8, BLOCK), F32)
        for k in range(CONV):
            small_ref[G_CONV_W + k : G_CONV_W + k + 1, at] = jnp.sum(
                grad_mixed * ext[pl.ds(16 - EDGE + k, count), at], axis=0, keepdims=True
            )
            weight = v_ref[CONV_W + k : CONV_W + k + 1, at]
            total = total + weight * gm[pl.ds(8 + EDGE - k, count)]
            front = front + weight * gm[pl.ds(8 - k, 8)]
        low[:, at] = total.astype(BF16)
        tail[:, at] = total[count - 16 :]
        edge[:, at] = front
        small_ref[G_STATE : G_STATE + EDGE, at] = is_first * front[:EDGE]
        small_ref[G_STATE + EDGE :, at] = jnp.zeros((16 - G_STATE - EDGE, BLOCK), F32)
        return carry

    for x, j in ((3, 1), (3, 2)):
        gg[:, :, x, 16 * j : 16 * j + 16, :] = jnp.zeros((4, 4, 16, BLOCK), BF16)
    loop(0, blocks, grads_step, 1)
    edge_copy = push(edge, edge_in, edge_sem.at[0], edge_sem.at[1], behind)
    edge_copy.start()
    save(gg, gg_hbm)
    core = lax.axis_index("mp")
    result_half[...] = (hidden_ref[...] + sums.total()).astype(BF16)
    result_ref[core] = result_half[...]
    result_copy = push(result_half, result_ref.at[core], core_sem.at[0], core_sem.at[1], other)
    result_copy.start()
    edge_copy.wait_recv()
    last = jnp.concatenate([tail[0:13], tail[13:16] + has_next * edge_in[0:EDGE]], axis=0)
    low[count - 16 :] = last.astype(BF16)
    result_copy.wait()
    for copy in saves:
        copy.wait()
    sums.drain()
    prefix.drain()
    edge_copy.wait_send()


def rec_back(
    gh, branch, normed, gate_lin, states_ext, factors, vectors, hidden,
    w_back, ext, mixed, reset, gated, gates, w_gate, mlp_part, cid,
):
    count, rec = gate_lin.shape
    half, width = hidden.shape

    def like(array):
        return pltpu.VMEM(array.shape, array.dtype)

    wide, low = pltpu.VMEM((count, rec), F32), pltpu.VMEM((count, rec), BF16)
    cube, gate_cube = (4, 4, 4, width // 64, rec), (4, 4, 4, GATE_ROWS, BLOCK)
    return pl.pallas_call(
        rec_back_kernel,
        out_shape=[
            jax.ShapeDtypeStruct((16, rec), F32),
            jax.ShapeDtypeStruct((2, half, width), F32),
            jax.ShapeDtypeStruct((count, rec), BF16),
            jax.ShapeDtypeStruct((2, half, width), BF16),
            jax.ShapeDtypeStruct(cube, BF16),
            jax.ShapeDtypeStruct(cube, BF16),
            jax.ShapeDtypeStruct(gate_cube, BF16),
        ],
        in_specs=[VM] * 8 + [ANY] * 8,
        out_specs=[VM] * 4 + [HBM] * 3,
        scratch_shapes=[
            like(w_back), like(ext), like(mixed), like(reset), like(gated), like(gates), like(w_gate), like(mlp_part),
            low, wide, wide, pltpu.VMEM((count + 16, BLOCK), F32),
            pltpu.VMEM(cube, BF16), pltpu.VMEM(cube, BF16), pltpu.VMEM(gate_cube, BF16),
            pltpu.VMEM((16, rec), F32), pltpu.VMEM((8, rec), F32), pltpu.VMEM((8, rec), F32),
            pltpu.VMEM((3, 4, 2, rec), F32), pltpu.VMEM((half, width), BF16),
            DMA((8,)),
            DMA((3,)),
            DMA((1, 3, 3)),
            DMA((1, 3, 3)),
            DMA((2,)),
            DMA((2,)),
        ]
        + ring_sum_scratch(half, width),
        compiler_params=params(cid, 61),
    )(
        gh, branch, normed, gate_lin, states_ext, factors, vectors, hidden,
        w_back, ext, mixed, reset, gated, gates, w_gate, mlp_part,
    )


def rec_end_kernel(
    part_in_ref, small_ref, gain_term_ref, gh_ref, tokens_in, inverse_ref, gain_ref, normed_ref, low_ref,
    dw0, dw1, gg_hbm, wl_hbm,
    total_ref, gains_ref, all_gates_ref, out0, out1, out2, tokens_hbm,
    *refs,
):
    bufs, refs = refs[: 78 + 3 * 6], refs[78 + 3 * 6 :]
    (
        part, dw2, wl, gates_out, part_low, part_in, tokens_v, gates_ref, ring_gains, gains0, small0, small1, small2,
        load_sem, own_sem, send, recv, gsend, grecv, small_send, small_recv, ring_send, ring_recv, core_sem,
    ) = refs
    half, width = gh_ref.shape
    load = pltpu.make_async_copy(wl_hbm, wl, load_sem.at[0])
    load.start()
    core = lax.axis_index("mp")
    other = {"mp": 1 - core}
    x_here = lax.axis_index("x")
    greet(axis_peers() + [other] + [{"x": peer, "mp": 1 - core} for peer in ring("x")[1:]])
    small = [
        Total(slots, small_send, small_recv, e, ORDERS[e])
        for e, slots in enumerate((small0, small1, small2))
    ]
    for flow, (start, wide) in zip(small, CHUNKS):
        flow.start(small_ref[:, start : start + wide])
    gates = [
        Scatter(
            9 + e, gg_hbm, (0, BLOCK), ORDERS[e], None, bufs[78 + 6 * e : 84 + 6 * e], gates_out,
            own_sem, send, recv, BANDS[e],
        )
        for e in range(3)
    ]
    flows = [
        Scatter(
            e, (dw0, dw1, dw2)[e // 3], CHUNKS[e % 3], SUM_ORDERS[e // 3][e % 3], ROW_HALVES,
            bufs[9 * e : 9 * e + 9] if e < 6 else bufs[8 * e + 6 : 8 * e + 14], (out0, out1, out2)[e // 3],
            own_sem, send, recv, rings=2 if e < 6 else 1,
        )
        for e in range(9)
    ]
    one, two, three = flows[:3], flows[3:6], flows[6:]
    spread = [Gather(e, gates_ref, ORDERS[e], (0, BLOCK), gsend, grecv, band=BANDS[e]) for e in range(3)]

    def each(group, name, *args):
        for flow in group:
            getattr(flow, name)(*args)

    each(gates, "begin", 0)
    each(one, "begin", 0)
    each(two, "begin", 0)

    def weight_grad(i, carry):
        cols = pl.ds(pl.multiple_of(i * 256, 256), 256)
        shard_rows(dw2, i, outer(normed_ref[:, cols], low_ref[...]).astype(BF16))
        return carry

    lax.fori_loop(0, width // 256, weight_grad, 0)
    each(three, "begin", 0)
    each(gates, "finish")
    each(gates, "begin", 1)
    for flow in small:
        flow.step()
    load.wait()

    def part_tile(i, carry):
        at = pl.ds(pl.multiple_of(i * 256, 256), 256)
        value = dot_t(low_ref[...], wl[at, :])
        part[0, :, at] = part_in_ref[0, :, at] + value[:half]
        part[1, :, at] = part_in_ref[1, :, at] + value[half:]
        return carry

    lax.fori_loop(0, width // 256, part_tile, 0)
    part_low[...] = part[1 - core].astype(BF16)
    part_copy = push(part_low, part_in, core_sem.at[0], core_sem.at[1], other)
    part_copy.start()
    each(one, "middle")
    part_copy.wait_recv()
    grad_normed = part[core] + part_in[...].astype(F32)
    mine = pl.ds(pl.multiple_of(core * half, half), half)
    inverse = inverse_ref[mine]
    hat = tokens_in[mine].astype(F32) * inverse
    gain_term = jnp.sum(grad_normed * hat, axis=0, keepdims=True)
    quarter = width // 4
    for k in range(4):
        cols = slice(k * quarter, (k + 1) * quarter)
        ring_gains[x_here, core, k : k + 1] = gain_term[:, cols]
        ring_gains[x_here, core, 4 + k : 5 + k] = gain_term_ref[:, cols]
    shares = []
    spot = ring_gains.at[x_here, core]
    group = [{"x": x, "mp": c} for x in ring("x") for c in (core, 1 - core)][1:]
    for k, peer in enumerate(group):
        copy = push(spot, spot, ring_send.at[k], ring_recv.at[k], peer)
        copy.start()
        shares.append(copy)
    grad_hat = grad_normed * gain_ref[...]
    inner = jnp.mean(grad_hat * hat, axis=-1, keepdims=True)
    tokens_v[...] = gh_ref[...] + inverse * (grad_hat - hat * inner)
    token_copy = push(tokens_v, tokens_hbm.at[core], core_sem.at[2], core_sem.at[3], other)
    token_copy.start()
    token_save = pltpu.make_async_copy(tokens_v, tokens_hbm.at[core], load_sem.at[1])
    token_save.start()
    each(two, "middle")
    each(gates, "finish")
    each(gates, "begin", 2)
    for flow in small:
        flow.step()
    each(one, "finish")
    each(one, "begin", 1)
    for copy in shares:
        copy.wait_recv()
    gains = Total(gains0, small_send, small_recv, 3, ("y", "z"))
    halves = [ring_gains[x, 0] + ring_gains[x, 1] for x in range(4)]
    gains.start((halves[0] + halves[1]) + (halves[2] + halves[3]))
    each(three, "middle")
    each(gates, "finish")
    gates_ref[lax.axis_index("z"), lax.axis_index("y"), x_here] = gates_out[...].astype(BF16)
    each(spread, "begin", 0)
    for flow, (start, wide) in zip(small, CHUNKS):
        total_ref[:, start : start + wide] = flow.step()
    each(two, "finish")
    each(two, "begin", 1)
    gains.step()
    each(one, "middle")
    each(spread, "finish")
    each(spread, "begin", 1)
    each(three, "finish")
    each(three, "begin", 1)
    each(two, "middle")
    each(one, "finish")
    each(one, "begin", 2)
    gains_ref[...] = gains.step()
    each(spread, "finish")
    each(spread, "begin", 2)
    each(two, "finish")
    each(two, "begin", 2)
    each(one, "finish")
    each(three, "finish")
    each(three, "begin", 2)
    each(two, "finish")
    each(spread, "finish")

    def unpack(b, carry):
        at = pl.ds(pl.multiple_of(16 * lax.rem(b, 3), 16), 16)
        all_gates_ref[b] = gates_ref[:, :, b // 3, at, :].reshape(BLOCK, BLOCK).astype(F32)
        return carry

    lax.fori_loop(0, all_gates_ref.shape[0], unpack, 0)
    each(three, "finish")
    for copy in (token_copy, token_save):
        copy.wait()
    each(flows + gates + spread + small, "drain")
    gains.drain()
    for copy in shares + [part_copy]:
        copy.wait_send()


def rec_end(part, small, gain_term, grad_hidden, tokens, inverse, gain, normed, low, weights, gates, w_lin, cid):
    half, width = grad_hidden.shape
    rows, rec = weights[0].shape[3:]
    gate_blocks = 2 * rec // BLOCK

    def sds(*shape):
        return jax.ShapeDtypeStruct(shape, F32)

    bufs = []
    for e in range(9):
        bufs += scatter_buffers(rows, CHUNKS[e % 3][1], 2 if e < 6 else 1)
    for _ in range(3):
        bufs += scatter_buffers(GATE_ROWS // 3, BLOCK, 0)
    return pl.pallas_call(
        rec_end_kernel,
        out_shape=[
            sds(16, rec),
            sds(8, width // 4),
            sds(gate_blocks, BLOCK, BLOCK),
            sds(rows, rec),
            sds(rows, rec),
            sds(rows, rec),
            sds(2, half, width),
        ],
        in_specs=[VM] * 9 + [ANY] * 4,
        out_specs=[VM] * 6 + [HBM],
        scratch_shapes=bufs
        + [
            pltpu.VMEM(part.shape, F32),
            pltpu.VMEM(weights[0].shape, BF16),
            pltpu.VMEM(w_lin.shape, BF16),
            pltpu.VMEM((GATE_ROWS, BLOCK), F32),
            pltpu.VMEM((half, width), BF16),
            pltpu.VMEM((half, width), BF16),
            pltpu.VMEM((half, width), F32),
            pltpu.VMEM(gates.shape, BF16),
            pltpu.VMEM((4, 2, 8, width // 4), F32),
            pltpu.VMEM((2, 4, 8, width // 4), F32),
        ]
        + [pltpu.VMEM((3, 4, 16, wide), F32) for _, wide in CHUNKS]
        + [
            DMA((2,)),
            DMA((12, 3)),
            DMA((12, 3, 3, 3)),
            DMA((12, 3, 3, 3)),
            DMA((3, 3, 1, 3)),
            DMA((3, 3, 1, 3)),
            DMA((4, 3, 3)),
            DMA((4, 3, 3)),
            DMA((7,)),
            DMA((7,)),
            DMA((4,)),
        ],
        compiler_params=params(cid, 60),
    )(part, small, gain_term, grad_hidden, tokens, inverse, gain, normed, low, *weights, gates, w_lin)


def mlp_end_kernel(in_ref, back, send, recv, own_sem):
    x_here = lax.axis_index("x")
    peers = ring("x")[1:]
    greet([{"x": peer} for peer in peers])
    moves = []
    for step, peer in enumerate(peers):
        copy = push(in_ref.at[peer], back.at[x_here], send.at[step], recv.at[step], {"x": peer})
        copy.start()
        moves.append(copy)
    own = pltpu.make_async_copy(in_ref.at[x_here], back.at[x_here], own_sem)
    own.start()
    for copy in moves:
        copy.wait()
    own.wait()


def mlp_end(quarters, cid):
    return pl.pallas_call(
        mlp_end_kernel,
        out_shape=jax.ShapeDtypeStruct(quarters.shape, quarters.dtype),
        in_specs=[HBM],
        out_specs=VM,
        scratch_shapes=[DMA((3,)), DMA((3,)), DMA],
        compiler_params=params(cid, 61),
    )(quarters)


def finish_kernel(
    small_hbm, gains_hbm, out_hbm, gate_hbm, lin_hbm, back_hbm, rms_hbm, rms_mlp_hbm, result_in, tokens_in, gates_in,
    result_ref, tokens_ref, gates_ref, rec_ref, out_ref, mlp_ref, down_ref, bias_ref, lam_ref, conv_w_ref, conv_b_ref,
    gain_rec_ref, gain_mlp_ref, h_ref, state_ref, rms_ref, rms_mlp_ref,
    small_ref, gains_ref, out_sums, gate_sums, lin_sums, back, rms_v, rms_mlp_v, result_v, tokens_v, gates_v, sem, out_sem,
):
    pairs = (
        (result_in, result_v), (tokens_in, tokens_v), (gates_in, gates_v),
        (small_hbm, small_ref), (gains_hbm, gains_ref), (out_hbm, out_sums), (gate_hbm, gate_sums),
        (lin_hbm, lin_sums), (back_hbm, back), (rms_hbm, rms_v), (rms_mlp_hbm, rms_mlp_v),
    )
    loads = [pltpu.make_async_copy(src, dst, sem.at[k]) for k, (src, dst) in enumerate(pairs)]
    for load in loads:
        load.start()
    copies = []
    for k, (src, dst) in enumerate(((result_v, result_ref), (tokens_v, tokens_ref), (gates_v, gates_ref))):
        loads[k].wait()
        copies.append(pltpu.make_async_copy(src, dst, out_sem.at[k]))
        copies[k].start()
    for load in loads[3:]:
        load.wait()
    rec_ref[:, 0, :] = gate_sums[...]
    rec_ref[:, 1, :] = lin_sums[...]
    out_ref[...] = out_sums[...]
    units = down_ref.shape[1] // 4
    for q in range(4):
        value = back[q].astype(F32)
        at = pl.ds(q * units, units)
        for k in range(2):
            mlp_ref[:, k, at] = value[:, k * units : (k + 1) * units]
        down_ref[:, at] = value[:, 2 * units :]
    bias_ref[...] = small_ref[G_BIAS : G_BIAS + 2]
    lam_ref[...] = small_ref[G_LAM]
    conv_w_ref[...] = small_ref[G_CONV_W : G_CONV_W + CONV]
    conv_b_ref[...] = small_ref[G_CONV_B]
    h_ref[...] = small_ref[G_H]
    state_ref[...] = small_ref[G_STATE : G_STATE + EDGE]
    quarter = gains_ref.shape[1]
    for k in range(4):
        at = pl.ds(k * quarter, quarter)
        gain_rec_ref[at] = gains_ref[k]
        gain_mlp_ref[at] = gains_ref[4 + k]
    half = rms_mlp_v.shape[1]
    square = (half, half)
    diagonal = lax.broadcasted_iota(jnp.int32, square, 0) == lax.broadcasted_iota(jnp.int32, square, 1)
    for core in range(2):
        at = pl.ds(core * half, half)
        for ref, column in ((rms_ref, rms_v[at, 0:1]), (rms_mlp_ref, rms_mlp_v[core, :, 0:1])):
            spread = jnp.where(diagonal, jnp.broadcast_to(column, square), 0.0)
            ref[at] = jnp.sum(spread, axis=0)
    for copy in copies:
        copy.wait()


def finish(small, gains, sums, back, rms, rms_mlp, result, tokens, gates):
    rec = small.shape[1]
    rows = back.shape[1]
    units = back.shape[2] // 3
    width = gains.size // 2

    def sds(*shape):
        return jax.ShapeDtypeStruct(shape, F32)

    return pl.pallas_call(
        finish_kernel,
        out_shape=[
            jax.ShapeDtypeStruct(result.shape, result.dtype),
            sds(*tokens.shape),
            sds(*gates.shape),
            sds(rows, 2, rec),
            sds(rows, rec),
            sds(rows, 2, 4 * units),
            sds(rows, 4 * units),
            sds(2, rec),
            sds(rec),
            sds(CONV, rec),
            sds(rec),
            sds(width),
            sds(width),
            sds(rec),
            sds(EDGE, rec),
            sds(rms.shape[0]),
            sds(rms.shape[0]),
        ],
        in_specs=[HBM] * 11,
        out_specs=[HBM] * 3 + [VM] * 14,
        scratch_shapes=[pltpu.VMEM(a.shape, a.dtype) for a in (small, gains, *sums, back, rms, rms_mlp, result, tokens, gates)]
        + [DMA((11,)), DMA((3,))],
        compiler_params=pltpu.CompilerParams(vmem_limit_bytes=61 * MIB),
    )(small, gains, *sums, back, rms, rms_mlp, result, tokens, gates)


def body(
    tokens,
    cotangent,
    starts,
    valid,
    w_rec,
    w_out,
    w_mlp,
    w_down,
    lru_gates,
    lru_bias,
    lam,
    conv_w,
    conv_b,
    gain_rec,
    gain_mlp,
    h_init,
    conv_state,
):
    count, width = tokens.shape
    shard, _, rec = w_rec.shape
    hidden_units = w_mlp.shape[2] // 4
    half = count // 2
    core = lax.axis_index("mp")

    (
        w_lin, w_gate, w_back, mlp_weights, ext, gate_lin, mixed, reset, gated, factors, states_ext, branch_in,
        normed_rec, grad_out_all, inverse_rec, rms_rec, hidden, normed_mlp, inverse_mlp, rms_half, grad_out, vectors,
    ) = rec_forward(
        tokens,
        gain_rec,
        gain_mlp,
        (conv_w, conv_b, lam, lru_bias, conv_state, h_init),
        (starts, valid),
        w_rec,
        w_out.T,
        w_mlp,
        w_down.T,
        cotangent,
        lru_gates,
        0,
    )
    w_lin, w_gate, w_back = (w.reshape(width, rec) for w in (w_lin, w_gate, w_back))
    grad_hidden, grad_hidden_low, gain_mlp_term, mlp_terms, mlp_part = mlp(
        normed_mlp, grad_out, hidden, inverse_mlp, gain_mlp[None], grad_out_all, mlp_weights, 1
    )
    mlp_sums = lax.psum_scatter(mlp_terms, ("z", "y"), scatter_dimension=0, tiled=True)
    grad_hidden_low = grad_hidden_low.reshape(count, width)
    small, normed_part, grad_rec_low, result, *weight_terms, gate_terms = rec_back(
        grad_hidden_low,
        branch_in,
        normed_rec,
        gate_lin,
        states_ext,
        factors,
        vectors,
        hidden,
        w_back,
        ext,
        mixed,
        reset,
        gated,
        lru_gates,
        w_gate,
        mlp_part,
        2,
    )
    small, gains, gate_blocks, out_sums, gate_sums, lin_sums, grad_tokens = rec_end(
        normed_part,
        small,
        gain_mlp_term,
        grad_hidden,
        tokens,
        inverse_rec,
        gain_rec[None],
        normed_rec,
        grad_rec_low,
        weight_terms,
        gate_terms,
        w_lin,
        3,
    )
    back = mlp_end(mlp_sums.reshape(4, shard, 3 * hidden_units), 4)
    (
        result, grad_tokens, grad_gates, grad_w_rec, grad_out_t, grad_w_mlp, grad_down_t, grad_bias, grad_lam,
        grad_conv_w, conv_bias_gradient, grad_gain_rec, grad_gain_mlp, grad_h_init, grad_conv_state, rms_rec, rms_mlp,
    ) = finish(
        small,
        gains,
        (out_sums, gate_sums, lin_sums),
        back,
        rms_rec,
        rms_half,
        result.reshape(count, width),
        grad_tokens.reshape(count, width),
        gate_blocks.reshape(lru_gates.shape),
    )
    return (
        result,
        rms_rec,
        rms_mlp,
        grad_tokens,
        grad_w_rec,
        grad_out_t.T,
        grad_w_mlp,
        grad_down_t.T,
        grad_gates,
        grad_bias,
        grad_lam,
        grad_conv_w,
        conv_bias_gradient,
        grad_gain_rec,
        grad_gain_mlp,
        grad_h_init,
        grad_conv_state,
    )


def solution(mesh):
    cube = Mesh(mesh.devices.reshape(4, 4, 4, 2), ("z", "y", "x", "mp"))
    placed = (
        P(SEQ, None),
        P(SEQ, None),
        P(SEQ),
        P(SEQ),
        P(SEQ, None, "mp"),
        P("mp", SEQ),
        P(SEQ, None, "mp"),
        P("mp", SEQ),
        P(None, "mp", None, None),
        P(None, "mp"),
        P("mp"),
        P(None, "mp"),
        P("mp"),
        P(),
        P(),
        P("mp"),
        P(None, "mp"),
    )
    return jax.shard_map(
        body,
        mesh=cube,
        in_specs=placed,
        out_specs=(
            P(SEQ, None),
            P(SEQ),
            P(SEQ),
            P(SEQ, None),
            P(SEQ, None, "mp"),
            P("mp", SEQ),
            P(SEQ, None, "mp"),
            P("mp", SEQ),
            P(None, "mp", None, None),
            P(None, "mp"),
            P("mp"),
            P(None, "mp"),
            P("mp"),
            P(),
            P(),
            P("mp"),
            P(None, "mp"),
        ),
        check_vma=False,
    )
```

```python
import functools
import jax
import jax.numpy as jnp
from jax import lax
from jax.experimental import pallas as pl
from jax.experimental.pallas import tpu as pltpu
from jax.sharding import Mesh, PartitionSpec as P

CONV = 4
EDGE = CONV - 1
BLOCK = 256
EPSILON = 1e-06
MESH = pl.DeviceIdType.MESH
ANY = pl.BlockSpec(memory_space=pl.ANY)
HBM = pl.BlockSpec(memory_space=pltpu.HBM)
VM = pl.BlockSpec(memory_space=pltpu.VMEM)
MIB = 1024 * 1024
AXES = ("z", "y", "x")
SEQ = ("z", "y", "x")
ORDERS = (("x", "y", "z"), ("y", "z", "x"), ("z", "x", "y"))
F32, BF16 = jnp.float32, jnp.bfloat16
GELU_C, GELU_A = 0.7978845608028654, 0.044715
DMA = pltpu.SemaphoreType.DMA


def loop(lower, upper, step, batch):
    main = lower + (upper - lower) // batch * batch

    def several(k, carry):
        for i in range(batch):
            step(lower + k * batch + i, 0)
        return carry

    if main > lower:
        lax.fori_loop(0, (main - lower) // batch, several, 0)
    for i in range(main, upper):
        step(i, 0)


def dot(left, right):
    return jnp.dot(left, right, preferred_element_type=F32)


def dot_t(left, right):
    return lax.dot_general(left, right, (((1,), (1,)), ((), ())), preferred_element_type=F32)


def outer(left, right):
    return lax.dot_general(left, right, (((0,), (0,)), ((), ())), preferred_element_type=F32)


def greet(peers):
    sem = pltpu.get_barrier_semaphore()
    for peer in peers:
        pl.semaphore_signal(sem, inc=1, device_id=peer, device_id_type=MESH)
    pl.semaphore_wait(sem, len(peers))


def push(src, dst, send, recv, peer):
    return pltpu.make_async_remote_copy(
        src_ref=src, dst_ref=dst, send_sem=send, recv_sem=recv, device_id=peer, device_id_type=MESH
    )


def ring(axis):
    me = lax.axis_index(axis)
    return me, lax.rem(me + 1, 4), lax.rem(me + 2, 4), lax.rem(me + 3, 4)


def all_neighbours():
    peers = []
    for axis in AXES:
        _, up, _, down = ring(axis)
        peers += [{axis: up}, {axis: down}]
    return peers


def params(cid, mib):
    return pltpu.CompilerParams(
        collective_id=cid, has_side_effects=True, vmem_limit_bytes=mib * MIB
    )


def part_of(done, axis, index, rows, cols):
    spot = []
    for name in AXES:
        if name in done:
            spot.append(pl.ds(0, 4))
        elif name == axis:
            spot.append(index)
        else:
            spot.append(lax.axis_index(name))
    return tuple(spot) + (rows, cols)


def pick(names, axis, index, others):
    spot, rest = [], iter(others)
    for name in names:
        spot.append(index if name == axis else next(rest))
    return tuple(spot)


class Scatter:
    def __init__(self, entry, src, cols, order, halves, bufs, out, own_sem, send, recv, band=None, rings=1):
        self.rings = 0 if halves is None else rings
        self.band, self.band_rows = band, src.shape[-2] if band is None else band[1]
        self.entry, self.src, self.order = entry, src, order
        self.start, self.width = cols
        self.halves, self.bufs, self.out = halves, list(bufs), out
        self.own_sem, self.send, self.recv = own_sem, send, recv
        self.left, self.sent = AXES, []

    def view(self, at, rows=None):
        if rows is None:
            first = self.band[0] if self.band is not None and self.phase == 0 else 0
            rows = pl.ds(first, self.band_rows)
        return at + (rows, pl.ds(self.start if self.phase == 0 else 0, self.width))

    def spread(self, i):
        return ((i // 4, lax.rem(i, 4)), (i,), ())[self.phase]

    def copy(self, src, dst, way, kind, peer):
        at = (self.entry, self.phase, way, kind)
        copy = push(src, dst, self.send.at[at], self.recv.at[at], {self.axis: peer})
        copy.start()
        self.sent.append(copy)
        return copy

    def load(self, index, dst, rows=None):
        src = self.src.at[self.view(pick(self.left, self.axis, index, self.full), rows)]
        copy = pltpu.make_async_copy(src, dst, self.own_sem.at[self.entry, len(self.loads)])
        copy.start()
        self.loads.append(copy)

    def begin(self, phase):
        self.phase, self.axis = phase, self.order[phase]
        self.full = (pl.ds(0, 4),) * (2 - phase)
        me, up, far, down = ring(self.axis)
        self.first, self.second, self.loads = [], [], []
        self.two_step = phase < self.rings
        if self.two_step:
            self.ones, self.twos = self.bufs.pop(0), self.bufs.pop(0)
            self.near = self.bufs.pop(0) if phase == 0 else None
            for way, peer in enumerate((up, down)):
                half = self.halves[way]
                src = self.src.at[self.view(pick(self.left, self.axis, far, self.full), half)]
                self.first.append(self.copy(src, self.ones.at[way], way, 0, peer))
            for way, peer in enumerate((up, down)):
                half = self.halves[1 - way]
                src = self.src.at[self.view(pick(self.left, self.axis, peer, self.full), half)]
                dst = self.twos.at[(way,) + self.full + (half,)]
                self.second.append(self.copy(src, dst, way, 1, peer))
            for way, peer in enumerate((up, down)):
                if phase == 0:
                    self.load(peer, self.near.at[way], self.halves[way])
        else:
            self.threes = self.bufs.pop(0)
            for step, peer in enumerate((up, far, down)):
                src = self.src.at[self.view(pick(self.left, self.axis, peer, self.full))]
                self.second.append(self.copy(src, self.threes.at[step], step, 0, peer))
        if phase == 0:
            self.own = self.bufs.pop(0)
            self.load(me, self.own)
        self.acc = self.bufs.pop(0) if phase < 2 else self.out

    def middle(self):
        _, up, _, down = ring(self.axis)
        for way, peer in enumerate((up, down)):
            self.first[way].wait_recv()
            if self.phase == 0:
                self.loads[way].wait()

            def add(i, carry, way=way, peer=peer):
                there = (way,) + self.spread(i)
                if self.phase == 0:
                    own = self.near[there]
                else:
                    at = pick(self.left, self.axis, peer, self.spread(i))
                    own = self.src[self.view(at, self.halves[way])]
                total = self.ones[there].astype(F32) + own.astype(F32)
                self.ones[there] = total.astype(BF16)
                return carry

            lax.fori_loop(0, 4 ** (2 - self.phase), add, 0)
            dst = self.twos.at[(way,) + self.full + (self.halves[way],)]
            self.second.append(self.copy(self.ones.at[way], dst, way, 2, peer))

    def finish(self):
        me = lax.axis_index(self.axis)
        for copy in self.second:
            copy.wait_recv()
        if self.phase == 0:
            self.loads[-1].wait()
        buf, slots = (self.twos, (0, 1)) if self.two_step else (self.threes, (0, 1, 2))

        def total(i, carry):
            there = self.spread(i)
            if self.phase == 0:
                whole = self.own[there].astype(F32)
            else:
                whole = self.src[self.view(pick(self.left, self.axis, me, there))].astype(F32)
            for slot in slots:
                whole = whole + buf[(slot,) + there].astype(F32)
            if self.phase < 2:
                self.acc[there] = whole.astype(self.acc.dtype)
            else:
                first = 0 if self.band is None else self.band[0]
                self.acc[pl.ds(first, self.band_rows), pl.ds(self.start, self.width)] = whole
            return carry

        lax.fori_loop(0, 4 ** (2 - self.phase), total, 0)
        self.src = self.acc
        self.left = tuple(name for name in self.left if name != self.axis)

    def drain(self):
        for copy in self.sent:
            copy.wait_send()


def scatter_buffers(rows, width, rings):
    bufs = []
    for phase in range(3):
        cube = (4,) * (2 - phase)
        if phase < rings:
            bufs.append(pltpu.VMEM((2,) + cube + (rows // 2, width), BF16))
            bufs.append(pltpu.VMEM((2,) + cube + (rows, width), BF16))
            if phase == 0:
                bufs.append(pltpu.VMEM((2,) + cube + (rows // 2, width), BF16))
        else:
            bufs.append(pltpu.VMEM((3,) + cube + (rows, width), BF16))
        if phase == 0:
            bufs.append(pltpu.VMEM(cube + (rows, width), BF16))
        if phase < 2:
            bufs.append(pltpu.VMEM(cube + (rows, width), BF16))
    return bufs


class Gather:
    def __init__(self, entry, out, order, cols, send, recv, done=(), ring_rounds=(), band=None):
        self.band = (0, out.shape[3]) if band is None else band
        self.entry, self.out, self.order, self.cols = entry, out, order, pl.ds(*cols)
        self.send, self.recv, self.sent = send, recv, []
        self.done, self.ring_rounds = done, ring_rounds

    def spot(self, origin, rows=None):
        rows = pl.ds(*self.band) if rows is None else rows
        return self.out.at[part_of(self.done, self.axis, origin, rows, self.cols)]

    def copy(self, src, dst, step, way, peer):
        at = (self.entry, self.phase, step, way)
        copy = push(src, dst, self.send.at[at], self.recv.at[at], {self.axis: peer})
        copy.start()
        self.sent.append(copy)
        return copy

    def begin(self, phase, src=None):
        self.phase, self.axis = phase, self.order[phase]
        me, up, far, down = ring(self.axis)
        here = self.spot(me)
        src = here if src is None else src.at[:, self.cols]
        peers = (up, down) if phase in self.ring_rounds else (up, far, down)
        self.copies = [self.copy(src, here, 0, way, peer) for way, peer in enumerate(peers)]

    def middle(self):
        _, up, _, down = ring(self.axis)
        half = self.out.shape[3] // 2
        first, self.copies = self.copies, []
        for way, (peer, origin) in enumerate(((up, down), (down, up))):
            first[way].wait_recv()
            spot = self.spot(origin, pl.ds(way * half, half))
            self.copies.append(self.copy(spot, spot, 1, way, peer))

    def hold(self):
        for copy in self.copies:
            copy.wait_recv()

    def finish(self):
        self.hold()
        self.done = self.done + (self.axis,)

    def drain(self):
        for copy in self.sent:
            copy.wait_send()


class Rounds:
    def __init__(self, slots, send, recv, entry=0, order=("x", "y", "z")):
        self.slots, self.send, self.recv, self.sent = slots, send, recv, []
        self.entry, self.order = entry, order

    def begin(self, phase, rows):
        self.phase, axis = phase, self.order[phase]
        me = lax.axis_index(axis)
        for at, value in rows:
            self.slots[phase, me, at] = value
        self.copies = []
        for step, peer in enumerate(ring(axis)[1:]):
            spot = self.slots.at[phase, me]
            at = (self.entry, phase, step)
            copy = push(spot, spot, self.send.at[at], self.recv.at[at], {axis: peer})
            copy.start()
            self.copies.append(copy)

    def finish(self):
        for copy in self.copies:
            copy.wait_recv()
        self.sent += self.copies

    def drain(self):
        for copy in self.sent:
            copy.wait_send()


class Prefix(Rounds):
    def start(self, pair, backward):
        self.backward, self.cur, self.head = backward, pair, None
        self.share(0)

    def share(self, phase):
        self.begin(phase, [(slice(0, 1), self.cur[0]), (slice(1, 2), self.cur[1])])

    def step(self):
        self.finish()
        me = lax.axis_index(self.order[self.phase])
        run = (jnp.ones_like(self.cur[0]), jnp.zeros_like(self.cur[1]))
        mine = run
        for j in (3, 2, 1, 0) if self.backward else (0, 1, 2, 3):
            take = me == j
            mine = (jnp.where(take, run[0], mine[0]), jnp.where(take, run[1], mine[1]))
            fac, val = self.slots[self.phase, j, 0:1], self.slots[self.phase, j, 1:2]
            run = (run[0] * fac, val + fac * run[1])
        self.cur = run
        if self.head is None:
            self.head = mine
        else:
            self.head = (mine[0] * self.head[0], self.head[1] + self.head[0] * mine[1])
        if self.phase < 2:
            self.share(self.phase + 1)
        return self.head


class Total(Rounds):
    def start(self, value):
        self.begin(0, [(slice(None), value)])

    def step(self):
        self.finish()
        at = self.slots
        k = self.phase
        value = (at[k, 0] + at[k, 1]) + (at[k, 2] + at[k, 3])
        if k + 1 < len(self.order):
            self.begin(k + 1, [(slice(None), value)])
        return value


def axis_peers():
    return [{axis: ring(axis)[step]} for axis in AXES for step in (1, 2, 3)]


def along_seq(distance):
    place = lax.axis_index("z") * 16 + lax.axis_index("y") * 4 + lax.axis_index("x")
    place = lax.rem(place + distance + 64, 64)
    return {"z": place // 16, "y": lax.rem(place // 4, 4), "x": lax.rem(place, 4)}


CHUNKS = ((0, 384), (384, 512), (896, 384))
SUM_ORDERS = (
    (("y", "z", "x"), ("x", "y", "z"), ("z", "x", "y")),
    (("x", "z", "y"), ("z", "x", "y"), ("y", "z", "x")),
    (("y", "x", "z"), ("x", "y", "z"), ("z", "y", "x")),
)
ROW_HALVES = (pl.ds(0, 16), pl.ds(16, 16))
BANDS = ((0, 16), (16, 16), (32, 16))


def gelu_parts(x):
    inner = GELU_C * (x + GELU_A * x * x * x)
    t = jnp.tanh(inner)
    slope = GELU_C * (1.0 + 3.0 * GELU_A * x * x)
    return 0.5 * x * (1.0 + t), 0.5 * (1.0 + t) + 0.5 * x * (1.0 - t * t) * slope


FAR, UP, DOWN, ME = 0, 1, 2, 3


class RingSum:
    def __init__(self, part, got, one, two, send, recv, sib_send, sib_recv):
        self.part, self.got, self.one, self.two = part, got, one, two
        self.send, self.recv, self.sib_send, self.sib_recv = send, recv, sib_send, sib_recv
        self.core, self.sums, self.sent = lax.axis_index("mp"), {}, []

    def across(self, *slots):
        for slot in slots:
            copy = push(
                self.part.at[slot, 1 - self.core],
                self.got.at[slot],
                self.sib_send.at[slot],
                self.sib_recv.at[slot],
                {"mp": 1 - self.core},
            )
            copy.start()
            self.sums[slot] = copy

    def add(self, dst, src):
        dst[...] = (dst[...].astype(F32) + src[...].astype(F32)).astype(dst.dtype)

    def collect(self, slot):
        self.sums[slot].wait_recv()
        self.add(self.got.at[slot], self.part.at[slot, self.core])

    def far(self):
        self.collect(FAR)
        half = self.one.shape[1]
        _, up, _, down = ring("x")
        self.first = []
        for way, peer in enumerate((up, down)):
            piece = self.got.at[FAR, pl.ds(way * half, half)]
            at = (0, way)
            copy = push(piece, self.one.at[way], self.send.at[at], self.recv.at[at], {"x": peer})
            copy.start()
            self.first.append(copy)

    def near(self):
        half = self.one.shape[1]
        _, up, _, down = ring("x")
        self.second = []
        for way, (peer, slot) in enumerate(((up, UP), (down, DOWN))):
            self.collect(slot)
            self.first[way].wait_recv()
            self.add(self.got.at[slot, pl.ds(way * half, half)], self.one.at[way])
            at = (1, way)
            copy = push(self.got.at[slot], self.two.at[way], self.send.at[at], self.recv.at[at], {"x": peer})
            copy.start()
            self.second.append(copy)

    def total(self):
        self.sums[ME].wait_recv()
        total = self.got[ME].astype(F32) + self.part[ME, self.core].astype(F32)
        for way in range(2):
            self.second[way].wait_recv()
            total = total + self.two[way].astype(F32)
        return total

    def drain(self):
        for copy in self.first + self.second + list(self.sums.values()):
            copy.wait_send()


def ring_sum_scratch(rows, width):
    return [
        pltpu.VMEM((4, rows, width), BF16),
        pltpu.VMEM((2, rows // 2, width), BF16),
        pltpu.VMEM((2, rows, width), BF16),
        DMA((2, 2)),
        DMA((2, 2)),
        DMA((4,)),
        DMA((4,)),
    ]


def mlp_kernel(
    nm_ref, go_ref, hidden_ref, inv_ref, gain_ref, go_hbm, w_hbm,
    grad_hidden_ref, low_ref, term_ref, dw_ref, opart_out,
    go, w, gathered, npart, opart, mlp_in, ggu, gmi, low_half,
    load_sem, wsend, wrecv, gsend, grecv, gsib_send, gsib_recv, core_sem, *sum_refs,
):
    rows, width = nm_ref.shape
    half = rows // 2
    units = mlp_in.shape[1]
    me, up, far, down = ring("x")
    core = lax.axis_index("mp")
    other = {"mp": 1 - core}
    loads = [pltpu.make_async_copy(nm_ref, gathered.at[ME, core], load_sem.at[0])]
    wide = w.shape[4] // 2
    full, every = pl.ds(0, 4), pl.ds(0, w.shape[3])
    last = (("z", 0), ("y", wide))

    def weight_set(axis, index, at, cols):
        return ((index, full) if axis == "z" else (full, index)) + (full, at, pl.ds(cols, wide))

    for e, (axis, cols) in enumerate(last):
        here, ahead, _, behind = ring(axis)
        for k, index in enumerate((here, ahead, behind)):
            spot = weight_set(axis, index, every, cols)
            loads.append(pltpu.make_async_copy(w_hbm.at[spot], w.at[spot], load_sem.at[1 + 3 * e + k]))
    for slot, chip in ((FAR, far), (UP, up), (DOWN, down), (ME, me)):
        at = pl.ds(slot * 2 * rows, 2 * rows)
        loads.append(pltpu.make_async_copy(go_hbm.at[chip], go.at[at], load_sem.at[7 + slot]))
    for load in loads:
        load.start()
    peers = [{"x": up}, {"x": down}, other]
    for axis in ("y", "z"):
        peers += [{axis: ring(axis)[1]}, {axis: ring(axis)[3]}]
    greet(peers)
    top, low = pl.ds(0, half), pl.ds(half, half)
    first = []
    for way, (peer, slot) in enumerate(((up, DOWN), (down, UP))):
        spot = gathered.at[slot, core]
        copy = push(nm_ref, spot, gsend.at[0, way], grecv.at[0, way], {"x": peer})
        copy.start()
        first.append(copy)
    across = [push(nm_ref, gathered.at[ME, core], gsib_send.at[0], gsib_recv.at[0], other)]
    across[0].start()
    rest = []
    for e, (axis, cols) in enumerate(last):
        _, ahead, _, behind = ring(axis)
        deep = w.shape[3] // 2
        for way, (peer, origin) in enumerate(((ahead, behind), (behind, ahead))):
            spot = weight_set(axis, origin, pl.ds(way * deep, deep), cols)
            copy = push(w_hbm.at[spot], w.at[spot], wsend.at[e, way], wrecv.at[e, way], {axis: peer})
            copy.start()
            rest.append(copy)
    second = []
    for way, (peer, slot, piece) in enumerate(((up, DOWN, top), (down, UP, low))):
        first[way].wait_recv()
        spot = gathered.at[slot, core]
        copy = push(
            spot.at[piece], gathered.at[FAR, core, piece], gsend.at[1, way], grecv.at[1, way], {"x": peer}
        )
        copy.start()
        second.append(copy)
        copy = push(spot, spot, gsib_send.at[1 + way], gsib_recv.at[1 + way], other)
        copy.start()
        across.append(copy)
    for copy in rest:
        copy.wait_recv()
    for load in loads:
        load.wait()

    def tile(j, start=0):
        return pl.ds(pl.multiple_of(start + j * 256, 256), 256)

    def columns(at):
        return w[:, :, :, :, at].reshape(width, 256)

    def shard_tile(i, at):
        return w[i // 2, pl.ds(2 * lax.rem(i, 2), 2), :, :, at].reshape(256, -1)

    def grad_tile(j, carry):
        gmi[:, tile(j)] = dot(go[...], columns(tile(j, 2 * units)))
        return carry

    loop(0, units // 256, grad_tile, 1)
    for way, piece in enumerate((top, low)):
        second[way].wait_recv()
        spot = gathered.at[FAR, core, piece]
        copy = push(spot, spot, gsib_send.at[3 + way], gsib_recv.at[3 + way], other)
        copy.start()
        across.append(copy)

    def tokens_step(slot):
        at = pl.ds(slot * 2 * rows, 4 * rows)

        def hidden_tile(j, carry):
            tokens_in = gathered[slot : slot + 2].reshape(4 * rows, width)
            gate = dot(tokens_in, columns(tile(j)))
            up_lin = dot(tokens_in, columns(tile(j, units)))
            grad = gmi[at, tile(j)]
            act, slope = gelu_parts(gate)
            mlp_in[at, tile(j)] = (act * up_lin).astype(BF16)
            ggu[at, tile(j)] = (slope * (grad * up_lin)).astype(BF16)
            ggu[at, tile(j, units)] = (grad * act).astype(BF16)
            return carry

        loop(0, units // 256, hidden_tile, 1)

        def back_tile(j, carry):
            back = dot_t(ggu[at], shard_tile(j, pl.ds(0, 2 * units)))
            npart[slot : slot + 2, :, :, tile(j)] = back.astype(BF16).reshape(2, 2, rows, 256)
            return carry

        loop(0, width // 256, back_tile, 1)

    def out_tile(j, carry):
        part = dot_t(mlp_in[...], shard_tile(j, pl.ds(2 * units, units)))
        opart[:, :, :, tile(j)] = part.astype(BF16).reshape(4, 2, rows, 256)
        return carry

    def weight_grads(lower, upper):
        def step(i, carry):
            left = gathered[:, :, :, tile(i)].reshape(8 * rows, 256)
            dw_ref[tile(i), pl.ds(0, 2 * units)] = outer(left, ggu[...]).astype(BF16)
            dw_ref[tile(i), pl.ds(2 * units, units)] = outer(go[:, tile(i)], mlp_in[...]).astype(BF16)
            return carry

        loop(lower, upper, step, 2)

    sums = RingSum(npart, *sum_refs)
    for copy in across:
        copy.wait_recv()
    tokens_step(FAR)
    sums.across(FAR, UP)
    sums.far()
    tokens_step(DOWN)
    sums.across(DOWN, ME)
    sums.near()
    loop(0, width // 256, out_tile, 1)
    save = pltpu.make_async_copy(opart, opart_out, load_sem.at[11])
    save.start()
    weight_grads(0, 5)
    grad_normed = sums.total()
    hat = hidden_ref[...] * inv_ref[...]
    grad_hat = grad_normed * gain_ref[...]
    inner = jnp.mean(grad_hat * hat, axis=-1, keepdims=True)
    grad_hidden = go_ref[...].astype(F32) + inv_ref[...] * (grad_hat - hat * inner)
    grad_hidden_ref[...] = grad_hidden
    term_ref[...] = jnp.sum(grad_normed * hat, axis=0, keepdims=True)
    low_half[...] = grad_hidden.astype(BF16)
    low_ref[core] = low_half[...]
    swap = push(low_half, low_ref.at[core], core_sem.at[0], core_sem.at[1], other)
    swap.start()
    weight_grads(5, 8)
    swap.wait()
    save.wait()
    sums.drain()
    for copy in first + second + across + rest:
        copy.wait_send()


def mlp(normed, grad_out, hidden, inverse, gain, grad_out_all, weights, cid):
    rows, width = normed.shape
    units = weights.shape[4] // 3

    def block(dtype, *shape):
        return pltpu.VMEM(shape, dtype)

    return pl.pallas_call(
        mlp_kernel,
        out_shape=[
            jax.ShapeDtypeStruct((rows, width), F32),
            jax.ShapeDtypeStruct((2, rows, width), BF16),
            jax.ShapeDtypeStruct((1, width), F32),
            jax.ShapeDtypeStruct((width, 3 * units), BF16),
            jax.ShapeDtypeStruct((4, 2, rows, width), BF16),
        ],
        in_specs=[VM] * 5 + [ANY] * 2,
        out_specs=[VM] * 4 + [HBM],
        scratch_shapes=[
            block(BF16, 8 * rows, width),
            block(BF16, *weights.shape),
            block(BF16, 4, 2, rows, width),
            block(BF16, 4, 2, rows, width),
            block(BF16, 4, 2, rows, width),
            block(BF16, 8 * rows, units),
            block(BF16, 8 * rows, 2 * units),
            block(F32, 8 * rows, units),
            block(BF16, rows, width),
        ]
        + [DMA((12,)), DMA((2, 2)), DMA((2, 2)), DMA((2, 2)), DMA((2, 2)), DMA((5,)), DMA((5,)), DMA((2,))]
        + ring_sum_scratch(rows, width),
        compiler_params=params(cid, 60),
    )(normed, grad_out, hidden, inverse, gain, grad_out_all.reshape(4, 2 * rows, width), weights)


def lanes(n):
    return pl.ds(pl.multiple_of(n * BLOCK, BLOCK), BLOCK)


def minus_expm1(x):
    series = jnp.ones_like(x)
    for k in (9, 8, 7, 6, 5, 4, 3, 2):
        series = 1.0 + x * (1.0 / k) * series
    return jnp.where(x > -0.4, -x * series, 1.0 - jnp.exp(x))


def log1p(x):
    series = jnp.zeros_like(x)
    for k in (7, 6, 5, 4, 3, 2, 1):
        series = 1.0 / k - x * series
    return jnp.where(x < 0.05, x * series, jnp.log(1.0 + x))


CONV_W, CONV_B, RATES, BIAS, CONV_STATE, H_INIT, SLOPE = 0, 4, 5, 6, 8, 11, 12


def rec_forward_kernel(*refs):
    (
        tokens_ref, gain_ref, gain_mlp_ref, conv_w_ref, conv_b_ref, lam_ref, bias_ref, conv_state_ref,
        h_init_ref, starts_ref, valid_ref, rec_raw, back_in, mlp_raw, down_in, cot_ref, g_hbm,
        lin_out, gate_out, back_out, mlp_out, ext_out, act_out, mixed_out, reset_out, input_out, f_out, states_out,
        branch_out, normed_out, go_all, inv_ref, rms_ref, hidden_ref, nm_ref, inv_mlp_ref, rms_mlp_ref, go_ref, v_ref,
        wl, wg, wb, ext, gate_lin, mixed_v, reset_v, input_v, f_v, states, branch_v, normed, tail_in, driven, cf_v,
        part, part_low, part_in, g_v, rms_v, slots, mask_ref, rec_in, mlp_in,
        tail_sem, load_sem, save_sem, own_sem, move_send, move_recv, send, recv, small_send, small_recv, core_sem,
        go_send, go_recv, go_sib_send, go_sib_recv,
    ) = refs
    count, width = tokens_ref.shape
    rec = f_v.shape[1]
    for k in range(2):
        rec_in[:, k * rec : (k + 1) * rec] = rec_raw[:, k, :]
        mlp_in[:, k * mlp_raw.shape[2] : (k + 1) * mlp_raw.shape[2]] = mlp_raw[:, k, :]
    gate_in, lin_in = rec_in.at[:, pl.ds(0, rec)], rec_in.at[:, pl.ds(rec, rec)]
    blocks = rec // BLOCK
    half = count // 2
    core = lax.axis_index("mp")
    other = {"mp": 1 - core}
    here = tuple(lax.axis_index(name) for name in AXES)
    load = pltpu.make_async_copy(g_hbm, g_v, load_sem)
    load.start()
    owns = [
        pltpu.make_async_copy(lin_in, wl.at[here], own_sem.at[0]),
        pltpu.make_async_copy(gate_in, wg.at[here], own_sem.at[1]),
        pltpu.make_async_copy(back_in, wb.at[here], own_sem.at[2]),
    ]
    units = mlp_out.shape[4] // 3
    every = pl.ds(0, rec_in.shape[0])

    def quarter(k, chip):
        if k == 2:
            return down_in.at[every, pl.ds(pl.multiple_of(chip * units, units), units)]
        return mlp_in.at[every, pl.ds(pl.multiple_of((4 * k + chip) * units, units), units)]

    spots = [mlp_out.at[here + (every, pl.ds(k * units, units))] for k in range(3)]
    owns += [pltpu.make_async_copy(quarter(k, here[2]), spots[k], own_sem.at[3 + k]) for k in range(3)]
    for own in owns:
        own.start()
    greet(axis_peers() + [other, along_seq(1), along_seq(-1)])
    tail_copy = push(tokens_ref.at[pl.ds(count - 16, 16)], tail_in, tail_sem.at[0], tail_sem.at[1], along_seq(1))
    tail_copy.start()
    lin = [Gather(e, wl, ORDERS[e], CHUNKS[e], send, recv, ring_rounds=(2,)) for e in range(3)]
    gate = [
        Gather(3 + e, wg, ORDERS[(e + 1) % 3], CHUNKS[e], send, recv, ring_rounds=(1, 2)) for e in range(3)
    ]
    back = [
        Gather(6 + e, wb, ORDERS[(2, 1, 0)[e]], CHUNKS[e], send, recv, ring_rounds=(1, 2)) for e in range(3)
    ]
    rest = gate + back
    wide = mlp_out.shape[4] // 2
    mlp_flows = [
        Gather(9 + e, mlp_out, order, (e * wide, wide), send, recv, done=("x",), ring_rounds=(1,))
        for e, order in enumerate((("y", "z"), ("z", "y")))
    ]

    def each(group, name, *args):
        for flow in group:
            getattr(flow, name)(*args)

    each(lin, "begin", 0, lin_in)
    moves = []
    for step, peer in enumerate(ring("x")[1:]):
        for k in range(3):
            copy = push(quarter(k, peer), spots[k], move_send.at[step, k], move_recv.at[step, k], {"x": peer})
            copy.start()
            moves.append(copy)
    each(gate, "begin", 0, gate_in)
    each(back, "begin", 0, back_in)

    v_ref[CONV_W : CONV_W + CONV] = conv_w_ref[...]
    v_ref[BIAS : BIAS + 2] = bias_ref[...]
    v_ref[CONV_STATE : CONV_STATE + EDGE] = conv_state_ref[...]
    for at, ref in ((CONV_B, conv_b_ref), (H_INIT, h_init_ref)):
        v_ref[at : at + 1] = ref[...].reshape(1, rec)
    lam = lam_ref[...].reshape(1, rec)
    v_ref[RATES : RATES + 1] = jnp.maximum(-lam, 0.0) + log1p(jnp.exp(-jnp.abs(lam)))
    v_ref[SLOPE : SLOPE + 1] = 1.0 / (1.0 + jnp.exp(lam))
    v_ref[SLOPE + 1 :] = jnp.zeros((15 - SLOPE, rec), F32)
    square = (count, count)
    diagonal = lax.broadcasted_iota(jnp.int32, square, 0) == lax.broadcasted_iota(jnp.int32, square, 1)
    for k, row in enumerate((1.0 - starts_ref[...].astype(F32), valid_ref[...].astype(F32))):
        spread = jnp.where(diagonal, jnp.broadcast_to(row.reshape(1, count), square), 0.0)
        mask_ref[:, k : k + 1] = jnp.sum(spread, axis=1, keepdims=True)

    def norm(values):
        mean_sq = jnp.mean(values * values, axis=-1, keepdims=True)
        inverse = lax.rsqrt(mean_sq + EPSILON)
        return values * inverse, inverse, jnp.sqrt(mean_sq + EPSILON)

    def norm_step(i, carry):
        at = pl.ds(pl.multiple_of(i * 64, 64), 64)
        hat, inverse, rms = norm(tokens_ref[at].astype(F32))
        inv_ref[at] = inverse
        rms_ref[at] = rms
        normed[pl.ds(pl.multiple_of(16 + i * 64, 16), 64)] = (hat * gain_ref[...]).astype(BF16)
        return carry

    lax.fori_loop(0, count // 64, norm_step, 0)
    for own in owns:
        own.wait()
    each(lin, "finish")
    each(lin, "begin", 1)
    each(rest, "finish")
    each(rest, "begin", 1)
    tail_copy.wait_recv()
    normed[0:16] = (norm(tail_in[...].astype(F32))[0] * gain_ref[...]).astype(BF16)
    saves = []

    def save(src, dst):
        copy = pltpu.make_async_copy(src, dst, save_sem.at[len(saves)])
        copy.start()
        saves.append(copy)

    save(normed.at[pl.ds(16, count)], normed_out)
    each(lin, "finish")
    each(lin, "begin", 2)
    for copy in moves:
        copy.wait_recv()
    each(mlp_flows, "begin", 0)
    each(rest, "middle")
    each(lin, "middle")
    each(rest, "finish")
    each(rest, "begin", 2)
    mine = pl.ds(pl.multiple_of(core * half, half), half)
    go_ref[...] = (cot_ref[mine].astype(F32) * mask_ref[mine, 1:2]).astype(BF16)
    load.wait()
    each(lin, "finish")
    save(wl, lin_out)
    is_first = (here[0] + here[1] + here[2]) == 0

    def rec_step(n, carry):
        at = lanes(n)
        ext[:, at] = dot(normed[...], wl[:, :, :, :, at].reshape(width, BLOCK))

        @pl.when(is_first)
        def _():
            ext[16 - EDGE : 16, at] = v_ref[CONV_STATE : CONV_STATE + EDGE, at]

        total = v_ref[CONV_B : CONV_B + 1, at] + jnp.zeros((count, BLOCK), F32)
        for k in range(CONV):
            total = total + v_ref[CONV_W + k : CONV_W + k + 1, at] * ext[pl.ds(16 - EDGE + k, count), at]
        mixed = total.astype(BF16)
        mixed_v[:, at] = mixed
        reset = jax.nn.sigmoid(dot(mixed, g_v[0, n]) + v_ref[BIAS : BIAS + 1, at])
        gated = jax.nn.sigmoid(dot(mixed, g_v[1, n]) + v_ref[BIAS + 1 : BIAS + 2, at])
        reset_v[:, at] = reset
        input_v[:, at] = gated
        log_decay = -8.0 * v_ref[RATES : RATES + 1, at] * reset
        f_v[:, at] = jnp.exp(log_decay) * mask_ref[:, 0:1]
        driven[:, at] = jnp.sqrt(minus_expm1(2.0 * log_decay)) * gated * mixed.astype(F32)
        return carry

    lax.fori_loop(0, blocks, rec_step, 0)
    for src, dst in ((ext, ext_out), (mixed_v, mixed_out), (reset_v, reset_out), (input_v, input_out), (f_v, f_out)):
        save(src, dst)

    def group(i, carry):
        base = pl.multiple_of(i * 8, 8)
        f, d = f_v[pl.ds(base, 8)], driven[pl.ds(base, 8)]
        cf, cd = carry
        cfs, cds = [], []
        for r in range(8):
            cf = cf * f[r : r + 1]
            cd = cd * f[r : r + 1] + d[r : r + 1]
            cfs.append(cf)
            cds.append(cd)
        cf_v[pl.ds(base, 8)] = jnp.concatenate(cfs, axis=0)
        states[pl.ds(pl.multiple_of(base + 8, 8), 8)] = jnp.concatenate(cds, axis=0)
        return cf, cd

    zero = jnp.zeros((1, rec), F32)
    ends = lax.fori_loop(0, count // 8, group, (zero + 1.0, zero))
    prefix = Prefix(slots, small_send, small_recv)
    prefix.start(ends, False)
    by_axis = {axis: [flow for flow in rest if flow.axis == axis] for axis in AXES}
    each(by_axis["x"], "middle")
    prefix.step()
    each(by_axis["y"], "middle")
    each(mlp_flows, "finish")
    mlp_flows[1].begin(1)
    prefix.step()
    each(by_axis["z"], "middle")
    mlp_flows[0].begin(1)
    x_here, x_up, x_far, x_down = ring("x")
    spot = go_all.at[x_here, core]
    save(go_ref, spot)
    go_first = []
    for way, peer in enumerate((x_up, x_down)):
        copy = push(go_ref, spot, go_send.at[0, way], go_recv.at[0, way], {"x": peer})
        copy.start()
        go_first.append(copy)
    go_across = [push(go_ref, spot, go_sib_send.at[0], go_sib_recv.at[0], other)]
    go_across[0].start()
    head = prefix.step()
    carry_in = head[1] + head[0] * v_ref[H_INIT : H_INIT + 1]
    each(gate, "finish")
    save(wg, gate_out)

    def gate_step(n, carry):
        gate_lin[:, lanes(n)] = dot(normed[16:], wg[:, :, :, :, lanes(n)].reshape(width, BLOCK))
        return carry

    lax.fori_loop(0, blocks, gate_step, 0)
    save(gate_lin, act_out)
    states[0:8] = jnp.broadcast_to(carry_in, (8, rec))

    def branch_step(n, carry):
        at = lanes(n)
        value = states[8:, at] + cf_v[:, at] * states[0:1, at]
        states[8:, at] = value
        branch_v[:, at] = (gelu_parts(gate_lin[:, at])[0] * value).astype(BF16)
        return carry

    lax.fori_loop(0, blocks, branch_step, 0)
    save(states, states_out)
    save(branch_v, branch_out)
    each(back, "finish")
    save(wb, back_out)

    def out_step(i, carry):
        at = pl.ds(pl.multiple_of(i * 256, 256), 256)
        rows = wb[i // 2, pl.ds(2 * lax.rem(i, 2), 2)].reshape(256, rec)
        value = dot_t(branch_v[...], rows)
        part[0, :, at] = value[:half]
        part[1, :, at] = value[half:]
        return carry

    lax.fori_loop(0, width // 256, out_step, 0)
    part_low[...] = part[1 - core].astype(BF16)
    part_copy = push(part_low, part_in, core_sem.at[0], core_sem.at[1], other)
    part_copy.start()
    go_second = []
    for way, (peer, origin) in enumerate(((x_up, x_down), (x_down, x_up))):
        go_first[way].wait_recv()
        spot = go_all.at[origin, core]
        piece = spot.at[pl.ds(way * (half // 2), half // 2)]
        copy = push(piece, piece, go_send.at[1, way], go_recv.at[1, way], {"x": peer})
        copy.start()
        go_second.append(copy)
        copy = push(spot, spot, go_sib_send.at[1 + way], go_sib_recv.at[1 + way], other)
        copy.start()
        go_across.append(copy)
    part_copy.wait_recv()
    hidden = tokens_ref[mine].astype(F32) + (part[core] + part_in[...].astype(F32))
    hidden_ref[...] = hidden
    hat, inverse, rms = norm(hidden)
    inv_mlp_ref[...] = inverse
    rms_v[...] = jnp.broadcast_to(rms, (half, 128))
    rms_mlp_ref[core] = rms_v[...]
    rms_copy = push(rms_v, rms_mlp_ref.at[core], core_sem.at[2], core_sem.at[3], other)
    rms_copy.start()
    nm_ref[...] = (hat * gain_mlp_ref[...]).astype(BF16)
    for way in range(2):
        go_second[way].wait_recv()
        piece = go_all.at[x_far, core, pl.ds(way * (half // 2), half // 2)]
        copy = push(piece, piece, go_sib_send.at[3 + way], go_sib_recv.at[3 + way], other)
        copy.start()
        go_across.append(copy)
    each(mlp_flows, "hold")
    rms_copy.wait()
    for copy in go_across:
        copy.wait()
    for copy in go_first + go_second:
        copy.wait_send()
    for copy in moves:
        copy.wait_send()
    for copy in saves:
        copy.wait()
    each(lin, "drain")
    each(rest, "drain")
    each(mlp_flows, "drain")
    prefix.drain()
    part_copy.wait_send()
    tail_copy.wait_send()


def rec_forward(tokens, gain_rec, gain_mlp, vectors, masks, w_rec, back, w_mlp, down, cotangent, gates, cid):
    count, width = tokens.shape
    rows, rec = back.shape
    half = count // 2

    def cube(last):
        return (4, 4, 4, rows, last)

    def sds(shape, dtype):
        return jax.ShapeDtypeStruct(shape, dtype)

    saved = [
        (cube(rec), BF16),
        (cube(rec), BF16),
        (cube(rec), BF16),
        (cube(3 * down.shape[1] // 4), BF16),
        ((count + 16, rec), F32),
        ((count, rec), F32),
        ((count, rec), BF16),
        ((count, rec), F32),
        ((count, rec), F32),
        ((count, rec), F32),
        ((count + 8, rec), F32),
        ((count, rec), BF16),
        ((count, width), BF16),
        ((4, 2, half, width), BF16),
    ]
    small = [
        ((count, 1), F32),
        ((count, 1), F32),
        ((half, width), F32),
        ((half, width), BF16),
        ((half, 1), F32),
        ((2, half, 128), F32),
        ((half, width), BF16),
        ((16, rec), F32),
    ]
    scratch = saved[:3] + saved[4:12] + [((count + 16, width), BF16), ((16, width), BF16)]
    scratch += [((count, rec), F32), ((count, rec), F32), ((2, half, width), F32)]
    scratch += [((half, width), BF16), ((half, width), BF16), (gates.shape, BF16), ((half, 128), F32), ((3, 4, 2, rec), F32), ((count, 2), F32)]
    scratch += [((rows, 2 * rec), BF16), ((rows, 2 * w_mlp.shape[2]), BF16)]
    return pl.pallas_call(
        rec_forward_kernel,
        out_shape=[sds(*one) for one in saved + small],
        in_specs=[VM] * 16 + [ANY],
        out_specs=[HBM] * len(saved) + [VM] * len(small),
        scratch_shapes=[pltpu.VMEM(*one) for one in scratch]
        + [
            DMA((2,)),
            DMA,
            DMA((13,)),
            DMA((6,)),
            DMA((3, 3)),
            DMA((3, 3)),
            DMA((11, 3, 2, 3)),
            DMA((11, 3, 2, 3)),
            DMA((1, 3, 3)),
            DMA((1, 3, 3)),
            DMA((4,)),
            DMA((2, 2)),
            DMA((2, 2)),
            DMA((5,)),
            DMA((5,)),
        ],
        compiler_params=params(cid, 60),
    )(tokens, gain_rec[None], gain_mlp[None], *vectors, *masks, w_rec, back, w_mlp, down, cotangent, gates)


G_BIAS, G_LAM, G_CONV_W, G_CONV_B, G_H, G_STATE = 0, 2, 3, 7, 8, 9
GATE_ROWS = 48


def shard_rows(ref, i, value):
    value = value.reshape(2, 4, 32, value.shape[1])
    ref[i // 2, pl.ds(2 * lax.rem(i, 2), 2)] = value


def rec_back_kernel(
    gh_ref, branch_ref, normed_ref, gate_ref, states_ref, f_ref, v_ref, hidden_ref,
    wb_hbm, ext_hbm, mixed_hbm, reset_hbm, input_hbm, g_hbm, wg_hbm, opart_hbm,
    small_ref, part_ref, low, result_ref, dw_out_hbm, dw_gate_hbm, gg_hbm,
    wb, ext, mixed_v, reset_v, input_v, g_v, wg, opart, gate_low, cb, al, gm, dw_out, dw_gate, gg,
    tail, edge, edge_in, slots, result_half,
    *refs,
):
    load_sem, save_sem, small_send, small_recv, edge_sem, core_sem = refs[:6]
    sum_refs = refs[6:]
    count, rec = gate_ref.shape
    half = count // 2
    width = gh_ref.shape[1]
    blocks = rec // BLOCK
    pairs = (
        (wb_hbm, wb), (ext_hbm, ext), (mixed_hbm, mixed_v), (reset_hbm, reset_v), (input_hbm, input_v), (g_hbm, g_v),
        (wg_hbm, wg), (opart_hbm, opart),
    )
    loads = [pltpu.make_async_copy(src, dst, load_sem.at[k]) for k, (src, dst) in enumerate(pairs)]
    for load in loads:
        load.start()
    saves = []

    def save(src, dst):
        copy = pltpu.make_async_copy(src, dst, save_sem.at[len(saves)])
        copy.start()
        saves.append(copy)

    ahead, behind = along_seq(1), along_seq(-1)
    other = {"mp": 1 - lax.axis_index("mp")}
    greet(axis_peers() + [ahead, behind, other])
    place = lax.axis_index("z") * 16 + lax.axis_index("y") * 4 + lax.axis_index("x")
    is_first = jnp.where(place == 0, 1.0, 0.0)
    has_next = jnp.where(place == 63, 0.0, 1.0)

    def weight_grad(ref, left, right):
        def step(i, carry):
            cols = pl.ds(pl.multiple_of(i * 256, 256), 256)
            shard_rows(ref, i, outer(left[:, cols], right[...]).astype(BF16))
            return carry

        loop(0, left.shape[1] // 256, step, 1)

    loads[0].wait()

    def branch_step(n, carry):
        grad = dot(gh_ref[...], wb[:, lanes(n)])
        act, slope = gelu_parts(gate_ref[:, lanes(n)])
        gate_low[:, lanes(n)] = (slope * (grad * states_ref[8:, lanes(n)])).astype(BF16)
        al[:, lanes(n)] = grad * act
        return carry

    loop(0, blocks, branch_step, 1)
    loads[7].wait()
    sums = RingSum(opart, *sum_refs)
    sums.across(FAR, UP, DOWN, ME)

    def group(i, carry):
        base = pl.multiple_of(count - 8 - i * 8, 8)
        f, d = f_ref[pl.ds(base, 8)], al[pl.ds(base, 8)]
        follow, cf, cd = carry
        cfs, cds = [None] * 8, [None] * 8
        for r in (7, 6, 5, 4, 3, 2, 1, 0):
            cf = cf * follow
            cd = cd * follow + d[r : r + 1]
            cfs[r], cds[r] = cf, cd
            follow = f[r : r + 1]
        cb[pl.ds(base, 8)] = jnp.concatenate(cfs, axis=0)
        al[pl.ds(base, 8)] = jnp.concatenate(cds, axis=0)
        return follow, cf, cd

    zero = jnp.zeros((1, rec), F32)
    follow, cf, cd = lax.fori_loop(0, count // 8, group, (zero + 1.0, zero + 1.0, zero))
    prefix = Prefix(slots, small_send, small_recv)
    prefix.start((follow * cf, follow * cd), True)
    weight_grad(dw_out, gh_ref, branch_ref)
    save(dw_out, dw_out_hbm)
    prefix.step()
    sums.far()
    weight_grad(dw_gate, normed_ref, gate_low)
    save(dw_gate, dw_gate_hbm)
    prefix.step()
    for load in loads[1:7]:
        load.wait()

    def part_tile(i, carry):
        at = pl.ds(pl.multiple_of(i * 256, 256), 256)
        value = dot_t(gate_low[...], wg[at, :])
        part_ref[0, :, at] = value[:half]
        part_ref[1, :, at] = value[half:]
        return carry

    lax.fori_loop(0, width // 256, part_tile, 0)
    later = prefix.step()[1]
    sums.near()
    al[...] = al[...] + cb[...] * later

    def grads_step(n, carry):
        at = lanes(n)
        adjoint = al[:, at]
        factors, reset, gated = f_ref[:, at], reset_v[:, at], input_v[:, at]
        mixed_low = mixed_v[:, at]
        mixed = mixed_low.astype(F32)
        rates = v_ref[RATES : RATES + 1, at]
        log_decay = -8.0 * rates * reset
        decays = jnp.exp(log_decay)
        scale_in = jnp.sqrt(minus_expm1(2.0 * log_decay))
        grad_log = adjoint * states_ref[pl.ds(7, count), at] * factors
        grad_log = grad_log - adjoint * gated * mixed * decays * decays / scale_in
        small_ref[G_LAM : G_LAM + 1, at] = (
            8.0 * jnp.sum(grad_log * reset, axis=0, keepdims=True) * v_ref[SLOPE : SLOPE + 1, at]
        )
        small_ref[G_H : G_H + 1, at] = is_first * factors[0:1] * adjoint[0:1]
        grad_reset = (grad_log * (-8.0 * rates) * reset * (1.0 - reset)).astype(BF16)
        grad_input = (adjoint * scale_in * mixed * gated * (1.0 - gated)).astype(BF16)
        for g, grad in enumerate((grad_reset, grad_input)):
            small_ref[G_BIAS + g : G_BIAS + g + 1, at] = jnp.sum(
                grad.astype(F32), axis=0, keepdims=True
            )
            b = g * blocks + n
            rows = pl.ds(pl.multiple_of(16 * lax.rem(b, 3), 16), 16)
            gg[:, :, b // 3, rows, :] = outer(mixed_low, grad).astype(BF16).reshape(4, 4, 16, BLOCK)
        grad_mixed = adjoint * scale_in * gated
        grad_mixed = grad_mixed + dot_t(grad_reset, g_v[0, n]) + dot_t(grad_input, g_v[1, n])
        gm[0:8] = jnp.zeros((8, BLOCK), F32)
        gm[8 : 8 + count] = grad_mixed
        gm[8 + count :] = jnp.zeros((8, BLOCK), F32)
        small_ref[G_CONV_B : G_CONV_B + 1, at] = jnp.sum(grad_mixed, axis=0, keepdims=True)
        total = jnp.zeros((count, BLOCK), F32)
        front = jnp.zeros((8, BLOCK), F32)
        for k in range(CONV):
            small_ref[G_CONV_W + k : G_CONV_W + k + 1, at] = jnp.sum(
                grad_mixed * ext[pl.ds(16 - EDGE + k, count), at], axis=0, keepdims=True
            )
            weight = v_ref[CONV_W + k : CONV_W + k + 1, at]
            total = total + weight * gm[pl.ds(8 + EDGE - k, count)]
            front = front + weight * gm[pl.ds(8 - k, 8)]
        low[:, at] = total.astype(BF16)
        tail[:, at] = total[count - 16 :]
        edge[:, at] = front
        small_ref[G_STATE : G_STATE + EDGE, at] = is_first * front[:EDGE]
        small_ref[G_STATE + EDGE :, at] = jnp.zeros((16 - G_STATE - EDGE, BLOCK), F32)
        return carry

    for x, j in ((3, 1), (3, 2)):
        gg[:, :, x, 16 * j : 16 * j + 16, :] = jnp.zeros((4, 4, 16, BLOCK), BF16)
    loop(0, blocks, grads_step, 1)
    edge_copy = push(edge, edge_in, edge_sem.at[0], edge_sem.at[1], behind)
    edge_copy.start()
    save(gg, gg_hbm)
    core = lax.axis_index("mp")
    result_half[...] = (hidden_ref[...] + sums.total()).astype(BF16)
    result_ref[core] = result_half[...]
    result_copy = push(result_half, result_ref.at[core], core_sem.at[0], core_sem.at[1], other)
    result_copy.start()
    edge_copy.wait_recv()
    last = jnp.concatenate([tail[0:13], tail[13:16] + has_next * edge_in[0:EDGE]], axis=0)
    low[count - 16 :] = last.astype(BF16)
    result_copy.wait()
    for copy in saves:
        copy.wait()
    sums.drain()
    prefix.drain()
    edge_copy.wait_send()


def rec_back(
    gh, branch, normed, gate_lin, states_ext, factors, vectors, hidden,
    w_back, ext, mixed, reset, gated, gates, w_gate, mlp_part, cid,
):
    count, rec = gate_lin.shape
    half, width = hidden.shape

    def like(array):
        return pltpu.VMEM(array.shape, array.dtype)

    wide, low = pltpu.VMEM((count, rec), F32), pltpu.VMEM((count, rec), BF16)
    cube, gate_cube = (4, 4, 4, width // 64, rec), (4, 4, 4, GATE_ROWS, BLOCK)
    return pl.pallas_call(
        rec_back_kernel,
        out_shape=[
            jax.ShapeDtypeStruct((16, rec), F32),
            jax.ShapeDtypeStruct((2, half, width), F32),
            jax.ShapeDtypeStruct((count, rec), BF16),
            jax.ShapeDtypeStruct((2, half, width), BF16),
            jax.ShapeDtypeStruct(cube, BF16),
            jax.ShapeDtypeStruct(cube, BF16),
            jax.ShapeDtypeStruct(gate_cube, BF16),
        ],
        in_specs=[VM] * 8 + [ANY] * 8,
        out_specs=[VM] * 4 + [HBM] * 3,
        scratch_shapes=[
            like(w_back), like(ext), like(mixed), like(reset), like(gated), like(gates), like(w_gate), like(mlp_part),
            low, wide, wide, pltpu.VMEM((count + 16, BLOCK), F32),
            pltpu.VMEM(cube, BF16), pltpu.VMEM(cube, BF16), pltpu.VMEM(gate_cube, BF16),
            pltpu.VMEM((16, rec), F32), pltpu.VMEM((8, rec), F32), pltpu.VMEM((8, rec), F32),
            pltpu.VMEM((3, 4, 2, rec), F32), pltpu.VMEM((half, width), BF16),
            DMA((8,)),
            DMA((3,)),
            DMA((1, 3, 3)),
            DMA((1, 3, 3)),
            DMA((2,)),
            DMA((2,)),
        ]
        + ring_sum_scratch(half, width),
        compiler_params=params(cid, 61),
    )(
        gh, branch, normed, gate_lin, states_ext, factors, vectors, hidden,
        w_back, ext, mixed, reset, gated, gates, w_gate, mlp_part,
    )


def rec_end_kernel(
    part_in_ref, small_ref, gain_term_ref, gh_ref, tokens_in, inverse_ref, gain_ref, normed_ref, low_ref,
    dw0, dw1, gg_hbm, wl_hbm,
    total_ref, gains_ref, all_gates_ref, out0, out1, out2, tokens_hbm,
    *refs,
):
    bufs, refs = refs[: 78 + 3 * 6], refs[78 + 3 * 6 :]
    (
        part, dw2, wl, gates_out, part_low, part_in, tokens_v, gates_ref, ring_gains, gains0, small0, small1, small2,
        load_sem, own_sem, send, recv, gsend, grecv, small_send, small_recv, ring_send, ring_recv, core_sem,
    ) = refs
    half, width = gh_ref.shape
    load = pltpu.make_async_copy(wl_hbm, wl, load_sem.at[0])
    load.start()
    core = lax.axis_index("mp")
    other = {"mp": 1 - core}
    x_here = lax.axis_index("x")
    greet(axis_peers() + [other] + [{"x": peer, "mp": 1 - core} for peer in ring("x")[1:]])
    small = [
        Total(slots, small_send, small_recv, e, ORDERS[e])
        for e, slots in enumerate((small0, small1, small2))
    ]
    for flow, (start, wide) in zip(small, CHUNKS):
        flow.start(small_ref[:, start : start + wide])
    gates = [
        Scatter(
            9 + e, gg_hbm, (0, BLOCK), ORDERS[e], None, bufs[78 + 6 * e : 84 + 6 * e], gates_out,
            own_sem, send, recv, BANDS[e],
        )
        for e in range(3)
    ]
    flows = [
        Scatter(
            e, (dw0, dw1, dw2)[e // 3], CHUNKS[e % 3], SUM_ORDERS[e // 3][e % 3], ROW_HALVES,
            bufs[9 * e : 9 * e + 9] if e < 6 else bufs[8 * e + 6 : 8 * e + 14], (out0, out1, out2)[e // 3],
            own_sem, send, recv, rings=2 if e < 6 else 1,
        )
        for e in range(9)
    ]
    one, two, three = flows[:3], flows[3:6], flows[6:]
    spread = [Gather(e, gates_ref, ORDERS[e], (0, BLOCK), gsend, grecv, band=BANDS[e]) for e in range(3)]

    def each(group, name, *args):
        for flow in group:
            getattr(flow, name)(*args)

    each(gates, "begin", 0)
    each(one, "begin", 0)
    each(two, "begin", 0)

    def weight_grad(i, carry):
        cols = pl.ds(pl.multiple_of(i * 256, 256), 256)
        shard_rows(dw2, i, outer(normed_ref[:, cols], low_ref[...]).astype(BF16))
        return carry

    lax.fori_loop(0, width // 256, weight_grad, 0)
    each(three, "begin", 0)
    each(gates, "finish")
    each(gates, "begin", 1)
    for flow in small:
        flow.step()
    load.wait()

    def part_tile(i, carry):
        at = pl.ds(pl.multiple_of(i * 256, 256), 256)
        value = dot_t(low_ref[...], wl[at, :])
        part[0, :, at] = part_in_ref[0, :, at] + value[:half]
        part[1, :, at] = part_in_ref[1, :, at] + value[half:]
        return carry

    lax.fori_loop(0, width // 256, part_tile, 0)
    part_low[...] = part[1 - core].astype(BF16)
    part_copy = push(part_low, part_in, core_sem.at[0], core_sem.at[1], other)
    part_copy.start()
    each(one, "middle")
    part_copy.wait_recv()
    grad_normed = part[core] + part_in[...].astype(F32)
    mine = pl.ds(pl.multiple_of(core * half, half), half)
    inverse = inverse_ref[mine]
    hat = tokens_in[mine].astype(F32) * inverse
    gain_term = jnp.sum(grad_normed * hat, axis=0, keepdims=True)
    quarter = width // 4
    for k in range(4):
        cols = slice(k * quarter, (k + 1) * quarter)
        ring_gains[x_here, core, k : k + 1] = gain_term[:, cols]
        ring_gains[x_here, core, 4 + k : 5 + k] = gain_term_ref[:, cols]
    shares = []
    spot = ring_gains.at[x_here, core]
    group = [{"x": x, "mp": c} for x in ring("x") for c in (core, 1 - core)][1:]
    for k, peer in enumerate(group):
        copy = push(spot, spot, ring_send.at[k], ring_recv.at[k], peer)
        copy.start()
        shares.append(copy)
    grad_hat = grad_normed * gain_ref[...]
    inner = jnp.mean(grad_hat * hat, axis=-1, keepdims=True)
    tokens_v[...] = gh_ref[...] + inverse * (grad_hat - hat * inner)
    token_copy = push(tokens_v, tokens_hbm.at[core], core_sem.at[2], core_sem.at[3], other)
    token_copy.start()
    token_save = pltpu.make_async_copy(tokens_v, tokens_hbm.at[core], load_sem.at[1])
    token_save.start()
    each(two, "middle")
    each(gates, "finish")
    each(gates, "begin", 2)
    for flow in small:
        flow.step()
    each(one, "finish")
    each(one, "begin", 1)
    for copy in shares:
        copy.wait_recv()
    gains = Total(gains0, small_send, small_recv, 3, ("y", "z"))
    halves = [ring_gains[x, 0] + ring_gains[x, 1] for x in range(4)]
    gains.start((halves[0] + halves[1]) + (halves[2] + halves[3]))
    each(three, "middle")
    each(gates, "finish")
    gates_ref[lax.axis_index("z"), lax.axis_index("y"), x_here] = gates_out[...].astype(BF16)
    each(spread, "begin", 0)
    for flow, (start, wide) in zip(small, CHUNKS):
        total_ref[:, start : start + wide] = flow.step()
    each(two, "finish")
    each(two, "begin", 1)
    gains.step()
    each(one, "middle")
    each(spread, "finish")
    each(spread, "begin", 1)
    each(three, "finish")
    each(three, "begin", 1)
    each(two, "middle")
    each(one, "finish")
    each(one, "begin", 2)
    gains_ref[...] = gains.step()
    each(spread, "finish")
    each(spread, "begin", 2)
    each(two, "finish")
    each(two, "begin", 2)
    each(one, "finish")
    each(three, "finish")
    each(three, "begin", 2)
    each(two, "finish")
    each(spread, "finish")

    def unpack(b, carry):
        at = pl.ds(pl.multiple_of(16 * lax.rem(b, 3), 16), 16)
        all_gates_ref[b] = gates_ref[:, :, b // 3, at, :].reshape(BLOCK, BLOCK).astype(F32)
        return carry

    lax.fori_loop(0, all_gates_ref.shape[0], unpack, 0)
    each(three, "finish")
    for copy in (token_copy, token_save):
        copy.wait()
    each(flows + gates + spread + small, "drain")
    gains.drain()
    for copy in shares + [part_copy]:
        copy.wait_send()


def rec_end(part, small, gain_term, grad_hidden, tokens, inverse, gain, normed, low, weights, gates, w_lin, cid):
    half, width = grad_hidden.shape
    rows, rec = weights[0].shape[3:]
    gate_blocks = 2 * rec // BLOCK

    def sds(*shape):
        return jax.ShapeDtypeStruct(shape, F32)

    bufs = []
    for e in range(9):
        bufs += scatter_buffers(rows, CHUNKS[e % 3][1], 2 if e < 6 else 1)
    for _ in range(3):
        bufs += scatter_buffers(GATE_ROWS // 3, BLOCK, 0)
    return pl.pallas_call(
        rec_end_kernel,
        out_shape=[
            sds(16, rec),
            sds(8, width // 4),
            sds(gate_blocks, BLOCK, BLOCK),
            sds(rows, rec),
            sds(rows, rec),
            sds(rows, rec),
            sds(2, half, width),
        ],
        in_specs=[VM] * 9 + [ANY] * 4,
        out_specs=[VM] * 6 + [HBM],
        scratch_shapes=bufs
        + [
            pltpu.VMEM(part.shape, F32),
            pltpu.VMEM(weights[0].shape, BF16),
            pltpu.VMEM(w_lin.shape, BF16),
            pltpu.VMEM((GATE_ROWS, BLOCK), F32),
            pltpu.VMEM((half, width), BF16),
            pltpu.VMEM((half, width), BF16),
            pltpu.VMEM((half, width), F32),
            pltpu.VMEM(gates.shape, BF16),
            pltpu.VMEM((4, 2, 8, width // 4), F32),
            pltpu.VMEM((2, 4, 8, width // 4), F32),
        ]
        + [pltpu.VMEM((3, 4, 16, wide), F32) for _, wide in CHUNKS]
        + [
            DMA((2,)),
            DMA((12, 3)),
            DMA((12, 3, 3, 3)),
            DMA((12, 3, 3, 3)),
            DMA((3, 3, 1, 3)),
            DMA((3, 3, 1, 3)),
            DMA((4, 3, 3)),
            DMA((4, 3, 3)),
            DMA((7,)),
            DMA((7,)),
            DMA((4,)),
        ],
        compiler_params=params(cid, 60),
    )(part, small, gain_term, grad_hidden, tokens, inverse, gain, normed, low, *weights, gates, w_lin)


def mlp_end_kernel(in_ref, back, send, recv, own_sem):
    x_here = lax.axis_index("x")
    peers = ring("x")[1:]
    greet([{"x": peer} for peer in peers])
    moves = []
    for step, peer in enumerate(peers):
        copy = push(in_ref.at[peer], back.at[x_here], send.at[step], recv.at[step], {"x": peer})
        copy.start()
        moves.append(copy)
    own = pltpu.make_async_copy(in_ref.at[x_here], back.at[x_here], own_sem)
    own.start()
    for copy in moves:
        copy.wait()
    own.wait()


def mlp_end(quarters, cid):
    return pl.pallas_call(
        mlp_end_kernel,
        out_shape=jax.ShapeDtypeStruct(quarters.shape, quarters.dtype),
        in_specs=[HBM],
        out_specs=VM,
        scratch_shapes=[DMA((3,)), DMA((3,)), DMA],
        compiler_params=params(cid, 61),
    )(quarters)


def finish_kernel(
    small_hbm, gains_hbm, out_hbm, gate_hbm, lin_hbm, back_hbm, rms_hbm, rms_mlp_hbm, result_in, tokens_in, gates_in,
    result_ref, tokens_ref, gates_ref, rec_ref, out_ref, mlp_ref, down_ref, bias_ref, lam_ref, conv_w_ref, conv_b_ref,
    gain_rec_ref, gain_mlp_ref, h_ref, state_ref, rms_ref, rms_mlp_ref,
    small_ref, gains_ref, out_sums, gate_sums, lin_sums, back, rms_v, rms_mlp_v, result_v, tokens_v, gates_v, sem, out_sem,
):
    pairs = (
        (result_in, result_v), (tokens_in, tokens_v), (gates_in, gates_v),
        (small_hbm, small_ref), (gains_hbm, gains_ref), (out_hbm, out_sums), (gate_hbm, gate_sums),
        (lin_hbm, lin_sums), (back_hbm, back), (rms_hbm, rms_v), (rms_mlp_hbm, rms_mlp_v),
    )
    loads = [pltpu.make_async_copy(src, dst, sem.at[k]) for k, (src, dst) in enumerate(pairs)]
    for load in loads:
        load.start()
    copies = []
    for k, (src, dst) in enumerate(((result_v, result_ref), (tokens_v, tokens_ref), (gates_v, gates_ref))):
        loads[k].wait()
        copies.append(pltpu.make_async_copy(src, dst, out_sem.at[k]))
        copies[k].start()
    for load in loads[3:]:
        load.wait()
    rec_ref[:, 0, :] = gate_sums[...]
    rec_ref[:, 1, :] = lin_sums[...]
    out_ref[...] = out_sums[...]
    units = down_ref.shape[1] // 4
    for q in range(4):
        value = back[q].astype(F32)
        at = pl.ds(q * units, units)
        for k in range(2):
            mlp_ref[:, k, at] = value[:, k * units : (k + 1) * units]
        down_ref[:, at] = value[:, 2 * units :]
    bias_ref[...] = small_ref[G_BIAS : G_BIAS + 2]
    lam_ref[...] = small_ref[G_LAM]
    conv_w_ref[...] = small_ref[G_CONV_W : G_CONV_W + CONV]
    conv_b_ref[...] = small_ref[G_CONV_B]
    h_ref[...] = small_ref[G_H]
    state_ref[...] = small_ref[G_STATE : G_STATE + EDGE]
    quarter = gains_ref.shape[1]
    for k in range(4):
        at = pl.ds(k * quarter, quarter)
        gain_rec_ref[at] = gains_ref[k]
        gain_mlp_ref[at] = gains_ref[4 + k]
    half = rms_mlp_v.shape[1]
    square = (half, half)
    diagonal = lax.broadcasted_iota(jnp.int32, square, 0) == lax.broadcasted_iota(jnp.int32, square, 1)
    for core in range(2):
        at = pl.ds(core * half, half)
        for ref, column in ((rms_ref, rms_v[at, 0:1]), (rms_mlp_ref, rms_mlp_v[core, :, 0:1])):
            spread = jnp.where(diagonal, jnp.broadcast_to(column, square), 0.0)
            ref[at] = jnp.sum(spread, axis=0)
    for copy in copies:
        copy.wait()


def finish(small, gains, sums, back, rms, rms_mlp, result, tokens, gates):
    rec = small.shape[1]
    rows = back.shape[1]
    units = back.shape[2] // 3
    width = gains.size // 2

    def sds(*shape):
        return jax.ShapeDtypeStruct(shape, F32)

    return pl.pallas_call(
        finish_kernel,
        out_shape=[
            jax.ShapeDtypeStruct(result.shape, result.dtype),
            sds(*tokens.shape),
            sds(*gates.shape),
            sds(rows, 2, rec),
            sds(rows, rec),
            sds(rows, 2, 4 * units),
            sds(rows, 4 * units),
            sds(2, rec),
            sds(rec),
            sds(CONV, rec),
            sds(rec),
            sds(width),
            sds(width),
            sds(rec),
            sds(EDGE, rec),
            sds(rms.shape[0]),
            sds(rms.shape[0]),
        ],
        in_specs=[HBM] * 11,
        out_specs=[HBM] * 3 + [VM] * 14,
        scratch_shapes=[pltpu.VMEM(a.shape, a.dtype) for a in (small, gains, *sums, back, rms, rms_mlp, result, tokens, gates)]
        + [DMA((11,)), DMA((3,))],
        compiler_params=pltpu.CompilerParams(vmem_limit_bytes=61 * MIB),
    )(small, gains, *sums, back, rms, rms_mlp, result, tokens, gates)


def body(
    tokens,
    cotangent,
    starts,
    valid,
    w_rec,
    w_out,
    w_mlp,
    w_down,
    lru_gates,
    lru_bias,
    lam,
    conv_w,
    conv_b,
    gain_rec,
    gain_mlp,
    h_init,
    conv_state,
):
    count, width = tokens.shape
    shard, _, rec = w_rec.shape
    hidden_units = w_mlp.shape[2] // 4
    half = count // 2
    core = lax.axis_index("mp")

    (
        w_lin, w_gate, w_back, mlp_weights, ext, gate_lin, mixed, reset, gated, factors, states_ext, branch_in,
        normed_rec, grad_out_all, inverse_rec, rms_rec, hidden, normed_mlp, inverse_mlp, rms_half, grad_out, vectors,
    ) = rec_forward(
        tokens,
        gain_rec,
        gain_mlp,
        (conv_w, conv_b, lam, lru_bias, conv_state, h_init),
        (starts, valid),
        w_rec,
        w_out.T,
        w_mlp,
        w_down.T,
        cotangent,
        lru_gates,
        0,
    )
    w_lin, w_gate, w_back = (w.reshape(width, rec) for w in (w_lin, w_gate, w_back))
    grad_hidden, grad_hidden_low, gain_mlp_term, mlp_terms, mlp_part = mlp(
        normed_mlp, grad_out, hidden, inverse_mlp, gain_mlp[None], grad_out_all, mlp_weights, 1
    )
    mlp_sums = lax.psum_scatter(mlp_terms, ("z", "y"), scatter_dimension=0, tiled=True)
    grad_hidden_low = grad_hidden_low.reshape(count, width)
    small, normed_part, grad_rec_low, result, *weight_terms, gate_terms = rec_back(
        grad_hidden_low,
        branch_in,
        normed_rec,
        gate_lin,
        states_ext,
        factors,
        vectors,
        hidden,
        w_back,
        ext,
        mixed,
        reset,
        gated,
        lru_gates,
        w_gate,
        mlp_part,
        2,
    )
    small, gains, gate_blocks, out_sums, gate_sums, lin_sums, grad_tokens = rec_end(
        normed_part,
        small,
        gain_mlp_term,
        grad_hidden,
        tokens,
        inverse_rec,
        gain_rec[None],
        normed_rec,
        grad_rec_low,
        weight_terms,
        gate_terms,
        w_lin,
        3,
    )
    back = mlp_end(mlp_sums.reshape(4, shard, 3 * hidden_units), 4)
    (
        result, grad_tokens, grad_gates, grad_w_rec, grad_out_t, grad_w_mlp, grad_down_t, grad_bias, grad_lam,
        grad_conv_w, conv_bias_gradient, grad_gain_rec, grad_gain_mlp, grad_h_init, grad_conv_state, rms_rec, rms_mlp,
    ) = finish(
        small,
        gains,
        (out_sums, gate_sums, lin_sums),
        back,
        rms_rec,
        rms_half,
        result.reshape(count, width),
        grad_tokens.reshape(count, width),
        gate_blocks.reshape(lru_gates.shape),
    )
    return (
        result,
        rms_rec,
        rms_mlp,
        grad_tokens,
        grad_w_rec,
        grad_out_t.T,
        grad_w_mlp,
        grad_down_t.T,
        grad_gates,
        grad_bias,
        grad_lam,
        grad_conv_w,
        conv_bias_gradient,
        grad_gain_rec,
        grad_gain_mlp,
        grad_h_init,
        grad_conv_state,
    )


def solution(mesh):
    cube = Mesh(mesh.devices.reshape(4, 4, 4, 2), ("z", "y", "x", "mp"))
    placed = (
        P(SEQ, None),
        P(SEQ, None),
        P(SEQ),
        P(SEQ),
        P(SEQ, None, "mp"),
        P("mp", SEQ),
        P(SEQ, None, "mp"),
        P("mp", SEQ),
        P(None, "mp", None, None),
        P(None, "mp"),
        P("mp"),
        P(None, "mp"),
        P("mp"),
        P(),
        P(),
        P("mp"),
        P(None, "mp"),
    )
    return jax.shard_map(
        body,
        mesh=cube,
        in_specs=placed,
        out_specs=(
            P(SEQ, None),
            P(SEQ),
            P(SEQ),
            P(SEQ, None),
            P(SEQ, None, "mp"),
            P("mp", SEQ),
            P(SEQ, None, "mp"),
            P("mp", SEQ),
            P(None, "mp", None, None),
            P(None, "mp"),
            P("mp"),
            P(None, "mp"),
            P("mp"),
            P(),
            P(),
            P("mp"),
            P(None, "mp"),
        ),
        check_vma=False,
    )
```
